32 devices in a mesh: groups: 2 (over x), dp: 8 (over z, y), tp: 2 (over core).
Axes of the slice: x: 2, y: 2, z: 4, core: 2. Of those that a mesh axis runs over, the one named last changes fastest.
Arguments:
- pre_x: bfloat16 [2048, 12288], P(('groups', 'dp')), parts along dimension 0, may hold values from -6 to 6
- dec_x: bfloat16 [512, 12288], P(('groups', 'dp')), parts along dimension 0, may hold values from -6 to 6
- w_kv: bfloat16 [12288, 1024], P('dp', 'tp'), may hold values from -127 to 127, as said below
- kv_scale: float32 [1024], P('tp')
- dec_q: bfloat16 [512, 6144], P(('groups', 'dp'), 'tp'), parts along dimension 0
- cache: bfloat16 [512, 256, 1024], P(('groups', 'dp'), None, 'tp'), parts along dimension 0
- cache_len: int32 [512], P(('groups', 'dp')), parts along dimension 0, may hold values from 2 to 256
- prompt_owner: int32 [16], P('groups'), parts along dimension 0, may hold values from 0 to 7, each once
- prompt_len: int32 [16], P('groups'), parts along dimension 0, may hold values from 1 to 128, 512 in all
- sample_rows: int32 [16, 16], P('groups'), parts along dimension 0, may hold values from 0 to 255, as said below
Outputs:
- attended: bfloat16 [512, 6144], P(('groups', 'dp'), 'tp'), parts along dimension 0
- prompt_kv: bfloat16 [2048, 1024], P(('groups', 'dp'), 'tp'), parts along dimension 0
The draws below stay inside these ranges and needn't reach their ends.
There are 2 independent parts, one for each index of `groups`. The reference program is written for one: setup_inputs(seed, part) draws one part's arguments, and reference() takes and returns one part's arrays. A program takes and returns all parts, laid end to end along the dimension named above; an argument that names none is the same for every part. Nothing has to cross between parts.
Inputs may be any that keep to these rules, and one draw needn't show every extreme that they name: `sample_rows`: all entries distinct. `w_kv`: whole numbers.
All inputs are finite; a program needn't handle non-finite values.
Results may differ from the reference program's by a relative error of at most 0.0065.
Values may be sent and summed in bfloat16 or wider, within the bound.
No kernel may reach another device: no remote copies, remote signals or barrier semaphores. Data moves between devices by JAX's collectives and lax.ppermute only.
A program may use at most 128 MiB of HBM per device.

```python
import math
import jax
import jax.numpy as jnp
import numpy as np
from jax import lax

D = 12288
KVH = 4
HD = 128
REP = 12
GROUP = 16
SPAN = 128
CACHE = 256
NP = 8
SAMPLES = 256


def attention_base(key):
    first, second = jax.random.split(key, 2)
    stored = jax.random.normal(first, (SAMPLES, CACHE, KVH, 2, HD), jnp.float32)
    query = jax.random.normal(second, (SAMPLES, KVH, REP, HD), jnp.float32)
    return (stored, query)


def draw_cache(key, part):
    stored, query = attention_base(key)
    return stored.reshape(SAMPLES, CACHE, KVH * 2 * HD).astype(jnp.bfloat16)


def draw_dec_q(key, part):
    stored, query = attention_base(key)
    return query.reshape(SAMPLES, KVH * REP * HD).astype(jnp.bfloat16)


def draw_w_kv(key, part):
    key = jax.random.fold_in(key, 9)
    levels = jax.random.randint(key, (D, KVH * 2 * HD), -127, 128)
    return levels.astype(jnp.float32).astype(jnp.bfloat16)


def draw_kv_scale(key, part):
    key = jax.random.fold_in(key, 10)
    spread = jax.random.uniform(key, (KVH * 2 * HD,), jnp.float32, math.log(0.5), math.log(2.0))
    return jnp.exp(spread) / (73.3 * math.sqrt(D))


def draw_sample_rows(key, part):
    key = jax.random.fold_in(key, 11)
    first, second = jax.random.split(key)
    middle = (jax.random.permutation(first, SAMPLES - 2) + 1).astype(jnp.int32)
    ends = jnp.array([0, SAMPLES - 1], jnp.int32)
    chosen = jnp.concatenate([ends, middle[:NP * GROUP - 2]])
    return jax.random.permutation(second, chosen).reshape(NP, GROUP).astype(jnp.int32)


def draw_cache_len(key, part):
    key = jax.random.fold_in(key, 13)
    first, second = jax.random.split(key)
    lengths = jax.random.randint(first, (SAMPLES,), 2, CACHE + 1)
    spots = jax.random.permutation(second, SAMPLES)[:2]
    lengths = lengths.at[spots[0]].set(CACHE).at[spots[1]].set(2)
    return lengths.astype(jnp.int32)


def block_scale(stream_key, shape, cuts, least, high):
    loudness, own = 1.0, jax.random.fold_in(stream_key, 6)
    for axis_at, parts in cuts:
        steps = jnp.exp(jax.random.uniform(jax.random.fold_in(own, axis_at), (parts,), jnp.float32, least / len(cuts), high / len(cuts)))
        loudness = loudness * jnp.repeat(steps, shape[axis_at] // parts).reshape([-1 if axis == axis_at else 1 for axis in range(len(shape))])
    return loudness


def length_profile(number_of, total, bound, slope):
    loads = [(1 << 20) // math.isqrt(grade ** slope) + 1 for grade in range(2, number_of + 1)]
    rest, holding = total - bound - (number_of - 1), [1] * (number_of - 1)
    while rest > 0:
        movable = [i for i in range(number_of - 1) if holding[i] < bound]
        pool, left = sum([loads[i] for i in movable]), rest
        for i in movable:
            more = min(bound - holding[i], max(1, left * loads[i] // pool), rest)
            holding[i] = holding[i] + more
            rest = rest - more
    return np.array([bound] + holding)


def ragged_sizes(key, count, total, most, skew):
    if count == 2:
        one = jax.random.randint(key, (), max(1, total - most), min(most, total - 1) + 1)
        return jnp.stack([one, total - one])
    sizes = jnp.asarray(length_profile(count, total, most, skew), jnp.int32)
    couples = (count - 1) // 2
    source_of, taker = sizes[1:1 + 2 * couples:2], sizes[2:2 + 2 * couples:2]
    margin = jnp.minimum(source_of - 1, most - taker)
    passed = jax.random.randint(jax.random.fold_in(key, 1), (couples,), 0, 1 << 20) % (margin + 1)
    sizes = sizes.at[1:1 + 2 * couples:2].set(source_of - passed).at[2:2 + 2 * couples:2].set(taker + passed)
    return sizes[jax.random.permutation(jax.random.fold_in(key, 2), count)]


def scatter_about(rng, extent, scale, reach, pieces=(), held_as=jnp.bfloat16):
    values = scale * jax.random.normal(rng, extent, jnp.float32)
    if pieces:
        values = values * block_scale(rng, extent, pieces, -0.22, 0.18)
    return jnp.clip(values, -reach, reach).astype(held_as)


def setup_inputs(seed: int = 0, part: int = 0) -> dict:
    keys = jax.random.split(jax.random.key(seed), 11)
    part_splits = jax.random.split(jax.random.fold_in(keys[10], part), 11)
    return {
        "pre_x": scatter_about(part_splits[0], (NP * SPAN, D), 1.0, 6.0, ((0, 8),)),
        "dec_x": scatter_about(part_splits[1], (SAMPLES, D), 1.0, 6.0, ((0, 8),)),
        "w_kv": draw_w_kv(jax.random.fold_in(keys[10], 71), part),
        "kv_scale": draw_kv_scale(jax.random.fold_in(keys[10], 71), part),
        "dec_q": draw_dec_q(jax.random.fold_in(jax.random.fold_in(keys[10], part), 71), part),
        "cache": draw_cache(jax.random.fold_in(jax.random.fold_in(keys[10], part), 71), part),
        "cache_len": draw_cache_len(jax.random.fold_in(jax.random.fold_in(keys[10], part), 71), part),
        "prompt_owner": jax.random.permutation(part_splits[7], NP).astype(jnp.int32),
        "prompt_len": ragged_sizes(part_splits[8], NP, NP * SPAN // 2, SPAN, 1).astype(jnp.int32),
        "sample_rows": draw_sample_rows(jax.random.fold_in(jax.random.fold_in(keys[10], part), 71), part),
    }


NEG = -1e+30

def split_heads(block, heads):
    shaped = block.reshape(block.shape[:-1] + (heads, 2, block.shape[-1] // (2 * heads)))
    return (shaped[..., 0, :], shaped[..., 1, :])

def reference(pre_x, dec_x, w_kv, kv_scale, dec_q, cache, cache_len, prompt_owner, prompt_len, sample_rows):
    rows = jnp.concatenate([pre_x, dec_x], 0)
    kv = (jnp.dot(rows, w_kv, preferred_element_type=jnp.float32) * kv_scale).astype(jnp.bfloat16)
    prompt_kv = kv[:NP * SPAN]
    own_kv = kv[NP * SPAN:]
    order = jnp.repeat(jnp.arange(NP, dtype=jnp.int32), GROUP)
    sample_prompt = jnp.full((SAMPLES,), -1, jnp.int32).at[sample_rows.reshape(-1)].set(order)
    found = sample_prompt >= 0
    chosen = jnp.maximum(sample_prompt, 0)
    source = prompt_owner[chosen]
    live = jnp.where(found, prompt_len[chosen], 0)
    table = prompt_kv.reshape(NP, SPAN, KVH * 2 * HD)
    factor = 1.0 / math.sqrt(HD)
    block = 32

    def one_block(start):
        query = lax.dynamic_slice_in_dim(dec_q, start, block, 0).astype(jnp.float32).reshape(block, KVH, REP, HD)
        stored = lax.dynamic_slice_in_dim(cache, start, block, 0).astype(jnp.float32)
        lens = lax.dynamic_slice_in_dim(cache_len, start, block, 0)
        picks = lax.dynamic_slice_in_dim(source, start, block, 0)
        lives = lax.dynamic_slice_in_dim(live, start, block, 0)
        own = lax.dynamic_slice_in_dim(own_kv, start, block, 0).astype(jnp.float32)
        prompt_block = table[picks].astype(jnp.float32)
        cache_k, cache_v = split_heads(stored, KVH)
        prompt_k, prompt_v = split_heads(prompt_block, KVH)
        own_k, own_v = split_heads(own, KVH)
        score_c = jnp.einsum('bhrd,bjhd->bhrj', query, cache_k) * factor
        mask_c = jnp.arange(CACHE)[None, :] < lens[:, None]
        score_c = jnp.where(mask_c[:, None, None, :], score_c, NEG)
        score_p = jnp.einsum('bhrd,bjhd->bhrj', query, prompt_k) * factor
        mask_p = jnp.arange(SPAN)[None, :] < lives[:, None]
        score_p = jnp.where(mask_p[:, None, None, :], score_p, NEG)
        score_o = jnp.einsum('bhrd,bhd->bhr', query, own_k)[..., None] * factor
        scores = jnp.concatenate([score_c, score_p, score_o], -1)
        top = lax.optimization_barrier(jnp.max(scores, -1, keepdims=True))
        weights = jnp.exp(scores - top)
        total = lax.optimization_barrier(jnp.sum(weights, -1))
        mixed = jnp.einsum('bhrj,bjhd->bhrd', weights[..., :CACHE], cache_v)
        mixed = mixed + jnp.einsum('bhrj,bjhd->bhrd', weights[..., CACHE:CACHE + SPAN], prompt_v)
        mixed = mixed + weights[..., CACHE + SPAN:] * own_v[:, :, None, :]
        return (mixed / total[..., None]).reshape(block, KVH * REP * HD).astype(jnp.bfloat16)
    starts = jnp.arange(SAMPLES // block, dtype=jnp.int32) * block
    attended = lax.map(one_block, starts).reshape(SAMPLES, KVH * REP * HD)
    return (attended, prompt_kv)
```

```python
import functools
import math

import jax
import jax.numpy as jnp
from jax import lax
from jax.sharding import PartitionSpec as P

HD = 128
REP = 12
NEG = -1e30
INNER = 4


def local(
    pre_x,
    dec_x,
    w_kv,
    kv_scale,
    dec_q,
    cache,
    cache_len,
    prompt_owner,
    prompt_len,
    sample_rows,
    *,
    shape,
):
    teams, ranks, cores = shape["groups"], shape["dp"], shape["tp"]
    inner = INNER
    outer = ranks // inner
    span, features = pre_x.shape
    count = dec_x.shape[0]
    depth, width = w_kv.shape
    heads = width // (2 * HD)
    slab = depth // teams
    factor = 1.0 / math.sqrt(HD)
    team = lax.axis_index("groups")
    rank = lax.axis_index("dp")
    core = lax.axis_index("tp")
    place, block = rank % inner, rank // inner

    def to_inner(value, step):
        pairs = [(r, r // inner * inner + (r % inner ^ step)) for r in range(ranks)]
        return lax.ppermute(value, "dp", pairs)

    def to_outer(value, step=1):
        pairs = [(r, (r + step * inner) % ranks) for r in range(ranks)]
        return lax.ppermute(value, "dp", pairs)

    def to_team(value, step):
        return lax.ppermute(value, "groups", [(i, (i + step) % teams) for i in range(teams)])

    def to_core(value, step):
        return lax.ppermute(value, "tp", [(i, (i + step) % cores) for i in range(cores)])

    slabs = [w_kv]
    moving = lax.dynamic_slice_in_dim(w_kv, team * slab, slab, 0)
    for step in range(1, outer):
        moving = to_outer(moving)
        slabs.append(moving)
        for other in range(1, teams):
            slabs.append(to_team(moving, other))

    pre_share, dec_share = span // cores, count // cores

    def share(which, owner):
        columns = [((block % outer) * inner + owner) * depth]
        sizes = [depth]
        for step in range(1, outer):
            start = (((block - step) % outer) * inner + owner) * depth
            for other in range(teams):
                columns.append(start + (team - other) % teams * slab)
                sizes.append(slab)
        pieces = []
        for at, size in zip(columns, sizes):
            pieces.append(
                jnp.concatenate(
                    [
                        lax.dynamic_slice(pre_x, (which * pre_share, at), (pre_share, size)),
                        lax.dynamic_slice(dec_x, (which * dec_share, at), (dec_share, size)),
                    ],
                    0,
                )
            )
        return jnp.concatenate(pieces, 1)

    rows = [share((core - step) % cores, place) for step in range(cores)]
    for step in range(1, inner):
        arrived = to_inner(share(core, place ^ step), step)
        rows.append(arrived)
        for other in range(1, cores):
            rows.append(to_core(arrived, other))
    rows = jnp.concatenate(rows, 0)
    at = 0
    summed = 0.0
    for piece in slabs:
        summed = summed + jnp.dot(
            rows[:, at : at + piece.shape[0]], piece, preferred_element_type=jnp.float32
        )
        at += piece.shape[0]
    total_rows = span + count
    mine = summed[:total_rows]
    for step in range(1, inner):
        part = summed[step * total_rows : (step + 1) * total_rows].astype(jnp.bfloat16)
        mine = mine + to_inner(part, step).astype(jnp.float32)
    kv = (mine * kv_scale).astype(jnp.bfloat16)
    shares = kv.reshape(cores, pre_share + dec_share, width)
    order = [(core - which) % cores for which in range(cores)]
    shares = [lax.dynamic_index_in_dim(shares, at, 0, False) for at in order]
    prompt_kv = jnp.concatenate([s[:pre_share] for s in shares], 0)
    own_kv = jnp.concatenate([s[pre_share:] for s in shares], 0)

    blocks = [prompt_kv]
    moving = prompt_kv
    for step in range(1, outer):
        moving = to_outer(moving)
        blocks.append(moving)
    column = jnp.concatenate(blocks, 0)
    gathered = [column] + [to_inner(column, step) for step in range(1, inner)]
    owners = [
        ((block - back) % outer) * inner + (place ^ step)
        for step in range(inner)
        for back in range(outer)
    ]
    piece = jnp.concatenate(gathered, 0)
    owner = jnp.repeat(jnp.stack(owners).astype(jnp.int32), span)
    position = jnp.tile(jnp.arange(span, dtype=jnp.int32), ranks)

    global_rows = rank * count + jnp.arange(count, dtype=jnp.int32)
    prompts = sample_rows.shape[0]
    match = sample_rows[:, :, None] == global_rows[None, None, :]
    found = jnp.any(match, axis=(0, 1))
    prompt_ids = jnp.arange(prompts, dtype=jnp.int32)
    chosen = jnp.sum(jnp.where(match, prompt_ids[:, None, None], 0), axis=(0, 1))
    picks = chosen[:, None] == prompt_ids[None, :]
    source = jnp.sum(jnp.where(picks, prompt_owner[None, :], 0), 1)
    live = jnp.where(found, jnp.sum(jnp.where(picks, prompt_len[None, :], 0), 1), 0)

    cache_mask = (jnp.arange(cache.shape[1])[None, :] < cache_len[:, None])[:, None, :]
    piece_mask = (owner[None, :] == source[:, None]) & (position[None, :] < live[:, None])
    query = dec_q.reshape(count, heads, REP, HD)
    outs = []
    for head in range(heads):
        low, mid, high = head * 2 * HD, head * 2 * HD + HD, head * 2 * HD + 2 * HD
        q = query[:, head]
        score_c = jnp.einsum(
            "srd,sjd->srj", q, cache[:, :, low:mid], preferred_element_type=jnp.float32
        )
        score_c = jnp.where(cache_mask, score_c * factor, NEG)
        top_c = jnp.max(score_c, -1)
        weight_c = jnp.exp(score_c - top_c[..., None])
        total_c = jnp.sum(weight_c, -1)
        mixed_c = jnp.einsum(
            "srj,sjd->srd",
            weight_c.astype(jnp.bfloat16),
            cache[:, :, mid:high],
            preferred_element_type=jnp.float32,
        )
        own_k, own_v = own_kv[:, low:mid], own_kv[:, mid:high]
        score_o = jnp.einsum("srd,sd->sr", q, own_k, preferred_element_type=jnp.float32) * factor
        top_1 = jnp.maximum(top_c, score_o)
        shrink = jnp.exp(top_c - top_1)
        weight_o = jnp.exp(score_o - top_1)
        total_1 = total_c * shrink + weight_o
        mixed_1 = (
            mixed_c * shrink[..., None]
            + weight_o[..., None] * own_v.astype(jnp.float32)[:, None, :]
        )
        score_p = jnp.einsum(
            "srd,jd->srj", q, piece[:, low:mid], preferred_element_type=jnp.float32
        )
        score_p = jnp.where(piece_mask[:, None, :], score_p * factor, NEG)
        top_2 = jnp.maximum(top_1, jnp.max(score_p, -1))
        shrink = jnp.exp(top_1 - top_2)
        weight_p = jnp.exp(score_p - top_2[..., None])
        total_2 = total_1 * shrink + jnp.sum(weight_p, -1)
        mixed_2 = mixed_1 * shrink[..., None] + jnp.einsum(
            "srj,jd->srd",
            weight_p.astype(jnp.bfloat16),
            piece[:, mid:high],
            preferred_element_type=jnp.float32,
        )
        outs.append((mixed_2 / total_2[..., None]).reshape(count, REP * HD))
    attended = jnp.concatenate(outs, 1).astype(jnp.bfloat16)
    return (attended, prompt_kv)


def solution(mesh):
    in_specs = (
        P(("groups", "dp"), None),
        P(("groups", "dp"), None),
        P("dp", "tp"),
        P("tp"),
        P(("groups", "dp"), "tp"),
        P(("groups", "dp"), None, "tp"),
        P(("groups", "dp")),
        P("groups"),
        P("groups"),
        P("groups", None),
    )
    out_specs = (P(("groups", "dp"), "tp"), P(("groups", "dp"), "tp"))
    body = functools.partial(local, shape=dict(mesh.shape))
    return jax.shard_map(body, mesh=mesh, in_specs=in_specs, out_specs=out_specs, check_vma=False)
```

```python
import functools
import math

import jax
import jax.numpy as jnp
from jax import lax
from jax.experimental import pallas as pl
from jax.experimental.pallas import tpu as pltpu
from jax.sharding import PartitionSpec as P

HD = 128
REP = 12
NEG = -1e30
INNER = 4


def copy_kernel(plan, n_in, n_out, at_ref, *refs):
    ins, outs, sems = refs[:n_in], refs[n_in : n_in + n_out], refs[n_in + n_out]
    copies = []
    for number, (src, shape, row, column, dst, to_row, to_column) in enumerate(plan):
        from_row = pl.multiple_of(at_ref[row], 16)
        from_column = pl.multiple_of(at_ref[column], 128)
        copy = pltpu.make_async_copy(
            ins[src].at[pl.ds(from_row, shape[0]), pl.ds(from_column, shape[1])],
            outs[dst].at[pl.ds(to_row, shape[0]), pl.ds(to_column, shape[1])],
            sems.at[number],
        )
        copy.start()
        copies.append(copy)
    for copy in copies:
        copy.wait()


def attend_kernel(
    heads,
    span,
    n_blocks,
    owner_ref,
    q_ref,
    source_ref,
    live_ref,
    top_ref,
    total_ref,
    mixed_ref,
    own_ref,
    *refs,
):
    blocks, out_ref = refs[:n_blocks], refs[n_blocks]
    count = q_ref.shape[0]
    factor = 1.0 / math.sqrt(HD)
    source = source_ref[...]
    live = live_ref[...]
    place = lax.broadcasted_iota(jnp.int32, (REP * count, span), 1)
    for head in range(heads):
        first = head * REP * HD
        low, mid, high = head * 2 * HD, head * 2 * HD + HD, head * 2 * HD + 2 * HD
        q = jnp.concatenate(
            [q_ref[:, first + r * HD : first + (r + 1) * HD] for r in range(REP)], 0
        )
        picked = jnp.zeros((REP * count, span), jnp.float32)
        for at in range(n_blocks):
            scores = lax.dot_general(
                q,
                blocks[at][:, low:mid],
                (((1,), (1,)), ((), ())),
                preferred_element_type=jnp.float32,
            )
            picked = jnp.where(source == owner_ref[at], scores, picked)
        picked = jnp.where(place < live, picked * factor, NEG)
        own_k = jnp.concatenate([own_ref[:, low:mid].astype(jnp.float32)] * REP, 0)
        own_v = jnp.concatenate([own_ref[:, mid:high].astype(jnp.float32)] * REP, 0)
        score_o = jnp.sum(q.astype(jnp.float32) * own_k, -1, keepdims=True) * factor
        top_c = top_ref[head]
        top = jnp.maximum(jnp.max(picked, -1, keepdims=True), jnp.maximum(top_c, score_o))
        weights = jnp.exp(picked - top)
        weight_o = jnp.exp(score_o - top)
        shrink = jnp.exp(top_c - top)
        total = (
            total_ref[head] * shrink + weight_o + jnp.sum(weights, -1, keepdims=True)
        )
        mixed = mixed_ref[head] * shrink + weight_o * own_v
        for at in range(n_blocks):
            mixed = mixed + jnp.dot(
                jnp.where(source == owner_ref[at], weights, 0.0).astype(jnp.bfloat16),
                blocks[at][:, mid:high],
                preferred_element_type=jnp.float32,
            )
        mixed = mixed / total
        for r in range(REP):
            out_ref[:, first + r * HD : first + (r + 1) * HD] = mixed[
                r * count : (r + 1) * count
            ].astype(out_ref.dtype)


def attend(owners, query, source, live, top, total, mixed, own_kv, blocks, heads):
    count = query.shape[0]
    span = blocks[0].shape[0]
    vmem = pl.BlockSpec(memory_space=pltpu.VMEM)
    return pl.pallas_call(
        functools.partial(attend_kernel, heads, span, len(blocks)),
        out_shape=jax.ShapeDtypeStruct(query.shape, jnp.bfloat16),
        in_specs=[pl.BlockSpec(memory_space=pltpu.SMEM)] + [vmem] * (7 + len(blocks)),
        out_specs=vmem,
        compiler_params=pltpu.CompilerParams(vmem_limit_bytes=48 * 1024 * 1024),
        cost_estimate=pl.CostEstimate(
            flops=4 * heads * REP * count * span * len(blocks) * HD,
            bytes_accessed=4 * 1024 * 1024,
            transcendentals=heads * REP * count * span,
        ),
    )(owners, query, source, live, top, total, mixed, own_kv, *blocks)


def stages(depth):
    unit = 128
    first = max(unit, depth // 6 // unit * unit)
    second = (depth - first) // 2 // unit * unit
    return (first, second, depth - first - second)


def local(
    pre_x,
    dec_x,
    w_kv,
    kv_scale,
    dec_q,
    cache,
    cache_len,
    prompt_owner,
    prompt_len,
    sample_rows,
    *,
    shape,
):
    teams, ranks, cores = shape["groups"], shape["dp"], shape["tp"]
    inner = INNER
    outer = ranks // inner
    span, features = pre_x.shape
    count = dec_x.shape[0]
    depth, width = w_kv.shape
    heads = width // (2 * HD)
    band = width // teams
    factor = 1.0 / math.sqrt(HD)
    team = lax.axis_index("groups")
    rank = lax.axis_index("dp")
    core = lax.axis_index("tp")
    place, block = rank % inner, rank // inner

    def to_inner(value, step):
        pairs = [(r, r // inner * inner + (r % inner ^ step)) for r in range(ranks)]
        return lax.ppermute(value, "dp", pairs)

    def to_outer(value, step=1):
        pairs = [(r, (r + step * inner) % ranks) for r in range(ranks)]
        return lax.ppermute(value, "dp", pairs)

    def to_team(value, step):
        return lax.ppermute(value, "groups", [(i, (i + step) % teams) for i in range(teams)])

    def to_core(value, step):
        return lax.ppermute(value, "tp", [(i, (i + step) % cores) for i in range(cores)])

    sizes = stages(depth)
    pre_share, dec_share = span // cores, count // cores
    both = pre_share + dec_share
    spots = [0, team * band, core * pre_share, core * dec_share]
    plan, outs = [], []
    at = 0
    for size in sizes:
        spots.append(jnp.int32(at))
        plan.append((2, (size, band), len(spots) - 1, 1, len(outs), 0, 0))
        outs.append(jax.ShapeDtypeStruct((size, band), jnp.bfloat16))
        at += size
    for step in range(1, inner):
        for back in range(outer):
            spots.append((((block - back) % outer) * inner + (place ^ step)) * depth)
            column = len(spots) - 1
            plan.append((0, (pre_share, depth), 2, column, len(outs), 0, back * depth))
            plan.append((1, (dec_share, depth), 3, column, len(outs), pre_share, back * depth))
        outs.append(jax.ShapeDtypeStruct((both, outer * depth), jnp.bfloat16))
    spots = jnp.stack([jnp.asarray(s, jnp.int32) for s in spots])
    hbm = pl.BlockSpec(memory_space=pl.ANY)
    sends = pl.pallas_call(
        functools.partial(copy_kernel, plan, 3, len(outs)),
        out_shape=outs,
        in_specs=[pl.BlockSpec(memory_space=pltpu.SMEM)] + [hbm] * 3,
        out_specs=[hbm] * len(outs),
        scratch_shapes=[pltpu.SemaphoreType.DMA((len(plan),))],
    )(spots, pre_x, dec_x, w_kv)
    moving, row_sends = list(sends[: len(sizes)]), sends[len(sizes) :]

    far = []
    for back in range(1, outer):
        for piece in range(len(sizes)):
            if piece >= 2 and back == 1:
                moving[piece], _ = lax.optimization_barrier((moving[piece], moving[piece - 2]))
            moving[piece] = to_outer(moving[piece])
        far.append([[m] + [to_team(m, turn) for turn in range(1, teams)] for m in moving])

    def local_share(which, back):
        column = (((block - back) % outer) * inner + place) * depth
        return jnp.concatenate(
            [
                lax.dynamic_slice(pre_x, (which * pre_share, column), (pre_share, depth)),
                lax.dynamic_slice(dec_x, (which * dec_share, column), (dec_share, depth)),
            ],
            0,
        )

    arrived = []
    for step in range(1, inner):
        got = to_inner(row_sends[step - 1], step)
        arrived.append(got)
        for turn in range(1, cores):
            arrived.append(to_core(got, turn))
    rows = [
        jnp.concatenate(
            [local_share((core - turn) % cores, back) for turn in range(cores)]
            + [a[:, back * depth : (back + 1) * depth] for a in arrived],
            0,
        )
        for back in range(outer)
    ]
    near = jnp.dot(rows[0], w_kv, preferred_element_type=jnp.float32)
    total_rows = span + count
    bands = []
    for turn in range(teams):
        column = (team - turn) % teams * band
        summed = lax.dynamic_slice(near, (0, column), (near.shape[0], band))
        for back in range(1, outer):
            at = 0
            for piece, size in enumerate(sizes):
                summed = summed + jnp.dot(
                    rows[back][:, at : at + size],
                    far[back - 1][piece][turn],
                    preferred_element_type=jnp.float32,
                )
                at += size
        mine = summed[:total_rows]
        for step in range(1, inner):
            part = summed[step * total_rows : (step + 1) * total_rows].astype(jnp.bfloat16)
            mine = mine + to_inner(part, step).astype(jnp.float32)
        scale = lax.dynamic_slice(kv_scale, (column,), (band,))
        bands.append((mine * scale).astype(jnp.bfloat16))
    bands = jnp.stack(bands)
    kv = jnp.concatenate(
        [lax.dynamic_index_in_dim(bands, (team - c) % teams, 0, False) for c in range(teams)], 1
    )
    shares = kv.reshape(cores, both, width)
    shares = [lax.dynamic_index_in_dim(shares, (core - c) % cores, 0, False) for c in range(cores)]
    prompt_kv = jnp.concatenate([s[:pre_share] for s in shares], 0)
    own_kv = jnp.concatenate([s[pre_share:] for s in shares], 0)

    blocks, owners = [], []
    shifted = prompt_kv
    for back in range(outer):
        if back:
            shifted = to_outer(shifted)
        for step in range(inner):
            blocks.append(to_inner(shifted, step) if step else shifted)
            owners.append(((block - back) % outer) * inner + (place ^ step))
    owners = jnp.stack(owners).astype(jnp.int32)

    global_rows = rank * count + jnp.arange(count, dtype=jnp.int32)
    prompts = sample_rows.shape[0]
    match = sample_rows[:, :, None] == global_rows[None, None, :]
    found = jnp.any(match, axis=(0, 1))
    prompt_ids = jnp.arange(prompts, dtype=jnp.int32)
    chosen = jnp.sum(jnp.where(match, prompt_ids[:, None, None], 0), axis=(0, 1))
    picks = chosen[:, None] == prompt_ids[None, :]
    source = jnp.sum(jnp.where(picks, prompt_owner[None, :], 0), 1)
    live = jnp.where(found, jnp.sum(jnp.where(picks, prompt_len[None, :], 0), 1), 0)

    cache_mask = (jnp.arange(cache.shape[1])[None, :] < cache_len[:, None])[:, None, :]
    query = dec_q.reshape(count, heads, REP, HD)
    tops, totals, mixes = [], [], []
    for head in range(heads):
        low, mid, high = head * 2 * HD, head * 2 * HD + HD, head * 2 * HD + 2 * HD
        score_c = jnp.einsum(
            "srd,sjd->srj",
            query[:, head],
            cache[:, :, low:mid],
            preferred_element_type=jnp.float32,
        )
        score_c = jnp.where(cache_mask, score_c * factor, NEG)
        top_c = jnp.max(score_c, -1)
        weight_c = jnp.exp(score_c - top_c[..., None])
        mixed_c = jnp.einsum(
            "srj,sjd->srd",
            weight_c.astype(jnp.bfloat16),
            cache[:, :, mid:high],
            preferred_element_type=jnp.float32,
        )
        tops.append(top_c.T.reshape(REP * count, 1))
        totals.append(jnp.sum(weight_c, -1).T.reshape(REP * count, 1))
        mixes.append(mixed_c.transpose(1, 0, 2).reshape(REP * count, HD))
    attended = attend(
        owners,
        dec_q,
        jnp.tile(source, REP)[:, None],
        jnp.tile(live, REP)[:, None],
        jnp.stack(tops),
        jnp.stack(totals),
        jnp.stack(mixes),
        own_kv,
        blocks,
        heads,
    )
    return (attended, prompt_kv)


def solution(mesh):
    in_specs = (
        P(("groups", "dp"), None),
        P(("groups", "dp"), None),
        P("dp", "tp"),
        P("tp"),
        P(("groups", "dp"), "tp"),
        P(("groups", "dp"), None, "tp"),
        P(("groups", "dp")),
        P("groups"),
        P("groups"),
        P("groups", None),
    )
    out_specs = (P(("groups", "dp"), "tp"), P(("groups", "dp"), "tp"))
    body = functools.partial(local, shape=dict(mesh.shape))
    return jax.shard_map(body, mesh=mesh, in_specs=in_specs, out_specs=out_specs, check_vma=False)
```

```python
import functools
import math

import jax
import jax.numpy as jnp
from jax import lax
from jax.experimental import pallas as pl
from jax.experimental.pallas import tpu as pltpu
from jax.sharding import PartitionSpec as P

HD = 128
REP = 12
NEG = -1e30
INNER = 4


def pack_kernel(plan, n_in, n_out, at_ref, *refs):
    ins, outs = refs[:n_in], refs[n_in : n_in + n_out]
    for src, shape, row, column, dst, to_row, to_column in plan:
        from_row = pl.multiple_of(at_ref[row], 16)
        from_column = pl.multiple_of(at_ref[column], 128)
        outs[dst][to_row : to_row + shape[0], to_column : to_column + shape[1]] = ins[src][
            pl.ds(from_row, shape[0]), pl.ds(from_column, shape[1])
        ]


def gather_kernel(inner, outer, cores, teams, depth, at_ref, *refs):
    n_arrived = (inner - 1) * cores
    pre_ref, dec_ref, w_ref = refs[:3]
    arrived = refs[3 : 3 + n_arrived]
    near_refs = refs[3 + n_arrived : 3 + n_arrived + teams]
    far_refs = refs[3 + n_arrived + teams : 2 + n_arrived + teams + outer]
    own_ref = refs[2 + n_arrived + teams + outer]
    pre_share, dec_share = pre_ref.shape[0] // cores, dec_ref.shape[0] // cores
    both = pre_share + dec_share
    place, core = at_ref[0], at_ref[1]
    targets = [own_ref] + list(far_refs)
    for back in range(outer):
        column = pl.multiple_of(at_ref[2 + back], 128)
        for turn in range(cores):
            which = lax.rem(core - turn + cores, cores)
            base = pl.multiple_of(place * (cores * both) + turn * both, 16)
            targets[back][pl.ds(base, pre_share), :] = pre_ref[
                pl.ds(pl.multiple_of(which * pre_share, 16), pre_share), pl.ds(column, depth)
            ]
            targets[back][pl.ds(base + pre_share, dec_share), :] = dec_ref[
                pl.ds(pl.multiple_of(which * dec_share, 16), dec_share), pl.ds(column, depth)
            ]
            for step in range(1, inner):
                base = pl.multiple_of((place ^ step) * (cores * both) + turn * both, 16)
                targets[back][pl.ds(base, both), :] = arrived[(step - 1) * cores + turn][
                    :, back * depth : (back + 1) * depth
                ]

    @pl.loop(0, inner)
    def _(peer):
        rows = pl.ds(pl.multiple_of(peer * (cores * both), 16), cores * both)
        for turn, near_ref in enumerate(near_refs):
            band = near_ref.shape[1]
            columns = pl.ds(pl.multiple_of(at_ref[2 + outer + turn], 128), band)
            near_ref[rows, :] = jnp.dot(
                own_ref[rows, :], w_ref[:, columns], preferred_element_type=jnp.float32
            )


def finish_kernel(inner, cores, at_ref, scale_ref, *refs):
    parts, (prompt_ref, own_ref, copies_ref) = refs[:-3], refs[-3:]
    span, count = prompt_ref.shape[0], own_ref.shape[0]
    pre_share, dec_share = span // cores, count // cores
    both = pre_share + dec_share
    for turn, part in enumerate(parts):
        columns = pl.ds(pl.multiple_of(at_ref[1 + turn], 128), part.shape[1])
        summed = part[: span + count, :].astype(jnp.float32)
        for peer in range(1, inner):
            rows = slice(peer * (span + count), (peer + 1) * (span + count))
            summed = summed + part[rows, :].astype(jnp.float32)
        done = (summed * scale_ref[:, columns]).astype(jnp.bfloat16)
        for share in range(cores):
            which = lax.rem(at_ref[0] - share + cores, cores)
            first = pl.multiple_of(which * pre_share, 16)
            piece = done[share * both : share * both + pre_share]
            prompt_ref[pl.ds(first, pre_share), columns] = piece
            for peer in range(inner):
                copies_ref[peer, pl.ds(first, pre_share), columns] = piece
            first = pl.multiple_of(which * dec_share, 16)
            own_ref[pl.ds(first, dec_share), columns] = done[
                share * both + pre_share : (share + 1) * both
            ]


def attend_kernel(
    heads,
    inner,
    outer,
    at_ref,
    owner_ref,
    len_ref,
    samples_ref,
    q_ref,
    top_ref,
    mixed_ref,
    own_ref,
    *refs,
):
    blocks, out_ref = refs[:outer], refs[outer]
    count = q_ref.shape[0]
    span = blocks[0].shape[0] // inner
    factor = 1.0 / math.sqrt(HD)
    row = at_ref[0] + lax.broadcasted_iota(jnp.int32, (count, 1), 0)
    source = jnp.zeros((count, 1), jnp.int32)
    live = jnp.zeros((count, 1), jnp.int32)
    for prompt in range(samples_ref.shape[0]):
        hit = jnp.max(
            jnp.where(samples_ref[prompt : prompt + 1, :] == row, 1, 0), -1, keepdims=True
        )
        source = source + hit * owner_ref[prompt]
        live = live + hit * len_ref[prompt]
    source = jnp.concatenate([source] * REP, 0)
    live = jnp.concatenate([live] * REP, 0)
    place = lax.broadcasted_iota(jnp.int32, (REP * count, span), 1)
    shown = place < live
    pieces = [(back, peer) for back in range(outer) for peer in range(inner)]
    for head in range(heads):
        first = head * REP * HD
        low, mid, high = head * 2 * HD, head * 2 * HD + HD, head * 2 * HD + 2 * HD
        q = jnp.concatenate(
            [q_ref[:, first + r * HD : first + (r + 1) * HD] for r in range(REP)], 0
        )
        picked = jnp.zeros((REP * count, span), jnp.float32)
        for back, peer in pieces:
            scores = lax.dot_general(
                q,
                blocks[back][peer * span : (peer + 1) * span, low:mid],
                (((1,), (1,)), ((), ())),
                preferred_element_type=jnp.float32,
            )
            picked = jnp.where(source == at_ref[1 + back] + peer, scores, picked)
        picked = jnp.where(shown, picked * factor, NEG)
        own_k = jnp.concatenate([own_ref[:, low:mid].astype(jnp.float32)] * REP, 0)
        own_v = jnp.concatenate([own_ref[:, mid:high].astype(jnp.float32)] * REP, 0)
        score_o = jnp.sum(q.astype(jnp.float32) * own_k, -1, keepdims=True) * factor
        top_c = top_ref[head]
        top = jnp.maximum(
            jnp.maximum(jnp.max(picked, -1, keepdims=True), score_o), top_c
        )
        weights = jnp.exp(picked - top)
        weight_o = jnp.exp(score_o - top)
        weight_c = jnp.exp(top_c - top)
        total = weight_c + weight_o + jnp.sum(weights, -1, keepdims=True)
        mixed = mixed_ref[head] * weight_c + weight_o * own_v
        for back, peer in pieces:
            mixed = mixed + jnp.dot(
                jnp.where(source == at_ref[1 + back] + peer, weights, 0.0).astype(jnp.bfloat16),
                blocks[back][peer * span : (peer + 1) * span, mid:high],
                preferred_element_type=jnp.float32,
            )
        mixed = mixed / total
        for r in range(REP):
            out_ref[:, first + r * HD : first + (r + 1) * HD] = mixed[
                r * count : (r + 1) * count
            ].astype(out_ref.dtype)


VMEM = pl.BlockSpec(memory_space=pltpu.VMEM)
SMEM = pl.BlockSpec(memory_space=pltpu.SMEM)
PARAMS = pltpu.CompilerParams(vmem_limit_bytes=48 * 1024 * 1024)


def numbers(values):
    return jnp.stack([jnp.asarray(v, jnp.int32) for v in values])


def stages(depth):
    unit = 128
    first = max(unit, depth // 6 // unit * unit)
    second = (depth - first) // 2 // unit * unit
    return (first, second, depth - first - second)


def local(
    pre_x,
    dec_x,
    w_kv,
    kv_scale,
    dec_q,
    cache,
    cache_len,
    prompt_owner,
    prompt_len,
    sample_rows,
    *,
    shape,
):
    teams, ranks, cores = shape["groups"], shape["dp"], shape["tp"]
    inner = INNER
    outer = ranks // inner
    span, features = pre_x.shape
    count = dec_x.shape[0]
    depth, width = w_kv.shape
    heads = width // (2 * HD)
    band = width // teams
    factor = 1.0 / math.sqrt(HD)
    team = lax.axis_index("groups")
    rank = lax.axis_index("dp")
    core = lax.axis_index("tp")
    place, block = rank % inner, rank // inner

    def to_inner(value, step):
        pairs = [(r, r // inner * inner + (r % inner ^ step)) for r in range(ranks)]
        return lax.ppermute(value, "dp", pairs)

    def to_outer(value, step=1):
        pairs = [(r, (r + step * inner) % ranks) for r in range(ranks)]
        return lax.ppermute(value, "dp", pairs)

    def to_team(value, step):
        return lax.ppermute(value, "groups", [(i, (i + step) % teams) for i in range(teams)])

    def to_core(value, step):
        return lax.ppermute(value, "tp", [(i, (i + step) % cores) for i in range(cores)])

    groups = [list(range(at, at + inner)) for at in range(0, ranks, inner)]

    def exchange(value):
        return lax.all_to_all(value, "dp", 0, 0, axis_index_groups=groups, tiled=True)

    sizes = stages(depth)
    pre_share, dec_share = span // cores, count // cores
    both = pre_share + dec_share
    spots = [0, team * band, core * pre_share, core * dec_share]
    plan, outs = [], []
    at = 0
    for size in sizes:
        spots.append(at)
        plan.append((2, (size, band), len(spots) - 1, 1, len(outs), 0, 0))
        outs.append(jax.ShapeDtypeStruct((size, band), jnp.bfloat16))
        at += size
    for step in range(1, inner):
        for back in range(outer):
            spots.append((((block - back) % outer) * inner + (place ^ step)) * depth)
            column = len(spots) - 1
            plan.append((0, (pre_share, depth), 2, column, len(outs), 0, back * depth))
            plan.append((1, (dec_share, depth), 3, column, len(outs), pre_share, back * depth))
        outs.append(jax.ShapeDtypeStruct((both, outer * depth), jnp.bfloat16))
    sends = pl.pallas_call(
        functools.partial(pack_kernel, plan, 3, len(outs)),
        out_shape=outs,
        in_specs=[SMEM] + [VMEM] * 3,
        out_specs=[VMEM] * len(outs),
        compiler_params=PARAMS,
    )(numbers(spots), pre_x, dec_x, w_kv)
    moving, row_sends = list(sends[: len(sizes)]), sends[len(sizes) :]

    far = []
    for back in range(1, outer):
        for piece in range(len(sizes)):
            if piece >= 2 and back == 1:
                moving[piece], _ = lax.optimization_barrier((moving[piece], moving[piece - 2]))
            moving[piece] = to_outer(moving[piece])
        far.append([[m] + [to_team(m, turn) for turn in range(1, teams)] for m in moving])

    arrived = []
    for step in range(1, inner):
        got = to_inner(row_sends[step - 1], step)
        arrived.append(got)
        for turn in range(1, cores):
            arrived.append(to_core(got, turn))
    total_rows = span + count
    all_rows = inner * total_rows
    turns = [(team - turn) % teams * band for turn in range(teams)]
    gathered = pl.pallas_call(
        functools.partial(gather_kernel, inner, outer, cores, teams, depth),
        out_shape=[jax.ShapeDtypeStruct((all_rows, band), jnp.float32)] * teams
        + [jax.ShapeDtypeStruct((all_rows, depth), jnp.bfloat16)] * (outer - 1),
        in_specs=[SMEM] + [VMEM] * (3 + len(arrived)),
        out_specs=[VMEM] * (teams + outer - 1),
        scratch_shapes=[pltpu.VMEM((all_rows, depth), jnp.bfloat16)],
        compiler_params=PARAMS,
    )(
        numbers(
            [place, core]
            + [(((block - back) % outer) * inner + place) * depth for back in range(outer)]
            + turns
        ),
        pre_x,
        dec_x,
        w_kv,
        *arrived,
    )
    near, far_rows = gathered[:teams], gathered[teams:]
    parts = []
    for turn in range(teams):
        summed = near[turn]
        for back in range(1, outer):
            at = 0
            for piece, size in enumerate(sizes):
                summed = summed + jnp.dot(
                    far_rows[back - 1][:, at : at + size],
                    far[back - 1][piece][turn],
                    preferred_element_type=jnp.float32,
                )
                at += size
        parts.append(exchange(summed.astype(jnp.bfloat16)))
    prompt_kv, own_kv, copies = pl.pallas_call(
        functools.partial(finish_kernel, inner, cores),
        out_shape=[
            jax.ShapeDtypeStruct((span, width), jnp.bfloat16),
            jax.ShapeDtypeStruct((count, width), jnp.bfloat16),
            jax.ShapeDtypeStruct((inner, span, width), jnp.bfloat16),
        ],
        in_specs=[SMEM] + [VMEM] * (1 + teams),
        out_specs=[VMEM] * 3,
        compiler_params=PARAMS,
    )(numbers([core] + turns), kv_scale[None, :], *parts)

    blocks = [exchange(copies.reshape(inner * span, width))]
    shifted = prompt_kv
    for back in range(1, outer):
        shifted = to_outer(shifted)
        blocks.append(exchange(jnp.concatenate([shifted] * inner, 0)))

    cache_mask = (jnp.arange(cache.shape[1])[None, :] < cache_len[:, None])[:, None, :]
    query = dec_q.reshape(count, heads, REP, HD)
    tops, mixes = [], []
    for head in range(heads):
        low, mid, high = head * 2 * HD, head * 2 * HD + HD, head * 2 * HD + 2 * HD
        score_c = jnp.einsum(
            "srd,sjd->srj",
            query[:, head],
            cache[:, :, low:mid],
            preferred_element_type=jnp.float32,
        )
        score_c = jnp.where(cache_mask, score_c * factor, NEG)
        top_c = jnp.max(score_c, -1, keepdims=True)
        weight_c = jnp.exp(score_c - top_c)
        total_c = jnp.sum(weight_c, -1, keepdims=True)
        mixed_c = jnp.einsum(
            "srj,sjd->srd",
            weight_c.astype(jnp.bfloat16),
            cache[:, :, mid:high],
            preferred_element_type=jnp.float32,
        )
        top_c = jnp.broadcast_to(top_c + jnp.log(total_c), (count, REP, HD))
        tops.append(top_c.transpose(1, 0, 2).reshape(REP * count, HD))
        mixes.append((mixed_c / total_c).transpose(1, 0, 2).reshape(REP * count, HD))
    attended = pl.pallas_call(
        functools.partial(attend_kernel, heads, inner, outer),
        out_shape=jax.ShapeDtypeStruct(dec_q.shape, jnp.bfloat16),
        in_specs=[SMEM] * 3 + [VMEM] * (5 + outer),
        out_specs=VMEM,
        compiler_params=PARAMS,
    )(
        numbers([rank * count] + [(block - back) % outer * inner for back in range(outer)]),
        prompt_owner,
        prompt_len,
        sample_rows,
        dec_q,
        jnp.stack(tops),
        jnp.stack(mixes),
        own_kv,
        *blocks,
    )
    return (attended, prompt_kv)


def solution(mesh):
    in_specs = (
        P(("groups", "dp"), None),
        P(("groups", "dp"), None),
        P("dp", "tp"),
        P("tp"),
        P(("groups", "dp"), "tp"),
        P(("groups", "dp"), None, "tp"),
        P(("groups", "dp")),
        P("groups"),
        P("groups"),
        P("groups", None),
    )
    out_specs = (P(("groups", "dp"), "tp"), P(("groups", "dp"), "tp"))
    body = functools.partial(local, shape=dict(mesh.shape))
    return jax.shard_map(body, mesh=mesh, in_specs=in_specs, out_specs=out_specs, check_vma=False)
```

```python
import functools
import math

import jax
import jax.numpy as jnp
from jax import lax
from jax.experimental import pallas as pl
from jax.experimental.pallas import tpu as pltpu
from jax.sharding import PartitionSpec as P

HD = 128
REP = 12
NEG = -1e30
INNER = 4


def pack_kernel(plan, n_in, n_out, at_ref, *refs):
    ins, outs = refs[:n_in], refs[n_in : n_in + n_out]
    for src, shape, row, column, dst, to_row, to_column in plan:
        from_row = pl.multiple_of(at_ref[row], 16)
        from_column = pl.multiple_of(at_ref[column], 128)
        outs[dst][to_row : to_row + shape[0], to_column : to_column + shape[1]] = ins[src][
            pl.ds(from_row, shape[0]), pl.ds(from_column, shape[1])
        ]


def near_kernel(inner, cores, at_ref, w_ref, *refs):
    halves, outs = refs[:cores], refs[cores:]
    depth = w_ref.shape[0]
    each = halves[0].shape[0] // 2

    @pl.loop(0, 2)
    def _(part):
        for turn, half in enumerate(halves):
            rows = pl.ds(pl.multiple_of(part * each, 16), each)
            for number, out in enumerate(outs):
                columns = pl.ds(pl.multiple_of(at_ref[number], 128), out.shape[1])
                out[pl.ds(pl.multiple_of(turn * 2 * each + part * each, 16), each), :] = jnp.dot(
                    half[rows, :depth], w_ref[:, columns], preferred_element_type=jnp.float32
                )


def finish_kernel(inner, cores, at_ref, scale_ref, *refs):
    parts, (prompt_ref, own_ref, copies_ref) = refs[:-3], refs[-3:]
    span, count = prompt_ref.shape[0], own_ref.shape[0]
    pre_share, dec_share = span // cores, count // cores
    both = pre_share + dec_share
    for turn, part in enumerate(parts):
        columns = pl.ds(pl.multiple_of(at_ref[1 + turn], 128), part.shape[1])
        summed = part[: span + count, :].astype(jnp.float32)
        for peer in range(1, inner):
            rows = slice(peer * (span + count), (peer + 1) * (span + count))
            summed = summed + part[rows, :].astype(jnp.float32)
        done = (summed * scale_ref[:, columns]).astype(jnp.bfloat16)
        for share in range(cores):
            which = lax.rem(at_ref[0] - share + cores, cores)
            first = pl.multiple_of(which * pre_share, 16)
            piece = done[share * both : share * both + pre_share]
            prompt_ref[pl.ds(first, pre_share), columns] = piece
            for peer in range(inner):
                copies_ref[peer, pl.ds(first, pre_share), columns] = piece
            first = pl.multiple_of(which * dec_share, 16)
            own_ref[pl.ds(first, dec_share), columns] = done[
                share * both + pre_share : (share + 1) * both
            ]


def attend_kernel(
    heads,
    inner,
    outer,
    at_ref,
    owner_ref,
    len_ref,
    samples_ref,
    q_ref,
    top_ref,
    mixed_ref,
    own_ref,
    *refs,
):
    blocks, out_ref = refs[:outer], refs[outer]
    count = q_ref.shape[0]
    span = blocks[0].shape[0] // inner
    factor = 1.0 / math.sqrt(HD)
    row = at_ref[0] + lax.broadcasted_iota(jnp.int32, (count, 1), 0)
    source = jnp.zeros((count, 1), jnp.int32)
    live = jnp.zeros((count, 1), jnp.int32)
    for prompt in range(samples_ref.shape[0]):
        hit = jnp.max(
            jnp.where(samples_ref[prompt : prompt + 1, :] == row, 1, 0), -1, keepdims=True
        )
        source = source + hit * owner_ref[prompt]
        live = live + hit * len_ref[prompt]
    source = jnp.concatenate([source] * REP, 0)
    live = jnp.concatenate([live] * REP, 0)
    place = lax.broadcasted_iota(jnp.int32, (REP * count, span), 1)
    shown = place < live
    pieces = [(back, peer) for back in range(outer) for peer in range(inner)]
    for head in range(heads):
        first = head * REP * HD
        low, mid, high = head * 2 * HD, head * 2 * HD + HD, head * 2 * HD + 2 * HD
        q = jnp.concatenate(
            [q_ref[:, first + r * HD : first + (r + 1) * HD] for r in range(REP)], 0
        )
        picked = jnp.zeros((REP * count, span), jnp.float32)
        for back, peer in pieces:
            scores = lax.dot_general(
                q,
                blocks[back][peer * span : (peer + 1) * span, low:mid],
                (((1,), (1,)), ((), ())),
                preferred_element_type=jnp.float32,
            )
            picked = jnp.where(source == at_ref[1 + back] + peer, scores, picked)
        picked = jnp.where(shown, picked * factor, NEG)
        own_k = jnp.concatenate([own_ref[:, low:mid].astype(jnp.float32)] * REP, 0)
        own_v = jnp.concatenate([own_ref[:, mid:high].astype(jnp.float32)] * REP, 0)
        score_o = jnp.sum(q.astype(jnp.float32) * own_k, -1, keepdims=True) * factor
        top_c = top_ref[head]
        top = jnp.maximum(
            jnp.maximum(jnp.max(picked, -1, keepdims=True), score_o), top_c
        )
        weights = jnp.exp(picked - top)
        weight_o = jnp.exp(score_o - top)
        weight_c = jnp.exp(top_c - top)
        total = weight_c + weight_o + jnp.sum(weights, -1, keepdims=True)
        mixed = mixed_ref[head] * weight_c + weight_o * own_v
        for back, peer in pieces:
            mixed = mixed + jnp.dot(
                jnp.where(source == at_ref[1 + back] + peer, weights, 0.0).astype(jnp.bfloat16),
                blocks[back][peer * span : (peer + 1) * span, mid:high],
                preferred_element_type=jnp.float32,
            )
        mixed = mixed / total
        for r in range(REP):
            out_ref[:, first + r * HD : first + (r + 1) * HD] = mixed[
                r * count : (r + 1) * count
            ].astype(out_ref.dtype)


VMEM = pl.BlockSpec(memory_space=pltpu.VMEM)
SMEM = pl.BlockSpec(memory_space=pltpu.SMEM)
PARAMS = pltpu.CompilerParams(vmem_limit_bytes=48 * 1024 * 1024)


def numbers(values):
    return jnp.stack([jnp.asarray(v, jnp.int32) for v in values])


def far_kernel(inner, cores, near_ref, *refs):
    halves, pieces, out_ref = refs[:cores], refs[cores:-1], refs[-1]
    both = halves[0].shape[0] // inner
    depth = halves[0].shape[1] - sum(piece.shape[0] for piece in pieces)

    @pl.loop(0, inner)
    def _(peer):
        rows = pl.ds(pl.multiple_of(peer * both, 16), both)
        for turn, half in enumerate(halves):
            summed = near_ref[pl.ds(pl.multiple_of((turn * inner + peer) * both, 16), both), :]
            at = depth
            for piece in pieces:
                summed = summed + jnp.dot(
                    half[rows, at : at + piece.shape[0]],
                    piece[...],
                    preferred_element_type=jnp.float32,
                )
                at += piece.shape[0]
            out_ref[pl.ds(pl.multiple_of((peer * cores + turn) * both, 16), both), :] = (
                summed.astype(jnp.bfloat16)
            )


def cached(query, cache, cache_len, heads):
    count = query.shape[0]
    factor = 1.0 / math.sqrt(HD)
    mask = (jnp.arange(cache.shape[1])[None, :] < cache_len[:, None])[:, None, :]
    query = query.reshape(count, heads, REP, HD)
    tops, mixes = [], []
    for head in range(heads):
        low, mid, high = head * 2 * HD, head * 2 * HD + HD, head * 2 * HD + 2 * HD
        scores = jnp.einsum(
            "srd,sjd->srj",
            query[:, head],
            cache[:, :, low:mid],
            preferred_element_type=jnp.float32,
        )
        scores = jnp.where(mask, scores * factor, NEG)
        top = jnp.max(scores, -1, keepdims=True)
        weights = jnp.exp(scores - top)
        total = jnp.sum(weights, -1, keepdims=True)
        mixed = jnp.einsum(
            "srj,sjd->srd",
            weights.astype(jnp.bfloat16),
            cache[:, :, mid:high],
            preferred_element_type=jnp.float32,
        )
        top = jnp.broadcast_to(top + jnp.log(total), (count, REP, HD))
        tops.append(top.transpose(1, 0, 2).reshape(REP * count, HD))
        mixes.append((mixed / total).transpose(1, 0, 2).reshape(REP * count, HD))
    return jnp.stack(tops), jnp.stack(mixes)


def stages(depth):
    unit = 128
    first = max(unit, depth // 6 // unit * unit)
    second = max(unit, (depth - first) * 3 // 5 // unit * unit)
    return (first, second, depth - first - second)


def local(
    pre_x,
    dec_x,
    w_kv,
    kv_scale,
    dec_q,
    cache,
    cache_len,
    prompt_owner,
    prompt_len,
    sample_rows,
    *,
    shape,
):
    teams, ranks, cores = shape["groups"], shape["dp"], shape["tp"]
    inner = INNER
    outer = ranks // inner
    span, features = pre_x.shape
    count = dec_x.shape[0]
    depth, width = w_kv.shape
    heads = width // (2 * HD)
    band = width // teams
    team = lax.axis_index("groups")
    rank = lax.axis_index("dp")
    core = lax.axis_index("tp")
    place, block = rank % inner, rank // inner

    def to_inner(value, step):
        pairs = [(r, r // inner * inner + (r % inner ^ step)) for r in range(ranks)]
        return lax.ppermute(value, "dp", pairs)

    def to_outer(value, step=1):
        pairs = [(r, (r + step * inner) % ranks) for r in range(ranks)]
        return lax.ppermute(value, "dp", pairs)

    def to_team(value, step):
        return lax.ppermute(value, "groups", [(i, (i + step) % teams) for i in range(teams)])

    def to_core(value, step):
        return lax.ppermute(value, "tp", [(i, (i + step) % cores) for i in range(cores)])

    groups = [list(range(at, at + inner)) for at in range(0, ranks, inner)]

    def exchange(value):
        return lax.all_to_all(value, "dp", 0, 0, axis_index_groups=groups, tiled=True)

    def pack(plan, spots, outs, *arrays):
        return pl.pallas_call(
            functools.partial(pack_kernel, plan, len(arrays), len(outs)),
            out_shape=outs,
            in_specs=[SMEM] + [VMEM] * len(arrays),
            out_specs=[VMEM] * len(outs),
            compiler_params=PARAMS,
        )(numbers(spots), *arrays)

    sizes = stages(depth)
    plan, at = [], 0
    for number, size in enumerate(sizes):
        plan.append((0, (size, band), 1 + number, 0, number, 0, 0))
        at += size
    starts = [sum(sizes[:number]) for number in range(len(sizes))]
    shapes = [jax.ShapeDtypeStruct((size, band), jnp.bfloat16) for size in sizes]
    moving = list(pack(plan, [team * band] + starts, shapes, w_kv))

    far = []
    for back in range(1, outer):
        moving = [to_outer(m) for m in moving]
        if back == 1:
            moving[0], pre_x, dec_x = lax.optimization_barrier((moving[0], pre_x, dec_x))
        pieces = []
        for m in moving:
            if pieces:
                m, pieces[-1] = lax.optimization_barrier((m, pieces[-1]))
            pieces.append([m] + [to_team(m, turn) for turn in range(1, teams)])
        far.append(pieces)

    pre_share, dec_share = span // cores, count // cores
    both = pre_share + dec_share
    spots = [core * pre_share, core * dec_share]
    plan = []
    for peer in range(inner):
        for back in range(outer):
            spots.append((((block - back) % outer) * inner + peer) * depth)
            column, first = len(spots) - 1, peer * both
            plan.append((0, (pre_share, depth), 0, column, 0, first, back * depth))
            plan.append((1, (dec_share, depth), 1, column, 0, first + pre_share, back * depth))
    shapes = [jax.ShapeDtypeStruct((inner * both, outer * depth), jnp.bfloat16)]
    (row_sends,) = pack(plan, spots, shapes, pre_x, dec_x)
    row_sends, query = lax.optimization_barrier((row_sends, dec_q))
    arrived = [exchange(row_sends)]
    for turn in range(1, cores):
        arrived.append(to_core(arrived[0], turn))
    top_c, mixed_c = cached(query, cache, cache_len, heads)
    arrived, top_c, mixed_c = lax.optimization_barrier((arrived, top_c, mixed_c))
    total_rows = span + count
    all_rows = inner * total_rows
    turns = [(team - turn) % teams * band for turn in range(teams)]
    near = pl.pallas_call(
        functools.partial(near_kernel, inner, cores),
        out_shape=[jax.ShapeDtypeStruct((all_rows, band), jnp.float32)] * teams,
        in_specs=[SMEM] + [VMEM] * (1 + cores),
        out_specs=[VMEM] * teams,
        compiler_params=PARAMS,
    )(numbers(turns), w_kv, *arrived)
    parts, summed = [], None
    for turn in range(teams):
        pieces = [far[back - 1][piece][turn] for back in range(1, outer) for piece in range(len(sizes))]
        start = near[turn]
        if summed is not None:
            start, summed = lax.optimization_barrier((start, summed))
            parts[-1] = exchange(summed)
        summed = pl.pallas_call(
            functools.partial(far_kernel, inner, cores),
            out_shape=jax.ShapeDtypeStruct((all_rows, band), jnp.bfloat16),
            in_specs=[VMEM] * (1 + cores + len(pieces)),
            out_specs=VMEM,
            compiler_params=PARAMS,
        )(start, *arrived, *pieces)
        parts.append(summed)
    parts[-1] = exchange(summed)
    prompt_kv, own_kv, copies = pl.pallas_call(
        functools.partial(finish_kernel, inner, cores),
        out_shape=[
            jax.ShapeDtypeStruct((span, width), jnp.bfloat16),
            jax.ShapeDtypeStruct((count, width), jnp.bfloat16),
            jax.ShapeDtypeStruct((inner, span, width), jnp.bfloat16),
        ],
        in_specs=[SMEM] + [VMEM] * (1 + teams),
        out_specs=[VMEM] * 3,
        compiler_params=PARAMS,
    )(numbers([core] + turns), kv_scale[None, :], *parts)

    blocks = [exchange(copies.reshape(inner * span, width))]
    shifted = prompt_kv
    for back in range(1, outer):
        shifted = to_outer(shifted)
        copies = jnp.broadcast_to(shifted[None], (inner, span, width))
        blocks.append(exchange(copies.reshape(inner * span, width)))

    attended = pl.pallas_call(
        functools.partial(attend_kernel, heads, inner, outer),
        out_shape=jax.ShapeDtypeStruct(dec_q.shape, jnp.bfloat16),
        in_specs=[SMEM] * 3 + [VMEM] * (5 + outer),
        out_specs=VMEM,
        compiler_params=PARAMS,
    )(
        numbers([rank * count] + [(block - back) % outer * inner for back in range(outer)]),
        prompt_owner,
        prompt_len,
        sample_rows,
        dec_q,
        top_c,
        mixed_c,
        own_kv,
        *blocks,
    )
    return (attended, prompt_kv)


def solution(mesh):
    in_specs = (
        P(("groups", "dp"), None),
        P(("groups", "dp"), None),
        P("dp", "tp"),
        P("tp"),
        P(("groups", "dp"), "tp"),
        P(("groups", "dp"), None, "tp"),
        P(("groups", "dp")),
        P("groups"),
        P("groups"),
        P("groups", None),
    )
    out_specs = (P(("groups", "dp"), "tp"), P(("groups", "dp"), "tp"))
    body = functools.partial(local, shape=dict(mesh.shape))
    return jax.shard_map(body, mesh=mesh, in_specs=in_specs, out_specs=out_specs, check_vma=False)
```

```python
import functools
import math

import jax
import jax.numpy as jnp
from jax import lax
from jax.experimental import pallas as pl
from jax.experimental.pallas import tpu as pltpu
from jax.sharding import PartitionSpec as P

HD = 128
REP = 12
NEG = -1e30
INNER = 4


def pack_kernel(plan, n_in, n_out, at_ref, *refs):
    ins, outs = refs[:n_in], refs[n_in : n_in + n_out]
    for src, shape, row, column, dst, to_row, to_column in plan:
        from_row = pl.multiple_of(at_ref[row], 16)
        from_column = pl.multiple_of(at_ref[column], 128)
        outs[dst][to_row : to_row + shape[0], to_column : to_column + shape[1]] = ins[src][
            pl.ds(from_row, shape[0]), pl.ds(from_column, shape[1])
        ]


def gather_kernel(inner, outer, cores, depth, teams, at_ref, w_ref, *refs):
    blocks, refs = refs[: inner * cores], refs[inner * cores :]
    near_refs, far_ref, own_ref = refs[:teams], refs[teams], refs[teams + 1]
    both = blocks[0].shape[0]
    for step in range(inner):
        for turn in range(cores):
            base = pl.multiple_of((at_ref[0] ^ step) * (cores * both) + turn * both, 16)
            block = blocks[step * cores + turn]
            own_ref[pl.ds(base, both), :] = block[:, :depth]
            far_ref[pl.ds(base, both), :] = block[:, depth:]
    half = own_ref.shape[0] // 2
    for part in range(2):
        rows = slice(part * half, (part + 1) * half)
        for turn, near_ref in enumerate(near_refs):
            columns = pl.ds(pl.multiple_of(at_ref[1 + turn], 128), near_ref.shape[1])
            near_ref[rows, :] = jnp.dot(
                own_ref[rows, :], w_ref[:, columns], preferred_element_type=jnp.float32
            )


def finish_kernel(inner, cores, at_ref, scale_ref, *refs):
    parts, (prompt_ref, own_ref) = refs[:-2], refs[-2:]
    span, count = prompt_ref.shape[0], own_ref.shape[0]
    pre_share, dec_share = span // cores, count // cores
    both = pre_share + dec_share
    for turn, part in enumerate(parts):
        columns = pl.ds(pl.multiple_of(at_ref[1 + turn], 128), part.shape[1])
        summed = part[: span + count, :].astype(jnp.float32)
        for peer in range(1, inner):
            rows = slice(peer * (span + count), (peer + 1) * (span + count))
            summed = summed + part[rows, :].astype(jnp.float32)
        done = (summed * scale_ref[:, columns]).astype(jnp.bfloat16)
        for share in range(cores):
            which = lax.rem(at_ref[0] - share + cores, cores)
            first = pl.multiple_of(which * pre_share, 16)
            piece = done[share * both : share * both + pre_share]
            prompt_ref[pl.ds(first, pre_share), columns] = piece
            first = pl.multiple_of(which * dec_share, 16)
            own_ref[pl.ds(first, dec_share), columns] = done[
                share * both + pre_share : (share + 1) * both
            ]


def attend_kernel(
    heads,
    at_ref,
    owner_ref,
    len_ref,
    samples_ref,
    q_ref,
    top_ref,
    mixed_ref,
    own_ref,
    *refs,
):
    blocks, out_ref = refs[:-1], refs[-1]
    count = q_ref.shape[0]
    span = blocks[0].shape[0]
    factor = 1.0 / math.sqrt(HD)
    row = at_ref[0] + lax.broadcasted_iota(jnp.int32, (count, 1), 0)
    source = jnp.zeros((count, 1), jnp.int32)
    live = jnp.zeros((count, 1), jnp.int32)
    for prompt in range(samples_ref.shape[0]):
        hit = jnp.max(
            jnp.where(samples_ref[prompt : prompt + 1, :] == row, 1, 0), -1, keepdims=True
        )
        source = source + hit * owner_ref[prompt]
        live = live + hit * len_ref[prompt]
    source = jnp.concatenate([source] * REP, 0)
    live = jnp.concatenate([live] * REP, 0)
    place = lax.broadcasted_iota(jnp.int32, (REP * count, span), 1)
    shown = place < live
    for head in range(heads):
        first = head * REP * HD
        low, mid, high = head * 2 * HD, head * 2 * HD + HD, head * 2 * HD + 2 * HD
        q = jnp.concatenate(
            [q_ref[:, first + r * HD : first + (r + 1) * HD] for r in range(REP)], 0
        )
        picked = jnp.zeros((REP * count, span), jnp.float32)
        for at, block in enumerate(blocks):
            scores = lax.dot_general(
                q,
                block[:, low:mid],
                (((1,), (1,)), ((), ())),
                preferred_element_type=jnp.float32,
            )
            picked = jnp.where(source == at_ref[1 + at], scores, picked)
        picked = jnp.where(shown, picked * factor, NEG)
        own_k = jnp.concatenate([own_ref[:, low:mid].astype(jnp.float32)] * REP, 0)
        own_v = jnp.concatenate([own_ref[:, mid:high].astype(jnp.float32)] * REP, 0)
        score_o = jnp.sum(q.astype(jnp.float32) * own_k, -1, keepdims=True) * factor
        top_c = top_ref[head]
        top = jnp.maximum(
            jnp.maximum(jnp.max(picked, -1, keepdims=True), score_o), top_c
        )
        weights = jnp.exp(picked - top)
        weight_o = jnp.exp(score_o - top)
        weight_c = jnp.exp(top_c - top)
        total = weight_c + weight_o + jnp.sum(weights, -1, keepdims=True)
        mixed = mixed_ref[head] * weight_c + weight_o * own_v
        for at, block in enumerate(blocks):
            mixed = mixed + jnp.dot(
                jnp.where(source == at_ref[1 + at], weights, 0.0).astype(jnp.bfloat16),
                block[:, mid:high],
                preferred_element_type=jnp.float32,
            )
        mixed = mixed / total
        for r in range(REP):
            out_ref[:, first + r * HD : first + (r + 1) * HD] = mixed[
                r * count : (r + 1) * count
            ].astype(out_ref.dtype)


VMEM = pl.BlockSpec(memory_space=pltpu.VMEM)
SMEM = pl.BlockSpec(memory_space=pltpu.SMEM)
PARAMS = pltpu.CompilerParams(vmem_limit_bytes=48 * 1024 * 1024)


def numbers(values):
    return jnp.stack([jnp.asarray(v, jnp.int32) for v in values])


def far_kernel(near_ref, row_ref, *refs):
    pieces, out_ref = refs[:-1], refs[-1]
    half = out_ref.shape[0] // 2
    for part in range(2):
        rows = slice(part * half, (part + 1) * half)
        summed = near_ref[rows, :]
        at = 0
        for piece in pieces:
            summed = summed + jnp.dot(
                row_ref[rows, at : at + piece.shape[0]],
                piece[...],
                preferred_element_type=jnp.float32,
            )
            at += piece.shape[0]
        out_ref[rows, :] = summed.astype(jnp.bfloat16)


def cached(query, cache, cache_len, heads):
    count = query.shape[0]
    factor = 1.0 / math.sqrt(HD)
    mask = (jnp.arange(cache.shape[1])[None, :] < cache_len[:, None])[:, None, :]
    query = query.reshape(count, heads, REP, HD)
    tops, mixes = [], []
    for head in range(heads):
        low, mid, high = head * 2 * HD, head * 2 * HD + HD, head * 2 * HD + 2 * HD
        scores = jnp.einsum(
            "srd,sjd->srj",
            query[:, head],
            cache[:, :, low:mid],
            preferred_element_type=jnp.float32,
        )
        scores = jnp.where(mask, scores * factor, NEG)
        top = jnp.max(scores, -1, keepdims=True)
        weights = jnp.exp(scores - top)
        total = jnp.sum(weights, -1, keepdims=True)
        mixed = jnp.einsum(
            "srj,sjd->srd",
            weights.astype(jnp.bfloat16),
            cache[:, :, mid:high],
            preferred_element_type=jnp.float32,
        )
        top = jnp.broadcast_to(top + jnp.log(total), (count, REP, HD))
        tops.append(top.transpose(1, 0, 2).reshape(REP * count, HD))
        mixes.append((mixed / total).transpose(1, 0, 2).reshape(REP * count, HD))
    return jnp.stack(tops), jnp.stack(mixes)


def stages(depth):
    unit = 128
    first = max(unit, depth // 3 // unit * unit)
    second = max(unit, (depth - first) // 2 // unit * unit)
    return (first, second, depth - first - second)


def local(
    pre_x,
    dec_x,
    w_kv,
    kv_scale,
    dec_q,
    cache,
    cache_len,
    prompt_owner,
    prompt_len,
    sample_rows,
    *,
    shape,
):
    teams, ranks, cores = shape["groups"], shape["dp"], shape["tp"]
    inner = INNER
    outer = ranks // inner
    span, features = pre_x.shape
    count = dec_x.shape[0]
    depth, width = w_kv.shape
    heads = width // (2 * HD)
    band = width // teams
    team = lax.axis_index("groups")
    rank = lax.axis_index("dp")
    core = lax.axis_index("tp")
    place, block = rank % inner, rank // inner

    def to_inner(value, step):
        pairs = [(r, r // inner * inner + (r % inner ^ step)) for r in range(ranks)]
        return lax.ppermute(value, "dp", pairs)

    def to_outer(value, step=1):
        pairs = [(r, (r + step * inner) % ranks) for r in range(ranks)]
        return lax.ppermute(value, "dp", pairs)

    def to_team(value, step):
        return lax.ppermute(value, "groups", [(i, (i + step) % teams) for i in range(teams)])

    def to_core(value, step):
        return lax.ppermute(value, "tp", [(i, (i + step) % cores) for i in range(cores)])

    groups = [list(range(at, at + inner)) for at in range(0, ranks, inner)]

    def exchange(value):
        return lax.all_to_all(value, "dp", 0, 0, axis_index_groups=groups, tiled=True)

    sizes = stages(depth)
    pre_share, dec_share = span // cores, count // cores
    both = pre_share + dec_share
    spots = [team * band]
    plan, shapes = [], []
    for number, size in enumerate(sizes):
        spots.append(sum(sizes[:number]))
        plan.append((2, (size, band), len(spots) - 1, 0, number, 0, 0))
        shapes.append(jax.ShapeDtypeStruct((size, band), jnp.bfloat16))
    for step, turn in [(0, turn) for turn in range(cores)] + [(s, 0) for s in range(1, inner)]:
        which = (core - turn) % cores
        spots += [which * pre_share, which * dec_share]
        row = len(spots) - 2
        for back in range(outer):
            spots.append((((block - back) % outer) * inner + (place ^ step)) * depth)
            column, to = len(spots) - 1, back * depth
            plan.append((0, (pre_share, depth), row, column, len(shapes), 0, to))
            plan.append((1, (dec_share, depth), row + 1, column, len(shapes), pre_share, to))
        shapes.append(jax.ShapeDtypeStruct((both, outer * depth), jnp.bfloat16))
    sends = pl.pallas_call(
        functools.partial(pack_kernel, plan, 3, len(shapes)),
        out_shape=shapes,
        in_specs=[SMEM] + [VMEM] * 3,
        out_specs=[VMEM] * len(shapes),
        compiler_params=PARAMS,
    )(numbers(spots), pre_x, dec_x, w_kv)
    moving = list(sends[: len(sizes)])
    arrived = list(sends[len(sizes) : len(sizes) + cores])
    row_sends = [None] + list(sends[len(sizes) + cores :])

    far = []
    for back in range(1, outer):
        moving = [to_outer(m) for m in moving]
        if back == 1:
            moving[0], row_sends[-1] = lax.optimization_barrier((moving[0], row_sends[-1]))
        pieces = []
        for m in moving:
            if pieces:
                m, pieces[-1] = lax.optimization_barrier((m, pieces[-1]))
            pieces.append([m] + [to_team(m, turn) for turn in range(1, teams)])
        far.append(pieces)

    for step in range(1, inner):
        got = to_inner(row_sends[step], step)
        arrived += [got] + [to_core(got, turn) for turn in range(1, cores)]
    top_c, mixed_c = cached(dec_q, cache, cache_len, heads)
    arrived, top_c, mixed_c = lax.optimization_barrier((arrived, top_c, mixed_c))
    total_rows = span + count
    all_rows = inner * total_rows
    turns = [(team - turn) % teams * band for turn in range(teams)]
    *near, far_rows = pl.pallas_call(
        functools.partial(gather_kernel, inner, outer, cores, depth, teams),
        out_shape=[jax.ShapeDtypeStruct((all_rows, band), jnp.float32)] * teams
        + [jax.ShapeDtypeStruct((all_rows, (outer - 1) * depth), jnp.bfloat16)],
        in_specs=[SMEM] + [VMEM] * (1 + len(arrived)),
        out_specs=[VMEM] * (1 + teams),
        scratch_shapes=[pltpu.VMEM((all_rows, depth), jnp.bfloat16)],
        compiler_params=PARAMS,
    )(numbers([place] + turns), w_kv, *arrived)
    parts, summed = [], None
    for turn in range(teams):
        pieces = [far[back - 1][piece][turn] for back in range(1, outer) for piece in range(len(sizes))]
        start = near[turn]
        if summed is not None:
            start, summed = lax.optimization_barrier((start, summed))
            parts[-1] = exchange(summed)
        summed = pl.pallas_call(
            far_kernel,
            out_shape=jax.ShapeDtypeStruct((all_rows, band), jnp.bfloat16),
            in_specs=[VMEM] * (2 + len(pieces)),
            out_specs=VMEM,
            compiler_params=PARAMS,
        )(start, far_rows, *pieces)
        parts.append(summed)
    parts[-1] = exchange(summed)
    prompt_kv, own_kv = pl.pallas_call(
        functools.partial(finish_kernel, inner, cores),
        out_shape=[
            jax.ShapeDtypeStruct((span, width), jnp.bfloat16),
            jax.ShapeDtypeStruct((count, width), jnp.bfloat16),
        ],
        in_specs=[SMEM] + [VMEM] * (1 + teams),
        out_specs=[VMEM] * 2,
        compiler_params=PARAMS,
    )(numbers([core] + turns), kv_scale[None, :], *parts)

    blocks, owners = [], []
    shifted = prompt_kv
    for back in range(outer):
        if back:
            shifted = to_outer(shifted)
        for step in range(inner):
            blocks.append(to_inner(shifted, step) if step else shifted)
            owners.append(((block - back) % outer) * inner + (place ^ step))

    attended = pl.pallas_call(
        functools.partial(attend_kernel, heads),
        out_shape=jax.ShapeDtypeStruct(dec_q.shape, jnp.bfloat16),
        in_specs=[SMEM] * 3 + [VMEM] * (5 + len(blocks)),
        out_specs=VMEM,
        compiler_params=PARAMS,
    )(
        numbers([rank * count] + owners),
        prompt_owner,
        prompt_len,
        sample_rows,
        dec_q,
        top_c,
        mixed_c,
        own_kv,
        *blocks,
    )
    return (attended, prompt_kv)


def solution(mesh):
    in_specs = (
        P(("groups", "dp"), None),
        P(("groups", "dp"), None),
        P("dp", "tp"),
        P("tp"),
        P(("groups", "dp"), "tp"),
        P(("groups", "dp"), None, "tp"),
        P(("groups", "dp")),
        P("groups"),
        P("groups"),
        P("groups", None),
    )
    out_specs = (P(("groups", "dp"), "tp"), P(("groups", "dp"), "tp"))
    body = functools.partial(local, shape=dict(mesh.shape))
    return jax.shard_map(body, mesh=mesh, in_specs=in_specs, out_specs=out_specs, check_vma=False)
```

```python
import functools
import math

import jax
import jax.numpy as jnp
from jax import lax
from jax.experimental import pallas as pl
from jax.experimental.pallas import tpu as pltpu
from jax.sharding import PartitionSpec as P

HD = 128
REP = 12
NEG = -1e30
INNER = 4


def pack_kernel(plan, n_in, n_out, at_ref, *refs):
    ins, outs = refs[:n_in], refs[n_in : n_in + n_out]
    for src, shape, row, column, dst, to_row, to_column in plan:
        from_row = pl.multiple_of(at_ref[row], 16)
        from_column = pl.multiple_of(at_ref[column], 128)
        outs[dst][to_row : to_row + shape[0], to_column : to_column + shape[1]] = ins[src][
            pl.ds(from_row, shape[0]), pl.ds(from_column, shape[1])
        ]


def gather_kernel(inner, outer, cores, depth, teams, at_ref, w_ref, *refs):
    blocks, refs = refs[: inner * cores], refs[inner * cores :]
    near_refs, far_ref, own_ref = refs[:teams], refs[teams], refs[teams + 1]
    both = blocks[0].shape[0]
    for step in range(inner):
        for turn in range(cores):
            base = pl.multiple_of((at_ref[0] ^ step) * (cores * both) + turn * both, 16)
            block = blocks[step * cores + turn]
            own_ref[pl.ds(base, both), :] = block[:, :depth]
            far_ref[pl.ds(base, both), :] = block[:, depth:]
    half = own_ref.shape[0] // 2
    for part in range(2):
        rows = slice(part * half, (part + 1) * half)
        for turn, near_ref in enumerate(near_refs):
            columns = pl.ds(pl.multiple_of(at_ref[1 + turn], 128), near_ref.shape[1])
            near_ref[rows, :] = jnp.dot(
                own_ref[rows, :], w_ref[:, columns], preferred_element_type=jnp.float32
            )


def finish_kernel(inner, cores, teams, at_ref, scale_ref, *refs):
    part, prompt_ref, own_ref = refs
    span, count = prompt_ref.shape[0], own_ref.shape[0]
    pre_share, dec_share = span // cores, count // cores
    both = pre_share + dec_share
    band = part.shape[1] // teams
    for turn in range(teams):
        columns = pl.ds(pl.multiple_of(at_ref[1 + turn], 128), band)
        taken = slice(turn * band, (turn + 1) * band)
        summed = part[: span + count, taken].astype(jnp.float32)
        for peer in range(1, inner):
            rows = slice(peer * (span + count), (peer + 1) * (span + count))
            summed = summed + part[rows, taken].astype(jnp.float32)
        done = (summed * scale_ref[:, columns]).astype(jnp.bfloat16)
        for share in range(cores):
            which = lax.rem(at_ref[0] - share + cores, cores)
            first = pl.multiple_of(which * pre_share, 16)
            piece = done[share * both : share * both + pre_share]
            prompt_ref[pl.ds(first, pre_share), columns] = piece
            first = pl.multiple_of(which * dec_share, 16)
            own_ref[pl.ds(first, dec_share), columns] = done[
                share * both + pre_share : (share + 1) * both
            ]


def attend_kernel(
    heads,
    at_ref,
    owner_ref,
    len_ref,
    samples_ref,
    q_ref,
    top_ref,
    mixed_ref,
    own_ref,
    *refs,
):
    blocks, out_ref = refs[:-1], refs[-1]
    count = q_ref.shape[0]
    span = blocks[0].shape[0]
    factor = 1.0 / math.sqrt(HD)
    row = at_ref[0] + lax.broadcasted_iota(jnp.int32, (count, 1), 0)
    source = jnp.zeros((count, 1), jnp.int32)
    live = jnp.zeros((count, 1), jnp.int32)
    for prompt in range(samples_ref.shape[0]):
        hit = jnp.max(
            jnp.where(samples_ref[prompt : prompt + 1, :] == row, 1, 0), -1, keepdims=True
        )
        source = source + hit * owner_ref[prompt]
        live = live + hit * len_ref[prompt]
    source = jnp.concatenate([source] * REP, 0)
    live = jnp.concatenate([live] * REP, 0)
    place = lax.broadcasted_iota(jnp.int32, (REP * count, span), 1)
    shown = place < live
    for head in range(heads):
        first = head * REP * HD
        low, mid, high = head * 2 * HD, head * 2 * HD + HD, head * 2 * HD + 2 * HD
        q = jnp.concatenate(
            [q_ref[:, first + r * HD : first + (r + 1) * HD] for r in range(REP)], 0
        )
        picked = jnp.zeros((REP * count, span), jnp.float32)
        for at, block in enumerate(blocks):
            scores = lax.dot_general(
                q,
                block[:, low:mid],
                (((1,), (1,)), ((), ())),
                preferred_element_type=jnp.float32,
            )
            picked = jnp.where(source == at_ref[1 + at], scores, picked)
        picked = jnp.where(shown, picked * factor, NEG)
        own_k = jnp.concatenate([own_ref[:, low:mid].astype(jnp.float32)] * REP, 0)
        own_v = jnp.concatenate([own_ref[:, mid:high].astype(jnp.float32)] * REP, 0)
        score_o = jnp.sum(q.astype(jnp.float32) * own_k, -1, keepdims=True) * factor
        top_c = top_ref[head]
        top = jnp.maximum(
            jnp.maximum(jnp.max(picked, -1, keepdims=True), score_o), top_c
        )
        weights = jnp.exp(picked - top)
        weight_o = jnp.exp(score_o - top)
        weight_c = jnp.exp(top_c - top)
        total = weight_c + weight_o + jnp.sum(weights, -1, keepdims=True)
        mixed = mixed_ref[head] * weight_c + weight_o * own_v
        for at, block in enumerate(blocks):
            mixed = mixed + jnp.dot(
                jnp.where(source == at_ref[1 + at], weights, 0.0).astype(jnp.bfloat16),
                block[:, mid:high],
                preferred_element_type=jnp.float32,
            )
        mixed = mixed / total
        for r in range(REP):
            out_ref[:, first + r * HD : first + (r + 1) * HD] = mixed[
                r * count : (r + 1) * count
            ].astype(out_ref.dtype)


VMEM = pl.BlockSpec(memory_space=pltpu.VMEM)
SMEM = pl.BlockSpec(memory_space=pltpu.SMEM)
PARAMS = pltpu.CompilerParams(vmem_limit_bytes=48 * 1024 * 1024)


def numbers(values):
    return jnp.stack([jnp.asarray(v, jnp.int32) for v in values])


def far_kernel(teams, *refs):
    near_refs, row_ref, pieces, out_ref = refs[:teams], refs[teams], refs[teams + 1 : -1], refs[-1]
    half = out_ref.shape[0] // 2
    band = out_ref.shape[1] // teams
    for part in range(2):
        rows = slice(part * half, (part + 1) * half)
        for turn in range(teams):
            summed = near_refs[turn][rows, :]
            at = 0
            for piece in pieces[turn::teams]:
                summed = summed + jnp.dot(
                    row_ref[rows, at : at + piece.shape[0]],
                    piece[...],
                    preferred_element_type=jnp.float32,
                )
                at += piece.shape[0]
            out_ref[rows, turn * band : (turn + 1) * band] = summed.astype(jnp.bfloat16)


def cached(query, cache, cache_len, heads):
    count = query.shape[0]
    factor = 1.0 / math.sqrt(HD)
    mask = (jnp.arange(cache.shape[1])[None, :] < cache_len[:, None])[:, None, :]
    query = query.reshape(count, heads, REP, HD)
    tops, mixes = [], []
    for head in range(heads):
        low, mid, high = head * 2 * HD, head * 2 * HD + HD, head * 2 * HD + 2 * HD
        scores = jnp.einsum(
            "srd,sjd->srj",
            query[:, head],
            cache[:, :, low:mid],
            preferred_element_type=jnp.float32,
        )
        scores = jnp.where(mask, scores * factor, NEG)
        top = jnp.max(scores, -1, keepdims=True)
        weights = jnp.exp(scores - top)
        total = jnp.sum(weights, -1, keepdims=True)
        mixed = jnp.einsum(
            "srj,sjd->srd",
            weights.astype(jnp.bfloat16),
            cache[:, :, mid:high],
            preferred_element_type=jnp.float32,
        )
        top = jnp.broadcast_to(top + jnp.log(total), (count, REP, HD))
        tops.append(top.transpose(1, 0, 2).reshape(REP * count, HD))
        mixes.append((mixed / total).transpose(1, 0, 2).reshape(REP * count, HD))
    return jnp.stack(tops), jnp.stack(mixes)


def stages(depth):
    unit = 128
    first = max(unit, depth // 3 // unit * unit)
    second = max(unit, depth * 5 // 12 // unit * unit)
    return (first, second, depth - first - second)


def local(
    pre_x,
    dec_x,
    w_kv,
    kv_scale,
    dec_q,
    cache,
    cache_len,
    prompt_owner,
    prompt_len,
    sample_rows,
    *,
    shape,
):
    teams, ranks, cores = shape["groups"], shape["dp"], shape["tp"]
    inner = INNER
    outer = ranks // inner
    span, features = pre_x.shape
    count = dec_x.shape[0]
    depth, width = w_kv.shape
    heads = width // (2 * HD)
    band = width // teams
    team = lax.axis_index("groups")
    rank = lax.axis_index("dp")
    core = lax.axis_index("tp")
    place, block = rank % inner, rank // inner

    def to_inner(value, step):
        pairs = [(r, r // inner * inner + (r % inner ^ step)) for r in range(ranks)]
        return lax.ppermute(value, "dp", pairs)

    def to_outer(value, step=1):
        pairs = [(r, (r + step * inner) % ranks) for r in range(ranks)]
        return lax.ppermute(value, "dp", pairs)

    def to_team(value, step):
        return lax.ppermute(value, "groups", [(i, (i + step) % teams) for i in range(teams)])

    def to_core(value, step):
        return lax.ppermute(value, "tp", [(i, (i + step) % cores) for i in range(cores)])

    groups = [list(range(at, at + inner)) for at in range(0, ranks, inner)]

    def exchange(value):
        return lax.all_to_all(value, "dp", 0, 0, axis_index_groups=groups, tiled=True)

    sizes = stages(depth)
    pre_share, dec_share = span // cores, count // cores
    both = pre_share + dec_share
    spots = [team * band]
    plan, shapes = [], []
    for number, size in enumerate(sizes):
        spots.append(sum(sizes[:number]))
        plan.append((2, (size, band), len(spots) - 1, 0, number, 0, 0))
        shapes.append(jax.ShapeDtypeStruct((size, band), jnp.bfloat16))
    for step, turn in [(0, turn) for turn in range(cores)] + [(s, 0) for s in range(1, inner)]:
        which = (core - turn) % cores
        spots += [which * pre_share, which * dec_share]
        row = len(spots) - 2
        for back in range(outer):
            spots.append((((block - back) % outer) * inner + (place ^ step)) * depth)
            column, to = len(spots) - 1, back * depth
            plan.append((0, (pre_share, depth), row, column, len(shapes), 0, to))
            plan.append((1, (dec_share, depth), row + 1, column, len(shapes), pre_share, to))
        shapes.append(jax.ShapeDtypeStruct((both, outer * depth), jnp.bfloat16))
    sends = pl.pallas_call(
        functools.partial(pack_kernel, plan, 3, len(shapes)),
        out_shape=shapes,
        in_specs=[SMEM] + [VMEM] * 3,
        out_specs=[VMEM] * len(shapes),
        compiler_params=PARAMS,
    )(numbers(spots), pre_x, dec_x, w_kv)
    moving = list(sends[: len(sizes)])
    arrived = list(sends[len(sizes) : len(sizes) + cores])
    row_sends = [None] + list(sends[len(sizes) + cores :])

    got = [None, to_inner(row_sends[1], 1)]
    got[1], moving[-1] = lax.optimization_barrier((got[1], moving[-1]))
    for step in range(2, inner):
        got.append(to_inner(row_sends[step], step))
        if step + 1 < inner:
            got[step], row_sends[step + 1] = lax.optimization_barrier(
                (got[step], row_sends[step + 1])
            )

    far = []
    for back in range(1, outer):
        moving = [to_outer(m) for m in moving]
        pieces = []
        for m in moving:
            if pieces:
                m, pieces[-1] = lax.optimization_barrier((m, pieces[-1]))
            pieces.append([m] + [to_team(m, turn) for turn in range(1, teams)])
        far.append(pieces)

    for rows in got[1:]:
        arrived += [rows] + [to_core(rows, turn) for turn in range(1, cores)]
    top_c, mixed_c = cached(dec_q, cache, cache_len, heads)
    arrived, top_c, mixed_c = lax.optimization_barrier((arrived, top_c, mixed_c))
    total_rows = span + count
    all_rows = inner * total_rows
    turns = [(team - turn) % teams * band for turn in range(teams)]
    *near, far_rows = pl.pallas_call(
        functools.partial(gather_kernel, inner, outer, cores, depth, teams),
        out_shape=[jax.ShapeDtypeStruct((all_rows, band), jnp.float32)] * teams
        + [jax.ShapeDtypeStruct((all_rows, (outer - 1) * depth), jnp.bfloat16)],
        in_specs=[SMEM] + [VMEM] * (1 + len(arrived)),
        out_specs=[VMEM] * (1 + teams),
        scratch_shapes=[pltpu.VMEM((all_rows, depth), jnp.bfloat16)],
        compiler_params=PARAMS,
    )(numbers([place] + turns), w_kv, *arrived)
    pieces = [moved for back in range(1, outer) for piece in far[back - 1] for moved in piece]
    summed = pl.pallas_call(
        functools.partial(far_kernel, teams),
        out_shape=jax.ShapeDtypeStruct((all_rows, width), jnp.bfloat16),
        in_specs=[VMEM] * (1 + teams + len(pieces)),
        out_specs=VMEM,
        compiler_params=PARAMS,
    )(*near, far_rows, *pieces)
    parts = exchange(summed)
    prompt_kv, own_kv = pl.pallas_call(
        functools.partial(finish_kernel, inner, cores, teams),
        out_shape=[
            jax.ShapeDtypeStruct((span, width), jnp.bfloat16),
            jax.ShapeDtypeStruct((count, width), jnp.bfloat16),
        ],
        in_specs=[SMEM] + [VMEM] * 2,
        out_specs=[VMEM] * 2,
        compiler_params=PARAMS,
    )(numbers([core] + turns), kv_scale[None, :], parts)

    blocks, owners = [], []
    shifted = prompt_kv
    for back in range(outer):
        if back:
            shifted = to_outer(shifted)
        for step in range(inner):
            blocks.append(to_inner(shifted, step) if step else shifted)
            owners.append(((block - back) % outer) * inner + (place ^ step))

    attended = pl.pallas_call(
        functools.partial(attend_kernel, heads),
        out_shape=jax.ShapeDtypeStruct(dec_q.shape, jnp.bfloat16),
        in_specs=[SMEM] * 3 + [VMEM] * (5 + len(blocks)),
        out_specs=VMEM,
        compiler_params=PARAMS,
    )(
        numbers([rank * count] + owners),
        prompt_owner,
        prompt_len,
        sample_rows,
        dec_q,
        top_c,
        mixed_c,
        own_kv,
        *blocks,
    )
    return (attended, prompt_kv)


def solution(mesh):
    in_specs = (
        P(("groups", "dp"), None),
        P(("groups", "dp"), None),
        P("dp", "tp"),
        P("tp"),
        P(("groups", "dp"), "tp"),
        P(("groups", "dp"), None, "tp"),
        P(("groups", "dp")),
        P("groups"),
        P("groups"),
        P("groups", None),
    )
    out_specs = (P(("groups", "dp"), "tp"), P(("groups", "dp"), "tp"))
    body = functools.partial(local, shape=dict(mesh.shape))
    return jax.shard_map(body, mesh=mesh, in_specs=in_specs, out_specs=out_specs, check_vma=False)
```

```python
import functools
import math

import jax
import jax.numpy as jnp
from jax import lax
from jax.experimental import pallas as pl
from jax.experimental.pallas import tpu as pltpu
from jax.sharding import PartitionSpec as P

HD = 128
REP = 12
NEG = -1e30
INNER = 4


def pack_kernel(plan, n_in, n_out, at_ref, *refs):
    ins, outs = refs[:n_in], refs[n_in : n_in + n_out]
    for src, shape, row, column, dst, to_row, to_column in plan:
        from_row = pl.multiple_of(at_ref[row], 16)
        from_column = pl.multiple_of(at_ref[column], 128)
        outs[dst][to_row : to_row + shape[0], to_column : to_column + shape[1]] = ins[src][
            pl.ds(from_row, shape[0]), pl.ds(from_column, shape[1])
        ]


def gather_kernel(inner, outer, cores, teams, last, at_ref, pre_ref, dec_ref, w_ref, *refs):
    n_arrived = (inner - 1) * cores
    arrived, pieces = refs[:n_arrived], refs[n_arrived:-3]
    sum_ref, last_ref, row_ref = refs[-3:]
    depth = w_ref.shape[0]
    early = depth - last
    pre_share, dec_share = pre_ref.shape[0] // cores, dec_ref.shape[0] // cores
    both = pre_share + dec_share

    def place(back):
        if back == 0:
            return [(row_ref, 0, 0, depth)]
        return [
            (row_ref, 0, depth + (back - 1) * early, early),
            (last_ref, early, (back - 1) * last, last),
        ]

    for back in range(outer):
        for target, start, to, size in place(back):
            for turn in range(cores):
                which = lax.rem(at_ref[0] - turn + cores, cores)
                columns = pl.ds(pl.multiple_of(at_ref[1 + back] + start, 128), size)
                base = turn * both
                target[base : base + pre_share, to : to + size] = pre_ref[
                    pl.ds(pl.multiple_of(which * pre_share, 16), pre_share), columns
                ]
                target[base + pre_share : base + both, to : to + size] = dec_ref[
                    pl.ds(pl.multiple_of(which * dec_share, 16), dec_share), columns
                ]
            for number, block in enumerate(arrived):
                base = (cores + number) * both
                start_at = back * depth + start
                target[base : base + both, to : to + size] = block[:, start_at : start_at + size]
    half = row_ref.shape[0] // 2
    band = sum_ref.shape[1] // teams
    for part in range(2):
        rows = slice(part * half, (part + 1) * half)
        for turn in range(teams):
            columns = pl.ds(pl.multiple_of(at_ref[1 + outer + turn], 128), band)
            summed = jnp.dot(
                row_ref[rows, :depth], w_ref[:, columns], preferred_element_type=jnp.float32
            )
            at = depth
            for piece in pieces[turn::teams]:
                summed = summed + jnp.dot(
                    row_ref[rows, at : at + piece.shape[0]],
                    piece[...],
                    preferred_element_type=jnp.float32,
                )
                at += piece.shape[0]
            sum_ref[rows, turn * band : (turn + 1) * band] = summed


def last_kernel(inner, teams, sum_ref, row_ref, *refs):
    pieces, outs = refs[:-inner], refs[-inner:]
    each = outs[0].shape[0]
    band = sum_ref.shape[1] // teams
    half = inner // 2
    for part in range(2):
        rows = slice(part * half * each, (part + 1) * half * each)
        for turn in range(teams):
            taken = slice(turn * band, (turn + 1) * band)
            summed = sum_ref[rows, taken]
            at = 0
            for piece in pieces[turn::teams]:
                summed = summed + jnp.dot(
                    row_ref[rows, at : at + piece.shape[0]],
                    piece[...],
                    preferred_element_type=jnp.float32,
                )
                at += piece.shape[0]
            for step in range(half):
                out = outs[part * half + step]
                out[:, taken] = summed[step * each : (step + 1) * each].astype(out.dtype)


def finish_kernel(cores, teams, at_ref, scale_ref, *refs):
    parts, (prompt_ref, own_ref) = refs[:-2], refs[-2:]
    span, count = prompt_ref.shape[0], own_ref.shape[0]
    pre_share, dec_share = span // cores, count // cores
    both = pre_share + dec_share
    band = scale_ref.shape[1] // teams
    for turn in range(teams):
        columns = pl.ds(pl.multiple_of(at_ref[1 + turn], 128), band)
        taken = slice(turn * band, (turn + 1) * band)
        summed = parts[0][:, taken]
        for part in parts[1:]:
            summed = summed + part[:, taken].astype(jnp.float32)
        done = (summed * scale_ref[:, columns]).astype(jnp.bfloat16)
        for share in range(cores):
            which = lax.rem(at_ref[0] - share + cores, cores)
            prompt_ref[pl.ds(pl.multiple_of(which * pre_share, 16), pre_share), columns] = done[
                share * both : share * both + pre_share
            ]
            own_ref[pl.ds(pl.multiple_of(which * dec_share, 16), dec_share), columns] = done[
                share * both + pre_share : (share + 1) * both
            ]


def match_rows(at_ref, owner_ref, len_ref, samples_ref, count):
    row = at_ref[0] + lax.broadcasted_iota(jnp.int32, (count, 1), 0)
    source = jnp.zeros((count, 1), jnp.int32)
    live = jnp.zeros((count, 1), jnp.int32)
    for prompt in range(samples_ref.shape[0]):
        hit = jnp.max(
            jnp.where(samples_ref[prompt : prompt + 1, :] == row, 1, 0), -1, keepdims=True
        )
        source = source + hit * owner_ref[prompt]
        live = live + hit * len_ref[prompt]
    return source, live


def absorb(at_ref, q_ref, source, live, head, blocks, top, mixed, own_ref):
    count, span = q_ref.shape[0], blocks[0].shape[0]
    factor = 1.0 / math.sqrt(HD)
    first = head * REP * HD
    low, mid, high = head * 2 * HD, head * 2 * HD + HD, head * 2 * HD + 2 * HD
    q = jnp.concatenate([q_ref[:, first + r * HD : first + (r + 1) * HD] for r in range(REP)], 0)
    picked = jnp.full((REP * count, span), NEG, jnp.float32)
    place = lax.broadcasted_iota(jnp.int32, (REP * count, span), 1)
    for at, block in enumerate(blocks):
        scores = lax.dot_general(
            q,
            block[:, low:mid],
            (((1,), (1,)), ((), ())),
            preferred_element_type=jnp.float32,
        )
        picked = jnp.where(source == at_ref[1 + at], scores * factor, picked)
    picked = jnp.where(place < live, picked, NEG)
    new = jnp.maximum(jnp.max(picked, -1, keepdims=True), top)
    if own_ref is not None:
        own_k = jnp.concatenate([own_ref[:, low:mid].astype(jnp.float32)] * REP, 0)
        own_v = jnp.concatenate([own_ref[:, mid:high].astype(jnp.float32)] * REP, 0)
        score = jnp.sum(q.astype(jnp.float32) * own_k, -1, keepdims=True) * factor
        new = jnp.maximum(new, score)
    weights = jnp.exp(picked - new)
    kept = jnp.exp(top - new)
    total = kept + jnp.sum(weights, -1, keepdims=True)
    mixed = mixed * kept
    if own_ref is not None:
        weight = jnp.exp(score - new)
        total = total + weight
        mixed = mixed + weight * own_v
    for at, block in enumerate(blocks):
        mixed = mixed + jnp.dot(
            jnp.where(source == at_ref[1 + at], weights, 0.0).astype(jnp.bfloat16),
            block[:, mid:high],
            preferred_element_type=jnp.float32,
        )
    return new + jnp.log(total), mixed / total


def first_kernel(
    heads, at_ref, owner_ref, len_ref, samples_ref, q_ref, top_ref, mixed_ref, own_ref, *refs
):
    blocks, (new_top, new_mixed, source_ref, live_ref) = refs[:-4], refs[-4:]
    source, live = match_rows(at_ref, owner_ref, len_ref, samples_ref, q_ref.shape[0])
    source = jnp.concatenate([source] * REP, 0)
    live = jnp.concatenate([live] * REP, 0)
    source_ref[...] = jnp.broadcast_to(source, source_ref.shape)
    live_ref[...] = jnp.broadcast_to(live, live_ref.shape)
    for head in range(heads):
        new_top[head], new_mixed[head] = absorb(
            at_ref, q_ref, source, live, head, blocks, top_ref[head], mixed_ref[head], own_ref
        )


def second_kernel(heads, at_ref, q_ref, source_ref, live_ref, top_ref, mixed_ref, *refs):
    blocks, out_ref = refs[:-1], refs[-1]
    count = q_ref.shape[0]
    for head in range(heads):
        _, mixed = absorb(
            at_ref,
            q_ref,
            source_ref[...],
            live_ref[...],
            head,
            blocks,
            top_ref[head],
            mixed_ref[head],
            None,
        )
        first = head * REP * HD
        for r in range(REP):
            out_ref[:, first + r * HD : first + (r + 1) * HD] = mixed[
                r * count : (r + 1) * count
            ].astype(out_ref.dtype)


VMEM = pl.BlockSpec(memory_space=pltpu.VMEM)
SMEM = pl.BlockSpec(memory_space=pltpu.SMEM)
PARAMS = pltpu.CompilerParams(vmem_limit_bytes=48 * 1024 * 1024)


def numbers(values):
    return jnp.stack([jnp.asarray(v, jnp.int32) for v in values])


def cached(query, cache, cache_len, heads):
    count = query.shape[0]
    factor = 1.0 / math.sqrt(HD)
    mask = (jnp.arange(cache.shape[1])[None, :] < cache_len[:, None])[:, None, :]
    query = query.reshape(count, heads, REP, HD)
    tops, mixes = [], []
    for head in range(heads):
        low, mid, high = head * 2 * HD, head * 2 * HD + HD, head * 2 * HD + 2 * HD
        scores = jnp.einsum(
            "srd,sjd->srj",
            query[:, head],
            cache[:, :, low:mid],
            preferred_element_type=jnp.float32,
        )
        scores = jnp.where(mask, scores * factor, NEG)
        top = jnp.max(scores, -1, keepdims=True)
        weights = jnp.exp(scores - top)
        total = jnp.sum(weights, -1, keepdims=True)
        mixed = jnp.einsum(
            "srj,sjd->srd",
            weights.astype(jnp.bfloat16),
            cache[:, :, mid:high],
            preferred_element_type=jnp.float32,
        )
        top = jnp.broadcast_to(top + jnp.log(total), (count, REP, HD))
        tops.append(top.transpose(1, 0, 2).reshape(REP * count, HD))
        mixes.append((mixed / total).transpose(1, 0, 2).reshape(REP * count, HD))
    return jnp.stack(tops), jnp.stack(mixes)


def stages(depth):
    unit = 128
    last = max(unit, depth // 3 // unit * unit)
    return (depth - last, last)


def local(
    pre_x,
    dec_x,
    w_kv,
    kv_scale,
    dec_q,
    cache,
    cache_len,
    prompt_owner,
    prompt_len,
    sample_rows,
    *,
    shape,
):
    teams, ranks, cores = shape["groups"], shape["dp"], shape["tp"]
    inner = INNER
    outer = ranks // inner
    span, features = pre_x.shape
    count = dec_x.shape[0]
    depth, width = w_kv.shape
    heads = width // (2 * HD)
    band = width // teams
    team = lax.axis_index("groups")
    rank = lax.axis_index("dp")
    core = lax.axis_index("tp")
    place, block = rank % inner, rank // inner

    def to_inner(value, step):
        pairs = [(r, r // inner * inner + (r % inner ^ step)) for r in range(ranks)]
        return lax.ppermute(value, "dp", pairs)

    def to_outer(value, step=1):
        pairs = [(r, (r + step * inner) % ranks) for r in range(ranks)]
        return lax.ppermute(value, "dp", pairs)

    def to_team(value, step):
        return lax.ppermute(value, "groups", [(i, (i + step) % teams) for i in range(teams)])

    def to_core(value, step):
        return lax.ppermute(value, "tp", [(i, (i + step) % cores) for i in range(cores)])

    sizes = stages(depth)
    pre_share, dec_share = span // cores, count // cores
    both = pre_share + dec_share
    spots = [team * band]
    plan, shapes = [], []
    for number, size in enumerate(sizes):
        spots.append(sum(sizes[:number]))
        plan.append((2, (size, band), len(spots) - 1, 0, number, 0, 0))
        shapes.append(jax.ShapeDtypeStruct((size, band), jnp.bfloat16))
    spots += [core * pre_share, core * dec_share]
    row = len(spots) - 2
    for step in range(1, inner):
        for back in range(outer):
            spots.append((((block - back) % outer) * inner + (place ^ step)) * depth)
            column, to = len(spots) - 1, back * depth
            plan.append((0, (pre_share, depth), row, column, len(shapes), 0, to))
            plan.append((1, (dec_share, depth), row + 1, column, len(shapes), pre_share, to))
        shapes.append(jax.ShapeDtypeStruct((both, outer * depth), jnp.bfloat16))
    sends = pl.pallas_call(
        functools.partial(pack_kernel, plan, 3, len(shapes)),
        out_shape=shapes,
        in_specs=[SMEM] + [VMEM] * 3,
        out_specs=[VMEM] * len(shapes),
        compiler_params=PARAMS,
    )(numbers(spots), pre_x, dec_x, w_kv)
    moving, row_sends = list(sends[: len(sizes)]), sends[len(sizes) :]

    far = []
    for back in range(1, outer):
        moving = [to_outer(m) for m in moving]
        pieces = []
        for m in moving:
            if pieces:
                m, pieces[-1] = lax.optimization_barrier((m, pieces[-1]))
            pieces.append([m] + [to_team(m, turn) for turn in range(1, teams)])
        far.append(pieces)

    arrived = []
    for step in range(1, inner):
        got = to_inner(row_sends[step - 1], step)
        arrived += [got] + [to_core(got, turn) for turn in range(1, cores)]
    top_c, mixed_c = cached(dec_q, cache, cache_len, heads)
    arrived, top_c, mixed_c = lax.optimization_barrier((arrived, top_c, mixed_c))
    total_rows = span + count
    all_rows = inner * total_rows
    turns = [(team - turn) % teams * band for turn in range(teams)]
    last = sizes[-1]
    early = [m for pieces in far for piece in pieces[:-1] for m in piece]
    late = [m for pieces in far for m in pieces[-1]]
    summed, last_rows = pl.pallas_call(
        functools.partial(gather_kernel, inner, outer, cores, teams, last),
        out_shape=[
            jax.ShapeDtypeStruct((all_rows, width), jnp.float32),
            jax.ShapeDtypeStruct((all_rows, (outer - 1) * last), jnp.bfloat16),
        ],
        in_specs=[SMEM] + [VMEM] * (3 + len(arrived) + len(early)),
        out_specs=[VMEM] * 2,
        scratch_shapes=[
            pltpu.VMEM((all_rows, outer * depth - (outer - 1) * last), jnp.bfloat16)
        ],
        compiler_params=PARAMS,
    )(
        numbers(
            [core]
            + [(((block - back) % outer) * inner + place) * depth for back in range(outer)]
            + turns
        ),
        pre_x,
        dec_x,
        w_kv,
        *arrived,
        *early,
    )
    parts = pl.pallas_call(
        functools.partial(last_kernel, inner, teams),
        out_shape=[jax.ShapeDtypeStruct((total_rows, width), jnp.float32)]
        + [jax.ShapeDtypeStruct((total_rows, width), jnp.bfloat16)] * (inner - 1),
        in_specs=[VMEM] * (2 + len(late)),
        out_specs=[VMEM] * inner,
        compiler_params=PARAMS,
    )(summed, last_rows, *late)
    parts = [parts[0]] + [to_inner(parts[step], step) for step in range(1, inner)]
    prompt_kv, own_kv = pl.pallas_call(
        functools.partial(finish_kernel, cores, teams),
        out_shape=[
            jax.ShapeDtypeStruct((span, width), jnp.bfloat16),
            jax.ShapeDtypeStruct((count, width), jnp.bfloat16),
        ],
        in_specs=[SMEM] + [VMEM] * (1 + inner),
        out_specs=[VMEM] * 2,
        compiler_params=PARAMS,
    )(numbers([core] + turns), kv_scale[None, :], *parts)

    blocks, owners = [], []
    shifted = prompt_kv
    for back in range(outer):
        if back:
            shifted = to_outer(shifted)
        for step in range(inner):
            blocks.append(to_inner(shifted, step) if step else shifted)
            owners.append(((block - back) % outer) * inner + (place ^ step))

    state = jax.ShapeDtypeStruct(top_c.shape, jnp.float32)
    labels = jax.ShapeDtypeStruct((REP * count, HD), jnp.int32)
    *state, source, live = pl.pallas_call(
        functools.partial(first_kernel, heads),
        out_shape=[state, state, labels, labels],
        in_specs=[SMEM] * 3 + [VMEM] * (5 + inner),
        out_specs=[VMEM] * 4,
        compiler_params=PARAMS,
    )(
        numbers([rank * count] + owners[:inner]),
        prompt_owner,
        prompt_len,
        sample_rows,
        dec_q,
        top_c,
        mixed_c,
        own_kv,
        *blocks[:inner],
    )
    attended = pl.pallas_call(
        functools.partial(second_kernel, heads),
        out_shape=jax.ShapeDtypeStruct(dec_q.shape, jnp.bfloat16),
        in_specs=[SMEM] + [VMEM] * (5 + len(blocks) - inner),
        out_specs=VMEM,
        compiler_params=PARAMS,
    )(numbers([rank * count] + owners[inner:]), dec_q, source, live, *state, *blocks[inner:])
    return (attended, prompt_kv)


def solution(mesh):
    in_specs = (
        P(("groups", "dp"), None),
        P(("groups", "dp"), None),
        P("dp", "tp"),
        P("tp"),
        P(("groups", "dp"), "tp"),
        P(("groups", "dp"), None, "tp"),
        P(("groups", "dp")),
        P("groups"),
        P("groups"),
        P("groups", None),
    )
    out_specs = (P(("groups", "dp"), "tp"), P(("groups", "dp"), "tp"))
    body = functools.partial(local, shape=dict(mesh.shape))
    return jax.shard_map(body, mesh=mesh, in_specs=in_specs, out_specs=out_specs, check_vma=False)
```

```python
import functools
import math

import jax
import jax.numpy as jnp
from jax import lax
from jax.experimental import pallas as pl
from jax.experimental.pallas import tpu as pltpu
from jax.sharding import PartitionSpec as P

HD = 128
REP = 12
NEG = -1e30
INNER = 4


def pack_kernel(plan, n_in, n_out, at_ref, *refs):
    ins, outs, sems = refs[:n_in], refs[n_in : n_in + n_out], refs[n_in + n_out]
    copies = []
    for number, (src, shape, row, column, dst, to_row, to_column) in enumerate(plan):
        from_row = pl.multiple_of(at_ref[row], 16)
        from_column = pl.multiple_of(at_ref[column], 128)
        copy = pltpu.make_async_copy(
            ins[src].at[pl.ds(from_row, shape[0]), pl.ds(from_column, shape[1])],
            outs[dst].at[pl.ds(to_row, shape[0]), pl.ds(to_column, shape[1])],
            sems.at[number],
        )
        copy.start()
        copies.append(copy)
    for copy in copies:
        copy.wait()


def gather_kernel(inner, outer, cores, teams, last, at_ref, pre_ref, dec_ref, w_ref, *refs):
    n_arrived = (inner - 1) * cores
    arrived, pieces = refs[:n_arrived], refs[n_arrived:-3]
    sum_ref, last_ref, row_ref = refs[-3:]
    depth = w_ref.shape[0]
    early = depth - last
    pre_share, dec_share = pre_ref.shape[0] // cores, dec_ref.shape[0] // cores
    both = pre_share + dec_share

    def place(back):
        if back == 0:
            return [(row_ref, 0, 0, depth)]
        return [
            (row_ref, 0, depth + (back - 1) * early, early),
            (last_ref, early, (back - 1) * last, last),
        ]

    for back in range(outer):
        for target, start, to, size in place(back):
            for turn in range(cores):
                which = lax.rem(at_ref[0] - turn + cores, cores)
                columns = pl.ds(pl.multiple_of(at_ref[1 + back] + start, 128), size)
                base = turn * both
                target[base : base + pre_share, to : to + size] = pre_ref[
                    pl.ds(pl.multiple_of(which * pre_share, 16), pre_share), columns
                ]
                target[base + pre_share : base + both, to : to + size] = dec_ref[
                    pl.ds(pl.multiple_of(which * dec_share, 16), dec_share), columns
                ]
            for number, block in enumerate(arrived):
                base = (cores + number) * both
                start_at = back * depth + start
                target[base : base + both, to : to + size] = block[:, start_at : start_at + size]
    half = row_ref.shape[0] // 2
    band = sum_ref.shape[1] // teams
    for part in range(2):
        rows = slice(part * half, (part + 1) * half)
        for turn in range(teams):
            columns = pl.ds(pl.multiple_of(at_ref[1 + outer + turn], 128), band)
            summed = jnp.dot(
                row_ref[rows, :depth], w_ref[:, columns], preferred_element_type=jnp.float32
            )
            at = depth
            for piece in pieces[turn::teams]:
                summed = summed + jnp.dot(
                    row_ref[rows, at : at + piece.shape[0]],
                    piece[...],
                    preferred_element_type=jnp.float32,
                )
                at += piece.shape[0]
            sum_ref[rows, turn * band : (turn + 1) * band] = summed


def last_kernel(inner, teams, sum_ref, row_ref, *refs):
    pieces, outs = refs[:-inner], refs[-inner:]
    each = outs[0].shape[0]
    band = sum_ref.shape[1] // teams
    half = inner // 2
    for part in range(2):
        rows = slice(part * half * each, (part + 1) * half * each)
        for turn in range(teams):
            taken = slice(turn * band, (turn + 1) * band)
            summed = sum_ref[rows, taken]
            at = 0
            for piece in pieces[turn::teams]:
                summed = summed + jnp.dot(
                    row_ref[rows, at : at + piece.shape[0]],
                    piece[...],
                    preferred_element_type=jnp.float32,
                )
                at += piece.shape[0]
            for step in range(half):
                out = outs[part * half + step]
                out[:, taken] = summed[step * each : (step + 1) * each].astype(out.dtype)


def finish_kernel(cores, teams, at_ref, scale_ref, *refs):
    parts, (prompt_ref, sent_ref, own_ref) = refs[:-3], refs[-3:]
    span, count = prompt_ref.shape[0], own_ref.shape[0]
    pre_share, dec_share = span // cores, count // cores
    both = pre_share + dec_share
    band = scale_ref.shape[1] // teams
    for turn in range(teams):
        columns = pl.ds(pl.multiple_of(at_ref[1 + turn], 128), band)
        taken = slice(turn * band, (turn + 1) * band)
        summed = parts[0][:, taken]
        for part in parts[1:]:
            summed = summed + part[:, taken].astype(jnp.float32)
        done = (summed * scale_ref[:, columns]).astype(jnp.bfloat16)
        for share in range(cores):
            which = lax.rem(at_ref[0] - share + cores, cores)
            rows = pl.ds(pl.multiple_of(which * pre_share, 16), pre_share)
            prompt_ref[rows, columns] = done[share * both : share * both + pre_share]
            sent_ref[rows, columns] = done[share * both : share * both + pre_share]
            own_ref[pl.ds(pl.multiple_of(which * dec_share, 16), dec_share), columns] = done[
                share * both + pre_share : (share + 1) * both
            ]


def match_rows(at_ref, owner_ref, len_ref, samples_ref, count):
    row = at_ref[0] + lax.broadcasted_iota(jnp.int32, (count, 1), 0)
    source = jnp.zeros((count, 1), jnp.int32)
    live = jnp.zeros((count, 1), jnp.int32)
    for prompt in range(samples_ref.shape[0]):
        hit = jnp.max(
            jnp.where(samples_ref[prompt : prompt + 1, :] == row, 1, 0), -1, keepdims=True
        )
        source = source + hit * owner_ref[prompt]
        live = live + hit * len_ref[prompt]
    return source, live


def absorb(at_ref, q_ref, source, live, head, blocks, top, mixed, own_ref):
    count, span = q_ref.shape[0], blocks[0].shape[0]
    factor = 1.0 / math.sqrt(HD)
    first = head * REP * HD
    low, mid, high = head * 2 * HD, head * 2 * HD + HD, head * 2 * HD + 2 * HD
    q = jnp.concatenate([q_ref[:, first + r * HD : first + (r + 1) * HD] for r in range(REP)], 0)
    picked = jnp.full((REP * count, span), NEG, jnp.float32)
    place = lax.broadcasted_iota(jnp.int32, (REP * count, span), 1)
    for at, block in enumerate(blocks):
        scores = lax.dot_general(
            q,
            block[:, low:mid],
            (((1,), (1,)), ((), ())),
            preferred_element_type=jnp.float32,
        )
        picked = jnp.where(source == at_ref[1 + at], scores * factor, picked)
    picked = jnp.where(place < live, picked, NEG)
    new = jnp.maximum(jnp.max(picked, -1, keepdims=True), top)
    if own_ref is not None:
        own_k = jnp.concatenate([own_ref[:, low:mid].astype(jnp.float32)] * REP, 0)
        own_v = jnp.concatenate([own_ref[:, mid:high].astype(jnp.float32)] * REP, 0)
        score = jnp.sum(q.astype(jnp.float32) * own_k, -1, keepdims=True) * factor
        new = jnp.maximum(new, score)
    weights = jnp.exp(picked - new)
    kept = jnp.exp(top - new)
    total = kept + jnp.sum(weights, -1, keepdims=True)
    mixed = mixed * kept
    if own_ref is not None:
        weight = jnp.exp(score - new)
        total = total + weight
        mixed = mixed + weight * own_v
    for at, block in enumerate(blocks):
        mixed = mixed + jnp.dot(
            jnp.where(source == at_ref[1 + at], weights, 0.0).astype(jnp.bfloat16),
            block[:, mid:high],
            preferred_element_type=jnp.float32,
        )
    return new + jnp.log(total), mixed / total


def first_kernel(
    heads, at_ref, owner_ref, len_ref, samples_ref, q_ref, top_ref, mixed_ref, own_ref, *refs
):
    blocks, (new_top, new_mixed, source_ref, live_ref) = refs[:-4], refs[-4:]
    source, live = match_rows(at_ref, owner_ref, len_ref, samples_ref, q_ref.shape[0])
    source = jnp.concatenate([source] * REP, 0)
    live = jnp.concatenate([live] * REP, 0)
    source_ref[...] = jnp.broadcast_to(source, source_ref.shape)
    live_ref[...] = jnp.broadcast_to(live, live_ref.shape)
    for head in range(heads):
        new_top[head], new_mixed[head] = absorb(
            at_ref, q_ref, source, live, head, blocks, top_ref[head], mixed_ref[head], own_ref
        )


def second_kernel(heads, at_ref, q_ref, source_ref, live_ref, top_ref, mixed_ref, *refs):
    blocks, out_ref = refs[:-1], refs[-1]
    count = q_ref.shape[0]
    for head in range(heads):
        _, mixed = absorb(
            at_ref,
            q_ref,
            source_ref[...],
            live_ref[...],
            head,
            blocks,
            top_ref[head],
            mixed_ref[head],
            None,
        )
        first = head * REP * HD
        for r in range(REP):
            out_ref[:, first + r * HD : first + (r + 1) * HD] = mixed[
                r * count : (r + 1) * count
            ].astype(out_ref.dtype)


VMEM = pl.BlockSpec(memory_space=pltpu.VMEM)
SMEM = pl.BlockSpec(memory_space=pltpu.SMEM)
HBM = pl.BlockSpec(memory_space=pltpu.HBM)
PARAMS = pltpu.CompilerParams(vmem_limit_bytes=24 * 1024 * 1024)


def numbers(values):
    return jnp.stack([jnp.asarray(v, jnp.int32) for v in values])


def cached(query, cache, cache_len, heads):
    count = query.shape[0]
    factor = 1.0 / math.sqrt(HD)
    mask = (jnp.arange(cache.shape[1])[None, :] < cache_len[:, None])[:, None, :]
    query = query.reshape(count, heads, REP, HD)
    tops, mixes = [], []
    for head in range(heads):
        low, mid, high = head * 2 * HD, head * 2 * HD + HD, head * 2 * HD + 2 * HD
        scores = jnp.einsum(
            "srd,sjd->srj",
            query[:, head],
            cache[:, :, low:mid],
            preferred_element_type=jnp.float32,
        )
        scores = jnp.where(mask, scores * factor, NEG)
        top = jnp.max(scores, -1, keepdims=True)
        weights = jnp.exp(scores - top)
        total = jnp.sum(weights, -1, keepdims=True)
        mixed = jnp.einsum(
            "srj,sjd->srd",
            weights.astype(jnp.bfloat16),
            cache[:, :, mid:high],
            preferred_element_type=jnp.float32,
        )
        top = jnp.broadcast_to(top + jnp.log(total), (count, REP, HD))
        tops.append(top.transpose(1, 0, 2).reshape(REP * count, HD))
        mixes.append((mixed / total).transpose(1, 0, 2).reshape(REP * count, HD))
    return jnp.stack(tops), jnp.stack(mixes)


def stages(depth):
    unit = 128
    first = max(unit, depth * 5 // 12 // unit * unit)
    return (first, depth - first)


def local(
    pre_x,
    dec_x,
    w_kv,
    kv_scale,
    dec_q,
    cache,
    cache_len,
    prompt_owner,
    prompt_len,
    sample_rows,
    *,
    shape,
):
    teams, ranks, cores = shape["groups"], shape["dp"], shape["tp"]
    inner = INNER
    outer = ranks // inner
    span, features = pre_x.shape
    count = dec_x.shape[0]
    depth, width = w_kv.shape
    heads = width // (2 * HD)
    band = width // teams
    team = lax.axis_index("groups")
    rank = lax.axis_index("dp")
    core = lax.axis_index("tp")
    place, block = rank % inner, rank // inner

    def to_inner(value, step):
        pairs = [(r, r // inner * inner + (r % inner ^ step)) for r in range(ranks)]
        return lax.ppermute(value, "dp", pairs)

    def to_outer(value, step=1):
        pairs = [(r, (r + step * inner) % ranks) for r in range(ranks)]
        return lax.ppermute(value, "dp", pairs)

    def to_team(value, step):
        return lax.ppermute(value, "groups", [(i, (i + step) % teams) for i in range(teams)])

    def to_core(value, step):
        return lax.ppermute(value, "tp", [(i, (i + step) % cores) for i in range(cores)])

    sizes = stages(depth)
    pre_share, dec_share = span // cores, count // cores
    both = pre_share + dec_share
    spots = [team * band]
    plan, shapes = [], []
    for number, size in enumerate(sizes):
        spots.append(sum(sizes[:number]))
        plan.append((2, (size, band), len(spots) - 1, 0, number, 0, 0))
        shapes.append(jax.ShapeDtypeStruct((size, band), jnp.bfloat16))
    spots += [core * pre_share, core * dec_share]
    row = len(spots) - 2
    for step in range(1, inner):
        for back in range(outer):
            spots.append((((block - back) % outer) * inner + (place ^ step)) * depth)
            column, to = len(spots) - 1, back * depth
            plan.append((0, (pre_share, depth), row, column, len(shapes), 0, to))
            plan.append((1, (dec_share, depth), row + 1, column, len(shapes), pre_share, to))
        shapes.append(jax.ShapeDtypeStruct((both, outer * depth), jnp.bfloat16))
    sends = pl.pallas_call(
        functools.partial(pack_kernel, plan, 3, len(shapes)),
        out_shape=shapes,
        in_specs=[SMEM] + [HBM] * 3,
        out_specs=[VMEM] * len(shapes),
        scratch_shapes=[pltpu.SemaphoreType.DMA((len(plan),))],
        compiler_params=PARAMS,
    )(numbers(spots), pre_x, dec_x, w_kv)
    moving, row_sends = list(sends[: len(sizes)]), list(sends[len(sizes) :])

    far = []
    for back in range(1, outer):
        moving = [to_outer(m) for m in moving]
        if back == 1:
            moving[0], row_sends[-1] = lax.optimization_barrier((moving[0], row_sends[-1]))
        pieces = []
        for m in moving:
            if pieces:
                m, pieces[-1] = lax.optimization_barrier((m, pieces[-1]))
            pieces.append([m] + [to_team(m, turn) for turn in range(1, teams)])
        far.append(pieces)

    arrived = []
    for step in range(1, inner):
        got = to_inner(row_sends[step - 1], step)
        arrived += [got] + [to_core(got, turn) for turn in range(1, cores)]
    top_c, mixed_c = cached(dec_q, cache, cache_len, heads)
    arrived, top_c, mixed_c = lax.optimization_barrier((arrived, top_c, mixed_c))
    total_rows = span + count
    all_rows = inner * total_rows
    turns = [(team - turn) % teams * band for turn in range(teams)]
    last = sizes[-1]
    early = [m for pieces in far for piece in pieces[:-1] for m in piece]
    late = [m for pieces in far for m in pieces[-1]]
    summed, last_rows = pl.pallas_call(
        functools.partial(gather_kernel, inner, outer, cores, teams, last),
        out_shape=[
            jax.ShapeDtypeStruct((all_rows, width), jnp.float32),
            jax.ShapeDtypeStruct((all_rows, (outer - 1) * last), jnp.bfloat16),
        ],
        in_specs=[SMEM] + [VMEM] * (3 + len(arrived) + len(early)),
        out_specs=[VMEM] * 2,
        scratch_shapes=[
            pltpu.VMEM((all_rows, outer * depth - (outer - 1) * last), jnp.bfloat16)
        ],
        compiler_params=PARAMS,
    )(
        numbers(
            [core]
            + [(((block - back) % outer) * inner + place) * depth for back in range(outer)]
            + turns
        ),
        pre_x,
        dec_x,
        w_kv,
        *arrived,
        *early,
    )
    parts = pl.pallas_call(
        functools.partial(last_kernel, inner, teams),
        out_shape=[jax.ShapeDtypeStruct((total_rows, width), jnp.float32)]
        + [jax.ShapeDtypeStruct((total_rows, width), jnp.bfloat16)] * (inner - 1),
        in_specs=[VMEM] * (2 + len(late)),
        out_specs=[VMEM] * inner,
        compiler_params=PARAMS,
    )(summed, last_rows, *late)
    parts = [parts[0]] + [to_inner(parts[step], step) for step in range(1, inner)]
    prompt_kv, shifted, own_kv = pl.pallas_call(
        functools.partial(finish_kernel, cores, teams),
        out_shape=[
            jax.ShapeDtypeStruct((span, width), jnp.bfloat16),
            jax.ShapeDtypeStruct((span, width), jnp.bfloat16),
            jax.ShapeDtypeStruct((count, width), jnp.bfloat16),
        ],
        in_specs=[SMEM] + [VMEM] * (1 + inner),
        out_specs=[VMEM] * 3,
        compiler_params=PARAMS,
    )(numbers([core] + turns), kv_scale[None, :], *parts)

    blocks, owners = [], []
    for back in range(outer):
        if back:
            shifted = to_outer(shifted)
        for step in range(inner):
            blocks.append(to_inner(shifted, step) if step else shifted)
            owners.append(((block - back) % outer) * inner + (place ^ step))

    state = jax.ShapeDtypeStruct(top_c.shape, jnp.float32)
    labels = jax.ShapeDtypeStruct((REP * count, HD), jnp.int32)
    *state, source, live = pl.pallas_call(
        functools.partial(first_kernel, heads),
        out_shape=[state, state, labels, labels],
        in_specs=[SMEM] * 3 + [VMEM] * (5 + inner),
        out_specs=[VMEM] * 4,
        compiler_params=PARAMS,
    )(
        numbers([rank * count] + owners[:inner]),
        prompt_owner,
        prompt_len,
        sample_rows,
        dec_q,
        top_c,
        mixed_c,
        own_kv,
        *blocks[:inner],
    )
    attended = pl.pallas_call(
        functools.partial(second_kernel, heads),
        out_shape=jax.ShapeDtypeStruct(dec_q.shape, jnp.bfloat16),
        in_specs=[SMEM] + [VMEM] * (5 + len(blocks) - inner),
        out_specs=VMEM,
        compiler_params=PARAMS,
    )(numbers([rank * count] + owners[inner:]), dec_q, source, live, *state, *blocks[inner:])
    return (attended, prompt_kv)


def solution(mesh):
    in_specs = (
        P(("groups", "dp"), None),
        P(("groups", "dp"), None),
        P("dp", "tp"),
        P("tp"),
        P(("groups", "dp"), "tp"),
        P(("groups", "dp"), None, "tp"),
        P(("groups", "dp")),
        P("groups"),
        P("groups"),
        P("groups", None),
    )
    out_specs = (P(("groups", "dp"), "tp"), P(("groups", "dp"), "tp"))
    body = functools.partial(local, shape=dict(mesh.shape))
    return jax.shard_map(body, mesh=mesh, in_specs=in_specs, out_specs=out_specs, check_vma=False)
```

```python
import functools
import math

import jax
import jax.numpy as jnp
from jax import lax
from jax.experimental import pallas as pl
from jax.experimental.pallas import tpu as pltpu
from jax.sharding import PartitionSpec as P

HD = 128
REP = 12
NEG = -1e30
INNER = 4


def pack_kernel(plan, n_in, n_out, at_ref, *refs):
    ins, outs, sems = refs[:n_in], refs[n_in : n_in + n_out], refs[n_in + n_out]
    copies = []
    for number, (src, shape, row, column, dst, to_row, to_column) in enumerate(plan):
        from_row = pl.multiple_of(at_ref[row], 16)
        from_column = pl.multiple_of(at_ref[column], 128)
        copy = pltpu.make_async_copy(
            ins[src].at[pl.ds(from_row, shape[0]), pl.ds(from_column, shape[1])],
            outs[dst].at[pl.ds(to_row, shape[0]), pl.ds(to_column, shape[1])],
            sems.at[number],
        )
        copy.start()
        copies.append(copy)
    for copy in copies:
        copy.wait()


def gather_kernel(inner, outer, cores, teams, last, at_ref, pre_ref, dec_ref, w_ref, *refs):
    n_arrived = (inner - 1) * cores
    arrived, pieces = refs[:n_arrived], refs[n_arrived : -2 - teams]
    sum_refs, (last_ref, row_ref) = refs[-2 - teams : -2], refs[-2:]
    depth = w_ref.shape[0]
    early = depth - last
    pre_share, dec_share = pre_ref.shape[0] // cores, dec_ref.shape[0] // cores
    both = pre_share + dec_share

    def place(back):
        if back == 0:
            return [(row_ref, 0, 0, depth)]
        return [
            (row_ref, 0, depth + (back - 1) * early, early),
            (last_ref, early, (back - 1) * last, last),
        ]

    for back in range(outer):
        for target, start, to, size in place(back):
            for turn in range(cores):
                which = lax.rem(at_ref[0] - turn + cores, cores)
                columns = pl.ds(pl.multiple_of(at_ref[1 + back] + start, 128), size)
                base = turn * both
                target[base : base + pre_share, to : to + size] = pre_ref[
                    pl.ds(pl.multiple_of(which * pre_share, 16), pre_share), columns
                ]
                target[base + pre_share : base + both, to : to + size] = dec_ref[
                    pl.ds(pl.multiple_of(which * dec_share, 16), dec_share), columns
                ]
            for number, block in enumerate(arrived):
                base = (cores + number) * both
                start_at = back * depth + start
                target[base : base + both, to : to + size] = block[:, start_at : start_at + size]
    half = row_ref.shape[0] // 2
    band = sum_refs[0].shape[1]
    for part in range(2):
        rows = slice(part * half, (part + 1) * half)
        for turn in range(teams):
            columns = pl.ds(pl.multiple_of(at_ref[1 + outer + turn], 128), band)
            summed = jnp.dot(
                row_ref[rows, :depth], w_ref[:, columns], preferred_element_type=jnp.float32
            )
            at = depth
            for piece in pieces[turn::teams]:
                summed = summed + jnp.dot(
                    row_ref[rows, at : at + piece.shape[0]],
                    piece[...],
                    preferred_element_type=jnp.float32,
                )
                at += piece.shape[0]
            sum_refs[turn][rows, :] = summed


def last_kernel(inner, sum_ref, row_ref, *refs):
    pieces, outs = refs[:-inner], refs[-inner:]
    each = outs[0].shape[0]
    half = inner // 2
    for part in range(2):
        rows = slice(part * half * each, (part + 1) * half * each)
        summed = sum_ref[rows, :]
        at = 0
        for piece in pieces:
            summed = summed + jnp.dot(
                row_ref[rows, at : at + piece.shape[0]],
                piece[...],
                preferred_element_type=jnp.float32,
            )
            at += piece.shape[0]
        for step in range(half):
            out = outs[part * half + step]
            out[...] = summed[step * each : (step + 1) * each].astype(out.dtype)


def finish_kernel(cores, teams, at_ref, scale_ref, *refs):
    parts, (prompt_ref, sent_ref, own_ref) = refs[:-3], refs[-3:]
    span, count = prompt_ref.shape[0], own_ref.shape[0]
    pre_share, dec_share = span // cores, count // cores
    both = pre_share + dec_share
    band = scale_ref.shape[1] // teams
    for turn in range(teams):
        columns = pl.ds(pl.multiple_of(at_ref[1 + turn], 128), band)
        own, *others = parts[turn * len(parts) // teams : (turn + 1) * len(parts) // teams]
        summed = own[...]
        for part in others:
            summed = summed + part[...].astype(jnp.float32)
        done = (summed * scale_ref[:, columns]).astype(jnp.bfloat16)
        for share in range(cores):
            which = lax.rem(at_ref[0] - share + cores, cores)
            rows = pl.ds(pl.multiple_of(which * pre_share, 16), pre_share)
            prompt_ref[rows, columns] = done[share * both : share * both + pre_share]
            sent_ref[rows, columns] = done[share * both : share * both + pre_share]
            own_ref[pl.ds(pl.multiple_of(which * dec_share, 16), dec_share), columns] = done[
                share * both + pre_share : (share + 1) * both
            ]


def match_rows(at_ref, owner_ref, len_ref, samples_ref, count):
    row = at_ref[0] + lax.broadcasted_iota(jnp.int32, (count, 1), 0)
    source = jnp.zeros((count, 1), jnp.int32)
    live = jnp.zeros((count, 1), jnp.int32)
    for prompt in range(samples_ref.shape[0]):
        hit = jnp.max(
            jnp.where(samples_ref[prompt : prompt + 1, :] == row, 1, 0), -1, keepdims=True
        )
        source = source + hit * owner_ref[prompt]
        live = live + hit * len_ref[prompt]
    return source, live


def absorb(at_ref, q_ref, source, live, head, blocks, top, mixed, own_ref):
    count, span = q_ref.shape[0], blocks[0].shape[0]
    factor = 1.0 / math.sqrt(HD)
    first = head * REP * HD
    low, mid, high = head * 2 * HD, head * 2 * HD + HD, head * 2 * HD + 2 * HD
    q = jnp.concatenate([q_ref[:, first + r * HD : first + (r + 1) * HD] for r in range(REP)], 0)
    picked = jnp.full((REP * count, span), NEG, jnp.float32)
    place = lax.broadcasted_iota(jnp.int32, (REP * count, span), 1)
    for at, block in enumerate(blocks):
        scores = lax.dot_general(
            q,
            block[:, low:mid],
            (((1,), (1,)), ((), ())),
            preferred_element_type=jnp.float32,
        )
        picked = jnp.where(source == at_ref[1 + at], scores * factor, picked)
    picked = jnp.where(place < live, picked, NEG)
    new = jnp.maximum(jnp.max(picked, -1, keepdims=True), top)
    if own_ref is not None:
        own_k = jnp.concatenate([own_ref[:, low:mid].astype(jnp.float32)] * REP, 0)
        own_v = jnp.concatenate([own_ref[:, mid:high].astype(jnp.float32)] * REP, 0)
        score = jnp.sum(q.astype(jnp.float32) * own_k, -1, keepdims=True) * factor
        new = jnp.maximum(new, score)
    weights = jnp.exp(picked - new)
    kept = jnp.exp(top - new)
    total = kept + jnp.sum(weights, -1, keepdims=True)
    mixed = mixed * kept
    if own_ref is not None:
        weight = jnp.exp(score - new)
        total = total + weight
        mixed = mixed + weight * own_v
    for at, block in enumerate(blocks):
        mixed = mixed + jnp.dot(
            jnp.where(source == at_ref[1 + at], weights, 0.0).astype(jnp.bfloat16),
            block[:, mid:high],
            preferred_element_type=jnp.float32,
        )
    return new + jnp.log(total), mixed / total


def cache_kernel(heads, len_ref, q_ref, cache_ref, top_ref, mixed_ref):
    count, rows, _ = q_ref.shape
    factor = 1.0 / math.sqrt(HD)
    head_of = lax.broadcasted_iota(jnp.int32, (rows, 1), 0) // REP
    spot = lax.broadcasted_iota(jnp.int32, (rows, cache_ref.shape[1]), 1)
    tops, mixes = [], []
    for sample in range(count):
        length = len_ref[pl.program_id(0) * count + sample]
        scores = mixed = None
        for head in range(heads):
            key = cache_ref[sample, :, head * 2 * HD : head * 2 * HD + HD]
            found = lax.dot_general(
                q_ref[sample], key, (((1,), (1,)), ((), ())), preferred_element_type=jnp.float32
            )
            scores = found if head == 0 else jnp.where(head_of == head, found, scores)
        scores = jnp.where(spot < length, scores * factor, NEG)
        top = jnp.max(scores, -1, keepdims=True)
        weights = jnp.exp(scores - top)
        total = jnp.sum(weights, -1, keepdims=True)
        for head in range(heads):
            value = cache_ref[sample, :, head * 2 * HD + HD : (head + 1) * 2 * HD]
            found = jnp.dot(
                weights.astype(jnp.bfloat16), value, preferred_element_type=jnp.float32
            )
            mixed = found if head == 0 else jnp.where(head_of == head, found, mixed)
        tops.append(jnp.broadcast_to(top + jnp.log(total), (rows, HD)))
        mixes.append(mixed / total)
    top_ref[...] = jnp.swapaxes(jnp.stack(tops), 0, 1)
    mixed_ref[...] = jnp.swapaxes(jnp.stack(mixes), 0, 1)


def cached(dec_q, cache, cache_len, heads):
    count, slots, width = cache.shape
    rows, each = heads * REP, 8
    state = jax.ShapeDtypeStruct((rows, count, HD), jnp.float32)
    return pl.pallas_call(
        functools.partial(cache_kernel, heads),
        grid=(count // each,),
        out_shape=[state, state],
        in_specs=[
            SMEM,
            pl.BlockSpec((each, rows, HD), lambda i: (i, 0, 0)),
            pl.BlockSpec((each, slots, width), lambda i: (i, 0, 0)),
        ],
        out_specs=[pl.BlockSpec((rows, each, HD), lambda i: (0, i, 0))] * 2,
        compiler_params=PARAMS,
        cost_estimate=pl.CostEstimate(
            flops=4 * count * rows * slots * HD * heads,
            bytes_accessed=2 * cache.size,
            transcendentals=count * rows * slots,
        ),
    )(cache_len, dec_q.reshape(count, rows, HD), cache)


def first_kernel(
    heads, at_ref, owner_ref, len_ref, samples_ref, q_ref, top_ref, mixed_ref, own_ref, *refs
):
    blocks, (new_top, new_mixed, source_ref, live_ref) = refs[:-4], refs[-4:]
    source, live = match_rows(at_ref, owner_ref, len_ref, samples_ref, q_ref.shape[0])
    source = jnp.concatenate([source] * REP, 0)
    live = jnp.concatenate([live] * REP, 0)
    source_ref[...] = jnp.broadcast_to(source, source_ref.shape)
    live_ref[...] = jnp.broadcast_to(live, live_ref.shape)
    for head in range(heads):
        mine = slice(head * REP, (head + 1) * REP)
        top = top_ref[mine].reshape(new_top.shape[1:])
        mixed = mixed_ref[mine].reshape(new_top.shape[1:])
        new_top[head], new_mixed[head] = absorb(
            at_ref, q_ref, source, live, head, blocks, top, mixed, own_ref
        )


def second_kernel(heads, at_ref, q_ref, source_ref, live_ref, top_ref, mixed_ref, *refs):
    blocks, out_ref = refs[:-1], refs[-1]
    count = q_ref.shape[0]
    for head in range(heads):
        _, mixed = absorb(
            at_ref,
            q_ref,
            source_ref[...],
            live_ref[...],
            head,
            blocks,
            top_ref[head],
            mixed_ref[head],
            None,
        )
        first = head * REP * HD
        for r in range(REP):
            out_ref[:, first + r * HD : first + (r + 1) * HD] = mixed[
                r * count : (r + 1) * count
            ].astype(out_ref.dtype)


VMEM = pl.BlockSpec(memory_space=pltpu.VMEM)
SMEM = pl.BlockSpec(memory_space=pltpu.SMEM)
HBM = pl.BlockSpec(memory_space=pltpu.HBM)
PARAMS = pltpu.CompilerParams(vmem_limit_bytes=24 * 1024 * 1024)


def numbers(values):
    return jnp.stack([jnp.asarray(v, jnp.int32) for v in values])


def stages(depth):
    unit = 128
    first = max(unit, depth * 7 // 12 // unit * unit)
    return (first, depth - first)


def local(
    pre_x,
    dec_x,
    w_kv,
    kv_scale,
    dec_q,
    cache,
    cache_len,
    prompt_owner,
    prompt_len,
    sample_rows,
    *,
    shape,
):
    teams, ranks, cores = shape["groups"], shape["dp"], shape["tp"]
    inner = INNER
    outer = ranks // inner
    span, features = pre_x.shape
    count = dec_x.shape[0]
    depth, width = w_kv.shape
    heads = width // (2 * HD)
    band = width // teams
    team = lax.axis_index("groups")
    rank = lax.axis_index("dp")
    core = lax.axis_index("tp")
    place, block = rank % inner, rank // inner

    def to_inner(value, step):
        pairs = [(r, r // inner * inner + (r % inner ^ step)) for r in range(ranks)]
        return lax.ppermute(value, "dp", pairs)

    def to_outer(value, step=1):
        pairs = [(r, (r + step * inner) % ranks) for r in range(ranks)]
        return lax.ppermute(value, "dp", pairs)

    def to_team(value, step):
        return lax.ppermute(value, "groups", [(i, (i + step) % teams) for i in range(teams)])

    def to_core(value, step):
        return lax.ppermute(value, "tp", [(i, (i + step) % cores) for i in range(cores)])

    sizes = stages(depth)
    pre_share, dec_share = span // cores, count // cores
    both = pre_share + dec_share
    spots = [team * band]
    plan, shapes = [], []
    for number, size in enumerate(sizes):
        spots.append(sum(sizes[:number]))
        plan.append((2, (size, band), len(spots) - 1, 0, number, 0, 0))
        shapes.append(jax.ShapeDtypeStruct((size, band), jnp.bfloat16))
    spots += [core * pre_share, core * dec_share]
    row = len(spots) - 2
    for step in range(1, inner):
        for back in range(outer):
            spots.append((((block - back) % outer) * inner + (place ^ step)) * depth)
            column, to = len(spots) - 1, back * depth
            plan.append((0, (pre_share, depth), row, column, len(shapes), 0, to))
            plan.append((1, (dec_share, depth), row + 1, column, len(shapes), pre_share, to))
        shapes.append(jax.ShapeDtypeStruct((both, outer * depth), jnp.bfloat16))
    sends = pl.pallas_call(
        functools.partial(pack_kernel, plan, 3, len(shapes)),
        out_shape=shapes,
        in_specs=[SMEM] + [HBM] * 3,
        out_specs=[VMEM] * len(shapes),
        scratch_shapes=[pltpu.SemaphoreType.DMA((len(plan),))],
        compiler_params=pltpu.CompilerParams(vmem_limit_bytes=56 * 1024 * 1024),
    )(numbers(spots), pre_x, dec_x, w_kv)
    moving, row_sends = list(sends[: len(sizes)]), list(sends[len(sizes) :])

    row_sends, query = lax.optimization_barrier((row_sends, dec_q))
    top_c, mixed_c = cached(query, cache, cache_len, heads)

    far = []
    for back in range(1, outer):
        moving = [to_outer(m) for m in moving]
        if back == 1:
            moving[0], row_sends[-1] = lax.optimization_barrier((moving[0], row_sends[-1]))
        far.append([[m] for m in moving])

    arrived = []
    got = [to_inner(row_sends[step - 1], step) for step in range(1, inner)]
    top_c, mixed_c, *got[:-1] = lax.optimization_barrier((top_c, mixed_c, *got[:-1]))
    for rows in got:
        arrived += [rows] + [to_core(rows, turn) for turn in range(1, cores)]
    for pieces in far:
        for number, piece in enumerate(pieces):
            if number:
                piece[0], pieces[number - 1][-1] = lax.optimization_barrier(
                    (piece[0], pieces[number - 1][-1])
                )
            piece += [to_team(piece[0], turn) for turn in range(1, teams)]
    total_rows = span + count
    all_rows = inner * total_rows
    turns = [(team - turn) % teams * band for turn in range(teams)]
    last = sizes[-1]
    early = [m for pieces in far for piece in pieces[:-1] for m in piece]
    *summed, last_rows = pl.pallas_call(
        functools.partial(gather_kernel, inner, outer, cores, teams, last),
        out_shape=[
            *[jax.ShapeDtypeStruct((all_rows, band), jnp.float32)] * teams,
            jax.ShapeDtypeStruct((all_rows, (outer - 1) * last), jnp.bfloat16),
        ],
        in_specs=[SMEM] + [VMEM] * (3 + len(arrived) + len(early)),
        out_specs=[VMEM] * (1 + teams),
        scratch_shapes=[
            pltpu.VMEM((all_rows, outer * depth - (outer - 1) * last), jnp.bfloat16)
        ],
        compiler_params=PARAMS,
    )(
        numbers(
            [core]
            + [(((block - back) % outer) * inner + place) * depth for back in range(outer)]
            + turns
        ),
        pre_x,
        dec_x,
        w_kv,
        *arrived,
        *early,
    )
    parts = []
    for turn in range(teams):
        late = [pieces[-1][turn] for pieces in far]
        mine, *others = pl.pallas_call(
            functools.partial(last_kernel, inner),
            out_shape=[jax.ShapeDtypeStruct((total_rows, band), jnp.float32)]
            + [jax.ShapeDtypeStruct((total_rows, band), jnp.bfloat16)] * (inner - 1),
            in_specs=[VMEM] * (2 + len(late)),
            out_specs=[VMEM] * inner,
            compiler_params=PARAMS,
        )(summed[turn], last_rows, *late)
        parts += [mine] + [to_inner(part, step + 1) for step, part in enumerate(others)]
    prompt_kv, shifted, own_kv = pl.pallas_call(
        functools.partial(finish_kernel, cores, teams),
        out_shape=[
            jax.ShapeDtypeStruct((span, width), jnp.bfloat16),
            jax.ShapeDtypeStruct((span, width), jnp.bfloat16),
            jax.ShapeDtypeStruct((count, width), jnp.bfloat16),
        ],
        in_specs=[SMEM] + [VMEM] * (1 + len(parts)),
        out_specs=[VMEM] * 3,
        compiler_params=PARAMS,
    )(numbers([core] + turns), kv_scale[None, :], *parts)

    blocks, owners = [], []
    for back in range(outer):
        if back:
            shifted = to_outer(shifted)
        for step in range(inner):
            blocks.append(to_inner(shifted, step) if step else shifted)
            owners.append(((block - back) % outer) * inner + (place ^ step))

    state = jax.ShapeDtypeStruct((heads, REP * count, HD), jnp.float32)
    labels = jax.ShapeDtypeStruct((REP * count, HD), jnp.int32)
    *state, source, live = pl.pallas_call(
        functools.partial(first_kernel, heads),
        out_shape=[state, state, labels, labels],
        in_specs=[SMEM] * 3 + [VMEM] * (5 + inner),
        out_specs=[VMEM] * 4,
        compiler_params=PARAMS,
    )(
        numbers([rank * count] + owners[:inner]),
        prompt_owner,
        prompt_len,
        sample_rows,
        dec_q,
        top_c,
        mixed_c,
        own_kv,
        *blocks[:inner],
    )
    attended = pl.pallas_call(
        functools.partial(second_kernel, heads),
        out_shape=jax.ShapeDtypeStruct(dec_q.shape, jnp.bfloat16),
        in_specs=[SMEM] + [VMEM] * (5 + len(blocks) - inner),
        out_specs=VMEM,
        compiler_params=PARAMS,
    )(numbers([rank * count] + owners[inner:]), dec_q, source, live, *state, *blocks[inner:])
    return (attended, prompt_kv)


def solution(mesh):
    in_specs = (
        P(("groups", "dp"), None),
        P(("groups", "dp"), None),
        P("dp", "tp"),
        P("tp"),
        P(("groups", "dp"), "tp"),
        P(("groups", "dp"), None, "tp"),
        P(("groups", "dp")),
        P("groups"),
        P("groups"),
        P("groups", None),
    )
    out_specs = (P(("groups", "dp"), "tp"), P(("groups", "dp"), "tp"))
    body = functools.partial(local, shape=dict(mesh.shape))
    return jax.shard_map(body, mesh=mesh, in_specs=in_specs, out_specs=out_specs, check_vma=False)
```

```python
import functools
import math

import jax
import jax.numpy as jnp
from jax import lax
from jax.experimental import pallas as pl
from jax.experimental.pallas import tpu as pltpu
from jax.sharding import PartitionSpec as P

HD = 128
REP = 12
NEG = -1e30
INNER = 4


def pack_kernel(plan, n_in, n_out, at_ref, *refs):
    ins, outs, sems = refs[:n_in], refs[n_in : n_in + n_out], refs[n_in + n_out]
    copies = []
    for number, (src, shape, row, column, dst, to_row, to_column) in enumerate(plan):
        from_row = pl.multiple_of(at_ref[row], 16)
        from_column = pl.multiple_of(at_ref[column], 128)
        copy = pltpu.make_async_copy(
            ins[src].at[pl.ds(from_row, shape[0]), pl.ds(from_column, shape[1])],
            outs[dst].at[pl.ds(to_row, shape[0]), pl.ds(to_column, shape[1])],
            sems.at[number],
        )
        copy.start()
        copies.append(copy)
    for copy in copies:
        copy.wait()


def early_kernel(outer, teams, last, at_ref, w_ref, *refs):
    n_late = teams + 2
    pieces, refs = refs[: teams * (outer - 1)], refs[teams * (outer - 1) :]
    blocks, sum_refs, (last_ref, row_ref) = refs[:-n_late], refs[-n_late:-2], refs[-2:]
    depth = w_ref.shape[0]
    early = depth - last
    base = 0
    for block in blocks:
        rows = slice(base, base + block.shape[0])
        row_ref[rows, :depth] = block[:, :depth]
        for back in range(1, outer):
            at = depth + (back - 1) * early
            row_ref[rows, at : at + early] = block[:, back * depth : back * depth + early]
            last_ref[rows, (back - 1) * last : back * last] = block[
                :, back * depth + early : (back + 1) * depth
            ]
        base += block.shape[0]
    for turn, sum_ref in enumerate(sum_refs):
        columns = pl.ds(pl.multiple_of(at_ref[turn], 128), sum_ref.shape[1])
        summed = jnp.dot(row_ref[:, :depth], w_ref[:, columns], preferred_element_type=jnp.float32)
        for back in range(1, outer):
            at = depth + (back - 1) * early
            summed = summed + jnp.dot(
                row_ref[:, at : at + early],
                pieces[(back - 1) * teams + turn][...],
                preferred_element_type=jnp.float32,
            )
        sum_ref[...] = summed


def late_kernel(outer, cores, teams, inner, at_ref, w_ref, last_ref, *refs):
    each_back = 2 * teams
    pieces, refs = refs[: each_back * (outer - 1)], refs[each_back * (outer - 1) :]
    sum_refs, halves, refs = refs[:teams], refs[teams : teams + cores], refs[teams + cores :]
    outs, row_ref = refs[:inner], refs[inner]
    depth = w_ref.shape[0]
    last = last_ref.shape[1] // (outer - 1)
    each, both = outs[0].shape[0], halves[0].shape[0]
    for turn, half in enumerate(halves):
        row_ref[turn * both : (turn + 1) * both, :] = half[...]
    for turn, sum_ref in enumerate(sum_refs):
        band = sum_ref.shape[1]
        taken = slice(turn * band, (turn + 1) * band)
        columns = pl.ds(pl.multiple_of(at_ref[turn], 128), band)
        first = sum_ref[...]
        final = jnp.dot(row_ref[:, :depth], w_ref[:, columns], preferred_element_type=jnp.float32)
        for back in range(1, outer):
            early_piece, last_piece = pieces[(back - 1) * each_back + turn :: teams][:2]
            at = back * depth
            cut = at + depth - last
            final = final + jnp.dot(
                row_ref[:, at:cut], early_piece[...], preferred_element_type=jnp.float32
            )
            final = final + jnp.dot(
                row_ref[:, cut : cut + last], last_piece[...], preferred_element_type=jnp.float32
            )
            first = first + jnp.dot(
                last_ref[:, (back - 1) * last : back * last],
                last_piece[...],
                preferred_element_type=jnp.float32,
            )
        for step in range(inner - 1):
            out = outs[step]
            out[:, taken] = first[step * each : (step + 1) * each].astype(out.dtype)
        outs[-1][:, taken] = final.astype(outs[-1].dtype)


def finish_kernel(cores, teams, at_ref, scale_ref, *refs):
    parts, (prompt_ref, sent_ref, own_ref) = refs[:-3], refs[-3:]
    span, count = prompt_ref.shape[0], own_ref.shape[0]
    pre_share, dec_share = span // cores, count // cores
    both = pre_share + dec_share
    band = scale_ref.shape[1] // teams
    for turn in range(teams):
        columns = pl.ds(pl.multiple_of(at_ref[1 + turn], 128), band)
        taken = slice(turn * band, (turn + 1) * band)
        summed = parts[0][:, taken]
        for part in parts[1:]:
            summed = summed + part[:, taken].astype(jnp.float32)
        done = (summed * scale_ref[:, columns]).astype(jnp.bfloat16)
        for share in range(cores):
            which = lax.rem(at_ref[0] - share + cores, cores)
            rows = pl.ds(pl.multiple_of(which * pre_share, 16), pre_share)
            prompt_ref[rows, columns] = done[share * both : share * both + pre_share]
            sent_ref[rows, columns] = done[share * both : share * both + pre_share]
            own_ref[pl.ds(pl.multiple_of(which * dec_share, 16), dec_share), columns] = done[
                share * both + pre_share : (share + 1) * both
            ]


def match_rows(at_ref, owner_ref, len_ref, samples_ref, count):
    row = at_ref[0] + lax.broadcasted_iota(jnp.int32, (count, 1), 0)
    source = jnp.zeros((count, 1), jnp.int32)
    live = jnp.zeros((count, 1), jnp.int32)
    for prompt in range(samples_ref.shape[0]):
        hit = jnp.max(
            jnp.where(samples_ref[prompt : prompt + 1, :] == row, 1, 0), -1, keepdims=True
        )
        source = source + hit * owner_ref[prompt]
        live = live + hit * len_ref[prompt]
    return source, live


def absorb(at_ref, q_ref, source, live, head, blocks, top, mixed, own_ref):
    count, span = q_ref.shape[0], blocks[0].shape[0]
    factor = 1.0 / math.sqrt(HD)
    first = head * REP * HD
    low, mid, high = head * 2 * HD, head * 2 * HD + HD, head * 2 * HD + 2 * HD
    q = jnp.concatenate([q_ref[:, first + r * HD : first + (r + 1) * HD] for r in range(REP)], 0)
    picked = jnp.full((REP * count, span), NEG, jnp.float32)
    place = lax.broadcasted_iota(jnp.int32, (REP * count, span), 1)
    for at, block in enumerate(blocks):
        scores = lax.dot_general(
            q,
            block[:, low:mid],
            (((1,), (1,)), ((), ())),
            preferred_element_type=jnp.float32,
        )
        picked = jnp.where(source == at_ref[1 + at], scores * factor, picked)
    picked = jnp.where(place < live, picked, NEG)
    new = jnp.maximum(jnp.max(picked, -1, keepdims=True), top)
    if own_ref is not None:
        own_k = jnp.concatenate([own_ref[:, low:mid].astype(jnp.float32)] * REP, 0)
        own_v = jnp.concatenate([own_ref[:, mid:high].astype(jnp.float32)] * REP, 0)
        score = jnp.sum(q.astype(jnp.float32) * own_k, -1, keepdims=True) * factor
        new = jnp.maximum(new, score)
    weights = jnp.exp(picked - new)
    kept = jnp.exp(top - new)
    total = kept + jnp.sum(weights, -1, keepdims=True)
    mixed = mixed * kept
    if own_ref is not None:
        weight = jnp.exp(score - new)
        total = total + weight
        mixed = mixed + weight * own_v
    for at, block in enumerate(blocks):
        mixed = mixed + jnp.dot(
            jnp.where(source == at_ref[1 + at], weights, 0.0).astype(jnp.bfloat16),
            block[:, mid:high],
            preferred_element_type=jnp.float32,
        )
    return new + jnp.log(total), mixed / total


def cache_kernel(heads, first, len_ref, q_ref, cache_ref, top_ref, mixed_ref):
    count, rows, _ = q_ref.shape
    factor = 1.0 / math.sqrt(HD)
    head_of = lax.broadcasted_iota(jnp.int32, (rows, 1), 0) // REP
    spot = lax.broadcasted_iota(jnp.int32, (rows, cache_ref.shape[1]), 1)
    tops, mixes = [], []
    for sample in range(count):
        length = len_ref[(first + pl.program_id(0)) * count + sample]
        scores = mixed = None
        for head in range(heads):
            key = cache_ref[sample, :, head * 2 * HD : head * 2 * HD + HD]
            found = lax.dot_general(
                q_ref[sample], key, (((1,), (1,)), ((), ())), preferred_element_type=jnp.float32
            )
            scores = found if head == 0 else jnp.where(head_of == head, found, scores)
        scores = jnp.where(spot < length, scores * factor, NEG)
        top = jnp.max(scores, -1, keepdims=True)
        weights = jnp.exp(scores - top)
        total = jnp.sum(weights, -1, keepdims=True)
        for head in range(heads):
            value = cache_ref[sample, :, head * 2 * HD + HD : (head + 1) * 2 * HD]
            found = jnp.dot(
                weights.astype(jnp.bfloat16), value, preferred_element_type=jnp.float32
            )
            mixed = found if head == 0 else jnp.where(head_of == head, found, mixed)
        tops.append(jnp.broadcast_to(top + jnp.log(total), (rows, HD)))
        mixes.append(mixed / total)
    top_ref[...] = jnp.swapaxes(jnp.stack(tops), 0, 1)
    mixed_ref[...] = jnp.swapaxes(jnp.stack(mixes), 0, 1)


def cached(query, cache, cache_len, heads, part, parts):
    slots, width = cache.shape[1:]
    count, rows, each = cache.shape[0] // parts, heads * REP, 8
    first = part * count // each
    state = jax.ShapeDtypeStruct((rows, count, HD), jnp.float32)
    return pl.pallas_call(
        functools.partial(cache_kernel, heads, first),
        grid=(count // each,),
        out_shape=[state, state],
        in_specs=[
            SMEM,
            pl.BlockSpec((each, rows, HD), lambda i: (first + i, 0, 0)),
            pl.BlockSpec((each, slots, width), lambda i: (first + i, 0, 0)),
        ],
        out_specs=[pl.BlockSpec((rows, each, HD), lambda i: (0, i, 0))] * 2,
        compiler_params=ALONE,
        cost_estimate=pl.CostEstimate(
            flops=4 * count * rows * slots * HD * heads,
            bytes_accessed=2 * cache.size // parts,
            transcendentals=count * rows * slots,
        ),
    )(cache_len, query, cache)


def first_kernel(
    heads, parts, at_ref, owner_ref, len_ref, samples_ref, q_ref, own_ref, *refs
):
    top_refs, mixed_refs, refs = refs[:parts], refs[parts : 2 * parts], refs[2 * parts :]
    blocks, (new_top, new_mixed, source_ref, live_ref) = refs[:-4], refs[-4:]
    source, live = match_rows(at_ref, owner_ref, len_ref, samples_ref, q_ref.shape[0])
    source = jnp.concatenate([source] * REP, 0)
    live = jnp.concatenate([live] * REP, 0)
    source_ref[...] = jnp.broadcast_to(source, source_ref.shape)
    live_ref[...] = jnp.broadcast_to(live, live_ref.shape)
    for head in range(heads):
        mine = slice(head * REP, (head + 1) * REP)
        top, mixed = [
            jnp.concatenate([ref[mine] for ref in some], 1).reshape(new_top.shape[1:])
            for some in (top_refs, mixed_refs)
        ]
        new_top[head], new_mixed[head] = absorb(
            at_ref, q_ref, source, live, head, blocks, top, mixed, own_ref
        )


def second_kernel(heads, at_ref, q_ref, source_ref, live_ref, top_ref, mixed_ref, *refs):
    blocks, out_ref = refs[:-1], refs[-1]
    count = q_ref.shape[0]
    for head in range(heads):
        _, mixed = absorb(
            at_ref,
            q_ref,
            source_ref[...],
            live_ref[...],
            head,
            blocks,
            top_ref[head],
            mixed_ref[head],
            None,
        )
        first = head * REP * HD
        for r in range(REP):
            out_ref[:, first + r * HD : first + (r + 1) * HD] = mixed[
                r * count : (r + 1) * count
            ].astype(out_ref.dtype)


VMEM = pl.BlockSpec(memory_space=pltpu.VMEM)
SMEM = pl.BlockSpec(memory_space=pltpu.SMEM)
HBM = pl.BlockSpec(memory_space=pltpu.HBM)
PARAMS = pltpu.CompilerParams(vmem_limit_bytes=20 * 1024 * 1024)
ALONE = pltpu.CompilerParams(vmem_limit_bytes=56 * 1024 * 1024)


def numbers(values):
    return jnp.stack([jnp.asarray(v, jnp.int32) for v in values])


def stages(depth):
    unit = 128
    first = max(unit, depth // 3 // unit * unit)
    return (first, depth - first)


def local(
    pre_x,
    dec_x,
    w_kv,
    kv_scale,
    dec_q,
    cache,
    cache_len,
    prompt_owner,
    prompt_len,
    sample_rows,
    *,
    shape,
):
    teams, ranks, cores = shape["groups"], shape["dp"], shape["tp"]
    inner = INNER
    outer = ranks // inner
    span, features = pre_x.shape
    count = dec_x.shape[0]
    depth, width = w_kv.shape
    heads = width // (2 * HD)
    band = width // teams
    team = lax.axis_index("groups")
    rank = lax.axis_index("dp")
    core = lax.axis_index("tp")
    place, block = rank % inner, rank // inner

    def to_inner(value, step):
        pairs = [(r, r // inner * inner + (r % inner ^ step)) for r in range(ranks)]
        return lax.ppermute(value, "dp", pairs)

    def to_outer(value, step=1):
        pairs = [(r, (r + step * inner) % ranks) for r in range(ranks)]
        return lax.ppermute(value, "dp", pairs)

    def to_team(value, step):
        return lax.ppermute(value, "groups", [(i, (i + step) % teams) for i in range(teams)])

    def to_core(value, step):
        return lax.ppermute(value, "tp", [(i, (i + step) % cores) for i in range(cores)])

    sizes = stages(depth)
    pre_share, dec_share = span // cores, count // cores
    both = pre_share + dec_share
    spots = [team * band]
    plan, shapes = [], []
    for number, size in enumerate(sizes):
        spots.append(sum(sizes[:number]))
        plan.append((2, (size, band), len(spots) - 1, 0, number, 0, 0))
        shapes.append(jax.ShapeDtypeStruct((size, band), jnp.bfloat16))
    spots += [core * pre_share, core * dec_share]
    row = len(spots) - 2
    for step in range(1, inner):
        for back in range(outer):
            spots.append((((block - back) % outer) * inner + (place ^ step)) * depth)
            column, to = len(spots) - 1, back * depth
            plan.append((0, (pre_share, depth), row, column, len(shapes), 0, to))
            plan.append((1, (dec_share, depth), row + 1, column, len(shapes), pre_share, to))
        shapes.append(jax.ShapeDtypeStruct((both, outer * depth), jnp.bfloat16))
    def pack(plan, spots, shapes, *arrays):
        return pl.pallas_call(
            functools.partial(pack_kernel, plan, len(arrays), len(shapes)),
            out_shape=shapes,
            in_specs=[SMEM] + [HBM] * len(arrays),
            out_specs=[VMEM] * len(shapes),
            scratch_shapes=[pltpu.SemaphoreType.DMA((len(plan),))],
            compiler_params=ALONE,
        )(numbers(spots), *arrays)

    sends = pack(plan, spots, shapes, pre_x, dec_x, w_kv)
    moving, row_sends = list(sends[: len(sizes)]), list(sends[len(sizes) :])
    row_sends, query = lax.optimization_barrier((row_sends, dec_q.reshape(count, heads * REP, HD)))

    states = [cached(query, cache, cache_len, heads, part, 2) for part in range(2)]
    far = []
    for back in range(1, outer):
        moving = [to_outer(m) for m in moving]
        if back == 1:
            moving[0], row_sends[-1], states, pre_x, dec_x = lax.optimization_barrier(
                (moving[0], row_sends[-1], states, pre_x, dec_x)
            )
        far.append([[m] for m in moving])
    tops, mixes = [state[0] for state in states], [state[1] for state in states]

    got = [to_inner(row_sends[step - 1], step) for step in range(1, inner)]
    far[0][-1][0], *got[:-1] = lax.optimization_barrier((far[0][-1][0], *got[:-1]))
    arrived = [[rows] + [to_core(rows, turn) for turn in range(1, cores)] for rows in got]

    for pieces in far:
        for number, piece in enumerate(pieces):
            if number:
                piece[0], pieces[number - 1][-1] = lax.optimization_barrier(
                    (piece[0], pieces[number - 1][-1])
                )
            piece += [to_team(piece[0], turn) for turn in range(1, teams)]

    spots, plan = [], []
    for turn in range(cores):
        spots += [(core - turn) % cores * pre_share, (core - turn) % cores * dec_share]
    for back in range(outer):
        spots.append((((block - back) % outer) * inner + place) * depth)
        for turn in range(cores):
            column, to, base = len(spots) - 1, back * depth, turn * both
            plan.append((0, (pre_share, depth), 2 * turn, column, 0, base, to))
            plan.append((1, (dec_share, depth), 2 * turn + 1, column, 0, base + pre_share, to))
    total_rows = span + count
    shapes = [jax.ShapeDtypeStruct((total_rows, outer * depth), jnp.bfloat16)]
    (own_rows,) = pack(plan, spots, shapes, pre_x, dec_x)

    last = sizes[-1]
    turns = numbers([(team - turn) % teams * band for turn in range(teams)])
    blocks = [own_rows] + [rows for step in arrived[:-1] for rows in step]
    early = [m for pieces in far for m in pieces[0]]
    first_rows = (inner - 1) * total_rows
    *summed, last_rows = pl.pallas_call(
        functools.partial(early_kernel, outer, teams, last),
        out_shape=[
            *[jax.ShapeDtypeStruct((first_rows, band), jnp.float32)] * teams,
            jax.ShapeDtypeStruct((first_rows, (outer - 1) * last), jnp.bfloat16),
        ],
        in_specs=[SMEM] + [VMEM] * (1 + len(early) + len(blocks)),
        out_specs=[VMEM] * (1 + teams),
        scratch_shapes=[
            pltpu.VMEM((first_rows, outer * depth - (outer - 1) * last), jnp.bfloat16)
        ],
        compiler_params=PARAMS,
    )(turns, w_kv, *early, *blocks)
    pieces = [m for some in far for piece in some for m in piece]
    parts = pl.pallas_call(
        functools.partial(late_kernel, outer, cores, teams, inner),
        out_shape=[jax.ShapeDtypeStruct((total_rows, width), jnp.float32)]
        + [jax.ShapeDtypeStruct((total_rows, width), jnp.bfloat16)] * (inner - 1),
        in_specs=[SMEM] + [VMEM] * (2 + len(pieces) + teams + cores),
        out_specs=[VMEM] * inner,
        scratch_shapes=[pltpu.VMEM((total_rows, outer * depth), jnp.bfloat16)],
        compiler_params=PARAMS,
    )(turns, w_kv, last_rows, *pieces, *summed, *arrived[-1])
    parts = [parts[0]] + [to_inner(parts[step], step) for step in range(1, inner)]
    prompt_kv, shifted, own_kv = pl.pallas_call(
        functools.partial(finish_kernel, cores, teams),
        out_shape=[
            jax.ShapeDtypeStruct((span, width), jnp.bfloat16),
            jax.ShapeDtypeStruct((span, width), jnp.bfloat16),
            jax.ShapeDtypeStruct((count, width), jnp.bfloat16),
        ],
        in_specs=[SMEM] + [VMEM] * (1 + len(parts)),
        out_specs=[VMEM] * 3,
        compiler_params=PARAMS,
    )(
        numbers([core] + [(team - turn) % teams * band for turn in range(teams)]),
        kv_scale[None, :],
        *parts,
    )

    blocks, owners = [], []
    for back in range(outer):
        if back:
            shifted = to_outer(shifted)
        for step in range(inner):
            blocks.append(to_inner(shifted, step) if step else shifted)
            owners.append(((block - back) % outer) * inner + (place ^ step))

    state = jax.ShapeDtypeStruct((heads, REP * count, HD), jnp.float32)
    labels = jax.ShapeDtypeStruct((REP * count, HD), jnp.int32)
    *state, source, live = pl.pallas_call(
        functools.partial(first_kernel, heads, len(tops)),
        out_shape=[state, state, labels, labels],
        in_specs=[SMEM] * 3 + [VMEM] * (3 + 2 * len(tops) + inner),
        out_specs=[VMEM] * 4,
        compiler_params=PARAMS,
    )(
        numbers([rank * count] + owners[:inner]),
        prompt_owner,
        prompt_len,
        sample_rows,
        dec_q,
        own_kv,
        *tops,
        *mixes,
        *blocks[:inner],
    )
    attended = pl.pallas_call(
        functools.partial(second_kernel, heads),
        out_shape=jax.ShapeDtypeStruct(dec_q.shape, jnp.bfloat16),
        in_specs=[SMEM] + [VMEM] * (5 + len(blocks) - inner),
        out_specs=VMEM,
        compiler_params=PARAMS,
    )(numbers([rank * count] + owners[inner:]), dec_q, source, live, *state, *blocks[inner:])
    return (attended, prompt_kv)


def solution(mesh):
    in_specs = (
        P(("groups", "dp"), None),
        P(("groups", "dp"), None),
        P("dp", "tp"),
        P("tp"),
        P(("groups", "dp"), "tp"),
        P(("groups", "dp"), None, "tp"),
        P(("groups", "dp")),
        P("groups"),
        P("groups"),
        P("groups", None),
    )
    out_specs = (P(("groups", "dp"), "tp"), P(("groups", "dp"), "tp"))
    body = functools.partial(local, shape=dict(mesh.shape))
    return jax.shard_map(body, mesh=mesh, in_specs=in_specs, out_specs=out_specs, check_vma=False)
```

```python
import functools
import math

import jax
import jax.numpy as jnp
from jax import lax
from jax.experimental import pallas as pl
from jax.experimental.pallas import tpu as pltpu
from jax.sharding import PartitionSpec as P

HD = 128
REP = 12
NEG = -1e30
INNER = 4
STEPS = (2, 3, 1)


def pack_kernel(plan, places, n_in, n_out, *refs):
    ins, outs = refs[:n_in], refs[n_in : n_in + n_out]
    held, (in_sems, out_sems) = refs[n_in + n_out : -2], refs[-2:]
    at = places()
    arriving, leaving = [], []
    for number, (src, shape, row, column, dst, to_row, to_column) in enumerate(plan):
        rows, columns = pl.ds(to_row, shape[0]), pl.ds(to_column, shape[1])
        from_row = pl.multiple_of(at[row], 16)
        from_column = pl.multiple_of(at[column], 128)
        arriving.append(
            pltpu.make_async_copy(
                ins[src].at[pl.ds(from_row, shape[0]), pl.ds(from_column, shape[1])],
                held[dst].at[rows, columns],
                in_sems.at[number],
            )
        )
        leaving.append(
            pltpu.make_async_copy(
                held[dst].at[rows, columns], outs[dst].at[rows, columns], out_sems.at[number]
            )
        )
        arriving[-1].start()
    for came, left in zip(arriving, leaving):
        came.wait()
        left.start()
    for left in leaving:
        left.wait()


def early_kernel(outer, teams, last, at_ref, w_ref, *refs):
    n_late = teams + 2
    pieces, refs = refs[: teams * (outer - 1)], refs[teams * (outer - 1) :]
    blocks, sum_refs, (last_ref, row_ref) = refs[:-n_late], refs[-n_late:-2], refs[-2:]
    depth = w_ref.shape[0]
    early = depth - last
    base = 0
    for block in blocks:
        rows = slice(base, base + block.shape[0])
        row_ref[rows, :depth] = block[:, :depth]
        for back in range(1, outer):
            at = depth + (back - 1) * early
            row_ref[rows, at : at + early] = block[:, back * depth : back * depth + early]
            last_ref[rows, (back - 1) * last : back * last] = block[
                :, back * depth + early : (back + 1) * depth
            ]
        base += block.shape[0]
    for turn, sum_ref in enumerate(sum_refs):
        columns = pl.ds(pl.multiple_of(at_ref[turn], 128), sum_ref.shape[1])
        summed = jnp.dot(row_ref[:, :depth], w_ref[:, columns], preferred_element_type=jnp.float32)
        for back in range(1, outer):
            at = depth + (back - 1) * early
            summed = summed + jnp.dot(
                row_ref[:, at : at + early],
                pieces[(back - 1) * teams + turn][...],
                preferred_element_type=jnp.float32,
            )
        sum_ref[...] = summed


def late_kernel(outer, cores, turn, at_ref, w_ref, sum_ref, last_ref, *refs):
    pieces, refs = refs[: 2 * (outer - 1)], refs[2 * (outer - 1) :]
    halves, outs, row_ref = refs[:cores], refs[cores:-1], refs[-1]
    depth = w_ref.shape[0]
    last = last_ref.shape[1] // (outer - 1)
    each, both = outs[0].shape[0], halves[0].shape[0]
    for number, half in enumerate(halves):
        row_ref[number * both : (number + 1) * both, :] = half[...]
    columns = pl.ds(pl.multiple_of(at_ref[turn], 128), sum_ref.shape[1])
    first = sum_ref[...]
    final = jnp.dot(row_ref[:, :depth], w_ref[:, columns], preferred_element_type=jnp.float32)
    for back in range(1, outer):
        early_piece, last_piece = pieces[2 * back - 2 : 2 * back]
        at = back * depth
        cut = at + depth - last
        final = final + jnp.dot(
            row_ref[:, at:cut], early_piece[...], preferred_element_type=jnp.float32
        )
        final = final + jnp.dot(
            row_ref[:, cut : cut + last], last_piece[...], preferred_element_type=jnp.float32
        )
        first = first + jnp.dot(
            last_ref[:, (back - 1) * last : back * last],
            last_piece[...],
            preferred_element_type=jnp.float32,
        )
    for step, out in enumerate(outs[:-1]):
        out[...] = first[step * each : (step + 1) * each].astype(out.dtype)
    outs[-1][...] = final.astype(outs[-1].dtype)


def finish_kernel(cores, teams, at_ref, scale_ref, *refs):
    parts, (prompt_ref, sent_ref, own_ref) = refs[:-3], refs[-3:]
    span, count = prompt_ref.shape[0], own_ref.shape[0]
    pre_share, dec_share = span // cores, count // cores
    both = pre_share + dec_share
    band = scale_ref.shape[1] // teams
    for turn in range(teams):
        columns = pl.ds(pl.multiple_of(at_ref[1 + turn], 128), band)
        own, *others = parts[turn * len(parts) // teams : (turn + 1) * len(parts) // teams]
        summed = own[...]
        for part in others:
            summed = summed + part[...].astype(jnp.float32)
        done = (summed * scale_ref[:, columns]).astype(jnp.bfloat16)
        for share in range(cores):
            which = lax.rem(at_ref[0] - share + cores, cores)
            rows = pl.ds(pl.multiple_of(which * pre_share, 16), pre_share)
            prompt_ref[rows, columns] = done[share * both : share * both + pre_share]
            sent_ref[rows, columns] = done[share * both : share * both + pre_share]
            own_ref[pl.ds(pl.multiple_of(which * dec_share, 16), dec_share), columns] = done[
                share * both + pre_share : (share + 1) * both
            ]


def match_rows(at_ref, owner_ref, len_ref, samples_ref, count):
    row = at_ref[0] + lax.broadcasted_iota(jnp.int32, (count, 1), 0)
    source = jnp.zeros((count, 1), jnp.int32)
    live = jnp.zeros((count, 1), jnp.int32)
    for prompt in range(samples_ref.shape[0]):
        hit = jnp.max(
            jnp.where(samples_ref[prompt : prompt + 1, :] == row, 1, 0), -1, keepdims=True
        )
        source = source + hit * owner_ref[prompt]
        live = live + hit * len_ref[prompt]
    return source, live


def absorb(at_ref, q_ref, source, live, head, blocks, top, mixed, own_ref):
    count, span = q_ref.shape[0], blocks[0].shape[0]
    factor = 1.0 / math.sqrt(HD)
    first = head * REP * HD
    low, mid, high = head * 2 * HD, head * 2 * HD + HD, head * 2 * HD + 2 * HD
    q = jnp.concatenate([q_ref[:, first + r * HD : first + (r + 1) * HD] for r in range(REP)], 0)
    picked = jnp.full((REP * count, span), NEG, jnp.float32)
    place = lax.broadcasted_iota(jnp.int32, (REP * count, span), 1)
    for at, block in enumerate(blocks):
        scores = lax.dot_general(
            q,
            block[:, low:mid],
            (((1,), (1,)), ((), ())),
            preferred_element_type=jnp.float32,
        )
        picked = jnp.where(source == at_ref[1 + at], scores * factor, picked)
    picked = jnp.where(place < live, picked, NEG)
    new = jnp.maximum(jnp.max(picked, -1, keepdims=True), top)
    if own_ref is not None:
        own_k = jnp.concatenate([own_ref[:, low:mid].astype(jnp.float32)] * REP, 0)
        own_v = jnp.concatenate([own_ref[:, mid:high].astype(jnp.float32)] * REP, 0)
        score = jnp.sum(q.astype(jnp.float32) * own_k, -1, keepdims=True) * factor
        new = jnp.maximum(new, score)
    weights = jnp.exp(picked - new)
    kept = jnp.exp(top - new)
    total = kept + jnp.sum(weights, -1, keepdims=True)
    mixed = mixed * kept
    if own_ref is not None:
        weight = jnp.exp(score - new)
        total = total + weight
        mixed = mixed + weight * own_v
    for at, block in enumerate(blocks):
        mixed = mixed + jnp.dot(
            jnp.where(source == at_ref[1 + at], weights, 0.0).astype(jnp.bfloat16),
            block[:, mid:high],
            preferred_element_type=jnp.float32,
        )
    return new + jnp.log(total), mixed / total


def cache_kernel(heads, len_ref, q_ref, cache_ref, top_ref, mixed_ref):
    count, rows, _ = q_ref.shape
    factor = 1.0 / math.sqrt(HD)
    head_of = lax.broadcasted_iota(jnp.int32, (rows, 1), 0) // REP
    spot = lax.broadcasted_iota(jnp.int32, (rows, cache_ref.shape[1]), 1)
    tops, mixes = [], []
    for sample in range(count):
        length = len_ref[pl.program_id(0) * count + sample]
        scores = mixed = None
        for head in range(heads):
            key = cache_ref[sample, :, head * 2 * HD : head * 2 * HD + HD]
            found = lax.dot_general(
                q_ref[sample], key, (((1,), (1,)), ((), ())), preferred_element_type=jnp.float32
            )
            scores = found if head == 0 else jnp.where(head_of == head, found, scores)
        scores = jnp.where(spot < length, scores * factor, NEG)
        top = jnp.max(scores, -1, keepdims=True)
        weights = jnp.exp(scores - top)
        total = jnp.sum(weights, -1, keepdims=True)
        for head in range(heads):
            value = cache_ref[sample, :, head * 2 * HD + HD : (head + 1) * 2 * HD]
            found = jnp.dot(
                weights.astype(jnp.bfloat16), value, preferred_element_type=jnp.float32
            )
            mixed = found if head == 0 else jnp.where(head_of == head, found, mixed)
        tops.append(jnp.broadcast_to(top + jnp.log(total), (rows, HD)))
        mixes.append(mixed / total)
    top_ref[...] = jnp.swapaxes(jnp.stack(tops), 0, 1)
    mixed_ref[...] = jnp.swapaxes(jnp.stack(mixes), 0, 1)


def cached(query, cache, cache_len, heads):
    count, slots, width = cache.shape
    rows, each = heads * REP, 8
    state = jax.ShapeDtypeStruct((rows, count, HD), jnp.float32)
    return pl.pallas_call(
        functools.partial(cache_kernel, heads),
        grid=(count // each,),
        out_shape=[state, state],
        in_specs=[
            SMEM,
            pl.BlockSpec((each, rows, HD), lambda i: (i, 0, 0)),
            pl.BlockSpec((each, slots, width), lambda i: (i, 0, 0)),
        ],
        out_specs=[pl.BlockSpec((rows, each, HD), lambda i: (0, i, 0))] * 2,
        compiler_params=PARAMS,
        cost_estimate=pl.CostEstimate(
            flops=4 * count * rows * slots * HD * heads,
            bytes_accessed=2 * cache.size,
            transcendentals=count * rows * slots,
        ),
    )(cache_len, query, cache)


def first_kernel(
    heads, at_ref, owner_ref, len_ref, samples_ref, q_ref, top_ref, mixed_ref, own_ref, *refs
):
    blocks, (new_top, new_mixed, source_ref, live_ref) = refs[:-4], refs[-4:]
    source, live = match_rows(at_ref, owner_ref, len_ref, samples_ref, q_ref.shape[0])
    source = jnp.concatenate([source] * REP, 0)
    live = jnp.concatenate([live] * REP, 0)
    source_ref[...] = jnp.broadcast_to(source, source_ref.shape)
    live_ref[...] = jnp.broadcast_to(live, live_ref.shape)
    for head in range(heads):
        mine = slice(head * REP, (head + 1) * REP)
        top = top_ref[mine].reshape(new_top.shape[1:])
        mixed = mixed_ref[mine].reshape(new_top.shape[1:])
        new_top[head], new_mixed[head] = absorb(
            at_ref, q_ref, source, live, head, blocks, top, mixed, own_ref
        )


def second_kernel(heads, at_ref, q_ref, source_ref, live_ref, top_ref, mixed_ref, *refs):
    blocks, out_ref = refs[:-1], refs[-1]
    count = q_ref.shape[0]
    for head in range(heads):
        _, mixed = absorb(
            at_ref,
            q_ref,
            source_ref[...],
            live_ref[...],
            head,
            blocks,
            top_ref[head],
            mixed_ref[head],
            None,
        )
        first = head * REP * HD
        for r in range(REP):
            out_ref[:, first + r * HD : first + (r + 1) * HD] = mixed[
                r * count : (r + 1) * count
            ].astype(out_ref.dtype)


VMEM = pl.BlockSpec(memory_space=pltpu.VMEM)
SMEM = pl.BlockSpec(memory_space=pltpu.SMEM)
HBM = pl.BlockSpec(memory_space=pltpu.HBM)
PARAMS = pltpu.CompilerParams(vmem_limit_bytes=20 * 1024 * 1024)
ALONE = pltpu.CompilerParams(vmem_limit_bytes=56 * 1024 * 1024)


def numbers(values):
    return jnp.stack([jnp.asarray(v, jnp.int32) for v in values])


def stages(depth):
    unit = 128
    first = max(unit, depth // 3 // unit * unit)
    return (first, depth - first)


def local(
    pre_x,
    dec_x,
    w_kv,
    kv_scale,
    dec_q,
    cache,
    cache_len,
    prompt_owner,
    prompt_len,
    sample_rows,
    *,
    shape,
):
    teams, ranks, cores = shape["groups"], shape["dp"], shape["tp"]
    inner = INNER
    outer = ranks // inner
    span, features = pre_x.shape
    count = dec_x.shape[0]
    depth, width = w_kv.shape
    heads = width // (2 * HD)
    band = width // teams
    team = lax.axis_index("groups")
    rank = lax.axis_index("dp")
    core = lax.axis_index("tp")
    place, block = rank % inner, rank // inner

    def to_inner(value, step):
        pairs = [(r, r // inner * inner + (r % inner ^ step)) for r in range(ranks)]
        return lax.ppermute(value, "dp", pairs)

    def to_outer(value, step=1):
        pairs = [(r, (r + step * inner) % ranks) for r in range(ranks)]
        return lax.ppermute(value, "dp", pairs)

    def to_team(value, step):
        return lax.ppermute(value, "groups", [(i, (i + step) % teams) for i in range(teams)])

    def to_core(value, step):
        return lax.ppermute(value, "tp", [(i, (i + step) % cores) for i in range(cores)])

    def pack(plan, places, shapes, *arrays):
        sems = pltpu.SemaphoreType.DMA((len(plan),))
        return pl.pallas_call(
            functools.partial(pack_kernel, plan, places, len(arrays), len(shapes)),
            out_shape=shapes,
            in_specs=[HBM] * len(arrays),
            out_specs=[HBM] * len(shapes),
            scratch_shapes=[pltpu.VMEM(s.shape, s.dtype) for s in shapes] + [sems, sems],
            compiler_params=ALONE,
        )(*arrays)

    sizes = stages(depth)
    pre_share, dec_share = span // cores, count // cores
    both = pre_share + dec_share
    plan, shapes = [], []
    for number, size in enumerate(sizes):
        plan.append((2, (size, band), number, len(sizes), number, 0, 0))
        shapes.append(jax.ShapeDtypeStruct((size, band), jnp.bfloat16))
    row = len(sizes) + 1
    for number in range(inner - 1):
        for back in range(outer):
            column, to = row + 2 + number * outer + back, back * depth
            plan.append((0, (pre_share, depth), row, column, len(shapes), 0, to))
            plan.append((1, (dec_share, depth), row + 1, column, len(shapes), pre_share, to))
        shapes.append(jax.ShapeDtypeStruct((both, outer * depth), jnp.bfloat16))

    def features(back, step):
        rank = lax.axis_index("dp")
        return ((rank // inner - back + outer) % outer * inner + (rank % inner ^ step)) * depth

    def send_places():
        core = lax.axis_index("tp")
        at = [sum(sizes[:number]) for number in range(len(sizes))]
        at += [lax.axis_index("groups") * band, core * pre_share, core * dec_share]
        return at + [features(back, step) for step in STEPS for back in range(outer)]

    sends = pack(plan, send_places, shapes, pre_x, dec_x, w_kv)
    moving, row_sends = list(sends[: len(sizes)]), list(sends[len(sizes) :])
    row_sends, query, pre_x, dec_x = lax.optimization_barrier(
        (row_sends, dec_q.reshape(count, heads * REP, HD), pre_x, dec_x)
    )

    plan = []
    for back in range(outer):
        for turn in range(cores):
            column, to, base = 2 * cores + back, back * depth, turn * both
            plan.append((0, (pre_share, depth), 2 * turn, column, 0, base, to))
            plan.append((1, (dec_share, depth), 2 * turn + 1, column, 0, base + pre_share, to))

    def own_places():
        core, at = lax.axis_index("tp"), []
        for turn in range(cores):
            which = (core - turn + cores) % cores
            at += [which * pre_share, which * dec_share]
        return at + [features(back, 0) for back in range(outer)]

    total_rows = span + count
    shapes = [jax.ShapeDtypeStruct((total_rows, outer * depth), jnp.bfloat16)]
    (own_rows,) = pack(plan, own_places, shapes, pre_x, dec_x)

    top_c, mixed_c = cached(query, cache, cache_len, heads)
    far = []
    for back in range(1, outer):
        moving = [to_outer(m) for m in moving]
        if back == 1:
            moving[0], row_sends[-1], top_c, mixed_c, own_rows = lax.optimization_barrier(
                (moving[0], row_sends[-1], top_c, mixed_c, own_rows)
            )
        far.append([[m] for m in moving])

    got = [to_inner(rows, step) for rows, step in zip(row_sends, STEPS)]
    far[0][-1][0], *got[:-1] = lax.optimization_barrier((far[0][-1][0], *got[:-1]))
    arrived = [[rows] + [to_core(rows, turn) for turn in range(1, cores)] for rows in got]

    for pieces in far:
        for number, piece in enumerate(pieces):
            if number:
                piece[0], pieces[number - 1][-1] = lax.optimization_barrier(
                    (piece[0], pieces[number - 1][-1])
                )
            piece += [to_team(piece[0], turn) for turn in range(1, teams)]

    last = sizes[-1]
    turns = numbers([(team - turn) % teams * band for turn in range(teams)])
    own_rows, got[-1] = lax.optimization_barrier((own_rows, got[-1]))
    blocks = [own_rows] + [rows for step in arrived[:-1] for rows in step]
    early = [m for pieces in far for m in pieces[0]]
    first_rows = (inner - 1) * total_rows
    *summed, last_rows = pl.pallas_call(
        functools.partial(early_kernel, outer, teams, last),
        out_shape=[
            *[jax.ShapeDtypeStruct((first_rows, band), jnp.float32)] * teams,
            jax.ShapeDtypeStruct((first_rows, (outer - 1) * last), jnp.bfloat16),
        ],
        in_specs=[SMEM] + [VMEM] * (1 + len(early) + len(blocks)),
        out_specs=[VMEM] * (1 + teams),
        scratch_shapes=[
            pltpu.VMEM((first_rows, outer * depth - (outer - 1) * last), jnp.bfloat16)
        ],
        compiler_params=PARAMS,
    )(turns, w_kv, *early, *blocks)
    parts = []
    for turn in range(teams):
        pieces = [piece[turn] for some in far for piece in some]
        mine, *others = pl.pallas_call(
            functools.partial(late_kernel, outer, cores, turn),
            out_shape=[jax.ShapeDtypeStruct((total_rows, band), jnp.float32)]
            + [jax.ShapeDtypeStruct((total_rows, band), jnp.bfloat16)] * (inner - 1),
            in_specs=[SMEM] + [VMEM] * (3 + len(pieces) + cores),
            out_specs=[VMEM] * inner,
            scratch_shapes=[pltpu.VMEM((total_rows, outer * depth), jnp.bfloat16)],
            compiler_params=PARAMS,
        )(turns, w_kv, summed[turn], last_rows, *pieces, *arrived[-1])
        parts += [mine] + [to_inner(part, step) for part, step in zip(others, STEPS)]
    prompt_kv, shifted, own_kv = pl.pallas_call(
        functools.partial(finish_kernel, cores, teams),
        out_shape=[
            jax.ShapeDtypeStruct((span, width), jnp.bfloat16),
            jax.ShapeDtypeStruct((span, width), jnp.bfloat16),
            jax.ShapeDtypeStruct((count, width), jnp.bfloat16),
        ],
        in_specs=[SMEM] + [VMEM] * (1 + len(parts)),
        out_specs=[VMEM] * 3,
        compiler_params=PARAMS,
    )(
        numbers([core] + [(team - turn) % teams * band for turn in range(teams)]),
        kv_scale[None, :],
        *parts,
    )

    blocks, owners = [], []
    for back in range(outer):
        if back:
            shifted = to_outer(shifted)
        for step in range(inner):
            blocks.append(to_inner(shifted, step) if step else shifted)
            owners.append(((block - back) % outer) * inner + (place ^ step))

    state = jax.ShapeDtypeStruct((heads, REP * count, HD), jnp.float32)
    labels = jax.ShapeDtypeStruct((REP * count, HD), jnp.int32)
    *state, source, live = pl.pallas_call(
        functools.partial(first_kernel, heads),
        out_shape=[state, state, labels, labels],
        in_specs=[SMEM] * 3 + [VMEM] * (5 + inner),
        out_specs=[VMEM] * 4,
        compiler_params=PARAMS,
    )(
        numbers([rank * count] + owners[:inner]),
        prompt_owner,
        prompt_len,
        sample_rows,
        dec_q,
        top_c,
        mixed_c,
        own_kv,
        *blocks[:inner],
    )
    attended = pl.pallas_call(
        functools.partial(second_kernel, heads),
        out_shape=jax.ShapeDtypeStruct(dec_q.shape, jnp.bfloat16),
        in_specs=[SMEM] + [VMEM] * (5 + len(blocks) - inner),
        out_specs=VMEM,
        compiler_params=PARAMS,
    )(numbers([rank * count] + owners[inner:]), dec_q, source, live, *state, *blocks[inner:])
    return (attended, prompt_kv)


def solution(mesh):
    in_specs = (
        P(("groups", "dp"), None),
        P(("groups", "dp"), None),
        P("dp", "tp"),
        P("tp"),
        P(("groups", "dp"), "tp"),
        P(("groups", "dp"), None, "tp"),
        P(("groups", "dp")),
        P("groups"),
        P("groups"),
        P("groups", None),
    )
    out_specs = (P(("groups", "dp"), "tp"), P(("groups", "dp"), "tp"))
    body = functools.partial(local, shape=dict(mesh.shape))
    return jax.shard_map(body, mesh=mesh, in_specs=in_specs, out_specs=out_specs, check_vma=False)
```

```python
import functools
import math

import jax
import jax.numpy as jnp
from jax import lax
from jax.experimental import pallas as pl
from jax.experimental.pallas import tpu as pltpu
from jax.sharding import PartitionSpec as P

HD = 128
REP = 12
NEG = -1e30
INNER = 4
STEPS = (2, 3, 1)


def pack_kernel(plan, places, n_in, n_out, *refs):
    ins, outs = refs[:n_in], refs[n_in : n_in + n_out]
    held, (in_sems, out_sems) = refs[n_in + n_out : -2], refs[-2:]
    at = places()
    arriving, leaving = [], []
    for number, (src, shape, row, column, dst, to_row, to_column) in enumerate(plan):
        rows, columns = pl.ds(to_row, shape[0]), pl.ds(to_column, shape[1])
        from_row = pl.multiple_of(at[row], 16)
        from_column = pl.multiple_of(at[column], 128)
        arriving.append(
            pltpu.make_async_copy(
                ins[src].at[pl.ds(from_row, shape[0]), pl.ds(from_column, shape[1])],
                held[dst].at[rows, columns],
                in_sems.at[number],
            )
        )
        leaving.append(
            pltpu.make_async_copy(
                held[dst].at[rows, columns], outs[dst].at[rows, columns], out_sems.at[number]
            )
        )
        arriving[-1].start()
    for came, left in zip(arriving, leaving):
        came.wait()
        left.start()
    for left in leaving:
        left.wait()


def early_kernel(outer, teams, last, at_ref, w_ref, *refs):
    n_late = teams + 2
    pieces, refs = refs[: teams * (outer - 1)], refs[teams * (outer - 1) :]
    blocks, sum_refs, (last_ref, row_ref) = refs[:-n_late], refs[-n_late:-2], refs[-2:]
    depth = w_ref.shape[0]
    early = depth - last
    base = 0
    for block in blocks:
        rows = slice(base, base + block.shape[0])
        row_ref[rows, :depth] = block[:, :depth]
        for back in range(1, outer):
            at = depth + (back - 1) * early
            row_ref[rows, at : at + early] = block[:, back * depth : back * depth + early]
            last_ref[rows, (back - 1) * last : back * last] = block[
                :, back * depth + early : (back + 1) * depth
            ]
        base += block.shape[0]
    for turn, sum_ref in enumerate(sum_refs):
        columns = pl.ds(pl.multiple_of(at_ref[turn], 128), sum_ref.shape[1])
        summed = jnp.dot(row_ref[:, :depth], w_ref[:, columns], preferred_element_type=jnp.float32)
        for back in range(1, outer):
            at = depth + (back - 1) * early
            summed = summed + jnp.dot(
                row_ref[:, at : at + early],
                pieces[(back - 1) * teams + turn][...],
                preferred_element_type=jnp.float32,
            )
        sum_ref[...] = summed


def late_kernel(outer, cores, turn, at_ref, w_ref, sum_ref, last_ref, *refs):
    pieces, refs = refs[: 2 * (outer - 1)], refs[2 * (outer - 1) :]
    halves, outs, row_ref = refs[:cores], refs[cores:-1], refs[-1]
    depth = w_ref.shape[0]
    last = last_ref.shape[1] // (outer - 1)
    each, both = outs[0].shape[0], halves[0].shape[0]
    for number, half in enumerate(halves):
        row_ref[number * both : (number + 1) * both, :] = half[...]
    columns = pl.ds(pl.multiple_of(at_ref[turn], 128), sum_ref.shape[1])
    first = sum_ref[...]
    final = jnp.dot(row_ref[:, :depth], w_ref[:, columns], preferred_element_type=jnp.float32)
    for back in range(1, outer):
        early_piece, last_piece = pieces[2 * back - 2 : 2 * back]
        at = back * depth
        cut = at + depth - last
        final = final + jnp.dot(
            row_ref[:, at:cut], early_piece[...], preferred_element_type=jnp.float32
        )
        final = final + jnp.dot(
            row_ref[:, cut : cut + last], last_piece[...], preferred_element_type=jnp.float32
        )
        first = first + jnp.dot(
            last_ref[:, (back - 1) * last : back * last],
            last_piece[...],
            preferred_element_type=jnp.float32,
        )
    for step, out in enumerate(outs[:-1]):
        out[...] = first[step * each : (step + 1) * each].astype(out.dtype)
    outs[-1][...] = final.astype(outs[-1].dtype)


def finish_kernel(cores, teams, at_ref, scale_ref, *refs):
    parts, (prompt_ref, sent_ref, own_ref) = refs[:-3], refs[-3:]
    span, count = prompt_ref.shape[0], own_ref.shape[0]
    pre_share, dec_share = span // cores, count // cores
    both = pre_share + dec_share
    band = scale_ref.shape[1] // teams
    for turn in range(teams):
        columns = pl.ds(pl.multiple_of(at_ref[1 + turn], 128), band)
        own, *others = parts[turn * len(parts) // teams : (turn + 1) * len(parts) // teams]
        summed = own[...]
        for part in others:
            summed = summed + part[...].astype(jnp.float32)
        done = (summed * scale_ref[:, columns]).astype(jnp.bfloat16)
        for share in range(cores):
            which = lax.rem(at_ref[0] - share + cores, cores)
            rows = pl.ds(pl.multiple_of(which * pre_share, 16), pre_share)
            prompt_ref[rows, columns] = done[share * both : share * both + pre_share]
            sent_ref[rows, columns] = done[share * both : share * both + pre_share]
            own_ref[pl.ds(pl.multiple_of(which * dec_share, 16), dec_share), columns] = done[
                share * both + pre_share : (share + 1) * both
            ]


def match_rows(at_ref, owner_ref, len_ref, samples_ref, count):
    row = at_ref[0] + lax.broadcasted_iota(jnp.int32, (count, 1), 0)
    source = jnp.zeros((count, 1), jnp.int32)
    live = jnp.zeros((count, 1), jnp.int32)
    for prompt in range(samples_ref.shape[0]):
        hit = jnp.max(
            jnp.where(samples_ref[prompt : prompt + 1, :] == row, 1, 0), -1, keepdims=True
        )
        source = source + hit * owner_ref[prompt]
        live = live + hit * len_ref[prompt]
    return source, live


def absorb(at_ref, q_ref, source, live, head, blocks, top, mixed, own_ref):
    count, span = q_ref.shape[0], blocks[0].shape[0]
    factor = 1.0 / math.sqrt(HD)
    first = head * REP * HD
    low, mid, high = head * 2 * HD, head * 2 * HD + HD, head * 2 * HD + 2 * HD
    q = jnp.concatenate([q_ref[:, first + r * HD : first + (r + 1) * HD] for r in range(REP)], 0)
    picked = jnp.full((REP * count, span), NEG, jnp.float32)
    place = lax.broadcasted_iota(jnp.int32, (REP * count, span), 1)
    for at, block in enumerate(blocks):
        scores = lax.dot_general(
            q,
            block[:, low:mid],
            (((1,), (1,)), ((), ())),
            preferred_element_type=jnp.float32,
        )
        picked = jnp.where(source == at_ref[1 + at], scores * factor, picked)
    picked = jnp.where(place < live, picked, NEG)
    new = jnp.maximum(jnp.max(picked, -1, keepdims=True), top)
    if own_ref is not None:
        own_k = jnp.concatenate([own_ref[:, low:mid].astype(jnp.float32)] * REP, 0)
        own_v = jnp.concatenate([own_ref[:, mid:high].astype(jnp.float32)] * REP, 0)
        score = jnp.sum(q.astype(jnp.float32) * own_k, -1, keepdims=True) * factor
        new = jnp.maximum(new, score)
    weights = jnp.exp(picked - new)
    kept = jnp.exp(top - new)
    total = kept + jnp.sum(weights, -1, keepdims=True)
    mixed = mixed * kept
    if own_ref is not None:
        weight = jnp.exp(score - new)
        total = total + weight
        mixed = mixed + weight * own_v
    for at, block in enumerate(blocks):
        mixed = mixed + jnp.dot(
            jnp.where(source == at_ref[1 + at], weights, 0.0).astype(jnp.bfloat16),
            block[:, mid:high],
            preferred_element_type=jnp.float32,
        )
    return new + jnp.log(total), mixed / total


def cache_kernel(heads, len_ref, q_ref, cache_ref, top_ref, mixed_ref):
    count, rows, _ = q_ref.shape
    factor = 1.0 / math.sqrt(HD)
    head_of = lax.broadcasted_iota(jnp.int32, (rows, 1), 0) // REP
    spot = lax.broadcasted_iota(jnp.int32, (rows, cache_ref.shape[1]), 1)
    tops, mixes = [], []
    for sample in range(count):
        length = len_ref[pl.program_id(0) * count + sample]
        scores = mixed = None
        for head in range(heads):
            key = cache_ref[sample, :, head * 2 * HD : head * 2 * HD + HD]
            found = lax.dot_general(
                q_ref[sample], key, (((1,), (1,)), ((), ())), preferred_element_type=jnp.float32
            )
            scores = found if head == 0 else jnp.where(head_of == head, found, scores)
        scores = jnp.where(spot < length, scores * factor, NEG)
        top = jnp.max(scores, -1, keepdims=True)
        weights = jnp.exp(scores - top)
        total = jnp.sum(weights, -1, keepdims=True)
        for head in range(heads):
            value = cache_ref[sample, :, head * 2 * HD + HD : (head + 1) * 2 * HD]
            found = jnp.dot(
                weights.astype(jnp.bfloat16), value, preferred_element_type=jnp.float32
            )
            mixed = found if head == 0 else jnp.where(head_of == head, found, mixed)
        tops.append(jnp.broadcast_to(top + jnp.log(total), (rows, HD)))
        mixes.append(mixed / total)
    top_ref[...] = jnp.swapaxes(jnp.stack(tops), 0, 1)
    mixed_ref[...] = jnp.swapaxes(jnp.stack(mixes), 0, 1)


def cached(query, cache, cache_len, heads):
    count, slots, width = cache.shape
    rows, each = heads * REP, 8
    state = jax.ShapeDtypeStruct((rows, count, HD), jnp.float32)
    return pl.pallas_call(
        functools.partial(cache_kernel, heads),
        grid=(count // each,),
        out_shape=[state, state],
        in_specs=[
            SMEM,
            pl.BlockSpec((each, rows, HD), lambda i: (i, 0, 0)),
            pl.BlockSpec((each, slots, width), lambda i: (i, 0, 0)),
        ],
        out_specs=[pl.BlockSpec((rows, each, HD), lambda i: (0, i, 0))] * 2,
        compiler_params=grant(12),
        cost_estimate=pl.CostEstimate(
            flops=4 * count * rows * slots * HD * heads,
            bytes_accessed=2 * cache.size,
            transcendentals=count * rows * slots,
        ),
    )(cache_len, query, cache)


def first_kernel(
    heads, at_ref, owner_ref, len_ref, samples_ref, q_ref, top_ref, mixed_ref, own_ref, *refs
):
    blocks, (new_top, new_mixed, source_ref, live_ref) = refs[:-4], refs[-4:]
    source, live = match_rows(at_ref, owner_ref, len_ref, samples_ref, q_ref.shape[0])
    source = jnp.concatenate([source] * REP, 0)
    live = jnp.concatenate([live] * REP, 0)
    source_ref[...] = jnp.broadcast_to(source, source_ref.shape)
    live_ref[...] = jnp.broadcast_to(live, live_ref.shape)
    for head in range(heads):
        mine = slice(head * REP, (head + 1) * REP)
        top = top_ref[mine].reshape(new_top.shape[1:])
        mixed = mixed_ref[mine].reshape(new_top.shape[1:])
        new_top[head], new_mixed[head] = absorb(
            at_ref, q_ref, source, live, head, blocks, top, mixed, own_ref
        )


def second_kernel(heads, at_ref, q_ref, source_ref, live_ref, top_ref, mixed_ref, *refs):
    blocks, out_ref = refs[:-1], refs[-1]
    count = q_ref.shape[0]
    for head in range(heads):
        _, mixed = absorb(
            at_ref,
            q_ref,
            source_ref[...],
            live_ref[...],
            head,
            blocks,
            top_ref[head],
            mixed_ref[head],
            None,
        )
        first = head * REP * HD
        for r in range(REP):
            out_ref[:, first + r * HD : first + (r + 1) * HD] = mixed[
                r * count : (r + 1) * count
            ].astype(out_ref.dtype)


VMEM = pl.BlockSpec(memory_space=pltpu.VMEM)
SMEM = pl.BlockSpec(memory_space=pltpu.SMEM)
HBM = pl.BlockSpec(memory_space=pltpu.HBM)


def grant(mib):
    return pltpu.CompilerParams(vmem_limit_bytes=mib * 1024 * 1024)


def numbers(values):
    return jnp.stack([jnp.asarray(v, jnp.int32) for v in values])


def stages(depth):
    unit = 128
    first = max(unit, depth // 3 // unit * unit)
    return (first, depth - first)


def local(
    pre_x,
    dec_x,
    w_kv,
    kv_scale,
    dec_q,
    cache,
    cache_len,
    prompt_owner,
    prompt_len,
    sample_rows,
    *,
    shape,
):
    teams, ranks, cores = shape["groups"], shape["dp"], shape["tp"]
    inner = INNER
    outer = ranks // inner
    span, features = pre_x.shape
    count = dec_x.shape[0]
    depth, width = w_kv.shape
    heads = width // (2 * HD)
    band = width // teams
    team = lax.axis_index("groups")
    rank = lax.axis_index("dp")
    core = lax.axis_index("tp")
    place, block = rank % inner, rank // inner

    def to_inner(value, step):
        pairs = [(r, r // inner * inner + (r % inner ^ step)) for r in range(ranks)]
        return lax.ppermute(value, "dp", pairs)

    def to_outer(value, step=1):
        pairs = [(r, (r + step * inner) % ranks) for r in range(ranks)]
        return lax.ppermute(value, "dp", pairs)

    def to_team(value, step):
        return lax.ppermute(value, "groups", [(i, (i + step) % teams) for i in range(teams)])

    def to_core(value, step):
        return lax.ppermute(value, "tp", [(i, (i + step) % cores) for i in range(cores)])

    def pack(plan, places, shapes, mib, *arrays):
        sems = pltpu.SemaphoreType.DMA((len(plan),))
        return pl.pallas_call(
            functools.partial(pack_kernel, plan, places, len(arrays), len(shapes)),
            out_shape=shapes,
            in_specs=[HBM] * len(arrays),
            out_specs=[HBM] * len(shapes),
            scratch_shapes=[pltpu.VMEM(s.shape, s.dtype) for s in shapes] + [sems, sems],
            compiler_params=grant(mib),
        )(*arrays)

    sizes = stages(depth)
    pre_share, dec_share = span // cores, count // cores
    both = pre_share + dec_share
    plan, shapes = [], []
    for number, size in enumerate(sizes):
        plan.append((2, (size, band), number, len(sizes), number, 0, 0))
        shapes.append(jax.ShapeDtypeStruct((size, band), jnp.bfloat16))
    row = len(sizes) + 1
    for number in range(inner - 1):
        for back in range(outer):
            column, to = row + 2 + number * outer + back, back * depth
            plan.append((0, (pre_share, depth), row, column, len(shapes), 0, to))
            plan.append((1, (dec_share, depth), row + 1, column, len(shapes), pre_share, to))
        shapes.append(jax.ShapeDtypeStruct((both, outer * depth), jnp.bfloat16))

    def features(back, step):
        rank = lax.axis_index("dp")
        return ((rank // inner - back + outer) % outer * inner + (rank % inner ^ step)) * depth

    def send_places():
        core = lax.axis_index("tp")
        at = [sum(sizes[:number]) for number in range(len(sizes))]
        at += [lax.axis_index("groups") * band, core * pre_share, core * dec_share]
        return at + [features(back, step) for step in STEPS for back in range(outer)]

    sends = pack(plan, send_places, shapes, 56, pre_x, dec_x, w_kv)
    moving, row_sends = list(sends[: len(sizes)]), list(sends[len(sizes) :])
    row_sends, query, pre_x, dec_x = lax.optimization_barrier(
        (row_sends, dec_q.reshape(count, heads * REP, HD), pre_x, dec_x)
    )

    plan = []
    for back in range(outer):
        for turn in range(cores):
            column, to, base = 2 * cores + back, back * depth, turn * both
            plan.append((0, (pre_share, depth), 2 * turn, column, 0, base, to))
            plan.append((1, (dec_share, depth), 2 * turn + 1, column, 0, base + pre_share, to))

    def own_places():
        core, at = lax.axis_index("tp"), []
        for turn in range(cores):
            which = (core - turn + cores) % cores
            at += [which * pre_share, which * dec_share]
        return at + [features(back, 0) for back in range(outer)]

    total_rows = span + count
    shapes = [jax.ShapeDtypeStruct((total_rows, outer * depth), jnp.bfloat16)]
    (own_rows,) = pack(plan, own_places, shapes, 4, pre_x, dec_x)

    top_c, mixed_c = cached(query, cache, cache_len, heads)
    far = []
    for back in range(1, outer):
        moving = [to_outer(m) for m in moving]
        if back == 1:
            moving[0], row_sends[-1], top_c, mixed_c, own_rows = lax.optimization_barrier(
                (moving[0], row_sends[-1], top_c, mixed_c, own_rows)
            )
        far.append([[m] for m in moving])

    got = [to_inner(rows, step) for rows, step in zip(row_sends, STEPS)]
    far[0][-1][0], *got[:-1] = lax.optimization_barrier((far[0][-1][0], *got[:-1]))
    arrived = [[rows] + [to_core(rows, turn) for turn in range(1, cores)] for rows in got]

    for pieces in far:
        for number, piece in enumerate(pieces):
            if number:
                piece[0], pieces[number - 1][-1] = lax.optimization_barrier(
                    (piece[0], pieces[number - 1][-1])
                )
            piece += [to_team(piece[0], turn) for turn in range(1, teams)]

    last = sizes[-1]
    turns = numbers([(team - turn) % teams * band for turn in range(teams)])
    own_rows, got[-1] = lax.optimization_barrier((own_rows, got[-1]))
    blocks = [own_rows] + [rows for step in arrived[:-1] for rows in step]
    early = [m for pieces in far for m in pieces[0]]
    first_rows = (inner - 1) * total_rows
    *summed, last_rows = pl.pallas_call(
        functools.partial(early_kernel, outer, teams, last),
        out_shape=[
            *[jax.ShapeDtypeStruct((first_rows, band), jnp.float32)] * teams,
            jax.ShapeDtypeStruct((first_rows, (outer - 1) * last), jnp.bfloat16),
        ],
        in_specs=[SMEM] + [VMEM] * (1 + len(early) + len(blocks)),
        out_specs=[VMEM] * (1 + teams),
        scratch_shapes=[
            pltpu.VMEM((first_rows, outer * depth - (outer - 1) * last), jnp.bfloat16)
        ],
        compiler_params=grant(16),
    )(turns, w_kv, *early, *blocks)
    parts = []
    for turn in range(teams):
        pieces = [piece[turn] for some in far for piece in some]
        mine, *others = pl.pallas_call(
            functools.partial(late_kernel, outer, cores, turn),
            out_shape=[jax.ShapeDtypeStruct((total_rows, band), jnp.float32)]
            + [jax.ShapeDtypeStruct((total_rows, band), jnp.bfloat16)] * (inner - 1),
            in_specs=[SMEM] + [VMEM] * (3 + len(pieces) + cores),
            out_specs=[VMEM] * inner,
            scratch_shapes=[pltpu.VMEM((total_rows, outer * depth), jnp.bfloat16)],
            compiler_params=grant(12),
        )(turns, w_kv, summed[turn], last_rows, *pieces, *arrived[-1])
        parts += [mine] + [to_inner(part, step) for part, step in zip(others, STEPS)]
    prompt_kv, shifted, own_kv = pl.pallas_call(
        functools.partial(finish_kernel, cores, teams),
        out_shape=[
            jax.ShapeDtypeStruct((span, width), jnp.bfloat16),
            jax.ShapeDtypeStruct((span, width), jnp.bfloat16),
            jax.ShapeDtypeStruct((count, width), jnp.bfloat16),
        ],
        in_specs=[SMEM] + [VMEM] * (1 + len(parts)),
        out_specs=[VMEM] * 3,
        compiler_params=grant(6),
    )(
        numbers([core] + [(team - turn) % teams * band for turn in range(teams)]),
        kv_scale[None, :],
        *parts,
    )

    blocks, owners = [], []
    for back in range(outer):
        if back:
            shifted = to_outer(shifted)
        for step in range(inner):
            blocks.append(to_inner(shifted, step) if step else shifted)
            owners.append(((block - back) % outer) * inner + (place ^ step))

    state = jax.ShapeDtypeStruct((heads, REP * count, HD), jnp.float32)
    labels = jax.ShapeDtypeStruct((REP * count, HD), jnp.int32)
    *state, source, live = pl.pallas_call(
        functools.partial(first_kernel, heads),
        out_shape=[state, state, labels, labels],
        in_specs=[SMEM] * 3 + [VMEM] * (5 + inner),
        out_specs=[VMEM] * 4,
        compiler_params=grant(12),
    )(
        numbers([rank * count] + owners[:inner]),
        prompt_owner,
        prompt_len,
        sample_rows,
        dec_q,
        top_c,
        mixed_c,
        own_kv,
        *blocks[:inner],
    )
    attended = pl.pallas_call(
        functools.partial(second_kernel, heads),
        out_shape=jax.ShapeDtypeStruct(dec_q.shape, jnp.bfloat16),
        in_specs=[SMEM] + [VMEM] * (5 + len(blocks) - inner),
        out_specs=VMEM,
        compiler_params=grant(12),
    )(numbers([rank * count] + owners[inner:]), dec_q, source, live, *state, *blocks[inner:])
    return (attended, prompt_kv)


def solution(mesh):
    in_specs = (
        P(("groups", "dp"), None),
        P(("groups", "dp"), None),
        P("dp", "tp"),
        P("tp"),
        P(("groups", "dp"), "tp"),
        P(("groups", "dp"), None, "tp"),
        P(("groups", "dp")),
        P("groups"),
        P("groups"),
        P("groups", None),
    )
    out_specs = (P(("groups", "dp"), "tp"), P(("groups", "dp"), "tp"))
    body = functools.partial(local, shape=dict(mesh.shape))
    return jax.shard_map(body, mesh=mesh, in_specs=in_specs, out_specs=out_specs, check_vma=False)
```

```python
import functools
import math

import jax
import jax.numpy as jnp
from jax import lax
from jax.experimental import pallas as pl
from jax.experimental.pallas import tpu as pltpu
from jax.sharding import PartitionSpec as P

HD = 128
REP = 12
NEG = -1e30
INNER = 4
STEPS = (1, 2, 3)


def pack_kernel(plan, places, n_in, n_out, *refs):
    ins, outs = refs[:n_in], refs[n_in : n_in + n_out]
    held, (in_sems, out_sems) = refs[n_in + n_out : -2], refs[-2:]
    at = places()
    arriving, leaving = [], []
    for number, (src, shape, row, column, dst, to_row, to_column) in enumerate(plan):
        rows, columns = pl.ds(to_row, shape[0]), pl.ds(to_column, shape[1])
        from_row = pl.multiple_of(at[row], 16)
        from_column = pl.multiple_of(at[column], 128)
        arriving.append(
            pltpu.make_async_copy(
                ins[src].at[pl.ds(from_row, shape[0]), pl.ds(from_column, shape[1])],
                held[dst].at[rows, columns],
                in_sems.at[number],
            )
        )
        leaving.append(
            pltpu.make_async_copy(
                held[dst].at[rows, columns], outs[dst].at[rows, columns], out_sems.at[number]
            )
        )
        arriving[-1].start()
    for came, left in zip(arriving, leaving):
        came.wait()
        left.start()
    for left in leaving:
        left.wait()


def band_columns(teams, turn, band):
    team = lax.axis_index("groups")
    return pl.ds(pl.multiple_of((team - turn + teams) % teams * band, 128), band)


def early_kernel(outer, teams, last, w_ref, *refs):
    n_late = teams + 2
    pieces, refs = refs[: teams * (outer - 1)], refs[teams * (outer - 1) :]
    blocks, sum_refs, (last_ref, row_ref) = refs[:-n_late], refs[-n_late:-2], refs[-2:]
    depth = w_ref.shape[0]
    early = depth - last
    base = 0
    for block in blocks:
        rows = slice(base, base + block.shape[0])
        row_ref[rows, :depth] = block[:, :depth]
        for back in range(1, outer):
            at = depth + (back - 1) * early
            row_ref[rows, at : at + early] = block[:, back * depth : back * depth + early]
            last_ref[rows, (back - 1) * last : back * last] = block[
                :, back * depth + early : (back + 1) * depth
            ]
        base += block.shape[0]
    for turn, sum_ref in enumerate(sum_refs):
        columns = band_columns(teams, turn, sum_ref.shape[1])
        summed = jnp.dot(row_ref[:, :depth], w_ref[:, columns], preferred_element_type=jnp.float32)
        for back in range(1, outer):
            at = depth + (back - 1) * early
            summed = summed + jnp.dot(
                row_ref[:, at : at + early],
                pieces[(back - 1) * teams + turn][...],
                preferred_element_type=jnp.float32,
            )
        sum_ref[...] = summed


def late_kernel(outer, cores, teams, turn, w_ref, sum_ref, last_ref, *refs):
    pieces, refs = refs[: 2 * (outer - 1)], refs[2 * (outer - 1) :]
    halves, outs, row_ref = refs[:cores], refs[cores:-1], refs[-1]
    depth = w_ref.shape[0]
    last = last_ref.shape[1] // (outer - 1)
    each, both = outs[0].shape[0], halves[0].shape[0]
    for number, half in enumerate(halves):
        row_ref[number * both : (number + 1) * both, :] = half[...]
    columns = band_columns(teams, turn, sum_ref.shape[1])
    first = sum_ref[...]
    final = jnp.dot(row_ref[:, :depth], w_ref[:, columns], preferred_element_type=jnp.float32)
    for back in range(1, outer):
        early_piece, last_piece = pieces[2 * back - 2 : 2 * back]
        at = back * depth
        cut = at + depth - last
        final = final + jnp.dot(
            row_ref[:, at:cut], early_piece[...], preferred_element_type=jnp.float32
        )
        final = final + jnp.dot(
            row_ref[:, cut : cut + last], last_piece[...], preferred_element_type=jnp.float32
        )
        first = first + jnp.dot(
            last_ref[:, (back - 1) * last : back * last],
            last_piece[...],
            preferred_element_type=jnp.float32,
        )
    for step, out in enumerate(outs[:-1]):
        out[...] = first[step * each : (step + 1) * each].astype(out.dtype)
    outs[-1][...] = final.astype(outs[-1].dtype)


def finish_kernel(cores, teams, scale_ref, *refs):
    parts, (prompt_ref, sent_ref, own_ref) = refs[:-3], refs[-3:]
    span, count = prompt_ref.shape[0], own_ref.shape[0]
    pre_share, dec_share = span // cores, count // cores
    both = pre_share + dec_share
    band = scale_ref.shape[1] // teams
    for turn in range(teams):
        columns = band_columns(teams, turn, band)
        own, *others = parts[turn * len(parts) // teams : (turn + 1) * len(parts) // teams]
        summed = own[...]
        for part in others:
            summed = summed + part[...].astype(jnp.float32)
        done = (summed * scale_ref[:, columns]).astype(jnp.bfloat16)
        for share in range(cores):
            which = (lax.axis_index("tp") - share + cores) % cores
            rows = pl.ds(pl.multiple_of(which * pre_share, 16), pre_share)
            prompt_ref[rows, columns] = done[share * both : share * both + pre_share]
            sent_ref[rows, columns] = done[share * both : share * both + pre_share]
            own_ref[pl.ds(pl.multiple_of(which * dec_share, 16), dec_share), columns] = done[
                share * both + pre_share : (share + 1) * both
            ]


def match_rows(owner_ref, len_ref, samples_ref, count):
    row = lax.axis_index("dp") * count + lax.broadcasted_iota(jnp.int32, (count, 1), 0)
    source = jnp.zeros((count, 1), jnp.int32)
    live = jnp.zeros((count, 1), jnp.int32)
    for prompt in range(samples_ref.shape[0]):
        hit = jnp.max(
            jnp.where(samples_ref[prompt : prompt + 1, :] == row, 1, 0), -1, keepdims=True
        )
        source = source + hit * owner_ref[prompt]
        live = live + hit * len_ref[prompt]
    return source, live


def absorb(owners, q_ref, source, live, head, blocks, top, mixed, own_ref):
    count, span = q_ref.shape[0], blocks[0].shape[0]
    factor = 1.0 / math.sqrt(HD)
    first = head * REP * HD
    low, mid, high = head * 2 * HD, head * 2 * HD + HD, head * 2 * HD + 2 * HD
    q = jnp.concatenate([q_ref[:, first + r * HD : first + (r + 1) * HD] for r in range(REP)], 0)
    picked = jnp.full((REP * count, span), NEG, jnp.float32)
    place = lax.broadcasted_iota(jnp.int32, (REP * count, span), 1)
    for owner, block in zip(owners, blocks):
        scores = lax.dot_general(
            q,
            block[:, low:mid],
            (((1,), (1,)), ((), ())),
            preferred_element_type=jnp.float32,
        )
        picked = jnp.where(source == owner, scores * factor, picked)
    picked = jnp.where(place < live, picked, NEG)
    new = jnp.maximum(jnp.max(picked, -1, keepdims=True), top)
    if own_ref is not None:
        own_k = jnp.concatenate([own_ref[:, low:mid].astype(jnp.float32)] * REP, 0)
        own_v = jnp.concatenate([own_ref[:, mid:high].astype(jnp.float32)] * REP, 0)
        score = jnp.sum(q.astype(jnp.float32) * own_k, -1, keepdims=True) * factor
        new = jnp.maximum(new, score)
    weights = jnp.exp(picked - new)
    kept = jnp.exp(top - new)
    total = kept + jnp.sum(weights, -1, keepdims=True)
    mixed = mixed * kept
    if own_ref is not None:
        weight = jnp.exp(score - new)
        total = total + weight
        mixed = mixed + weight * own_v
    for owner, block in zip(owners, blocks):
        mixed = mixed + jnp.dot(
            jnp.where(source == owner, weights, 0.0).astype(jnp.bfloat16),
            block[:, mid:high],
            preferred_element_type=jnp.float32,
        )
    return new + jnp.log(total), mixed / total


def cache_kernel(heads, len_ref, q_ref, cache_ref, top_ref, mixed_ref):
    count, rows = q_ref.shape[0], heads * REP
    factor = 1.0 / math.sqrt(HD)
    query = [q_ref[:, r * HD : (r + 1) * HD].astype(jnp.float32) for r in range(rows)]
    query = jnp.swapaxes(jnp.stack(query), 0, 1).astype(jnp.bfloat16)
    head_of = lax.broadcasted_iota(jnp.int32, (rows, 1), 0) // REP
    spot = lax.broadcasted_iota(jnp.int32, (rows, cache_ref.shape[1]), 1)
    tops, mixes = [], []
    for sample in range(count):
        length = len_ref[pl.program_id(0) * count + sample]
        scores = mixed = None
        for head in range(heads):
            key = cache_ref[sample, :, head * 2 * HD : head * 2 * HD + HD]
            found = lax.dot_general(
                query[sample], key, (((1,), (1,)), ((), ())), preferred_element_type=jnp.float32
            )
            scores = found if head == 0 else jnp.where(head_of == head, found, scores)
        scores = jnp.where(spot < length, scores * factor, NEG)
        top = jnp.max(scores, -1, keepdims=True)
        weights = jnp.exp(scores - top)
        total = jnp.sum(weights, -1, keepdims=True)
        for head in range(heads):
            value = cache_ref[sample, :, head * 2 * HD + HD : (head + 1) * 2 * HD]
            found = jnp.dot(
                weights.astype(jnp.bfloat16), value, preferred_element_type=jnp.float32
            )
            mixed = found if head == 0 else jnp.where(head_of == head, found, mixed)
        tops.append(jnp.broadcast_to(top + jnp.log(total), (rows, HD)))
        mixes.append(mixed / total)
    top_ref[...] = jnp.swapaxes(jnp.stack(tops), 0, 1)
    mixed_ref[...] = jnp.swapaxes(jnp.stack(mixes), 0, 1)


def cached(query, cache, cache_len, heads):
    count, slots, width = cache.shape
    rows, each = heads * REP, 8
    state = jax.ShapeDtypeStruct((rows, count, HD), jnp.float32)
    return pl.pallas_call(
        functools.partial(cache_kernel, heads),
        grid=(count // each,),
        out_shape=[state, state],
        in_specs=[
            SMEM,
            pl.BlockSpec((each, rows * HD), lambda i: (i, 0)),
            pl.BlockSpec((each, slots, width), lambda i: (i, 0, 0)),
        ],
        out_specs=[pl.BlockSpec((rows, each, HD), lambda i: (0, i, 0))] * 2,
        compiler_params=grant(12),
        cost_estimate=pl.CostEstimate(
            flops=4 * count * rows * slots * HD * heads,
            bytes_accessed=2 * cache.size,
            transcendentals=count * rows * slots,
        ),
    )(cache_len, query, cache)


def first_kernel(
    heads, owners, owner_ref, len_ref, samples_ref, q_ref, top_ref, mixed_ref, own_ref, *refs
):
    blocks, (new_top, new_mixed, source_ref, live_ref) = refs[:-4], refs[-4:]
    source, live = match_rows(owner_ref, len_ref, samples_ref, q_ref.shape[0])
    source = jnp.concatenate([source] * REP, 0)
    live = jnp.concatenate([live] * REP, 0)
    source_ref[...] = jnp.broadcast_to(source, source_ref.shape)
    live_ref[...] = jnp.broadcast_to(live, live_ref.shape)
    for head in range(heads):
        mine = slice(head * REP, (head + 1) * REP)
        top = top_ref[mine].reshape(new_top.shape[1:])
        mixed = mixed_ref[mine].reshape(new_top.shape[1:])
        new_top[head], new_mixed[head] = absorb(
            owners(), q_ref, source, live, head, blocks, top, mixed, own_ref
        )


def second_kernel(heads, owners, q_ref, source_ref, live_ref, top_ref, mixed_ref, *refs):
    blocks, out_ref = refs[:-1], refs[-1]
    count = q_ref.shape[0]
    for head in range(heads):
        _, mixed = absorb(
            owners(),
            q_ref,
            source_ref[...],
            live_ref[...],
            head,
            blocks,
            top_ref[head],
            mixed_ref[head],
            None,
        )
        first = head * REP * HD
        for r in range(REP):
            out_ref[:, first + r * HD : first + (r + 1) * HD] = mixed[
                r * count : (r + 1) * count
            ].astype(out_ref.dtype)


VMEM = pl.BlockSpec(memory_space=pltpu.VMEM)
SMEM = pl.BlockSpec(memory_space=pltpu.SMEM)
HBM = pl.BlockSpec(memory_space=pltpu.HBM)


def after(value, *others):
    return lax.optimization_barrier((value, *others))[0]


def grant(mib):
    return pltpu.CompilerParams(vmem_limit_bytes=mib * 1024 * 1024)


def stages(depth):
    unit = 128
    first = max(unit, depth * 7 // 12 // unit * unit)
    return (first, depth - first)


def local(
    pre_x,
    dec_x,
    w_kv,
    kv_scale,
    dec_q,
    cache,
    cache_len,
    prompt_owner,
    prompt_len,
    sample_rows,
    *,
    shape,
):
    teams, ranks, cores = shape["groups"], shape["dp"], shape["tp"]
    inner = INNER
    outer = ranks // inner
    span, features = pre_x.shape
    count = dec_x.shape[0]
    depth, width = w_kv.shape
    heads = width // (2 * HD)
    band = width // teams

    def to_inner(value, step):
        pairs = [(r, r // inner * inner + (r % inner ^ step)) for r in range(ranks)]
        return lax.ppermute(value, "dp", pairs)

    def to_outer(value, step=1):
        pairs = [(r, (r + step * inner) % ranks) for r in range(ranks)]
        return lax.ppermute(value, "dp", pairs)

    def to_team(value, step):
        return lax.ppermute(value, "groups", [(i, (i + step) % teams) for i in range(teams)])

    def to_core(value, step):
        return lax.ppermute(value, "tp", [(i, (i + step) % cores) for i in range(cores)])

    def pack(plan, places, shapes, mib, *arrays):
        sems = pltpu.SemaphoreType.DMA((len(plan),))
        return pl.pallas_call(
            functools.partial(pack_kernel, plan, places, len(arrays), len(shapes)),
            out_shape=shapes,
            in_specs=[HBM] * len(arrays),
            out_specs=[HBM] * len(shapes),
            scratch_shapes=[pltpu.VMEM(s.shape, s.dtype) for s in shapes] + [sems, sems],
            compiler_params=grant(mib),
        )(*arrays)

    sizes = stages(depth)
    pre_share, dec_share = span // cores, count // cores
    both = pre_share + dec_share
    plan, shapes = [], []
    for number, size in enumerate(sizes):
        plan.append((2, (size, band), number, len(sizes), number, 0, 0))
        shapes.append(jax.ShapeDtypeStruct((size, band), jnp.bfloat16))
    row = len(sizes) + 1
    for number in range(inner - 1):
        for back in range(outer):
            column, to = row + 2 + number * outer + back, back * depth
            plan.append((0, (pre_share, depth), row, column, len(shapes), 0, to))
            plan.append((1, (dec_share, depth), row + 1, column, len(shapes), pre_share, to))
        shapes.append(jax.ShapeDtypeStruct((both, outer * depth), jnp.bfloat16))

    def features(back, step):
        rank = lax.axis_index("dp")
        return ((rank // inner - back + outer) % outer * inner + (rank % inner ^ step)) * depth

    def send_places():
        core = lax.axis_index("tp")
        at = [sum(sizes[:number]) for number in range(len(sizes))]
        at += [lax.axis_index("groups") * band, core * pre_share, core * dec_share]
        return at + [features(back, step) for step in STEPS for back in range(outer)]

    sends = pack(plan, send_places, shapes, 56, pre_x, dec_x, w_kv)
    moving, row_sends = list(sends[: len(sizes)]), list(sends[len(sizes) :])
    row_sends, query, pre_x, dec_x = lax.optimization_barrier((row_sends, dec_q, pre_x, dec_x))

    plan = []
    for back in range(outer):
        for turn in range(cores):
            column, to, base = 2 * cores + back, back * depth, turn * both
            plan.append((0, (pre_share, depth), 2 * turn, column, 0, base, to))
            plan.append((1, (dec_share, depth), 2 * turn + 1, column, 0, base + pre_share, to))

    def own_places():
        core, at = lax.axis_index("tp"), []
        for turn in range(cores):
            which = (core - turn + cores) % cores
            at += [which * pre_share, which * dec_share]
        return at + [features(back, 0) for back in range(outer)]

    total_rows = span + count
    shapes = [jax.ShapeDtypeStruct((total_rows, outer * depth), jnp.bfloat16)]
    (own_rows,) = pack(plan, own_places, shapes, 4, pre_x, dec_x)

    top_c, mixed_c = cached(query, cache, cache_len, heads)
    far = []
    for back in range(1, outer):
        moving = [to_outer(m) for m in moving]
        if back == 1:
            row_sends[-1] = after(row_sends[-1], moving[0], top_c, own_rows)
        far.append([[m] for m in moving])

    got = [to_inner(rows, step) for rows, step in zip(row_sends, STEPS)]
    arrived = [[rows] + [to_core(rows, turn) for turn in range(1, cores)] for rows in got]

    for pieces in far:
        for number, piece in enumerate(pieces):
            if number:
                sent = after(piece[0], pieces[number - 1][-1])
            else:
                sent = piece[0]
            piece += [to_team(sent, turn) for turn in range(1, teams)]

    last = sizes[-1]
    own_rows = after(own_rows, got[-1])
    blocks = [own_rows] + [rows for step in arrived[:-1] for rows in step]
    early = [m for pieces in far for m in pieces[0]]
    first_rows = (inner - 1) * total_rows
    *summed, last_rows = pl.pallas_call(
        functools.partial(early_kernel, outer, teams, last),
        out_shape=[
            *[jax.ShapeDtypeStruct((first_rows, band), jnp.float32)] * teams,
            jax.ShapeDtypeStruct((first_rows, (outer - 1) * last), jnp.bfloat16),
        ],
        in_specs=[VMEM] * (1 + len(early) + len(blocks)),
        out_specs=[VMEM] * (1 + teams),
        scratch_shapes=[
            pltpu.VMEM((first_rows, outer * depth - (outer - 1) * last), jnp.bfloat16)
        ],
        compiler_params=grant(16),
    )(w_kv, *early, *blocks)
    parts = []
    for turn in range(teams):
        pieces = [piece[turn] for some in far for piece in some]
        mine, *others = pl.pallas_call(
            functools.partial(late_kernel, outer, cores, teams, turn),
            out_shape=[jax.ShapeDtypeStruct((total_rows, band), jnp.float32)]
            + [jax.ShapeDtypeStruct((total_rows, band), jnp.bfloat16)] * (inner - 1),
            in_specs=[VMEM] * (3 + len(pieces) + cores),
            out_specs=[VMEM] * inner,
            scratch_shapes=[pltpu.VMEM((total_rows, outer * depth), jnp.bfloat16)],
            compiler_params=grant(12),
        )(w_kv, summed[turn], last_rows, *pieces, *arrived[-1])
        parts += [mine] + [to_inner(part, step) for part, step in zip(others, STEPS)]
    prompt_kv, shifted, own_kv = pl.pallas_call(
        functools.partial(finish_kernel, cores, teams),
        out_shape=[
            jax.ShapeDtypeStruct((span, width), jnp.bfloat16),
            jax.ShapeDtypeStruct((span, width), jnp.bfloat16),
            jax.ShapeDtypeStruct((count, width), jnp.bfloat16),
        ],
        in_specs=[VMEM] * (1 + len(parts)),
        out_specs=[VMEM] * 3,
        compiler_params=grant(6),
    )(kv_scale[None, :], *parts)

    def owners(backs):
        rank = lax.axis_index("dp")
        return [
            (rank // inner - back + outer) % outer * inner + (rank % inner ^ step)
            for back in backs
            for step in range(inner)
        ]

    blocks = []
    for back in range(outer):
        if back:
            shifted = to_outer(shifted)
        blocks += [to_inner(shifted, step) if step else shifted for step in range(inner)]

    state = jax.ShapeDtypeStruct((heads, REP * count, HD), jnp.float32)
    labels = jax.ShapeDtypeStruct((REP * count, HD), jnp.int32)
    *state, source, live = pl.pallas_call(
        functools.partial(first_kernel, heads, lambda: owners([0])),
        out_shape=[state, state, labels, labels],
        in_specs=[SMEM] * 2 + [VMEM] * (5 + inner),
        out_specs=[VMEM] * 4,
        compiler_params=grant(12),
    )(
        prompt_owner,
        prompt_len,
        sample_rows,
        dec_q,
        top_c,
        mixed_c,
        own_kv,
        *blocks[:inner],
    )
    attended = pl.pallas_call(
        functools.partial(second_kernel, heads, lambda: owners(range(1, outer))),
        out_shape=jax.ShapeDtypeStruct(dec_q.shape, jnp.bfloat16),
        in_specs=[VMEM] * (5 + len(blocks) - inner),
        out_specs=VMEM,
        compiler_params=grant(12),
    )(dec_q, source, live, *state, *blocks[inner:])
    return (attended, prompt_kv)


def solution(mesh):
    in_specs = (
        P(("groups", "dp"), None),
        P(("groups", "dp"), None),
        P("dp", "tp"),
        P("tp"),
        P(("groups", "dp"), "tp"),
        P(("groups", "dp"), None, "tp"),
        P(("groups", "dp")),
        P("groups"),
        P("groups"),
        P("groups", None),
    )
    out_specs = (P(("groups", "dp"), "tp"), P(("groups", "dp"), "tp"))
    body = functools.partial(local, shape=dict(mesh.shape))
    return jax.shard_map(body, mesh=mesh, in_specs=in_specs, out_specs=out_specs, check_vma=False)
```

```python
import functools
import math

import jax
import jax.numpy as jnp
from jax import lax
from jax.experimental import pallas as pl
from jax.experimental.pallas import tpu as pltpu
from jax.sharding import PartitionSpec as P

HD = 128
REP = 12
NEG = -1e30
INNER = 4
STEPS = (1, 2, 3)


def pack_kernel(plan, places, n_in, n_out, *refs):
    ins, outs = refs[:n_in], refs[n_in : n_in + n_out]
    held, (in_sems, out_sems) = refs[n_in + n_out : -2], refs[-2:]
    at = places()
    arriving, leaving = [], []
    for number, (src, shape, row, column, dst, to_row, to_column) in enumerate(plan):
        rows, columns = pl.ds(to_row, shape[0]), pl.ds(to_column, shape[1])
        from_row = pl.multiple_of(at[row], 16)
        from_column = pl.multiple_of(at[column], 128)
        arriving.append(
            pltpu.make_async_copy(
                ins[src].at[pl.ds(from_row, shape[0]), pl.ds(from_column, shape[1])],
                held[dst].at[rows, columns],
                in_sems.at[number],
            )
        )
        leaving.append(
            pltpu.make_async_copy(
                held[dst].at[rows, columns], outs[dst].at[rows, columns], out_sems.at[number]
            )
        )
        arriving[-1].start()
    for came, left in zip(arriving, leaving):
        came.wait()
        left.start()
    for left in leaving:
        left.wait()


def band_columns(teams, turn, band):
    team = lax.axis_index("groups")
    return pl.ds(pl.multiple_of((team - turn + teams) % teams * band, 128), band)


def early_kernel(outer, teams, last, w_ref, *refs):
    n_late = teams + 2
    pieces, refs = refs[: teams * (outer - 1)], refs[teams * (outer - 1) :]
    blocks, sum_refs, (last_ref, row_ref) = refs[:-n_late], refs[-n_late:-2], refs[-2:]
    depth = w_ref.shape[0]
    early = depth - last
    base = 0
    for block in blocks:
        rows = slice(base, base + block.shape[0])
        row_ref[rows, :depth] = block[:, :depth]
        for back in range(1, outer):
            at = depth + (back - 1) * early
            row_ref[rows, at : at + early] = block[:, back * depth : back * depth + early]
            last_ref[rows, (back - 1) * last : back * last] = block[
                :, back * depth + early : (back + 1) * depth
            ]
        base += block.shape[0]
    for turn, sum_ref in enumerate(sum_refs):
        columns = band_columns(teams, turn, sum_ref.shape[1])
        summed = jnp.dot(row_ref[:, :depth], w_ref[:, columns], preferred_element_type=jnp.float32)
        for back in range(1, outer):
            at = depth + (back - 1) * early
            summed = summed + jnp.dot(
                row_ref[:, at : at + early],
                pieces[(back - 1) * teams + turn][...],
                preferred_element_type=jnp.float32,
            )
        sum_ref[...] = summed


def late_kernel(outer, cores, teams, turn, w_ref, sum_ref, last_ref, *refs):
    pieces, refs = refs[: 2 * (outer - 1)], refs[2 * (outer - 1) :]
    halves, outs, row_ref = refs[:cores], refs[cores:-1], refs[-1]
    depth = w_ref.shape[0]
    last = last_ref.shape[1] // (outer - 1)
    each, both = outs[0].shape[0], halves[0].shape[0]
    for number, half in enumerate(halves):
        row_ref[number * both : (number + 1) * both, :] = half[...]
    columns = band_columns(teams, turn, sum_ref.shape[1])
    first = sum_ref[...]
    final = jnp.dot(row_ref[:, :depth], w_ref[:, columns], preferred_element_type=jnp.float32)
    for back in range(1, outer):
        early_piece, last_piece = pieces[2 * back - 2 : 2 * back]
        at = back * depth
        cut = at + depth - last
        final = final + jnp.dot(
            row_ref[:, at:cut], early_piece[...], preferred_element_type=jnp.float32
        )
        final = final + jnp.dot(
            row_ref[:, cut : cut + last], last_piece[...], preferred_element_type=jnp.float32
        )
        first = first + jnp.dot(
            last_ref[:, (back - 1) * last : back * last],
            last_piece[...],
            preferred_element_type=jnp.float32,
        )
    for step, out in enumerate(outs[:-1]):
        out[...] = first[step * each : (step + 1) * each].astype(out.dtype)
    outs[-1][...] = final.astype(outs[-1].dtype)


def finish_kernel(cores, teams, scale_ref, *refs):
    parts, (prompt_ref, sent_ref, own_ref) = refs[:-3], refs[-3:]
    span, count = prompt_ref.shape[0], own_ref.shape[0]
    pre_share, dec_share = span // cores, count // cores
    both = pre_share + dec_share
    band = scale_ref.shape[1] // teams
    for turn in range(teams):
        columns = band_columns(teams, turn, band)
        own, *others = parts[turn * len(parts) // teams : (turn + 1) * len(parts) // teams]
        summed = own[...]
        for part in others:
            summed = summed + part[...].astype(jnp.float32)
        done = (summed * scale_ref[:, columns]).astype(jnp.bfloat16)
        for share in range(cores):
            which = (lax.axis_index("tp") - share + cores) % cores
            rows = pl.ds(pl.multiple_of(which * pre_share, 16), pre_share)
            prompt_ref[rows, columns] = done[share * both : share * both + pre_share]
            sent_ref[rows, columns] = done[share * both : share * both + pre_share]
            own_ref[pl.ds(pl.multiple_of(which * dec_share, 16), dec_share), columns] = done[
                share * both + pre_share : (share + 1) * both
            ]


def match_rows(owner_ref, len_ref, samples_ref, count):
    row = lax.axis_index("dp") * count + lax.broadcasted_iota(jnp.int32, (count, 1), 0)
    source = jnp.zeros((count, 1), jnp.int32)
    live = jnp.zeros((count, 1), jnp.int32)
    for prompt in range(samples_ref.shape[0]):
        hit = jnp.max(
            jnp.where(samples_ref[prompt : prompt + 1, :] == row, 1, 0), -1, keepdims=True
        )
        source = source + hit * owner_ref[prompt]
        live = live + hit * len_ref[prompt]
    return source, live


def absorb(owners, q_ref, source, live, head, blocks, top, mixed, own_ref):
    count, span = q_ref.shape[0], blocks[0].shape[0]
    factor = 1.0 / math.sqrt(HD)
    first = head * REP * HD
    low, mid, high = head * 2 * HD, head * 2 * HD + HD, head * 2 * HD + 2 * HD
    q = jnp.concatenate([q_ref[:, first + r * HD : first + (r + 1) * HD] for r in range(REP)], 0)
    picked = jnp.full((REP * count, span), NEG, jnp.float32)
    place = lax.broadcasted_iota(jnp.int32, (REP * count, span), 1)
    for owner, block in zip(owners, blocks):
        scores = lax.dot_general(
            q,
            block[:, low:mid],
            (((1,), (1,)), ((), ())),
            preferred_element_type=jnp.float32,
        )
        picked = jnp.where(source == owner, scores * factor, picked)
    picked = jnp.where(place < live, picked, NEG)
    new = jnp.maximum(jnp.max(picked, -1, keepdims=True), top)
    if own_ref is not None:
        own_k = jnp.concatenate([own_ref[:, low:mid].astype(jnp.float32)] * REP, 0)
        own_v = jnp.concatenate([own_ref[:, mid:high].astype(jnp.float32)] * REP, 0)
        score = jnp.sum(q.astype(jnp.float32) * own_k, -1, keepdims=True) * factor
        new = jnp.maximum(new, score)
    weights = jnp.exp(picked - new)
    kept = jnp.exp(top - new)
    total = kept + jnp.sum(weights, -1, keepdims=True)
    mixed = mixed * kept
    if own_ref is not None:
        weight = jnp.exp(score - new)
        total = total + weight
        mixed = mixed + weight * own_v
    for owner, block in zip(owners, blocks):
        mixed = mixed + jnp.dot(
            jnp.where(source == owner, weights, 0.0).astype(jnp.bfloat16),
            block[:, mid:high],
            preferred_element_type=jnp.float32,
        )
    return new + jnp.log(total), mixed / total


def cache_kernel(heads, len_ref, q_ref, cache_ref, top_ref, mixed_ref):
    count, rows = q_ref.shape[0], heads * REP
    factor = 1.0 / math.sqrt(HD)
    query = [q_ref[:, r * HD : (r + 1) * HD].astype(jnp.float32) for r in range(rows)]
    query = jnp.swapaxes(jnp.stack(query), 0, 1).astype(jnp.bfloat16)
    head_of = lax.broadcasted_iota(jnp.int32, (rows, 1), 0) // REP
    spot = lax.broadcasted_iota(jnp.int32, (rows, cache_ref.shape[1]), 1)
    tops, mixes = [], []
    for sample in range(count):
        length = len_ref[pl.program_id(0) * count + sample]
        scores = mixed = None
        for head in range(heads):
            key = cache_ref[sample, :, head * 2 * HD : head * 2 * HD + HD]
            found = lax.dot_general(
                query[sample], key, (((1,), (1,)), ((), ())), preferred_element_type=jnp.float32
            )
            scores = found if head == 0 else jnp.where(head_of == head, found, scores)
        scores = jnp.where(spot < length, scores * factor, NEG)
        top = jnp.max(scores, -1, keepdims=True)
        weights = jnp.exp(scores - top)
        total = jnp.sum(weights, -1, keepdims=True)
        for head in range(heads):
            value = cache_ref[sample, :, head * 2 * HD + HD : (head + 1) * 2 * HD]
            found = jnp.dot(
                weights.astype(jnp.bfloat16), value, preferred_element_type=jnp.float32
            )
            mixed = found if head == 0 else jnp.where(head_of == head, found, mixed)
        tops.append(jnp.broadcast_to(top + jnp.log(total), (rows, HD)))
        mixes.append(mixed / total)
    top_ref[...] = jnp.swapaxes(jnp.stack(tops), 0, 1)
    mixed_ref[...] = jnp.swapaxes(jnp.stack(mixes), 0, 1)


def cached(query, cache, cache_len, heads):
    count, slots, width = cache.shape
    rows, each = heads * REP, 8
    state = jax.ShapeDtypeStruct((rows, count, HD), jnp.float32)
    return pl.pallas_call(
        functools.partial(cache_kernel, heads),
        grid=(count // each,),
        out_shape=[state, state],
        in_specs=[
            SMEM,
            pl.BlockSpec((each, rows * HD), lambda i: (i, 0)),
            pl.BlockSpec((each, slots, width), lambda i: (i, 0, 0)),
        ],
        out_specs=[pl.BlockSpec((rows, each, HD), lambda i: (0, i, 0))] * 2,
        compiler_params=grant(12),
        cost_estimate=pl.CostEstimate(
            flops=4 * count * rows * slots * HD * heads,
            bytes_accessed=2 * cache.size,
            transcendentals=count * rows * slots,
        ),
    )(cache_len, query, cache)


def first_kernel(
    heads, owners, owner_ref, len_ref, samples_ref, q_ref, top_ref, mixed_ref, own_ref, *refs
):
    blocks, (new_top, new_mixed, source_ref, live_ref) = refs[:-4], refs[-4:]
    source, live = match_rows(owner_ref, len_ref, samples_ref, q_ref.shape[0])
    source = jnp.concatenate([source] * REP, 0)
    live = jnp.concatenate([live] * REP, 0)
    source_ref[...] = jnp.broadcast_to(source, source_ref.shape)
    live_ref[...] = jnp.broadcast_to(live, live_ref.shape)
    for head in range(heads):
        mine = slice(head * REP, (head + 1) * REP)
        top = top_ref[mine].reshape(new_top.shape[1:])
        mixed = mixed_ref[mine].reshape(new_top.shape[1:])
        new_top[head], new_mixed[head] = absorb(
            owners(), q_ref, source, live, head, blocks, top, mixed, own_ref
        )


def second_kernel(heads, owners, q_ref, source_ref, live_ref, top_ref, mixed_ref, *refs):
    blocks, out_ref = refs[:-1], refs[-1]
    count = q_ref.shape[0]
    for head in range(heads):
        _, mixed = absorb(
            owners(),
            q_ref,
            source_ref[...],
            live_ref[...],
            head,
            blocks,
            top_ref[head],
            mixed_ref[head],
            None,
        )
        first = head * REP * HD
        for r in range(REP):
            out_ref[:, first + r * HD : first + (r + 1) * HD] = mixed[
                r * count : (r + 1) * count
            ].astype(out_ref.dtype)


VMEM = pl.BlockSpec(memory_space=pltpu.VMEM)
SMEM = pl.BlockSpec(memory_space=pltpu.SMEM)
HBM = pl.BlockSpec(memory_space=pltpu.HBM)


def after(value, *others):
    return lax.optimization_barrier((value, *others))[0]


def grant(mib):
    return pltpu.CompilerParams(vmem_limit_bytes=mib * 1024 * 1024)


def stages(depth):
    unit = 128
    first = max(unit, depth * 7 // 12 // unit * unit)
    return (first, depth - first)


def local(
    pre_x,
    dec_x,
    w_kv,
    kv_scale,
    dec_q,
    cache,
    cache_len,
    prompt_owner,
    prompt_len,
    sample_rows,
    *,
    shape,
):
    teams, ranks, cores = shape["groups"], shape["dp"], shape["tp"]
    inner = INNER
    outer = ranks // inner
    span, features = pre_x.shape
    count = dec_x.shape[0]
    depth, width = w_kv.shape
    heads = width // (2 * HD)
    band = width // teams

    def to_inner(value, step):
        pairs = [(r, r // inner * inner + (r % inner ^ step)) for r in range(ranks)]
        return lax.ppermute(value, "dp", pairs)

    def to_outer(value, step=1):
        pairs = [(r, (r + step * inner) % ranks) for r in range(ranks)]
        return lax.ppermute(value, "dp", pairs)

    def to_team(value, step):
        return lax.ppermute(value, "groups", [(i, (i + step) % teams) for i in range(teams)])

    def to_core(value, step):
        return lax.ppermute(value, "tp", [(i, (i + step) % cores) for i in range(cores)])

    def pack(plan, places, shapes, mib, *arrays):
        sems = pltpu.SemaphoreType.DMA((len(plan),))
        return pl.pallas_call(
            functools.partial(pack_kernel, plan, places, len(arrays), len(shapes)),
            out_shape=shapes,
            in_specs=[HBM] * len(arrays),
            out_specs=[HBM] * len(shapes),
            scratch_shapes=[pltpu.VMEM(s.shape, s.dtype) for s in shapes] + [sems, sems],
            compiler_params=grant(mib),
        )(*arrays)

    sizes = stages(depth)
    pre_share, dec_share = span // cores, count // cores
    both = pre_share + dec_share
    def features(back, step):
        rank = lax.axis_index("dp")
        return ((rank // inner - back + outer) % outer * inner + (rank % inner ^ step)) * depth

    def band_place():
        return [0, lax.axis_index("groups") * band]

    shape = jax.ShapeDtypeStruct((sizes[0], band), jnp.bfloat16)
    (first_piece,) = pack([(0, (sizes[0], band), 0, 1, 0, 0, 0)], band_place, [shape], 56, w_kv)
    first_piece, pre_x, dec_x, w_kv = lax.optimization_barrier((first_piece, pre_x, dec_x, w_kv))

    plan = [(2, (sizes[1], band), 0, 1, 0, 0, 0)]
    shapes = [jax.ShapeDtypeStruct((sizes[1], band), jnp.bfloat16)]
    for number in range(inner - 1):
        for back in range(outer):
            column, to = 4 + number * outer + back, back * depth
            plan.append((0, (pre_share, depth), 2, column, len(shapes), 0, to))
            plan.append((1, (dec_share, depth), 3, column, len(shapes), pre_share, to))
        shapes.append(jax.ShapeDtypeStruct((both, outer * depth), jnp.bfloat16))

    def send_places():
        core = lax.axis_index("tp")
        at = [sizes[0], lax.axis_index("groups") * band, core * pre_share, core * dec_share]
        return at + [features(back, step) for step in STEPS for back in range(outer)]

    last_piece, *row_sends = pack(plan, send_places, shapes, 56, pre_x, dec_x, w_kv)
    moving = [first_piece, last_piece]
    row_sends, query, pre_x, dec_x = lax.optimization_barrier((row_sends, dec_q, pre_x, dec_x))

    plan = []
    for back in range(outer):
        for turn in range(cores):
            column, to, base = 2 * cores + back, back * depth, turn * both
            plan.append((0, (pre_share, depth), 2 * turn, column, 0, base, to))
            plan.append((1, (dec_share, depth), 2 * turn + 1, column, 0, base + pre_share, to))

    def own_places():
        core, at = lax.axis_index("tp"), []
        for turn in range(cores):
            which = (core - turn + cores) % cores
            at += [which * pre_share, which * dec_share]
        return at + [features(back, 0) for back in range(outer)]

    total_rows = span + count
    shapes = [jax.ShapeDtypeStruct((total_rows, outer * depth), jnp.bfloat16)]
    (own_rows,) = pack(plan, own_places, shapes, 4, pre_x, dec_x)

    top_c, mixed_c = cached(query, cache, cache_len, heads)
    far = []
    for back in range(1, outer):
        moving = [to_outer(m) for m in moving]
        if back == 1:
            row_sends[-1] = after(row_sends[-1], moving[0], top_c, own_rows)
        far.append([[m] for m in moving])

    got = [to_inner(rows, step) for rows, step in zip(row_sends, STEPS)]
    arrived = [[rows] + [to_core(rows, turn) for turn in range(1, cores)] for rows in got]

    for pieces in far:
        for number, piece in enumerate(pieces):
            if number:
                sent = after(piece[0], pieces[number - 1][-1])
            else:
                sent = piece[0]
            piece += [to_team(sent, turn) for turn in range(1, teams)]

    last = sizes[-1]
    own_rows = after(own_rows, got[-1])
    blocks = [own_rows] + [rows for step in arrived[:-1] for rows in step]
    early = [m for pieces in far for m in pieces[0]]
    first_rows = (inner - 1) * total_rows
    *summed, last_rows = pl.pallas_call(
        functools.partial(early_kernel, outer, teams, last),
        out_shape=[
            *[jax.ShapeDtypeStruct((first_rows, band), jnp.float32)] * teams,
            jax.ShapeDtypeStruct((first_rows, (outer - 1) * last), jnp.bfloat16),
        ],
        in_specs=[VMEM] * (1 + len(early) + len(blocks)),
        out_specs=[VMEM] * (1 + teams),
        scratch_shapes=[
            pltpu.VMEM((first_rows, outer * depth - (outer - 1) * last), jnp.bfloat16)
        ],
        compiler_params=grant(16),
    )(w_kv, *early, *blocks)
    parts = []
    for turn in range(teams):
        pieces = [piece[turn] for some in far for piece in some]
        mine, *others = pl.pallas_call(
            functools.partial(late_kernel, outer, cores, teams, turn),
            out_shape=[jax.ShapeDtypeStruct((total_rows, band), jnp.float32)]
            + [jax.ShapeDtypeStruct((total_rows, band), jnp.bfloat16)] * (inner - 1),
            in_specs=[VMEM] * (3 + len(pieces) + cores),
            out_specs=[VMEM] * inner,
            scratch_shapes=[pltpu.VMEM((total_rows, outer * depth), jnp.bfloat16)],
            compiler_params=grant(12),
        )(w_kv, summed[turn], last_rows, *pieces, *arrived[-1])
        parts += [mine] + [to_inner(part, step) for part, step in zip(others, STEPS)]
    prompt_kv, shifted, own_kv = pl.pallas_call(
        functools.partial(finish_kernel, cores, teams),
        out_shape=[
            jax.ShapeDtypeStruct((span, width), jnp.bfloat16),
            jax.ShapeDtypeStruct((span, width), jnp.bfloat16),
            jax.ShapeDtypeStruct((count, width), jnp.bfloat16),
        ],
        in_specs=[VMEM] * (1 + len(parts)),
        out_specs=[VMEM] * 3,
        compiler_params=grant(6),
    )(kv_scale[None, :], *parts)

    def owners(backs):
        rank = lax.axis_index("dp")
        return [
            (rank // inner - back + outer) % outer * inner + (rank % inner ^ step)
            for back in backs
            for step in range(inner)
        ]

    blocks = []
    for back in range(outer):
        if back:
            shifted = to_outer(shifted)
        blocks += [shifted, to_inner(shifted, 1), to_inner(shifted, 2)]
        blocks.append(to_inner(shifted, 3) if back else to_inner(blocks[2], 1))

    state = jax.ShapeDtypeStruct((heads, REP * count, HD), jnp.float32)
    labels = jax.ShapeDtypeStruct((REP * count, HD), jnp.int32)
    *state, source, live = pl.pallas_call(
        functools.partial(first_kernel, heads, lambda: owners([0])),
        out_shape=[state, state, labels, labels],
        in_specs=[SMEM] * 2 + [VMEM] * (5 + inner),
        out_specs=[VMEM] * 4,
        compiler_params=grant(12),
    )(
        prompt_owner,
        prompt_len,
        sample_rows,
        dec_q,
        top_c,
        mixed_c,
        own_kv,
        *blocks[:inner],
    )
    attended = pl.pallas_call(
        functools.partial(second_kernel, heads, lambda: owners(range(1, outer))),
        out_shape=jax.ShapeDtypeStruct(dec_q.shape, jnp.bfloat16),
        in_specs=[VMEM] * (5 + len(blocks) - inner),
        out_specs=VMEM,
        compiler_params=grant(12),
    )(dec_q, source, live, *state, *blocks[inner:])
    return (attended, prompt_kv)


def solution(mesh):
    in_specs = (
        P(("groups", "dp"), None),
        P(("groups", "dp"), None),
        P("dp", "tp"),
        P("tp"),
        P(("groups", "dp"), "tp"),
        P(("groups", "dp"), None, "tp"),
        P(("groups", "dp")),
        P("groups"),
        P("groups"),
        P("groups", None),
    )
    out_specs = (P(("groups", "dp"), "tp"), P(("groups", "dp"), "tp"))
    body = functools.partial(local, shape=dict(mesh.shape))
    return jax.shard_map(body, mesh=mesh, in_specs=in_specs, out_specs=out_specs, check_vma=False)
```

```python
import functools
import math

import jax
import jax.numpy as jnp
from jax import lax
from jax.experimental import pallas as pl
from jax.experimental.pallas import tpu as pltpu
from jax.sharding import PartitionSpec as P

HD = 128
REP = 12
NEG = -1e30
INNER = 4
STEPS = (1, 2, 3)


def pack_kernel(plan, places, n_in, n_out, *refs):
    ins, outs = refs[:n_in], refs[n_in : n_in + n_out]
    held, (in_sems, out_sems) = refs[n_in + n_out : -2], refs[-2:]
    at = places()
    arriving, leaving = [], []
    for number, (src, shape, row, column, dst, to_row, to_column) in enumerate(plan):
        rows, columns = pl.ds(to_row, shape[0]), pl.ds(to_column, shape[1])
        from_row = pl.multiple_of(at[row], 16)
        from_column = pl.multiple_of(at[column], 128)
        arriving.append(
            pltpu.make_async_copy(
                ins[src].at[pl.ds(from_row, shape[0]), pl.ds(from_column, shape[1])],
                held[dst].at[rows, columns],
                in_sems.at[number],
            )
        )
        leaving.append(
            pltpu.make_async_copy(
                held[dst].at[rows, columns], outs[dst].at[rows, columns], out_sems.at[number]
            )
        )
        arriving[-1].start()
    for came, left in zip(arriving, leaving):
        came.wait()
        left.start()
    for left in leaving:
        left.wait()


def band_columns(teams, turn, band):
    team = lax.axis_index("groups")
    return pl.ds(pl.multiple_of((team - turn + teams) % teams * band, 128), band)


def early_kernel(outer, teams, last, w_ref, *refs):
    n_late = teams + 2
    pieces, refs = refs[: teams * (outer - 1)], refs[teams * (outer - 1) :]
    blocks, sum_refs, (last_ref, row_ref) = refs[:-n_late], refs[-n_late:-2], refs[-2:]
    depth = w_ref.shape[0]
    early = depth - last
    base = 0
    for block in blocks:
        rows = slice(base, base + block.shape[0])
        row_ref[rows, :depth] = block[:, :depth]
        for back in range(1, outer):
            at = depth + (back - 1) * early
            row_ref[rows, at : at + early] = block[:, back * depth : back * depth + early]
            last_ref[rows, (back - 1) * last : back * last] = block[
                :, back * depth + early : (back + 1) * depth
            ]
        base += block.shape[0]
    for turn, sum_ref in enumerate(sum_refs):
        columns = band_columns(teams, turn, sum_ref.shape[1])
        summed = jnp.dot(row_ref[:, :depth], w_ref[:, columns], preferred_element_type=jnp.float32)
        for back in range(1, outer):
            at = depth + (back - 1) * early
            summed = summed + jnp.dot(
                row_ref[:, at : at + early],
                pieces[(back - 1) * teams + turn][...],
                preferred_element_type=jnp.float32,
            )
        sum_ref[...] = summed


def late_kernel(outer, cores, teams, turn, w_ref, sum_ref, last_ref, *refs):
    pieces, refs = refs[: 2 * (outer - 1)], refs[2 * (outer - 1) :]
    halves, outs, row_ref = refs[:cores], refs[cores:-1], refs[-1]
    depth = w_ref.shape[0]
    last = last_ref.shape[1] // (outer - 1)
    each, both = outs[0].shape[0], halves[0].shape[0]
    for number, half in enumerate(halves):
        row_ref[number * both : (number + 1) * both, :] = half[...]
    columns = band_columns(teams, turn, sum_ref.shape[1])
    first = sum_ref[...]
    final = jnp.dot(row_ref[:, :depth], w_ref[:, columns], preferred_element_type=jnp.float32)
    for back in range(1, outer):
        early_piece, last_piece = pieces[2 * back - 2 : 2 * back]
        at = back * depth
        cut = at + depth - last
        final = final + jnp.dot(
            row_ref[:, at:cut], early_piece[...], preferred_element_type=jnp.float32
        )
        final = final + jnp.dot(
            row_ref[:, cut : cut + last], last_piece[...], preferred_element_type=jnp.float32
        )
        first = first + jnp.dot(
            last_ref[:, (back - 1) * last : back * last],
            last_piece[...],
            preferred_element_type=jnp.float32,
        )
    for step, out in enumerate(outs[:-1]):
        out[...] = first[step * each : (step + 1) * each].astype(out.dtype)
    outs[-1][...] = final.astype(outs[-1].dtype)


def finish_kernel(cores, teams, turn, scale_ref, *refs):
    parts, (prompt_ref, own_ref) = refs[:-2], refs[-2:]
    pre_share, dec_share = prompt_ref.shape[0] // cores, own_ref.shape[0] // cores
    both = pre_share + dec_share
    summed = parts[0][...]
    for part in parts[1:]:
        summed = summed + part[...].astype(jnp.float32)
    columns = band_columns(teams, turn, prompt_ref.shape[1])
    done = (summed * scale_ref[:, columns]).astype(jnp.bfloat16)
    for share in range(cores):
        which = (lax.axis_index("tp") - share + cores) % cores
        prompt_ref[pl.ds(pl.multiple_of(which * pre_share, 16), pre_share), :] = done[
            share * both : share * both + pre_share
        ]
        own_ref[pl.ds(pl.multiple_of(which * dec_share, 16), dec_share), :] = done[
            share * both + pre_share : (share + 1) * both
        ]


def join_bands(teams, bands, held):
    per = len(bands) // teams
    for turn in range(teams):
        for at, ref in enumerate(bands[turn * per : (turn + 1) * per]):
            held[at][:, band_columns(teams, turn, ref.shape[1])] = ref[...]


def match_rows(owner_ref, len_ref, samples_ref, count):
    row = lax.axis_index("dp") * count + lax.broadcasted_iota(jnp.int32, (count, 1), 0)
    source = jnp.zeros((count, 1), jnp.int32)
    live = jnp.zeros((count, 1), jnp.int32)
    for prompt in range(samples_ref.shape[0]):
        hit = jnp.max(
            jnp.where(samples_ref[prompt : prompt + 1, :] == row, 1, 0), -1, keepdims=True
        )
        source = source + hit * owner_ref[prompt]
        live = live + hit * len_ref[prompt]
    return source, live


def absorb(owners, q_ref, source, live, head, blocks, top, mixed, own_ref):
    count, span = q_ref.shape[0], blocks[0].shape[0]
    factor = 1.0 / math.sqrt(HD)
    first = head * REP * HD
    low, mid, high = head * 2 * HD, head * 2 * HD + HD, head * 2 * HD + 2 * HD
    q = jnp.concatenate([q_ref[:, first + r * HD : first + (r + 1) * HD] for r in range(REP)], 0)
    picked = jnp.full((REP * count, span), NEG, jnp.float32)
    place = lax.broadcasted_iota(jnp.int32, (REP * count, span), 1)
    for owner, block in zip(owners, blocks):
        scores = lax.dot_general(
            q,
            block[:, low:mid],
            (((1,), (1,)), ((), ())),
            preferred_element_type=jnp.float32,
        )
        picked = jnp.where(source == owner, scores * factor, picked)
    picked = jnp.where(place < live, picked, NEG)
    new = jnp.maximum(jnp.max(picked, -1, keepdims=True), top)
    if own_ref is not None:
        own_k = jnp.concatenate([own_ref[:, low:mid].astype(jnp.float32)] * REP, 0)
        own_v = jnp.concatenate([own_ref[:, mid:high].astype(jnp.float32)] * REP, 0)
        score = jnp.sum(q.astype(jnp.float32) * own_k, -1, keepdims=True) * factor
        new = jnp.maximum(new, score)
    weights = jnp.exp(picked - new)
    kept = jnp.exp(top - new)
    total = kept + jnp.sum(weights, -1, keepdims=True)
    mixed = mixed * kept
    if own_ref is not None:
        weight = jnp.exp(score - new)
        total = total + weight
        mixed = mixed + weight * own_v
    for owner, block in zip(owners, blocks):
        mixed = mixed + jnp.dot(
            jnp.where(source == owner, weights, 0.0).astype(jnp.bfloat16),
            block[:, mid:high],
            preferred_element_type=jnp.float32,
        )
    return new + jnp.log(total), mixed / total


def cache_kernel(heads, len_ref, q_ref, cache_ref, top_ref, mixed_ref):
    count, rows = q_ref.shape[0], heads * REP
    factor = 1.0 / math.sqrt(HD)
    query = [q_ref[:, r * HD : (r + 1) * HD].astype(jnp.float32) for r in range(rows)]
    query = jnp.swapaxes(jnp.stack(query), 0, 1).astype(jnp.bfloat16)
    head_of = lax.broadcasted_iota(jnp.int32, (rows, 1), 0) // REP
    spot = lax.broadcasted_iota(jnp.int32, (rows, cache_ref.shape[1]), 1)
    tops, mixes = [], []
    for sample in range(count):
        length = len_ref[pl.program_id(0) * count + sample]
        scores = mixed = None
        for head in range(heads):
            key = cache_ref[sample, :, head * 2 * HD : head * 2 * HD + HD]
            found = lax.dot_general(
                query[sample], key, (((1,), (1,)), ((), ())), preferred_element_type=jnp.float32
            )
            scores = found if head == 0 else jnp.where(head_of == head, found, scores)
        scores = jnp.where(spot < length, scores * factor, NEG)
        top = jnp.max(scores, -1, keepdims=True)
        weights = jnp.exp(scores - top)
        total = jnp.sum(weights, -1, keepdims=True)
        for head in range(heads):
            value = cache_ref[sample, :, head * 2 * HD + HD : (head + 1) * 2 * HD]
            found = jnp.dot(
                weights.astype(jnp.bfloat16), value, preferred_element_type=jnp.float32
            )
            mixed = found if head == 0 else jnp.where(head_of == head, found, mixed)
        tops.append(jnp.broadcast_to(top + jnp.log(total), (rows, HD)))
        mixes.append(mixed / total)
    top_ref[...] = jnp.swapaxes(jnp.stack(tops), 0, 1)
    mixed_ref[...] = jnp.swapaxes(jnp.stack(mixes), 0, 1)


def cached(query, cache, cache_len, heads):
    count, slots, width = cache.shape
    rows, each = heads * REP, 8
    state = jax.ShapeDtypeStruct((rows, count, HD), jnp.float32)
    return pl.pallas_call(
        functools.partial(cache_kernel, heads),
        grid=(count // each,),
        out_shape=[state, state],
        in_specs=[
            SMEM,
            pl.BlockSpec((each, rows * HD), lambda i: (i, 0)),
            pl.BlockSpec((each, slots, width), lambda i: (i, 0, 0)),
        ],
        out_specs=[pl.BlockSpec((rows, each, HD), lambda i: (0, i, 0))] * 2,
        compiler_params=grant(12),
        cost_estimate=pl.CostEstimate(
            flops=4 * count * rows * slots * HD * heads,
            bytes_accessed=2 * cache.size,
            transcendentals=count * rows * slots,
        ),
    )(cache_len, query, cache)


def first_kernel(
    heads, teams, owners, owner_ref, len_ref, samples_ref, q_ref, top_ref, mixed_ref, *refs
):
    per = len(owners())
    own, bands, refs = refs[:teams], refs[teams : teams * (1 + per)], refs[teams * (1 + per) :]
    new_top, new_mixed, source_ref, live_ref, prompt_ref, own_ref, *blocks = refs
    join_bands(teams, own, [own_ref])
    join_bands(teams, bands, blocks)
    prompt_ref[...] = blocks[0][...]
    source, live = match_rows(owner_ref, len_ref, samples_ref, q_ref.shape[0])
    source = jnp.concatenate([source] * REP, 0)
    live = jnp.concatenate([live] * REP, 0)
    source_ref[...] = jnp.broadcast_to(source, source_ref.shape)
    live_ref[...] = jnp.broadcast_to(live, live_ref.shape)
    for head in range(heads):
        mine = slice(head * REP, (head + 1) * REP)
        top = top_ref[mine].reshape(new_top.shape[1:])
        mixed = mixed_ref[mine].reshape(new_top.shape[1:])
        new_top[head], new_mixed[head] = absorb(
            owners(), q_ref, source, live, head, blocks, top, mixed, own_ref
        )


def second_kernel(heads, teams, owners, q_ref, source_ref, live_ref, top_ref, mixed_ref, *refs):
    per = len(owners())
    bands, out_ref, blocks = refs[: teams * per], refs[teams * per], refs[teams * per + 1 :]
    join_bands(teams, bands, blocks)
    count = q_ref.shape[0]
    for head in range(heads):
        _, mixed = absorb(
            owners(),
            q_ref,
            source_ref[...],
            live_ref[...],
            head,
            blocks,
            top_ref[head],
            mixed_ref[head],
            None,
        )
        first = head * REP * HD
        for r in range(REP):
            out_ref[:, first + r * HD : first + (r + 1) * HD] = mixed[
                r * count : (r + 1) * count
            ].astype(out_ref.dtype)


VMEM = pl.BlockSpec(memory_space=pltpu.VMEM)
SMEM = pl.BlockSpec(memory_space=pltpu.SMEM)
HBM = pl.BlockSpec(memory_space=pltpu.HBM)


def after(value, *others):
    return lax.optimization_barrier((value, *others))[0]


def grant(mib):
    return pltpu.CompilerParams(vmem_limit_bytes=mib * 1024 * 1024)


def stages(depth):
    unit = 128
    first = max(unit, depth * 7 // 12 // unit * unit)
    return (first, depth - first)


def local(
    pre_x,
    dec_x,
    w_kv,
    kv_scale,
    dec_q,
    cache,
    cache_len,
    prompt_owner,
    prompt_len,
    sample_rows,
    *,
    shape,
):
    teams, ranks, cores = shape["groups"], shape["dp"], shape["tp"]
    inner = INNER
    outer = ranks // inner
    span, features = pre_x.shape
    count = dec_x.shape[0]
    depth, width = w_kv.shape
    heads = width // (2 * HD)
    band = width // teams

    def to_inner(value, step):
        pairs = [(r, r // inner * inner + (r % inner ^ step)) for r in range(ranks)]
        return lax.ppermute(value, "dp", pairs)

    def to_outer(value, step=1):
        pairs = [(r, (r + step * inner) % ranks) for r in range(ranks)]
        return lax.ppermute(value, "dp", pairs)

    def to_team(value, step):
        return lax.ppermute(value, "groups", [(i, (i + step) % teams) for i in range(teams)])

    def to_core(value, step):
        return lax.ppermute(value, "tp", [(i, (i + step) % cores) for i in range(cores)])

    def pack(plan, places, shapes, mib, *arrays):
        sems = pltpu.SemaphoreType.DMA((len(plan),))
        return pl.pallas_call(
            functools.partial(pack_kernel, plan, places, len(arrays), len(shapes)),
            out_shape=shapes,
            in_specs=[HBM] * len(arrays),
            out_specs=[HBM] * len(shapes),
            scratch_shapes=[pltpu.VMEM(s.shape, s.dtype) for s in shapes] + [sems, sems],
            compiler_params=grant(mib),
        )(*arrays)

    sizes = stages(depth)
    pre_share, dec_share = span // cores, count // cores
    both = pre_share + dec_share
    def features(back, step):
        rank = lax.axis_index("dp")
        return ((rank // inner - back + outer) % outer * inner + (rank % inner ^ step)) * depth

    def band_place():
        return [0, lax.axis_index("groups") * band]

    shape = jax.ShapeDtypeStruct((sizes[0], band), jnp.bfloat16)
    (first_piece,) = pack([(0, (sizes[0], band), 0, 1, 0, 0, 0)], band_place, [shape], 56, w_kv)
    first_piece, pre_x, dec_x, w_kv = lax.optimization_barrier((first_piece, pre_x, dec_x, w_kv))

    plan = [(2, (sizes[1], band), 0, 1, 0, 0, 0)]
    shapes = [jax.ShapeDtypeStruct((sizes[1], band), jnp.bfloat16)]
    for number in range(inner - 1):
        for back in range(outer):
            column, to = 4 + number * outer + back, back * depth
            plan.append((0, (pre_share, depth), 2, column, len(shapes), 0, to))
            plan.append((1, (dec_share, depth), 3, column, len(shapes), pre_share, to))
        shapes.append(jax.ShapeDtypeStruct((both, outer * depth), jnp.bfloat16))

    def send_places():
        core = lax.axis_index("tp")
        at = [sizes[0], lax.axis_index("groups") * band, core * pre_share, core * dec_share]
        return at + [features(back, step) for step in STEPS for back in range(outer)]

    last_piece, *row_sends = pack(plan, send_places, shapes, 56, pre_x, dec_x, w_kv)
    moving = [first_piece, last_piece]
    row_sends, query, pre_x, dec_x = lax.optimization_barrier((row_sends, dec_q, pre_x, dec_x))

    plan = []
    for back in range(outer):
        for turn in range(cores):
            column, to, base = 2 * cores + back, back * depth, turn * both
            plan.append((0, (pre_share, depth), 2 * turn, column, 0, base, to))
            plan.append((1, (dec_share, depth), 2 * turn + 1, column, 0, base + pre_share, to))

    def own_places():
        core, at = lax.axis_index("tp"), []
        for turn in range(cores):
            which = (core - turn + cores) % cores
            at += [which * pre_share, which * dec_share]
        return at + [features(back, 0) for back in range(outer)]

    total_rows = span + count
    shapes = [jax.ShapeDtypeStruct((total_rows, outer * depth), jnp.bfloat16)]
    (own_rows,) = pack(plan, own_places, shapes, 4, pre_x, dec_x)

    top_c, mixed_c = cached(query, cache, cache_len, heads)
    far = []
    for back in range(1, outer):
        moving = [to_outer(m) for m in moving]
        if back == 1:
            row_sends[-1] = after(row_sends[-1], moving[0], top_c, own_rows)
        far.append([[m] for m in moving])

    got = [to_inner(rows, step) for rows, step in zip(row_sends, STEPS)]
    arrived = [[rows] + [to_core(rows, turn) for turn in range(1, cores)] for rows in got]

    for pieces in far:
        for number, piece in enumerate(pieces):
            if number:
                sent = after(piece[0], pieces[number - 1][-1])
            else:
                sent = piece[0]
            piece += [to_team(sent, turn) for turn in range(1, teams)]

    last = sizes[-1]
    own_rows = after(own_rows, got[-1])
    blocks = [own_rows] + [rows for step in arrived[:-1] for rows in step]
    early = [m for pieces in far for m in pieces[0]]
    first_rows = (inner - 1) * total_rows
    *summed, last_rows = pl.pallas_call(
        functools.partial(early_kernel, outer, teams, last),
        out_shape=[
            *[jax.ShapeDtypeStruct((first_rows, band), jnp.float32)] * teams,
            jax.ShapeDtypeStruct((first_rows, (outer - 1) * last), jnp.bfloat16),
        ],
        in_specs=[VMEM] * (1 + len(early) + len(blocks)),
        out_specs=[VMEM] * (1 + teams),
        scratch_shapes=[
            pltpu.VMEM((first_rows, outer * depth - (outer - 1) * last), jnp.bfloat16)
        ],
        compiler_params=grant(16),
    )(w_kv, *early, *blocks)
    parts = []
    for turn in range(teams):
        pieces = [piece[turn] for some in far for piece in some]
        mine, *others = pl.pallas_call(
            functools.partial(late_kernel, outer, cores, teams, turn),
            out_shape=[jax.ShapeDtypeStruct((total_rows, band), jnp.float32)]
            + [jax.ShapeDtypeStruct((total_rows, band), jnp.bfloat16)] * (inner - 1),
            in_specs=[VMEM] * (3 + len(pieces) + cores),
            out_specs=[VMEM] * inner,
            scratch_shapes=[pltpu.VMEM((total_rows, outer * depth), jnp.bfloat16)],
            compiler_params=grant(12),
        )(w_kv, summed[turn], last_rows, *pieces, *arrived[-1])
        parts += [mine] + [to_inner(part, step) for part, step in zip(others, STEPS)]
    near_bands, far_bands, own_bands = [], [], []
    for turn in range(teams):
        some = parts[turn * inner : (turn + 1) * inner]
        if turn:
            some[0] = after(some[0], *near_bands[-1][1:3])
        shifted, own = pl.pallas_call(
            functools.partial(finish_kernel, cores, teams, turn),
            out_shape=[
                jax.ShapeDtypeStruct((span, band), jnp.bfloat16),
                jax.ShapeDtypeStruct((count, band), jnp.bfloat16),
            ],
            in_specs=[VMEM] * (1 + inner),
            out_specs=[VMEM] * 2,
            compiler_params=grant(6),
        )(kv_scale[None, :], *some)
        own_bands.append(own)
        near = [shifted, to_inner(shifted, 1), to_inner(shifted, 2)]
        near_bands.append(near + [to_inner(near[2], 1)])
        blocks = []
        for back in range(1, outer):
            shifted = to_outer(shifted)
            blocks += [to_inner(shifted, step) if step else shifted for step in range(inner)]
        far_bands.append(blocks)

    def owners(backs):
        rank = lax.axis_index("dp")
        return [
            (rank // inner - back + outer) % outer * inner + (rank % inner ^ step)
            for back in backs
            for step in range(inner)
        ]

    state = jax.ShapeDtypeStruct((heads, REP * count, HD), jnp.float32)
    labels = jax.ShapeDtypeStruct((REP * count, HD), jnp.int32)
    block = pltpu.VMEM((span, width), jnp.bfloat16)
    *state, source, live, prompt_kv = pl.pallas_call(
        functools.partial(first_kernel, heads, teams, lambda: owners([0])),
        out_shape=[state, state, labels, labels, jax.ShapeDtypeStruct((span, width), jnp.bfloat16)],
        in_specs=[SMEM] * 2 + [VMEM] * (4 + teams * (1 + inner)),
        out_specs=[VMEM] * 5,
        scratch_shapes=[pltpu.VMEM((count, width), jnp.bfloat16)] + [block] * inner,
        compiler_params=grant(12),
    )(
        prompt_owner,
        prompt_len,
        sample_rows,
        dec_q,
        top_c,
        mixed_c,
        *own_bands,
        *[block for blocks in near_bands for block in blocks],
    )
    attended = pl.pallas_call(
        functools.partial(second_kernel, heads, teams, lambda: owners(range(1, outer))),
        out_shape=jax.ShapeDtypeStruct(dec_q.shape, jnp.bfloat16),
        in_specs=[VMEM] * (5 + teams * (outer - 1) * inner),
        out_specs=VMEM,
        scratch_shapes=[block] * ((outer - 1) * inner),
        compiler_params=grant(16),
    )(dec_q, source, live, *state, *[block for blocks in far_bands for block in blocks])
    return (attended, prompt_kv)


def solution(mesh):
    in_specs = (
        P(("groups", "dp"), None),
        P(("groups", "dp"), None),
        P("dp", "tp"),
        P("tp"),
        P(("groups", "dp"), "tp"),
        P(("groups", "dp"), None, "tp"),
        P(("groups", "dp")),
        P("groups"),
        P("groups"),
        P("groups", None),
    )
    out_specs = (P(("groups", "dp"), "tp"), P(("groups", "dp"), "tp"))
    body = functools.partial(local, shape=dict(mesh.shape))
    return jax.shard_map(body, mesh=mesh, in_specs=in_specs, out_specs=out_specs, check_vma=False)
```

```python
import functools
import math

import jax
import jax.numpy as jnp
from jax import lax
from jax.experimental import pallas as pl
from jax.experimental.pallas import tpu as pltpu
from jax.sharding import PartitionSpec as P

HD = 128
REP = 12
NEG = -1e30
INNER = 4
STEPS = (1, 2, 3)


def pack_kernel(plan, places, n_in, n_out, *refs):
    ins, outs = refs[:n_in], refs[n_in : n_in + n_out]
    held, (in_sems, out_sems) = refs[n_in + n_out : -2], refs[-2:]
    at = places()
    arriving, leaving = [], []
    for number, (src, shape, row, column, dst, to_row, to_column) in enumerate(plan):
        rows, columns = pl.ds(to_row, shape[0]), pl.ds(to_column, shape[1])
        from_row = pl.multiple_of(at[row], 16)
        from_column = pl.multiple_of(at[column], 128)
        arriving.append(
            pltpu.make_async_copy(
                ins[src].at[pl.ds(from_row, shape[0]), pl.ds(from_column, shape[1])],
                held[dst].at[rows, columns],
                in_sems.at[number],
            )
        )
        leaving.append(
            pltpu.make_async_copy(
                held[dst].at[rows, columns], outs[dst].at[rows, columns], out_sems.at[number]
            )
        )
        arriving[-1].start()
    for came, left in zip(arriving, leaving):
        came.wait()
        left.start()
    for left in leaving:
        left.wait()


def band_columns(teams, turn, band):
    team = lax.axis_index("groups")
    return pl.ds(pl.multiple_of((team - turn + teams) % teams * band, 128), band)


def early_kernel(outer, teams, last, w_ref, *refs):
    n_late = teams + 2
    pieces, refs = refs[: teams * (outer - 1)], refs[teams * (outer - 1) :]
    blocks, sum_refs, (last_ref, row_ref) = refs[:-n_late], refs[-n_late:-2], refs[-2:]
    depth = w_ref.shape[0]
    early = depth - last
    base = 0
    for block in blocks:
        rows = slice(base, base + block.shape[0])
        row_ref[rows, :depth] = block[:, :depth]
        for back in range(1, outer):
            at = depth + (back - 1) * early
            row_ref[rows, at : at + early] = block[:, back * depth : back * depth + early]
            last_ref[rows, (back - 1) * last : back * last] = block[
                :, back * depth + early : (back + 1) * depth
            ]
        base += block.shape[0]
    for turn, sum_ref in enumerate(sum_refs):
        columns = band_columns(teams, turn, sum_ref.shape[1])
        summed = jnp.dot(row_ref[:, :depth], w_ref[:, columns], preferred_element_type=jnp.float32)
        for back in range(1, outer):
            at = depth + (back - 1) * early
            summed = summed + jnp.dot(
                row_ref[:, at : at + early],
                pieces[(back - 1) * teams + turn][...],
                preferred_element_type=jnp.float32,
            )
        sum_ref[...] = summed


def late_kernel(outer, cores, teams, turn, w_ref, sum_ref, last_ref, *refs):
    pieces, refs = refs[: 2 * (outer - 1)], refs[2 * (outer - 1) :]
    halves, outs, row_ref = refs[:cores], refs[cores:-1], refs[-1]
    depth = w_ref.shape[0]
    last = last_ref.shape[1] // (outer - 1)
    each, both = outs[0].shape[0], halves[0].shape[0]
    for number, half in enumerate(halves):
        row_ref[number * both : (number + 1) * both, :] = half[...]
    columns = band_columns(teams, turn, sum_ref.shape[1])
    first = sum_ref[...]
    final = jnp.dot(row_ref[:, :depth], w_ref[:, columns], preferred_element_type=jnp.float32)
    for back in range(1, outer):
        early_piece, last_piece = pieces[2 * back - 2 : 2 * back]
        at = back * depth
        cut = at + depth - last
        final = final + jnp.dot(
            row_ref[:, at:cut], early_piece[...], preferred_element_type=jnp.float32
        )
        final = final + jnp.dot(
            row_ref[:, cut : cut + last], last_piece[...], preferred_element_type=jnp.float32
        )
        first = first + jnp.dot(
            last_ref[:, (back - 1) * last : back * last],
            last_piece[...],
            preferred_element_type=jnp.float32,
        )
    for step, out in enumerate(outs[:-1]):
        out[...] = first[step * each : (step + 1) * each].astype(out.dtype)
    outs[-1][...] = final.astype(outs[-1].dtype)


def finish_kernel(cores, teams, scale_ref, *refs):
    parts, (sent_ref, own_ref) = refs[:-2], refs[-2:]
    span, count = sent_ref.shape[0], own_ref.shape[0]
    pre_share, dec_share = span // cores, count // cores
    both = pre_share + dec_share
    band = scale_ref.shape[1] // teams
    for turn in range(teams):
        columns = band_columns(teams, turn, band)
        own, *others = parts[turn * len(parts) // teams : (turn + 1) * len(parts) // teams]
        summed = own[...]
        for part in others:
            summed = summed + part[...].astype(jnp.float32)
        done = (summed * scale_ref[:, columns]).astype(jnp.bfloat16)
        for share in range(cores):
            which = (lax.axis_index("tp") - share + cores) % cores
            rows = pl.ds(pl.multiple_of(which * pre_share, 16), pre_share)
            sent_ref[rows, columns] = done[share * both : share * both + pre_share]
            own_ref[pl.ds(pl.multiple_of(which * dec_share, 16), dec_share), columns] = done[
                share * both + pre_share : (share + 1) * both
            ]


def match_rows(owner_ref, len_ref, samples_ref, count):
    row = lax.axis_index("dp") * count + lax.broadcasted_iota(jnp.int32, (count, 1), 0)
    source = jnp.zeros((count, 1), jnp.int32)
    live = jnp.zeros((count, 1), jnp.int32)
    for prompt in range(samples_ref.shape[0]):
        hit = jnp.max(
            jnp.where(samples_ref[prompt : prompt + 1, :] == row, 1, 0), -1, keepdims=True
        )
        source = source + hit * owner_ref[prompt]
        live = live + hit * len_ref[prompt]
    return source, live


def absorb(owners, q_ref, source, live, head, blocks, top, mixed, own_ref):
    count, span = q_ref.shape[0], blocks[0].shape[0]
    factor = 1.0 / math.sqrt(HD)
    first = head * REP * HD
    low, mid, high = head * 2 * HD, head * 2 * HD + HD, head * 2 * HD + 2 * HD
    q = jnp.concatenate([q_ref[:, first + r * HD : first + (r + 1) * HD] for r in range(REP)], 0)
    picked = jnp.full((REP * count, span), NEG, jnp.float32)
    place = lax.broadcasted_iota(jnp.int32, (REP * count, span), 1)
    pairs = [slice(at, at + 2) for at in range(0, len(blocks), 2)]
    for pair in pairs:
        scores = lax.dot_general(
            q,
            jnp.concatenate([block[:, low:mid] for block in blocks[pair]], 0),
            (((1,), (1,)), ((), ())),
            preferred_element_type=jnp.float32,
        )
        for at, owner in enumerate(owners[pair]):
            mine = scores[:, at * span : (at + 1) * span]
            picked = jnp.where(source == owner, mine * factor, picked)
    picked = jnp.where(place < live, picked, NEG)
    new = jnp.maximum(jnp.max(picked, -1, keepdims=True), top)
    if own_ref is not None:
        own_k = jnp.concatenate([own_ref[:, low:mid].astype(jnp.float32)] * REP, 0)
        own_v = jnp.concatenate([own_ref[:, mid:high].astype(jnp.float32)] * REP, 0)
        score = jnp.sum(q.astype(jnp.float32) * own_k, -1, keepdims=True) * factor
        new = jnp.maximum(new, score)
    weights = jnp.exp(picked - new)
    kept = jnp.exp(top - new)
    total = kept + jnp.sum(weights, -1, keepdims=True)
    mixed = mixed * kept
    if own_ref is not None:
        weight = jnp.exp(score - new)
        total = total + weight
        mixed = mixed + weight * own_v
    for pair in pairs:
        shares = [jnp.where(source == owner, weights, 0.0) for owner in owners[pair]]
        mixed = mixed + jnp.dot(
            jnp.concatenate(shares, 1).astype(jnp.bfloat16),
            jnp.concatenate([block[:, mid:high] for block in blocks[pair]], 0),
            preferred_element_type=jnp.float32,
        )
    return new + jnp.log(total), mixed / total


def cache_kernel(heads, len_ref, q_ref, cache_ref, top_ref, mixed_ref):
    count, rows = q_ref.shape[0], heads * REP
    factor = 1.0 / math.sqrt(HD)
    query = [q_ref[:, r * HD : (r + 1) * HD].astype(jnp.float32) for r in range(rows)]
    query = jnp.swapaxes(jnp.stack(query), 0, 1).astype(jnp.bfloat16)
    head_of = lax.broadcasted_iota(jnp.int32, (rows, 1), 0) // REP
    spot = lax.broadcasted_iota(jnp.int32, (rows, cache_ref.shape[1]), 1)
    tops, mixes = [], []
    for sample in range(count):
        length = len_ref[pl.program_id(0) * count + sample]
        scores = mixed = None
        for head in range(heads):
            key = cache_ref[sample, :, head * 2 * HD : head * 2 * HD + HD]
            found = lax.dot_general(
                query[sample], key, (((1,), (1,)), ((), ())), preferred_element_type=jnp.float32
            )
            scores = found if head == 0 else jnp.where(head_of == head, found, scores)
        scores = jnp.where(spot < length, scores * factor, NEG)
        top = jnp.max(scores, -1, keepdims=True)
        weights = jnp.exp(scores - top)
        total = jnp.sum(weights, -1, keepdims=True)
        for head in range(heads):
            value = cache_ref[sample, :, head * 2 * HD + HD : (head + 1) * 2 * HD]
            found = jnp.dot(
                weights.astype(jnp.bfloat16), value, preferred_element_type=jnp.float32
            )
            mixed = found if head == 0 else jnp.where(head_of == head, found, mixed)
        tops.append(jnp.broadcast_to(top + jnp.log(total), (rows, HD)))
        mixes.append(mixed / total)
    top_ref[...] = jnp.swapaxes(jnp.stack(tops), 0, 1)
    mixed_ref[...] = jnp.swapaxes(jnp.stack(mixes), 0, 1)


def cached(query, cache, cache_len, heads):
    count, slots, width = cache.shape
    rows, each = heads * REP, 8
    state = jax.ShapeDtypeStruct((rows, count, HD), jnp.float32)
    return pl.pallas_call(
        functools.partial(cache_kernel, heads),
        grid=(count // each,),
        out_shape=[state, state],
        in_specs=[
            SMEM,
            pl.BlockSpec((each, rows * HD), lambda i: (i, 0)),
            pl.BlockSpec((each, slots, width), lambda i: (i, 0, 0)),
        ],
        out_specs=[pl.BlockSpec((rows, each, HD), lambda i: (0, i, 0))] * 2,
        compiler_params=grant(12),
        cost_estimate=pl.CostEstimate(
            flops=4 * count * rows * slots * HD * heads,
            bytes_accessed=2 * cache.size,
            transcendentals=count * rows * slots,
        ),
    )(cache_len, query, cache)


def first_kernel(
    heads, owners, owner_ref, len_ref, samples_ref, q_ref, top_ref, mixed_ref, own_ref, *refs
):
    blocks, (new_top, new_mixed, source_ref, live_ref, prompt_ref) = refs[:-5], refs[-5:]
    prompt_ref[...] = blocks[0][...]
    source, live = match_rows(owner_ref, len_ref, samples_ref, q_ref.shape[0])
    source = jnp.concatenate([source] * REP, 0)
    live = jnp.concatenate([live] * REP, 0)
    source_ref[...] = jnp.broadcast_to(source, source_ref.shape)
    live_ref[...] = jnp.broadcast_to(live, live_ref.shape)
    for head in range(heads):
        mine = slice(head * REP, (head + 1) * REP)
        top = top_ref[mine].reshape(new_top.shape[1:])
        mixed = mixed_ref[mine].reshape(new_top.shape[1:])
        new_top[head], new_mixed[head] = absorb(
            owners(), q_ref, source, live, head, blocks, top, mixed, own_ref
        )


def second_kernel(heads, owners, q_ref, source_ref, live_ref, top_ref, mixed_ref, *refs):
    blocks, out_ref = refs[:-1], refs[-1]
    count = q_ref.shape[0]
    for head in range(heads):
        _, mixed = absorb(
            owners(),
            q_ref,
            source_ref[...],
            live_ref[...],
            head,
            blocks,
            top_ref[head],
            mixed_ref[head],
            None,
        )
        first = head * REP * HD
        for r in range(REP):
            out_ref[:, first + r * HD : first + (r + 1) * HD] = mixed[
                r * count : (r + 1) * count
            ].astype(out_ref.dtype)


VMEM = pl.BlockSpec(memory_space=pltpu.VMEM)
SMEM = pl.BlockSpec(memory_space=pltpu.SMEM)
HBM = pl.BlockSpec(memory_space=pltpu.HBM)


def after(value, *others):
    return lax.optimization_barrier((value, *others))[0]


def grant(mib):
    return pltpu.CompilerParams(vmem_limit_bytes=mib * 1024 * 1024)


def stages(depth):
    unit = 128
    first = max(unit, depth * 7 // 12 // unit * unit)
    return (first, depth - first)


def local(
    pre_x,
    dec_x,
    w_kv,
    kv_scale,
    dec_q,
    cache,
    cache_len,
    prompt_owner,
    prompt_len,
    sample_rows,
    *,
    shape,
):
    teams, ranks, cores = shape["groups"], shape["dp"], shape["tp"]
    inner = INNER
    outer = ranks // inner
    span, features = pre_x.shape
    count = dec_x.shape[0]
    depth, width = w_kv.shape
    heads = width // (2 * HD)
    band = width // teams

    def to_inner(value, step):
        pairs = [(r, r // inner * inner + (r % inner ^ step)) for r in range(ranks)]
        return lax.ppermute(value, "dp", pairs)

    def to_outer(value, step=1):
        pairs = [(r, (r + step * inner) % ranks) for r in range(ranks)]
        return lax.ppermute(value, "dp", pairs)

    def to_team(value, step):
        return lax.ppermute(value, "groups", [(i, (i + step) % teams) for i in range(teams)])

    def to_core(value, step):
        return lax.ppermute(value, "tp", [(i, (i + step) % cores) for i in range(cores)])

    def pack(plan, places, shapes, mib, *arrays):
        sems = pltpu.SemaphoreType.DMA((len(plan),))
        return pl.pallas_call(
            functools.partial(pack_kernel, plan, places, len(arrays), len(shapes)),
            out_shape=shapes,
            in_specs=[HBM] * len(arrays),
            out_specs=[HBM] * len(shapes),
            scratch_shapes=[pltpu.VMEM(s.shape, s.dtype) for s in shapes] + [sems, sems],
            compiler_params=grant(mib),
        )(*arrays)

    sizes = stages(depth)
    pre_share, dec_share = span // cores, count // cores
    both = pre_share + dec_share
    def features(back, step):
        rank = lax.axis_index("dp")
        return ((rank // inner - back + outer) % outer * inner + (rank % inner ^ step)) * depth

    def band_place():
        return [0, lax.axis_index("groups") * band]

    shape = jax.ShapeDtypeStruct((sizes[0], band), jnp.bfloat16)
    (first_piece,) = pack([(0, (sizes[0], band), 0, 1, 0, 0, 0)], band_place, [shape], 56, w_kv)
    first_piece, pre_x, dec_x, w_kv = lax.optimization_barrier((first_piece, pre_x, dec_x, w_kv))

    plan = [(2, (sizes[1], band), 0, 1, 0, 0, 0)]
    shapes = [jax.ShapeDtypeStruct((sizes[1], band), jnp.bfloat16)]
    for number in range(inner - 1):
        for back in range(outer):
            column, to = 4 + number * outer + back, back * depth
            plan.append((0, (pre_share, depth), 2, column, len(shapes), 0, to))
            plan.append((1, (dec_share, depth), 3, column, len(shapes), pre_share, to))
        shapes.append(jax.ShapeDtypeStruct((both, outer * depth), jnp.bfloat16))

    def send_places():
        core = lax.axis_index("tp")
        at = [sizes[0], lax.axis_index("groups") * band, core * pre_share, core * dec_share]
        return at + [features(back, step) for step in STEPS for back in range(outer)]

    last_piece, *row_sends = pack(plan, send_places, shapes, 56, pre_x, dec_x, w_kv)
    moving = [first_piece, last_piece]
    row_sends, query, pre_x, dec_x = lax.optimization_barrier((row_sends, dec_q, pre_x, dec_x))

    plan = []
    for back in range(outer):
        for turn in range(cores):
            column, to, base = 2 * cores + back, back * depth, turn * both
            plan.append((0, (pre_share, depth), 2 * turn, column, 0, base, to))
            plan.append((1, (dec_share, depth), 2 * turn + 1, column, 0, base + pre_share, to))

    def own_places():
        core, at = lax.axis_index("tp"), []
        for turn in range(cores):
            which = (core - turn + cores) % cores
            at += [which * pre_share, which * dec_share]
        return at + [features(back, 0) for back in range(outer)]

    total_rows = span + count
    shapes = [jax.ShapeDtypeStruct((total_rows, outer * depth), jnp.bfloat16)]
    (own_rows,) = pack(plan, own_places, shapes, 4, pre_x, dec_x)

    top_c, mixed_c = cached(query, cache, cache_len, heads)
    far = []
    for back in range(1, outer):
        moving = [to_outer(m) for m in moving]
        if back == 1:
            row_sends[-1] = after(row_sends[-1], moving[0], top_c, own_rows)
        far.append([[m] for m in moving])

    got = [to_inner(rows, step) for rows, step in zip(row_sends, STEPS)]
    arrived = [[rows] + [to_core(rows, turn) for turn in range(1, cores)] for rows in got]

    for pieces in far:
        for number, piece in enumerate(pieces):
            if number:
                sent = after(piece[0], pieces[number - 1][-1])
            else:
                sent = piece[0]
            piece += [to_team(sent, turn) for turn in range(1, teams)]

    last = sizes[-1]
    own_rows = after(own_rows, got[-1])
    blocks = [own_rows] + [rows for step in arrived[:-1] for rows in step]
    early = [m for pieces in far for m in pieces[0]]
    first_rows = (inner - 1) * total_rows
    *summed, last_rows = pl.pallas_call(
        functools.partial(early_kernel, outer, teams, last),
        out_shape=[
            *[jax.ShapeDtypeStruct((first_rows, band), jnp.float32)] * teams,
            jax.ShapeDtypeStruct((first_rows, (outer - 1) * last), jnp.bfloat16),
        ],
        in_specs=[VMEM] * (1 + len(early) + len(blocks)),
        out_specs=[VMEM] * (1 + teams),
        scratch_shapes=[
            pltpu.VMEM((first_rows, outer * depth - (outer - 1) * last), jnp.bfloat16)
        ],
        compiler_params=grant(16),
    )(w_kv, *early, *blocks)
    parts = []
    for turn in range(teams):
        pieces = [piece[turn] for some in far for piece in some]
        mine, *others = pl.pallas_call(
            functools.partial(late_kernel, outer, cores, teams, turn),
            out_shape=[jax.ShapeDtypeStruct((total_rows, band), jnp.float32)]
            + [jax.ShapeDtypeStruct((total_rows, band), jnp.bfloat16)] * (inner - 1),
            in_specs=[VMEM] * (3 + len(pieces) + cores),
            out_specs=[VMEM] * inner,
            scratch_shapes=[pltpu.VMEM((total_rows, outer * depth), jnp.bfloat16)],
            compiler_params=grant(12),
        )(w_kv, summed[turn], last_rows, *pieces, *arrived[-1])
        sent = [to_inner(part, step) for part, step in zip(others[::-1], STEPS[::-1])]
        parts += [mine, *sent]
    shifted, own_kv = pl.pallas_call(
        functools.partial(finish_kernel, cores, teams),
        out_shape=[
            jax.ShapeDtypeStruct((span, width), jnp.bfloat16),
            jax.ShapeDtypeStruct((count, width), jnp.bfloat16),
        ],
        in_specs=[VMEM] * (1 + len(parts)),
        out_specs=[VMEM] * 2,
        compiler_params=grant(6),
    )(kv_scale[None, :], *parts)

    def owners(backs):
        rank = lax.axis_index("dp")
        return [
            (rank // inner - back + outer) % outer * inner + (rank % inner ^ step)
            for back in backs
            for step in ((0, 3, 2, 1) if back else range(inner))
        ]

    blocks = []
    for back in range(outer):
        if back:
            shifted = to_outer(shifted)
        if back:
            blocks += [to_inner(shifted, step) if step else shifted for step in (0, 3, 2, 1)]
        else:
            near = [shifted, to_inner(shifted, 1), to_inner(shifted, 2)]
            blocks += near + [to_inner(near[2], 1)]

    state = jax.ShapeDtypeStruct((heads, REP * count, HD), jnp.float32)
    labels = jax.ShapeDtypeStruct((REP * count, HD), jnp.int32)
    *state, source, live, prompt_kv = pl.pallas_call(
        functools.partial(first_kernel, heads, lambda: owners([0])),
        out_shape=[state, state, labels, labels, jax.ShapeDtypeStruct((span, width), jnp.bfloat16)],
        in_specs=[SMEM] * 2 + [VMEM] * (5 + inner),
        out_specs=[VMEM] * 5,
        compiler_params=grant(12),
    )(
        prompt_owner,
        prompt_len,
        sample_rows,
        dec_q,
        top_c,
        mixed_c,
        own_kv,
        *blocks[:inner],
    )
    attended = pl.pallas_call(
        functools.partial(second_kernel, heads, lambda: owners(range(1, outer))),
        out_shape=jax.ShapeDtypeStruct(dec_q.shape, jnp.bfloat16),
        in_specs=[VMEM] * (5 + len(blocks) - inner),
        out_specs=VMEM,
        compiler_params=grant(12),
    )(dec_q, source, live, *state, *blocks[inner:])
    return (attended, prompt_kv)


def solution(mesh):
    in_specs = (
        P(("groups", "dp"), None),
        P(("groups", "dp"), None),
        P("dp", "tp"),
        P("tp"),
        P(("groups", "dp"), "tp"),
        P(("groups", "dp"), None, "tp"),
        P(("groups", "dp")),
        P("groups"),
        P("groups"),
        P("groups", None),
    )
    out_specs = (P(("groups", "dp"), "tp"), P(("groups", "dp"), "tp"))
    body = functools.partial(local, shape=dict(mesh.shape))
    return jax.shard_map(body, mesh=mesh, in_specs=in_specs, out_specs=out_specs, check_vma=False)
```

```python
import functools
import math

import jax
import jax.numpy as jnp
from jax import lax
from jax.experimental import pallas as pl
from jax.experimental.pallas import tpu as pltpu
from jax.sharding import PartitionSpec as P

HD = 128
REP = 12
NEG = -1e30
INNER = 4
STEPS = (1, 2, 3)


def pack_kernel(plan, places, n_in, n_out, *refs):
    ins, outs = refs[:n_in], refs[n_in : n_in + n_out]
    held, (in_sems, out_sems) = refs[n_in + n_out : -2], refs[-2:]
    at = places()
    arriving, leaving = [], []
    for number, (src, shape, row, column, dst, to_row, to_column) in enumerate(plan):
        rows, columns = pl.ds(to_row, shape[0]), pl.ds(to_column, shape[1])
        from_row = pl.multiple_of(at[row], 16)
        from_column = pl.multiple_of(at[column], 128)
        arriving.append(
            pltpu.make_async_copy(
                ins[src].at[pl.ds(from_row, shape[0]), pl.ds(from_column, shape[1])],
                held[dst].at[rows, columns],
                in_sems.at[number],
            )
        )
        leaving.append(
            pltpu.make_async_copy(
                held[dst].at[rows, columns], outs[dst].at[rows, columns], out_sems.at[number]
            )
        )
        arriving[-1].start()
    for came, left in zip(arriving, leaving):
        came.wait()
        left.start()
    for left in leaving:
        left.wait()


def band_columns(teams, turn, band):
    team = lax.axis_index("groups")
    return pl.ds(pl.multiple_of((team - turn + teams) % teams * band, 128), band)


def early_kernel(outer, teams, last, w_ref, *refs):
    n_late = teams + 2
    pieces, refs = refs[: teams * (outer - 1)], refs[teams * (outer - 1) :]
    blocks, sum_refs, (last_ref, row_ref) = refs[:-n_late], refs[-n_late:-2], refs[-2:]
    depth = w_ref.shape[0]
    early = depth - last
    base = 0
    for block in blocks:
        rows = slice(base, base + block.shape[0])
        row_ref[rows, :depth] = block[:, :depth]
        for back in range(1, outer):
            at = depth + (back - 1) * early
            row_ref[rows, at : at + early] = block[:, back * depth : back * depth + early]
            last_ref[rows, (back - 1) * last : back * last] = block[
                :, back * depth + early : (back + 1) * depth
            ]
        base += block.shape[0]
    for turn, sum_ref in enumerate(sum_refs):
        columns = band_columns(teams, turn, sum_ref.shape[1])
        summed = jnp.dot(row_ref[:, :depth], w_ref[:, columns], preferred_element_type=jnp.float32)
        for back in range(1, outer):
            at = depth + (back - 1) * early
            summed = summed + jnp.dot(
                row_ref[:, at : at + early],
                pieces[(back - 1) * teams + turn][...],
                preferred_element_type=jnp.float32,
            )
        sum_ref[...] = summed


def late_kernel(outer, cores, teams, turn, w_ref, sum_ref, last_ref, *refs):
    pieces, refs = refs[: 2 * (outer - 1)], refs[2 * (outer - 1) :]
    halves, outs, row_ref = refs[:cores], refs[cores:-1], refs[-1]
    depth = w_ref.shape[0]
    last = last_ref.shape[1] // (outer - 1)
    each, both = outs[0].shape[0], halves[0].shape[0]
    for number, half in enumerate(halves):
        row_ref[number * both : (number + 1) * both, :] = half[...]
    columns = band_columns(teams, turn, sum_ref.shape[1])
    first = sum_ref[...]
    final = jnp.dot(row_ref[:, :depth], w_ref[:, columns], preferred_element_type=jnp.float32)
    for back in range(1, outer):
        early_piece, last_piece = pieces[2 * back - 2 : 2 * back]
        at = back * depth
        cut = at + depth - last
        final = final + jnp.dot(
            row_ref[:, at:cut], early_piece[...], preferred_element_type=jnp.float32
        )
        final = final + jnp.dot(
            row_ref[:, cut : cut + last], last_piece[...], preferred_element_type=jnp.float32
        )
        first = first + jnp.dot(
            last_ref[:, (back - 1) * last : back * last],
            last_piece[...],
            preferred_element_type=jnp.float32,
        )
    for step, out in enumerate(outs[:-1]):
        out[...] = first[step * each : (step + 1) * each].astype(out.dtype)
    outs[-1][...] = final.astype(outs[-1].dtype)


def finish_kernel(cores, teams, scale_ref, *refs):
    parts, (sent_ref, own_ref) = refs[:-2], refs[-2:]
    span, count = sent_ref.shape[0], own_ref.shape[0]
    pre_share, dec_share = span // cores, count // cores
    both = pre_share + dec_share
    band = scale_ref.shape[1] // teams
    for turn in range(teams):
        columns = band_columns(teams, turn, band)
        own, *others = parts[turn * len(parts) // teams : (turn + 1) * len(parts) // teams]
        summed = own[...]
        for part in others:
            summed = summed + part[...].astype(jnp.float32)
        done = (summed * scale_ref[:, columns]).astype(jnp.bfloat16)
        for share in range(cores):
            which = (lax.axis_index("tp") - share + cores) % cores
            rows = pl.ds(pl.multiple_of(which * pre_share, 16), pre_share)
            sent_ref[rows, columns] = done[share * both : share * both + pre_share]
            own_ref[pl.ds(pl.multiple_of(which * dec_share, 16), dec_share), columns] = done[
                share * both + pre_share : (share + 1) * both
            ]


def match_rows(owner_ref, len_ref, samples_ref, count):
    row = lax.axis_index("dp") * count + lax.broadcasted_iota(jnp.int32, (count, 1), 0)
    source = jnp.zeros((count, 1), jnp.int32)
    live = jnp.zeros((count, 1), jnp.int32)
    for prompt in range(samples_ref.shape[0]):
        hit = jnp.max(
            jnp.where(samples_ref[prompt : prompt + 1, :] == row, 1, 0), -1, keepdims=True
        )
        source = source + hit * owner_ref[prompt]
        live = live + hit * len_ref[prompt]
    return source, live


def absorb(owners, q_ref, source, live, head, blocks, top, mixed, own_ref):
    count, span = q_ref.shape[0], blocks[0].shape[0]
    factor = 1.0 / math.sqrt(HD)
    first = head * REP * HD
    low, mid, high = head * 2 * HD, head * 2 * HD + HD, head * 2 * HD + 2 * HD
    q = jnp.concatenate([q_ref[:, first + r * HD : first + (r + 1) * HD] for r in range(REP)], 0)
    picked = jnp.full((REP * count, span), NEG, jnp.float32)
    place = lax.broadcasted_iota(jnp.int32, (REP * count, span), 1)
    pairs = [slice(at, at + 2) for at in range(0, len(blocks), 2)]
    for pair in pairs:
        scores = lax.dot_general(
            q,
            jnp.concatenate([block[:, low:mid] for block in blocks[pair]], 0),
            (((1,), (1,)), ((), ())),
            preferred_element_type=jnp.float32,
        )
        for at, owner in enumerate(owners[pair]):
            mine = scores[:, at * span : (at + 1) * span]
            picked = jnp.where(source == owner, mine * factor, picked)
    picked = jnp.where(place < live, picked, NEG)
    new = jnp.maximum(jnp.max(picked, -1, keepdims=True), top)
    if own_ref is not None:
        own_k = jnp.concatenate([own_ref[:, low:mid].astype(jnp.float32)] * REP, 0)
        own_v = jnp.concatenate([own_ref[:, mid:high].astype(jnp.float32)] * REP, 0)
        score = jnp.sum(q.astype(jnp.float32) * own_k, -1, keepdims=True) * factor
        new = jnp.maximum(new, score)
    weights = jnp.exp(picked - new)
    kept = jnp.exp(top - new)
    total = kept + jnp.sum(weights, -1, keepdims=True)
    mixed = mixed * kept
    if own_ref is not None:
        weight = jnp.exp(score - new)
        total = total + weight
        mixed = mixed + weight * own_v
    for pair in pairs:
        shares = [jnp.where(source == owner, weights, 0.0) for owner in owners[pair]]
        mixed = mixed + jnp.dot(
            jnp.concatenate(shares, 1).astype(jnp.bfloat16),
            jnp.concatenate([block[:, mid:high] for block in blocks[pair]], 0),
            preferred_element_type=jnp.float32,
        )
    return new + jnp.log(total), mixed / total


def cache_kernel(heads, len_ref, q_ref, cache_ref, top_ref, mixed_ref):
    count, rows = q_ref.shape[0], heads * REP
    factor = 1.0 / math.sqrt(HD)
    query = [q_ref[:, r * HD : (r + 1) * HD].astype(jnp.float32) for r in range(rows)]
    query = jnp.swapaxes(jnp.stack(query), 0, 1).astype(jnp.bfloat16)
    head_of = lax.broadcasted_iota(jnp.int32, (rows, 1), 0) // REP
    spot = lax.broadcasted_iota(jnp.int32, (rows, cache_ref.shape[1]), 1)
    tops, mixes = [], []
    for sample in range(count):
        length = len_ref[pl.program_id(0) * count + sample]
        scores = mixed = None
        for head in range(heads):
            key = cache_ref[sample, :, head * 2 * HD : head * 2 * HD + HD]
            found = lax.dot_general(
                query[sample], key, (((1,), (1,)), ((), ())), preferred_element_type=jnp.float32
            )
            scores = found if head == 0 else jnp.where(head_of == head, found, scores)
        scores = jnp.where(spot < length, scores * factor, NEG)
        top = jnp.max(scores, -1, keepdims=True)
        weights = jnp.exp(scores - top)
        total = jnp.sum(weights, -1, keepdims=True)
        for head in range(heads):
            value = cache_ref[sample, :, head * 2 * HD + HD : (head + 1) * 2 * HD]
            found = jnp.dot(
                weights.astype(jnp.bfloat16), value, preferred_element_type=jnp.float32
            )
            mixed = found if head == 0 else jnp.where(head_of == head, found, mixed)
        tops.append(jnp.broadcast_to(top + jnp.log(total), (rows, HD)))
        mixes.append(mixed / total)
    top_ref[...] = jnp.swapaxes(jnp.stack(tops), 0, 1)
    mixed_ref[...] = jnp.swapaxes(jnp.stack(mixes), 0, 1)


def cached(query, cache, cache_len, heads):
    count, slots, width = cache.shape
    rows, each = heads * REP, 8
    state = jax.ShapeDtypeStruct((rows, count, HD), jnp.float32)
    return pl.pallas_call(
        functools.partial(cache_kernel, heads),
        grid=(count // each,),
        out_shape=[state, state],
        in_specs=[
            SMEM,
            pl.BlockSpec((each, rows * HD), lambda i: (i, 0)),
            pl.BlockSpec((each, slots, width), lambda i: (i, 0, 0)),
        ],
        out_specs=[pl.BlockSpec((rows, each, HD), lambda i: (0, i, 0))] * 2,
        compiler_params=grant(12),
        cost_estimate=pl.CostEstimate(
            flops=4 * count * rows * slots * HD * heads,
            bytes_accessed=2 * cache.size,
            transcendentals=count * rows * slots,
        ),
    )(cache_len, query, cache)


def first_kernel(
    heads, owners, owner_ref, len_ref, samples_ref, q_ref, top_ref, mixed_ref, own_ref, *refs
):
    blocks, (new_top, new_mixed, source_ref, live_ref, prompt_ref) = refs[:-5], refs[-5:]
    prompt_ref[...] = blocks[0][...]
    source, live = match_rows(owner_ref, len_ref, samples_ref, q_ref.shape[0])
    source = jnp.concatenate([source] * REP, 0)
    live = jnp.concatenate([live] * REP, 0)
    source_ref[...] = jnp.broadcast_to(source, source_ref.shape)
    live_ref[...] = jnp.broadcast_to(live, live_ref.shape)
    for head in range(heads):
        mine = slice(head * REP, (head + 1) * REP)
        top = top_ref[mine].reshape(new_top.shape[1:])
        mixed = mixed_ref[mine].reshape(new_top.shape[1:])
        new_top[head], new_mixed[head] = absorb(
            owners(), q_ref, source, live, head, blocks, top, mixed, own_ref
        )


def second_kernel(heads, owners, q_ref, source_ref, live_ref, top_ref, mixed_ref, *refs):
    blocks, out_ref = refs[:-1], refs[-1]
    count = q_ref.shape[0]
    for head in range(heads):
        _, mixed = absorb(
            owners(),
            q_ref,
            source_ref[...],
            live_ref[...],
            head,
            blocks,
            top_ref[head],
            mixed_ref[head],
            None,
        )
        first = head * REP * HD
        for r in range(REP):
            out_ref[:, first + r * HD : first + (r + 1) * HD] = mixed[
                r * count : (r + 1) * count
            ].astype(out_ref.dtype)


VMEM = pl.BlockSpec(memory_space=pltpu.VMEM)
SMEM = pl.BlockSpec(memory_space=pltpu.SMEM)
HBM = pl.BlockSpec(memory_space=pltpu.HBM)


def after(value, *others):
    return lax.optimization_barrier((value, *others))[0]


def grant(mib):
    return pltpu.CompilerParams(vmem_limit_bytes=mib * 1024 * 1024)


def stages(depth):
    unit = 128
    first = max(unit, depth * 7 // 12 // unit * unit)
    return (first, depth - first)


def local(
    pre_x,
    dec_x,
    w_kv,
    kv_scale,
    dec_q,
    cache,
    cache_len,
    prompt_owner,
    prompt_len,
    sample_rows,
    *,
    shape,
):
    teams, ranks, cores = shape["groups"], shape["dp"], shape["tp"]
    inner = INNER
    outer = ranks // inner
    span, features = pre_x.shape
    count = dec_x.shape[0]
    depth, width = w_kv.shape
    heads = width // (2 * HD)
    band = width // teams

    def to_inner(value, step):
        pairs = [(r, r // inner * inner + (r % inner ^ step)) for r in range(ranks)]
        return lax.ppermute(value, "dp", pairs)

    def to_outer(value, step=1):
        pairs = [(r, (r + step * inner) % ranks) for r in range(ranks)]
        return lax.ppermute(value, "dp", pairs)

    def to_team(value, step):
        return lax.ppermute(value, "groups", [(i, (i + step) % teams) for i in range(teams)])

    def to_core(value, step):
        return lax.ppermute(value, "tp", [(i, (i + step) % cores) for i in range(cores)])

    def pack(plan, places, shapes, mib, *arrays):
        sems = pltpu.SemaphoreType.DMA((len(plan),))
        return pl.pallas_call(
            functools.partial(pack_kernel, plan, places, len(arrays), len(shapes)),
            out_shape=shapes,
            in_specs=[HBM] * len(arrays),
            out_specs=[HBM] * len(shapes),
            scratch_shapes=[pltpu.VMEM(s.shape, s.dtype) for s in shapes] + [sems, sems],
            compiler_params=grant(mib),
        )(*arrays)

    sizes = stages(depth)
    pre_share, dec_share = span // cores, count // cores
    both = pre_share + dec_share
    def features(back, step):
        rank = lax.axis_index("dp")
        return ((rank // inner - back + outer) % outer * inner + (rank % inner ^ step)) * depth

    def band_place():
        return [0, lax.axis_index("groups") * band]

    shape = jax.ShapeDtypeStruct((sizes[0], band), jnp.bfloat16)
    (first_piece,) = pack([(0, (sizes[0], band), 0, 1, 0, 0, 0)], band_place, [shape], 56, w_kv)
    first_piece, pre_x, dec_x, w_kv = lax.optimization_barrier((first_piece, pre_x, dec_x, w_kv))

    plan = [(2, (sizes[1], band), 0, 1, 0, 0, 0)]
    shapes = [jax.ShapeDtypeStruct((sizes[1], band), jnp.bfloat16)]
    for number in range(inner - 1):
        for back in range(outer):
            column, to = 4 + number * outer + back, back * depth
            plan.append((0, (pre_share, depth), 2, column, len(shapes), 0, to))
            plan.append((1, (dec_share, depth), 3, column, len(shapes), pre_share, to))
        shapes.append(jax.ShapeDtypeStruct((both, outer * depth), jnp.bfloat16))

    def send_places():
        core = lax.axis_index("tp")
        at = [sizes[0], lax.axis_index("groups") * band, core * pre_share, core * dec_share]
        return at + [features(back, step) for step in STEPS for back in range(outer)]

    last_piece, *row_sends = pack(plan, send_places, shapes, 56, pre_x, dec_x, w_kv)
    moving = [first_piece, last_piece]
    row_sends, query, pre_x, dec_x = lax.optimization_barrier((row_sends, dec_q, pre_x, dec_x))

    plan = []
    for back in range(outer):
        for turn in range(cores):
            column, to, base = 2 * cores + back, back * depth, turn * both
            plan.append((0, (pre_share, depth), 2 * turn, column, 0, base, to))
            plan.append((1, (dec_share, depth), 2 * turn + 1, column, 0, base + pre_share, to))

    def own_places():
        core, at = lax.axis_index("tp"), []
        for turn in range(cores):
            which = (core - turn + cores) % cores
            at += [which * pre_share, which * dec_share]
        return at + [features(back, 0) for back in range(outer)]

    total_rows = span + count
    shapes = [jax.ShapeDtypeStruct((total_rows, outer * depth), jnp.bfloat16)]
    (own_rows,) = pack(plan, own_places, shapes, 4, pre_x, dec_x)

    top_c, mixed_c = cached(query, cache, cache_len, heads)
    far = []
    for back in range(1, outer):
        moving = [to_outer(m) for m in moving]
        if back == 1:
            row_sends[-1] = after(row_sends[-1], moving[0], top_c, own_rows)
        far.append([[m] for m in moving])

    got = [to_inner(rows, step) for rows, step in zip(row_sends, STEPS)]
    arrived = [[rows] + [to_core(rows, turn) for turn in range(1, cores)] for rows in got]

    for pieces in far:
        for number, piece in enumerate(pieces):
            if number:
                sent = after(piece[0], pieces[number - 1][-1])
            else:
                sent = piece[0]
            piece += [to_team(sent, turn) for turn in range(1, teams)]

    last = sizes[-1]
    own_rows = after(own_rows, got[-1])
    blocks = [own_rows] + [rows for step in arrived[:-1] for rows in step]
    early = [m for pieces in far for m in pieces[0]]
    first_rows = (inner - 1) * total_rows
    *summed, last_rows = pl.pallas_call(
        functools.partial(early_kernel, outer, teams, last),
        out_shape=[
            *[jax.ShapeDtypeStruct((first_rows, band), jnp.float32)] * teams,
            jax.ShapeDtypeStruct((first_rows, (outer - 1) * last), jnp.bfloat16),
        ],
        in_specs=[VMEM] * (1 + len(early) + len(blocks)),
        out_specs=[VMEM] * (1 + teams),
        scratch_shapes=[
            pltpu.VMEM((first_rows, outer * depth - (outer - 1) * last), jnp.bfloat16)
        ],
        compiler_params=grant(16),
    )(w_kv, *early, *blocks)
    parts = []
    for turn in range(teams):
        pieces = [piece[turn] for some in far for piece in some]
        mine, *others = pl.pallas_call(
            functools.partial(late_kernel, outer, cores, teams, turn),
            out_shape=[jax.ShapeDtypeStruct((total_rows, band), jnp.float32)]
            + [jax.ShapeDtypeStruct((total_rows, band), jnp.bfloat16)] * (inner - 1),
            in_specs=[VMEM] * (3 + len(pieces) + cores),
            out_specs=[VMEM] * inner,
            scratch_shapes=[pltpu.VMEM((total_rows, outer * depth), jnp.bfloat16)],
            compiler_params=grant(12),
        )(w_kv, summed[turn], last_rows, *pieces, *arrived[-1])
        sent = [to_inner(part, step) for part, step in zip(others[::-1], STEPS[::-1])]
        parts += [mine, *sent]
    shifted, own_kv = pl.pallas_call(
        functools.partial(finish_kernel, cores, teams),
        out_shape=[
            jax.ShapeDtypeStruct((span, width), jnp.bfloat16),
            jax.ShapeDtypeStruct((count, width), jnp.bfloat16),
        ],
        in_specs=[VMEM] * (1 + len(parts)),
        out_specs=[VMEM] * 2,
        compiler_params=grant(6),
    )(kv_scale[None, :], *parts)

    def owners(backs):
        rank = lax.axis_index("dp")
        return [
            (rank // inner - back + outer) % outer * inner + (rank % inner ^ step)
            for back in backs
            for step in ((0, 3, 2, 1) if back else range(inner))
        ]

    blocks = []
    for back in range(outer):
        if back:
            shifted = to_outer(shifted)
        if back:
            blocks += [to_inner(shifted, step) if step else shifted for step in (0, 3, 2, 1)]
        else:
            near = [shifted, to_inner(shifted, 1), to_inner(shifted, 2)]
            blocks += near + [to_inner(near[2], 1)]

    state = jax.ShapeDtypeStruct((heads, REP * count, HD), jnp.float32)
    labels = jax.ShapeDtypeStruct((REP * count, HD), jnp.int32)
    *state, source, live, prompt_kv = pl.pallas_call(
        functools.partial(first_kernel, heads, lambda: owners([0])[:3]),
        out_shape=[state, state, labels, labels, jax.ShapeDtypeStruct((span, width), jnp.bfloat16)],
        in_specs=[SMEM] * 2 + [VMEM] * (3 + 3 + 2),
        out_specs=[VMEM] * 5,
        compiler_params=grant(12),
    )(
        prompt_owner,
        prompt_len,
        sample_rows,
        dec_q,
        top_c,
        mixed_c,
        own_kv,
        *blocks[:3],
    )
    attended = pl.pallas_call(
        functools.partial(second_kernel, heads, lambda: owners(range(outer))[3:]),
        out_shape=jax.ShapeDtypeStruct(dec_q.shape, jnp.bfloat16),
        in_specs=[VMEM] * (5 + len(blocks) - 3),
        out_specs=VMEM,
        compiler_params=grant(12),
    )(dec_q, source, live, *state, *blocks[3:])
    return (attended, prompt_kv)


def solution(mesh):
    in_specs = (
        P(("groups", "dp"), None),
        P(("groups", "dp"), None),
        P("dp", "tp"),
        P("tp"),
        P(("groups", "dp"), "tp"),
        P(("groups", "dp"), None, "tp"),
        P(("groups", "dp")),
        P("groups"),
        P("groups"),
        P("groups", None),
    )
    out_specs = (P(("groups", "dp"), "tp"), P(("groups", "dp"), "tp"))
    body = functools.partial(local, shape=dict(mesh.shape))
    return jax.shard_map(body, mesh=mesh, in_specs=in_specs, out_specs=out_specs, check_vma=False)
```

```python
import functools
import math

import jax
import jax.numpy as jnp
from jax import lax
from jax.experimental import pallas as pl
from jax.experimental.pallas import tpu as pltpu
from jax.sharding import PartitionSpec as P

HD = 128
REP = 12
NEG = -1e30
INNER = 4
STEPS = (1, 2, 3)


def pack_kernel(plan, places, n_in, n_out, *refs):
    ins, outs = refs[:n_in], refs[n_in : n_in + n_out]
    held, (in_sems, out_sems) = refs[n_in + n_out : -2], refs[-2:]
    at = places()
    arriving, leaving = [], []
    for number, (src, shape, row, column, dst, to_row, to_column) in enumerate(plan):
        rows, columns = pl.ds(to_row, shape[0]), pl.ds(to_column, shape[1])
        from_row = pl.multiple_of(at[row], 16)
        from_column = pl.multiple_of(at[column], 128)
        arriving.append(
            pltpu.make_async_copy(
                ins[src].at[pl.ds(from_row, shape[0]), pl.ds(from_column, shape[1])],
                held[dst].at[rows, columns],
                in_sems.at[number],
            )
        )
        leaving.append(
            pltpu.make_async_copy(
                held[dst].at[rows, columns], outs[dst].at[rows, columns], out_sems.at[number]
            )
        )
        arriving[-1].start()
    for came, left in zip(arriving, leaving):
        came.wait()
        left.start()
    for left in leaving:
        left.wait()


def band_columns(teams, turn, band):
    team = lax.axis_index("groups")
    return pl.ds(pl.multiple_of((team - turn + teams) % teams * band, 128), band)


def early_kernel(outer, teams, last, w_ref, *refs):
    n_late = teams + 2
    pieces, refs = refs[: teams * (outer - 1)], refs[teams * (outer - 1) :]
    blocks, sum_refs, (last_ref, row_ref) = refs[:-n_late], refs[-n_late:-2], refs[-2:]
    depth = w_ref.shape[0]
    early = depth - last
    base = 0
    for block in blocks:
        rows = slice(base, base + block.shape[0])
        row_ref[rows, :depth] = block[:, :depth]
        for back in range(1, outer):
            at = depth + (back - 1) * early
            row_ref[rows, at : at + early] = block[:, back * depth : back * depth + early]
            last_ref[rows, (back - 1) * last : back * last] = block[
                :, back * depth + early : (back + 1) * depth
            ]
        base += block.shape[0]
    for turn, sum_ref in enumerate(sum_refs):
        columns = band_columns(teams, turn, sum_ref.shape[1])
        summed = jnp.dot(row_ref[:, :depth], w_ref[:, columns], preferred_element_type=jnp.float32)
        for back in range(1, outer):
            at = depth + (back - 1) * early
            summed = summed + jnp.dot(
                row_ref[:, at : at + early],
                pieces[(back - 1) * teams + turn][...],
                preferred_element_type=jnp.float32,
            )
        sum_ref[...] = summed


def late_kernel(outer, cores, teams, turn, w_ref, sum_ref, last_ref, *refs):
    pieces, refs = refs[: 2 * (outer - 1)], refs[2 * (outer - 1) :]
    halves, outs, row_ref = refs[:cores], refs[cores:-1], refs[-1]
    depth = w_ref.shape[0]
    last = last_ref.shape[1] // (outer - 1)
    each, both = outs[0].shape[0], halves[0].shape[0]
    for number, half in enumerate(halves):
        row_ref[number * both : (number + 1) * both, :] = half[...]
    columns = band_columns(teams, turn, sum_ref.shape[1])
    first = sum_ref[...]
    final = jnp.dot(row_ref[:, :depth], w_ref[:, columns], preferred_element_type=jnp.float32)
    for back in range(1, outer):
        early_piece, last_piece = pieces[2 * back - 2 : 2 * back]
        at = back * depth
        cut = at + depth - last
        final = final + jnp.dot(
            row_ref[:, at:cut], early_piece[...], preferred_element_type=jnp.float32
        )
        final = final + jnp.dot(
            row_ref[:, cut : cut + last], last_piece[...], preferred_element_type=jnp.float32
        )
        first = first + jnp.dot(
            last_ref[:, (back - 1) * last : back * last],
            last_piece[...],
            preferred_element_type=jnp.float32,
        )
    for step, out in enumerate(outs[:-1]):
        out[...] = first[step * each : (step + 1) * each].astype(out.dtype)
    outs[-1][...] = final.astype(outs[-1].dtype)


def finish_kernel(cores, teams, scale_ref, *refs):
    parts, (sent_ref, own_ref) = refs[:-2], refs[-2:]
    span, count = sent_ref.shape[0], own_ref.shape[0]
    pre_share, dec_share = span // cores, count // cores
    both = pre_share + dec_share
    band = scale_ref.shape[1] // teams
    for turn in range(teams):
        columns = band_columns(teams, turn, band)
        own, *others = parts[turn * len(parts) // teams : (turn + 1) * len(parts) // teams]
        summed = own[...]
        for part in others:
            summed = summed + part[...].astype(jnp.float32)
        done = (summed * scale_ref[:, columns]).astype(jnp.bfloat16)
        for share in range(cores):
            which = (lax.axis_index("tp") - share + cores) % cores
            rows = pl.ds(pl.multiple_of(which * pre_share, 16), pre_share)
            sent_ref[rows, columns] = done[share * both : share * both + pre_share]
            own_ref[pl.ds(pl.multiple_of(which * dec_share, 16), dec_share), columns] = done[
                share * both + pre_share : (share + 1) * both
            ]


def match_rows(owner_ref, len_ref, samples_ref, count):
    row = lax.axis_index("dp") * count + lax.broadcasted_iota(jnp.int32, (count, 1), 0)
    source = jnp.zeros((count, 1), jnp.int32)
    live = jnp.zeros((count, 1), jnp.int32)
    for prompt in range(samples_ref.shape[0]):
        hit = jnp.max(
            jnp.where(samples_ref[prompt : prompt + 1, :] == row, 1, 0), -1, keepdims=True
        )
        source = source + hit * owner_ref[prompt]
        live = live + hit * len_ref[prompt]
    return source, live


def absorb(owners, q_ref, source, live, head, blocks, top, mixed, own_ref):
    count, span = q_ref.shape[0], blocks[0].shape[0]
    factor = 1.0 / math.sqrt(HD)
    first = head * REP * HD
    low, mid, high = head * 2 * HD, head * 2 * HD + HD, head * 2 * HD + 2 * HD
    q = jnp.concatenate([q_ref[:, first + r * HD : first + (r + 1) * HD] for r in range(REP)], 0)
    picked = jnp.full((REP * count, span), NEG, jnp.float32)
    place = lax.broadcasted_iota(jnp.int32, (REP * count, span), 1)
    pairs = [slice(at, at + 2) for at in range(0, len(blocks), 2)]
    for pair in pairs:
        scores = lax.dot_general(
            q,
            jnp.concatenate([block[:, low:mid] for block in blocks[pair]], 0),
            (((1,), (1,)), ((), ())),
            preferred_element_type=jnp.float32,
        )
        for at, owner in enumerate(owners[pair]):
            mine = scores[:, at * span : (at + 1) * span]
            picked = jnp.where(source == owner, mine * factor, picked)
    picked = jnp.where(place < live, picked, NEG)
    new = jnp.maximum(jnp.max(picked, -1, keepdims=True), top)
    if own_ref is not None:
        own_k = jnp.concatenate([own_ref[:, low:mid].astype(jnp.float32)] * REP, 0)
        own_v = jnp.concatenate([own_ref[:, mid:high].astype(jnp.float32)] * REP, 0)
        score = jnp.sum(q.astype(jnp.float32) * own_k, -1, keepdims=True) * factor
        new = jnp.maximum(new, score)
    weights = jnp.exp(picked - new)
    kept = jnp.exp(top - new)
    total = kept + jnp.sum(weights, -1, keepdims=True)
    mixed = mixed * kept
    if own_ref is not None:
        weight = jnp.exp(score - new)
        total = total + weight
        mixed = mixed + weight * own_v
    for pair in pairs:
        shares = [jnp.where(source == owner, weights, 0.0) for owner in owners[pair]]
        mixed = mixed + jnp.dot(
            jnp.concatenate(shares, 1).astype(jnp.bfloat16),
            jnp.concatenate([block[:, mid:high] for block in blocks[pair]], 0),
            preferred_element_type=jnp.float32,
        )
    return new + jnp.log(total), mixed / total


def cache_kernel(heads, len_ref, q_ref, cache_ref, top_ref, mixed_ref):
    count, rows = q_ref.shape[0], heads * REP
    factor = 1.0 / math.sqrt(HD)
    query = [q_ref[:, r * HD : (r + 1) * HD].astype(jnp.float32) for r in range(rows)]
    query = jnp.swapaxes(jnp.stack(query), 0, 1).astype(jnp.bfloat16)
    head_of = lax.broadcasted_iota(jnp.int32, (rows, 1), 0) // REP
    spot = lax.broadcasted_iota(jnp.int32, (rows, cache_ref.shape[1]), 1)
    tops, mixes = [], []
    for sample in range(count):
        length = len_ref[pl.program_id(0) * count + sample]
        scores = mixed = None
        for head in range(heads):
            key = cache_ref[sample, :, head * 2 * HD : head * 2 * HD + HD]
            found = lax.dot_general(
                query[sample], key, (((1,), (1,)), ((), ())), preferred_element_type=jnp.float32
            )
            scores = found if head == 0 else jnp.where(head_of == head, found, scores)
        scores = jnp.where(spot < length, scores * factor, NEG)
        top = jnp.max(scores, -1, keepdims=True)
        weights = jnp.exp(scores - top)
        total = jnp.sum(weights, -1, keepdims=True)
        for head in range(heads):
            value = cache_ref[sample, :, head * 2 * HD + HD : (head + 1) * 2 * HD]
            found = jnp.dot(
                weights.astype(jnp.bfloat16), value, preferred_element_type=jnp.float32
            )
            mixed = found if head == 0 else jnp.where(head_of == head, found, mixed)
        tops.append(jnp.broadcast_to(top + jnp.log(total), (rows, HD)))
        mixes.append(mixed / total)
    top_ref[...] = jnp.swapaxes(jnp.stack(tops), 0, 1)
    mixed_ref[...] = jnp.swapaxes(jnp.stack(mixes), 0, 1)


def cached(query, cache, cache_len, heads):
    count, slots, width = cache.shape
    rows, each = heads * REP, 8
    state = jax.ShapeDtypeStruct((rows, count, HD), jnp.float32)
    return pl.pallas_call(
        functools.partial(cache_kernel, heads),
        grid=(count // each,),
        out_shape=[state, state],
        in_specs=[
            SMEM,
            pl.BlockSpec((each, rows * HD), lambda i: (i, 0)),
            pl.BlockSpec((each, slots, width), lambda i: (i, 0, 0)),
        ],
        out_specs=[pl.BlockSpec((rows, each, HD), lambda i: (0, i, 0))] * 2,
        compiler_params=grant(12),
        cost_estimate=pl.CostEstimate(
            flops=4 * count * rows * slots * HD * heads,
            bytes_accessed=2 * cache.size,
            transcendentals=count * rows * slots,
        ),
    )(cache_len, query, cache)


def first_kernel(
    heads, owners, owner_ref, len_ref, samples_ref, q_ref, top_ref, mixed_ref, own_ref, *refs
):
    blocks, (new_top, new_mixed, source_ref, live_ref, prompt_ref) = refs[:-5], refs[-5:]
    prompt_ref[...] = blocks[0][...]
    source, live = match_rows(owner_ref, len_ref, samples_ref, q_ref.shape[0])
    source = jnp.concatenate([source] * REP, 0)
    live = jnp.concatenate([live] * REP, 0)
    source_ref[...] = jnp.broadcast_to(source, source_ref.shape)
    live_ref[...] = jnp.broadcast_to(live, live_ref.shape)
    for head in range(heads):
        mine = slice(head * REP, (head + 1) * REP)
        top = top_ref[mine].reshape(new_top.shape[1:])
        mixed = mixed_ref[mine].reshape(new_top.shape[1:])
        new_top[head], new_mixed[head] = absorb(
            owners(), q_ref, source, live, head, blocks, top, mixed, own_ref
        )


def second_kernel(heads, owners, q_ref, source_ref, live_ref, top_ref, mixed_ref, *refs):
    blocks, out_ref = refs[:-1], refs[-1]
    count = q_ref.shape[0]
    for head in range(heads):
        _, mixed = absorb(
            owners(),
            q_ref,
            source_ref[...],
            live_ref[...],
            head,
            blocks,
            top_ref[head],
            mixed_ref[head],
            None,
        )
        first = head * REP * HD
        for r in range(REP):
            out_ref[:, first + r * HD : first + (r + 1) * HD] = mixed[
                r * count : (r + 1) * count
            ].astype(out_ref.dtype)


VMEM = pl.BlockSpec(memory_space=pltpu.VMEM)
SMEM = pl.BlockSpec(memory_space=pltpu.SMEM)
HBM = pl.BlockSpec(memory_space=pltpu.HBM)


def after(value, *others):
    return lax.optimization_barrier((value, *others))[0]


def grant(mib):
    return pltpu.CompilerParams(vmem_limit_bytes=mib * 1024 * 1024)


def stages(depth):
    unit = 128
    first = max(unit, depth * 7 // 12 // unit * unit)
    return (first, depth - first)


def local(
    pre_x,
    dec_x,
    w_kv,
    kv_scale,
    dec_q,
    cache,
    cache_len,
    prompt_owner,
    prompt_len,
    sample_rows,
    *,
    shape,
):
    teams, ranks, cores = shape["groups"], shape["dp"], shape["tp"]
    inner = INNER
    outer = ranks // inner
    span, features = pre_x.shape
    count = dec_x.shape[0]
    depth, width = w_kv.shape
    heads = width // (2 * HD)
    band = width // teams

    def to_inner(value, step):
        pairs = [(r, r // inner * inner + (r % inner ^ step)) for r in range(ranks)]
        return lax.ppermute(value, "dp", pairs)

    def to_outer(value, step=1):
        pairs = [(r, (r + step * inner) % ranks) for r in range(ranks)]
        return lax.ppermute(value, "dp", pairs)

    def to_team(value, step):
        return lax.ppermute(value, "groups", [(i, (i + step) % teams) for i in range(teams)])

    def to_core(value, step):
        return lax.ppermute(value, "tp", [(i, (i + step) % cores) for i in range(cores)])

    def pack(plan, places, shapes, mib, *arrays):
        sems = pltpu.SemaphoreType.DMA((len(plan),))
        return pl.pallas_call(
            functools.partial(pack_kernel, plan, places, len(arrays), len(shapes)),
            out_shape=shapes,
            in_specs=[HBM] * len(arrays),
            out_specs=[HBM] * len(shapes),
            scratch_shapes=[pltpu.VMEM(s.shape, s.dtype) for s in shapes] + [sems, sems],
            compiler_params=grant(mib),
        )(*arrays)

    sizes = stages(depth)
    pre_share, dec_share = span // cores, count // cores
    both = pre_share + dec_share
    def features(back, step):
        rank = lax.axis_index("dp")
        return ((rank // inner - back + outer) % outer * inner + (rank % inner ^ step)) * depth

    def band_place():
        return [0, lax.axis_index("groups") * band]

    shape = jax.ShapeDtypeStruct((sizes[0], band), jnp.bfloat16)
    (first_piece,) = pack([(0, (sizes[0], band), 0, 1, 0, 0, 0)], band_place, [shape], 56, w_kv)
    first_piece, pre_x, dec_x, w_kv = lax.optimization_barrier((first_piece, pre_x, dec_x, w_kv))

    plan = [(2, (sizes[1], band), 0, 1, 0, 0, 0)]
    shapes = [jax.ShapeDtypeStruct((sizes[1], band), jnp.bfloat16)]
    for number in range(inner - 1):
        for back in range(outer):
            column, to = 4 + number * outer + back, back * depth
            plan.append((0, (pre_share, depth), 2, column, len(shapes), 0, to))
            plan.append((1, (dec_share, depth), 3, column, len(shapes), pre_share, to))
        shapes.append(jax.ShapeDtypeStruct((both, outer * depth), jnp.bfloat16))

    def send_places():
        core = lax.axis_index("tp")
        at = [sizes[0], lax.axis_index("groups") * band, core * pre_share, core * dec_share]
        return at + [features(back, step) for step in STEPS for back in range(outer)]

    last_piece, *row_sends = pack(plan, send_places, shapes, 56, pre_x, dec_x, w_kv)
    moving = [first_piece, last_piece]
    row_sends, query, pre_x, dec_x = lax.optimization_barrier((row_sends, dec_q, pre_x, dec_x))

    plan = []
    for back in range(outer):
        for turn in range(cores):
            column, to, base = 2 * cores + back, back * depth, turn * both
            plan.append((0, (pre_share, depth), 2 * turn, column, 0, base, to))
            plan.append((1, (dec_share, depth), 2 * turn + 1, column, 0, base + pre_share, to))

    def own_places():
        core, at = lax.axis_index("tp"), []
        for turn in range(cores):
            which = (core - turn + cores) % cores
            at += [which * pre_share, which * dec_share]
        return at + [features(back, 0) for back in range(outer)]

    total_rows = span + count
    shapes = [jax.ShapeDtypeStruct((total_rows, outer * depth), jnp.bfloat16)]
    (own_rows,) = pack(plan, own_places, shapes, 4, pre_x, dec_x)

    top_c, mixed_c = cached(query, cache, cache_len, heads)
    far = []
    for back in range(1, outer):
        moving = [to_outer(m) for m in moving]
        if back == 1:
            row_sends[-1] = after(row_sends[-1], moving[0], top_c, own_rows)
        far.append([[m] for m in moving])

    got = [to_inner(rows, step) for rows, step in zip(row_sends, STEPS)]
    arrived = [[rows] + [to_core(rows, turn) for turn in range(1, cores)] for rows in got]

    for pieces in far:
        for number, piece in enumerate(pieces):
            if number:
                sent = after(piece[0], pieces[number - 1][-1])
            else:
                sent = piece[0]
            piece += [to_team(sent, turn) for turn in range(1, teams)]

    last = sizes[-1]
    own_rows = after(own_rows, got[-1])
    blocks = [own_rows] + [rows for step in arrived[:-1] for rows in step]
    early = [m for pieces in far for m in pieces[0]]
    first_rows = (inner - 1) * total_rows
    *summed, last_rows = pl.pallas_call(
        functools.partial(early_kernel, outer, teams, last),
        out_shape=[
            *[jax.ShapeDtypeStruct((first_rows, band), jnp.float32)] * teams,
            jax.ShapeDtypeStruct((first_rows, (outer - 1) * last), jnp.bfloat16),
        ],
        in_specs=[VMEM] * (1 + len(early) + len(blocks)),
        out_specs=[VMEM] * (1 + teams),
        scratch_shapes=[
            pltpu.VMEM((first_rows, outer * depth - (outer - 1) * last), jnp.bfloat16)
        ],
        compiler_params=grant(16),
    )(w_kv, *early, *blocks)
    parts = []
    for turn in range(teams):
        pieces = [piece[turn] for some in far for piece in some]
        mine, *others = pl.pallas_call(
            functools.partial(late_kernel, outer, cores, teams, turn),
            out_shape=[jax.ShapeDtypeStruct((total_rows, band), jnp.float32)]
            + [jax.ShapeDtypeStruct((total_rows, band), jnp.bfloat16)] * (inner - 1),
            in_specs=[VMEM] * (3 + len(pieces) + cores),
            out_specs=[VMEM] * inner,
            scratch_shapes=[pltpu.VMEM((total_rows, outer * depth), jnp.bfloat16)],
            compiler_params=grant(12),
        )(w_kv, summed[turn], last_rows, *pieces, *arrived[-1])
        sent = [to_inner(part, step) for part, step in zip(others[::-1], STEPS[::-1])]
        parts += [mine, *sent]
    shifted, own_kv = pl.pallas_call(
        functools.partial(finish_kernel, cores, teams),
        out_shape=[
            jax.ShapeDtypeStruct((span, width), jnp.bfloat16),
            jax.ShapeDtypeStruct((count, width), jnp.bfloat16),
        ],
        in_specs=[VMEM] * (1 + len(parts)),
        out_specs=[VMEM] * 2,
        compiler_params=grant(6),
    )(kv_scale[None, :], *parts)

    def owners(backs):
        rank = lax.axis_index("dp")
        return [
            (rank // inner - back + outer) % outer * inner + (rank % inner ^ step)
            for back in backs
            for step in ((0, 3, 2, 1) if back else range(inner))
        ]

    blocks = []
    for back in range(outer):
        if back:
            shifted = to_outer(shifted)
        if back:
            blocks += [to_inner(shifted, step) if step else shifted for step in (0, 3, 2, 1)]
        else:
            near = [shifted, to_inner(shifted, 1), to_inner(shifted, 2)]
            blocks += near + [to_inner(after(near[2], near[1]), 1)]

    state = jax.ShapeDtypeStruct((heads, REP * count, HD), jnp.float32)
    labels = jax.ShapeDtypeStruct((REP * count, HD), jnp.int32)
    *state, source, live, prompt_kv = pl.pallas_call(
        functools.partial(first_kernel, heads, lambda: owners([0])[:3]),
        out_shape=[state, state, labels, labels, jax.ShapeDtypeStruct((span, width), jnp.bfloat16)],
        in_specs=[SMEM] * 2 + [VMEM] * (3 + 3 + 2),
        out_specs=[VMEM] * 5,
        compiler_params=grant(12),
    )(
        prompt_owner,
        prompt_len,
        sample_rows,
        dec_q,
        top_c,
        mixed_c,
        own_kv,
        *blocks[:3],
    )
    attended = pl.pallas_call(
        functools.partial(second_kernel, heads, lambda: owners(range(outer))[3:]),
        out_shape=jax.ShapeDtypeStruct(dec_q.shape, jnp.bfloat16),
        in_specs=[VMEM] * (5 + len(blocks) - 3),
        out_specs=VMEM,
        compiler_params=grant(12),
    )(dec_q, source, live, *state, *blocks[3:])
    return (attended, prompt_kv)


def solution(mesh):
    in_specs = (
        P(("groups", "dp"), None),
        P(("groups", "dp"), None),
        P("dp", "tp"),
        P("tp"),
        P(("groups", "dp"), "tp"),
        P(("groups", "dp"), None, "tp"),
        P(("groups", "dp")),
        P("groups"),
        P("groups"),
        P("groups", None),
    )
    out_specs = (P(("groups", "dp"), "tp"), P(("groups", "dp"), "tp"))
    body = functools.partial(local, shape=dict(mesh.shape))
    return jax.shard_map(body, mesh=mesh, in_specs=in_specs, out_specs=out_specs, check_vma=False)
```

```python
import functools
import math

import jax
import jax.numpy as jnp
from jax import lax
from jax.experimental import pallas as pl
from jax.experimental.pallas import tpu as pltpu
from jax.sharding import PartitionSpec as P

HD = 128
REP = 12
NEG = -1e30
INNER = 4
STEPS = (1, 2, 3)


def pack_kernel(plan, places, n_in, n_out, *refs):
    ins, outs = refs[:n_in], refs[n_in : n_in + n_out]
    held, (in_sems, out_sems) = refs[n_in + n_out : -2], refs[-2:]
    at = places()
    arriving, leaving = [], []
    for number, (src, shape, row, column, dst, to_row, to_column) in enumerate(plan):
        rows, columns = pl.ds(to_row, shape[0]), pl.ds(to_column, shape[1])
        from_row = pl.multiple_of(at[row], 16)
        from_column = pl.multiple_of(at[column], 128)
        arriving.append(
            pltpu.make_async_copy(
                ins[src].at[pl.ds(from_row, shape[0]), pl.ds(from_column, shape[1])],
                held[dst].at[rows, columns],
                in_sems.at[number],
            )
        )
        leaving.append(
            pltpu.make_async_copy(
                held[dst].at[rows, columns], outs[dst].at[rows, columns], out_sems.at[number]
            )
        )
        arriving[-1].start()
    for came, left in zip(arriving, leaving):
        came.wait()
        left.start()
    for left in leaving:
        left.wait()


def band_columns(teams, turn, band):
    team = lax.axis_index("groups")
    return pl.ds(pl.multiple_of((team - turn + teams) % teams * band, 128), band)


def early_kernel(outer, teams, last, w_ref, *refs):
    n_late = teams + 2
    pieces, refs = refs[: teams * (outer - 1)], refs[teams * (outer - 1) :]
    blocks, sum_refs, (last_ref, row_ref) = refs[:-n_late], refs[-n_late:-2], refs[-2:]
    depth = w_ref.shape[0]
    early = depth - last
    base = 0
    for block in blocks:
        rows = slice(base, base + block.shape[0])
        row_ref[rows, :depth] = block[:, :depth]
        for back in range(1, outer):
            at = depth + (back - 1) * early
            row_ref[rows, at : at + early] = block[:, back * depth : back * depth + early]
            last_ref[rows, (back - 1) * last : back * last] = block[
                :, back * depth + early : (back + 1) * depth
            ]
        base += block.shape[0]
    for turn, sum_ref in enumerate(sum_refs):
        columns = band_columns(teams, turn, sum_ref.shape[1])
        summed = jnp.dot(row_ref[:, :depth], w_ref[:, columns], preferred_element_type=jnp.float32)
        for back in range(1, outer):
            at = depth + (back - 1) * early
            summed = summed + jnp.dot(
                row_ref[:, at : at + early],
                pieces[(back - 1) * teams + turn][...],
                preferred_element_type=jnp.float32,
            )
        sum_ref[...] = summed


def late_kernel(outer, cores, teams, turn, w_ref, sum_ref, last_ref, *refs):
    pieces, refs = refs[: 2 * (outer - 1)], refs[2 * (outer - 1) :]
    halves, outs, row_ref = refs[:cores], refs[cores:-1], refs[-1]
    depth = w_ref.shape[0]
    last = last_ref.shape[1] // (outer - 1)
    each, both = outs[0].shape[0], halves[0].shape[0]
    for number, half in enumerate(halves):
        row_ref[number * both : (number + 1) * both, :] = half[...]
    columns = band_columns(teams, turn, sum_ref.shape[1])
    first = sum_ref[...]
    final = jnp.dot(row_ref[:, :depth], w_ref[:, columns], preferred_element_type=jnp.float32)
    for back in range(1, outer):
        early_piece, last_piece = pieces[2 * back - 2 : 2 * back]
        at = back * depth
        cut = at + depth - last
        final = final + jnp.dot(
            row_ref[:, at:cut], early_piece[...], preferred_element_type=jnp.float32
        )
        final = final + jnp.dot(
            row_ref[:, cut : cut + last], last_piece[...], preferred_element_type=jnp.float32
        )
        first = first + jnp.dot(
            last_ref[:, (back - 1) * last : back * last],
            last_piece[...],
            preferred_element_type=jnp.float32,
        )
    for step, out in enumerate(outs[:-1]):
        out[...] = first[step * each : (step + 1) * each].astype(out.dtype)
    outs[-1][...] = final.astype(outs[-1].dtype)


def finish_kernel(cores, teams, scale_ref, *refs):
    parts, (sent_ref, own_ref) = refs[:-2], refs[-2:]
    span, count = sent_ref.shape[0], own_ref.shape[0]
    pre_share, dec_share = span // cores, count // cores
    both = pre_share + dec_share
    band = scale_ref.shape[1] // teams
    for turn in range(teams):
        columns = band_columns(teams, turn, band)
        own, *others = parts[turn * len(parts) // teams : (turn + 1) * len(parts) // teams]
        summed = own[...]
        for part in others:
            summed = summed + part[...].astype(jnp.float32)
        done = (summed * scale_ref[:, columns]).astype(jnp.bfloat16)
        for share in range(cores):
            which = (lax.axis_index("tp") - share + cores) % cores
            rows = pl.ds(pl.multiple_of(which * pre_share, 16), pre_share)
            sent_ref[rows, columns] = done[share * both : share * both + pre_share]
            own_ref[pl.ds(pl.multiple_of(which * dec_share, 16), dec_share), columns] = done[
                share * both + pre_share : (share + 1) * both
            ]


def match_rows(owner_ref, len_ref, samples_ref, count):
    row = lax.axis_index("dp") * count + lax.broadcasted_iota(jnp.int32, (count, 1), 0)
    source = jnp.zeros((count, 1), jnp.int32)
    live = jnp.zeros((count, 1), jnp.int32)
    for prompt in range(samples_ref.shape[0]):
        hit = jnp.max(
            jnp.where(samples_ref[prompt : prompt + 1, :] == row, 1, 0), -1, keepdims=True
        )
        source = source + hit * owner_ref[prompt]
        live = live + hit * len_ref[prompt]
    return source, live


def absorb(owners, q_ref, source, live, head, blocks, top, mixed, own_ref):
    count, span = q_ref.shape[0], blocks[0].shape[0]
    factor = 1.0 / math.sqrt(HD)
    first = head * REP * HD
    low, mid, high = head * 2 * HD, head * 2 * HD + HD, head * 2 * HD + 2 * HD
    q = jnp.concatenate([q_ref[:, first + r * HD : first + (r + 1) * HD] for r in range(REP)], 0)
    picked = jnp.full((REP * count, span), NEG, jnp.float32)
    place = lax.broadcasted_iota(jnp.int32, (REP * count, span), 1)
    pairs = [slice(at, at + 2) for at in range(0, len(blocks), 2)]
    for pair in pairs:
        scores = lax.dot_general(
            q,
            jnp.concatenate([block[:, low:mid] for block in blocks[pair]], 0),
            (((1,), (1,)), ((), ())),
            preferred_element_type=jnp.float32,
        )
        for at, owner in enumerate(owners[pair]):
            mine = scores[:, at * span : (at + 1) * span]
            picked = jnp.where(source == owner, mine * factor, picked)
    picked = jnp.where(place < live, picked, NEG)
    new = jnp.maximum(jnp.max(picked, -1, keepdims=True), top)
    if own_ref is not None:
        own_k = jnp.concatenate([own_ref[:, low:mid].astype(jnp.float32)] * REP, 0)
        own_v = jnp.concatenate([own_ref[:, mid:high].astype(jnp.float32)] * REP, 0)
        score = jnp.sum(q.astype(jnp.float32) * own_k, -1, keepdims=True) * factor
        new = jnp.maximum(new, score)
    weights = jnp.exp(picked - new)
    kept = jnp.exp(top - new)
    total = kept + jnp.sum(weights, -1, keepdims=True)
    mixed = mixed * kept
    if own_ref is not None:
        weight = jnp.exp(score - new)
        total = total + weight
        mixed = mixed + weight * own_v
    for pair in pairs:
        shares = [jnp.where(source == owner, weights, 0.0) for owner in owners[pair]]
        mixed = mixed + jnp.dot(
            jnp.concatenate(shares, 1).astype(jnp.bfloat16),
            jnp.concatenate([block[:, mid:high] for block in blocks[pair]], 0),
            preferred_element_type=jnp.float32,
        )
    return new + jnp.log(total), mixed / total


def cache_kernel(heads, len_ref, q_ref, cache_ref, top_ref, mixed_ref):
    count, rows = q_ref.shape[0], heads * REP
    factor = 1.0 / math.sqrt(HD)
    query = [q_ref[:, r * HD : (r + 1) * HD].astype(jnp.float32) for r in range(rows)]
    query = jnp.swapaxes(jnp.stack(query), 0, 1).astype(jnp.bfloat16)
    head_of = lax.broadcasted_iota(jnp.int32, (rows, 1), 0) // REP
    spot = lax.broadcasted_iota(jnp.int32, (rows, cache_ref.shape[1]), 1)
    tops, mixes = [], []
    for sample in range(count):
        length = len_ref[pl.program_id(0) * count + sample]
        scores = mixed = None
        for head in range(heads):
            key = cache_ref[sample, :, head * 2 * HD : head * 2 * HD + HD]
            found = lax.dot_general(
                query[sample], key, (((1,), (1,)), ((), ())), preferred_element_type=jnp.float32
            )
            scores = found if head == 0 else jnp.where(head_of == head, found, scores)
        scores = jnp.where(spot < length, scores * factor, NEG)
        top = jnp.max(scores, -1, keepdims=True)
        weights = jnp.exp(scores - top)
        total = jnp.sum(weights, -1, keepdims=True)
        for head in range(heads):
            value = cache_ref[sample, :, head * 2 * HD + HD : (head + 1) * 2 * HD]
            found = jnp.dot(
                weights.astype(jnp.bfloat16), value, preferred_element_type=jnp.float32
            )
            mixed = found if head == 0 else jnp.where(head_of == head, found, mixed)
        tops.append(jnp.broadcast_to(top + jnp.log(total), (rows, HD)))
        mixes.append(mixed / total)
    top_ref[...] = jnp.swapaxes(jnp.stack(tops), 0, 1)
    mixed_ref[...] = jnp.swapaxes(jnp.stack(mixes), 0, 1)


def cached(query, cache, cache_len, heads):
    count, slots, width = cache.shape
    rows, each = heads * REP, 8
    state = jax.ShapeDtypeStruct((rows, count, HD), jnp.float32)
    return pl.pallas_call(
        functools.partial(cache_kernel, heads),
        grid=(count // each,),
        out_shape=[state, state],
        in_specs=[
            SMEM,
            pl.BlockSpec((each, rows * HD), lambda i: (i, 0)),
            pl.BlockSpec((each, slots, width), lambda i: (i, 0, 0)),
        ],
        out_specs=[pl.BlockSpec((rows, each, HD), lambda i: (0, i, 0))] * 2,
        compiler_params=grant(12),
        cost_estimate=pl.CostEstimate(
            flops=4 * count * rows * slots * HD * heads,
            bytes_accessed=2 * cache.size,
            transcendentals=count * rows * slots,
        ),
    )(cache_len, query, cache)


def first_kernel(
    heads, owners, owner_ref, len_ref, samples_ref, q_ref, top_ref, mixed_ref, own_ref, *refs
):
    blocks, (new_top, new_mixed, source_ref, live_ref, prompt_ref) = refs[:-5], refs[-5:]
    prompt_ref[...] = blocks[0][...]
    source, live = match_rows(owner_ref, len_ref, samples_ref, q_ref.shape[0])
    source = jnp.concatenate([source] * REP, 0)
    live = jnp.concatenate([live] * REP, 0)
    source_ref[...] = jnp.broadcast_to(source, source_ref.shape)
    live_ref[...] = jnp.broadcast_to(live, live_ref.shape)
    for head in range(heads):
        mine = slice(head * REP, (head + 1) * REP)
        top = top_ref[mine].reshape(new_top.shape[1:])
        mixed = mixed_ref[mine].reshape(new_top.shape[1:])
        new_top[head], new_mixed[head] = absorb(
            owners(), q_ref, source, live, head, blocks, top, mixed, own_ref
        )


def second_kernel(heads, owners, q_ref, source_ref, live_ref, top_ref, mixed_ref, *refs):
    blocks, out_ref = refs[:-1], refs[-1]
    count = q_ref.shape[0]
    for head in range(heads):
        _, mixed = absorb(
            owners(),
            q_ref,
            source_ref[...],
            live_ref[...],
            head,
            blocks,
            top_ref[head],
            mixed_ref[head],
            None,
        )
        first = head * REP * HD
        for r in range(REP):
            out_ref[:, first + r * HD : first + (r + 1) * HD] = mixed[
                r * count : (r + 1) * count
            ].astype(out_ref.dtype)


VMEM = pl.BlockSpec(memory_space=pltpu.VMEM)
SMEM = pl.BlockSpec(memory_space=pltpu.SMEM)
HBM = pl.BlockSpec(memory_space=pltpu.HBM)


def after(value, *others):
    return lax.optimization_barrier((value, *others))[0]


def grant(mib):
    return pltpu.CompilerParams(vmem_limit_bytes=mib * 1024 * 1024)


def stages(depth):
    unit = 128
    first = max(unit, depth * 7 // 12 // unit * unit)
    return (first, depth - first)


def local(
    pre_x,
    dec_x,
    w_kv,
    kv_scale,
    dec_q,
    cache,
    cache_len,
    prompt_owner,
    prompt_len,
    sample_rows,
    *,
    shape,
):
    teams, ranks, cores = shape["groups"], shape["dp"], shape["tp"]
    inner = INNER
    outer = ranks // inner
    span, features = pre_x.shape
    count = dec_x.shape[0]
    depth, width = w_kv.shape
    heads = width // (2 * HD)
    band = width // teams

    def to_inner(value, step):
        pairs = [(r, r // inner * inner + (r % inner ^ step)) for r in range(ranks)]
        return lax.ppermute(value, "dp", pairs)

    def to_outer(value, step=1):
        pairs = [(r, (r + step * inner) % ranks) for r in range(ranks)]
        return lax.ppermute(value, "dp", pairs)

    def to_team(value, step):
        return lax.ppermute(value, "groups", [(i, (i + step) % teams) for i in range(teams)])

    def to_core(value, step):
        return lax.ppermute(value, "tp", [(i, (i + step) % cores) for i in range(cores)])

    def pack(plan, places, shapes, mib, *arrays):
        sems = pltpu.SemaphoreType.DMA((len(plan),))
        return pl.pallas_call(
            functools.partial(pack_kernel, plan, places, len(arrays), len(shapes)),
            out_shape=shapes,
            in_specs=[HBM] * len(arrays),
            out_specs=[HBM] * len(shapes),
            scratch_shapes=[pltpu.VMEM(s.shape, s.dtype) for s in shapes] + [sems, sems],
            compiler_params=grant(mib),
        )(*arrays)

    sizes = stages(depth)
    pre_share, dec_share = span // cores, count // cores
    both = pre_share + dec_share
    def features(back, step):
        rank = lax.axis_index("dp")
        return ((rank // inner - back + outer) % outer * inner + (rank % inner ^ step)) * depth

    def band_place():
        return [0, lax.axis_index("groups") * band]

    shape = jax.ShapeDtypeStruct((sizes[0], band), jnp.bfloat16)
    (first_piece,) = pack([(0, (sizes[0], band), 0, 1, 0, 0, 0)], band_place, [shape], 56, w_kv)
    first_piece, pre_x, dec_x, w_kv = lax.optimization_barrier((first_piece, pre_x, dec_x, w_kv))

    plan = [(2, (sizes[1], band), 0, 1, 0, 0, 0)]
    shapes = [jax.ShapeDtypeStruct((sizes[1], band), jnp.bfloat16)]
    for number in range(inner - 1):
        for back in range(outer):
            column, to = 4 + number * outer + back, back * depth
            plan.append((0, (pre_share, depth), 2, column, len(shapes), 0, to))
            plan.append((1, (dec_share, depth), 3, column, len(shapes), pre_share, to))
        shapes.append(jax.ShapeDtypeStruct((both, outer * depth), jnp.bfloat16))

    def send_places():
        core = lax.axis_index("tp")
        at = [sizes[0], lax.axis_index("groups") * band, core * pre_share, core * dec_share]
        return at + [features(back, step) for step in STEPS for back in range(outer)]

    last_piece, *row_sends = pack(plan, send_places, shapes, 56, pre_x, dec_x, w_kv)
    moving = [first_piece, last_piece]
    row_sends, query, pre_x, dec_x = lax.optimization_barrier((row_sends, dec_q, pre_x, dec_x))

    plan = []
    for back in range(outer):
        for turn in range(cores):
            column, to, base = 2 * cores + back, back * depth, turn * both
            plan.append((0, (pre_share, depth), 2 * turn, column, 0, base, to))
            plan.append((1, (dec_share, depth), 2 * turn + 1, column, 0, base + pre_share, to))

    def own_places():
        core, at = lax.axis_index("tp"), []
        for turn in range(cores):
            which = (core - turn + cores) % cores
            at += [which * pre_share, which * dec_share]
        return at + [features(back, 0) for back in range(outer)]

    total_rows = span + count
    shapes = [jax.ShapeDtypeStruct((total_rows, outer * depth), jnp.bfloat16)]
    (own_rows,) = pack(plan, own_places, shapes, 4, pre_x, dec_x)

    top_c, mixed_c = cached(query, cache, cache_len, heads)
    far = []
    for back in range(1, outer):
        moving = [to_outer(m) for m in moving]
        if back == 1:
            row_sends[-1] = after(row_sends[-1], moving[0], top_c, own_rows)
        far.append([[m] for m in moving])

    got = [to_inner(rows, step) for rows, step in zip(row_sends, STEPS)]
    arrived = [[rows] + [to_core(rows, turn) for turn in range(1, cores)] for rows in got]

    for pieces in far:
        for number, piece in enumerate(pieces):
            if number:
                sent = after(piece[0], pieces[number - 1][-1])
            else:
                sent = piece[0]
            piece += [to_team(sent, turn) for turn in range(1, teams)]

    last = sizes[-1]
    own_rows = after(own_rows, got[-1])
    blocks = [own_rows] + [rows for step in arrived[:-1] for rows in step]
    early = [m for pieces in far for m in pieces[0]]
    first_rows = (inner - 1) * total_rows
    *summed, last_rows = pl.pallas_call(
        functools.partial(early_kernel, outer, teams, last),
        out_shape=[
            *[jax.ShapeDtypeStruct((first_rows, band), jnp.float32)] * teams,
            jax.ShapeDtypeStruct((first_rows, (outer - 1) * last), jnp.bfloat16),
        ],
        in_specs=[VMEM] * (1 + len(early) + len(blocks)),
        out_specs=[VMEM] * (1 + teams),
        scratch_shapes=[
            pltpu.VMEM((first_rows, outer * depth - (outer - 1) * last), jnp.bfloat16)
        ],
        compiler_params=grant(16),
    )(w_kv, *early, *blocks)
    parts = []
    for turn in range(teams):
        pieces = [piece[turn] for some in far for piece in some]
        mine, *others = pl.pallas_call(
            functools.partial(late_kernel, outer, cores, teams, turn),
            out_shape=[jax.ShapeDtypeStruct((total_rows, band), jnp.float32)]
            + [jax.ShapeDtypeStruct((total_rows, band), jnp.bfloat16)] * (inner - 1),
            in_specs=[VMEM] * (3 + len(pieces) + cores),
            out_specs=[VMEM] * inner,
            scratch_shapes=[pltpu.VMEM((total_rows, outer * depth), jnp.bfloat16)],
            compiler_params=grant(12),
        )(w_kv, summed[turn], last_rows, *pieces, *arrived[-1])
        sent = [to_inner(part, step) for part, step in zip(others[::-1], STEPS[::-1])]
        parts += [mine, *sent]
    shifted, own_kv = pl.pallas_call(
        functools.partial(finish_kernel, cores, teams),
        out_shape=[
            jax.ShapeDtypeStruct((span, width), jnp.bfloat16),
            jax.ShapeDtypeStruct((count, width), jnp.bfloat16),
        ],
        in_specs=[VMEM] * (1 + len(parts)),
        out_specs=[VMEM] * 2,
        compiler_params=grant(6),
    )(kv_scale[None, :], *parts)

    def owners(backs):
        rank = lax.axis_index("dp")
        return [
            (rank // inner - back + outer) % outer * inner + (rank % inner ^ step)
            for back in backs
            for step in ((0, 3, 2, 1) if back else range(inner))
        ]

    far = [to_outer(shifted)]
    while len(far) < outer - 1:
        far.append(to_outer(far[-1]))
    blocks = [shifted, to_inner(shifted, 1), to_inner(shifted, 2)]
    handed = to_inner(blocks[2], 1)
    for moved in far:
        blocks += [to_inner(moved, step) if step else moved for step in (0, 3, 2, 1)]
    blocks.append(handed)

    state = jax.ShapeDtypeStruct((heads, REP * count, HD), jnp.float32)
    labels = jax.ShapeDtypeStruct((REP * count, HD), jnp.int32)
    *state, source, live, prompt_kv = pl.pallas_call(
        functools.partial(first_kernel, heads, lambda: owners([0])[:3]),
        out_shape=[state, state, labels, labels, jax.ShapeDtypeStruct((span, width), jnp.bfloat16)],
        in_specs=[SMEM] * 2 + [VMEM] * (3 + 3 + 2),
        out_specs=[VMEM] * 5,
        compiler_params=grant(12),
    )(
        prompt_owner,
        prompt_len,
        sample_rows,
        dec_q,
        top_c,
        mixed_c,
        own_kv,
        *blocks[:3],
    )
    attended = pl.pallas_call(
        functools.partial(second_kernel, heads, lambda: owners(range(1, outer)) + owners([0])[3:]),
        out_shape=jax.ShapeDtypeStruct(dec_q.shape, jnp.bfloat16),
        in_specs=[VMEM] * (5 + len(blocks) - 3),
        out_specs=VMEM,
        compiler_params=grant(12),
    )(dec_q, source, live, *state, *blocks[3:])
    return (attended, prompt_kv)


def solution(mesh):
    in_specs = (
        P(("groups", "dp"), None),
        P(("groups", "dp"), None),
        P("dp", "tp"),
        P("tp"),
        P(("groups", "dp"), "tp"),
        P(("groups", "dp"), None, "tp"),
        P(("groups", "dp")),
        P("groups"),
        P("groups"),
        P("groups", None),
    )
    out_specs = (P(("groups", "dp"), "tp"), P(("groups", "dp"), "tp"))
    body = functools.partial(local, shape=dict(mesh.shape))
    return jax.shard_map(body, mesh=mesh, in_specs=in_specs, out_specs=out_specs, check_vma=False)
```

```python
import functools
import math

import jax
import jax.numpy as jnp
from jax import lax
from jax.experimental import pallas as pl
from jax.experimental.pallas import tpu as pltpu
from jax.sharding import PartitionSpec as P

HD = 128
REP = 12
NEG = -1e30
INNER = 4
STEPS = (1, 2, 3)


def pack_kernel(plan, places, n_in, n_out, *refs):
    ins, outs = refs[:n_in], refs[n_in : n_in + n_out]
    held, (in_sems, out_sems) = refs[n_in + n_out : -2], refs[-2:]
    at = places()
    arriving, leaving = [], []
    for number, (src, shape, row, column, dst, to_row, to_column) in enumerate(plan):
        rows, columns = pl.ds(to_row, shape[0]), pl.ds(to_column, shape[1])
        from_row = pl.multiple_of(at[row], 16)
        from_column = pl.multiple_of(at[column], 128)
        arriving.append(
            pltpu.make_async_copy(
                ins[src].at[pl.ds(from_row, shape[0]), pl.ds(from_column, shape[1])],
                held[dst].at[rows, columns],
                in_sems.at[number],
            )
        )
        leaving.append(
            pltpu.make_async_copy(
                held[dst].at[rows, columns], outs[dst].at[rows, columns], out_sems.at[number]
            )
        )
        arriving[-1].start()
    for came, left in zip(arriving, leaving):
        came.wait()
        left.start()
    for left in leaving:
        left.wait()


def band_columns(teams, turn, band):
    team = lax.axis_index("groups")
    return pl.ds(pl.multiple_of((team - turn + teams) % teams * band, 128), band)


def early_kernel(outer, teams, last, w_ref, *refs):
    n_late = teams + 2
    pieces, refs = refs[: teams * (outer - 1)], refs[teams * (outer - 1) :]
    blocks, sum_refs, (last_ref, row_ref) = refs[:-n_late], refs[-n_late:-2], refs[-2:]
    depth = w_ref.shape[0]
    early = depth - last
    base = 0
    for block in blocks:
        rows = slice(base, base + block.shape[0])
        row_ref[rows, :depth] = block[:, :depth]
        for back in range(1, outer):
            at = depth + (back - 1) * early
            row_ref[rows, at : at + early] = block[:, back * depth : back * depth + early]
            last_ref[rows, (back - 1) * last : back * last] = block[
                :, back * depth + early : (back + 1) * depth
            ]
        base += block.shape[0]
    for turn, sum_ref in enumerate(sum_refs):
        columns = band_columns(teams, turn, sum_ref.shape[1])
        summed = jnp.dot(row_ref[:, :depth], w_ref[:, columns], preferred_element_type=jnp.float32)
        for back in range(1, outer):
            at = depth + (back - 1) * early
            summed = summed + jnp.dot(
                row_ref[:, at : at + early],
                pieces[(back - 1) * teams + turn][...],
                preferred_element_type=jnp.float32,
            )
        sum_ref[...] = summed


def late_kernel(outer, cores, teams, turn, w_ref, sum_ref, last_ref, *refs):
    pieces, refs = refs[: 2 * (outer - 1)], refs[2 * (outer - 1) :]
    halves, outs, row_ref = refs[:cores], refs[cores:-1], refs[-1]
    depth = w_ref.shape[0]
    last = last_ref.shape[1] // (outer - 1)
    each, both = outs[0].shape[0], halves[0].shape[0]
    for number, half in enumerate(halves):
        row_ref[number * both : (number + 1) * both, :] = half[...]
    columns = band_columns(teams, turn, sum_ref.shape[1])
    first = sum_ref[...]
    final = jnp.dot(row_ref[:, :depth], w_ref[:, columns], preferred_element_type=jnp.float32)
    for back in range(1, outer):
        early_piece, last_piece = pieces[2 * back - 2 : 2 * back]
        at = back * depth
        cut = at + depth - last
        final = final + jnp.dot(
            row_ref[:, at:cut], early_piece[...], preferred_element_type=jnp.float32
        )
        final = final + jnp.dot(
            row_ref[:, cut : cut + last], last_piece[...], preferred_element_type=jnp.float32
        )
        first = first + jnp.dot(
            last_ref[:, (back - 1) * last : back * last],
            last_piece[...],
            preferred_element_type=jnp.float32,
        )
    for step, out in enumerate(outs[:-1]):
        out[...] = first[step * each : (step + 1) * each].astype(out.dtype)
    outs[-1][...] = final.astype(outs[-1].dtype)


def finish_kernel(cores, teams, scale_ref, *refs):
    parts, (sent_ref, own_ref) = refs[:-2], refs[-2:]
    span, count = sent_ref.shape[0], own_ref.shape[0]
    pre_share, dec_share = span // cores, count // cores
    both = pre_share + dec_share
    band = scale_ref.shape[1] // teams
    for turn in range(teams):
        columns = band_columns(teams, turn, band)
        own, *others = parts[turn * len(parts) // teams : (turn + 1) * len(parts) // teams]
        summed = own[...]
        for part in others:
            summed = summed + part[...].astype(jnp.float32)
        done = (summed * scale_ref[:, columns]).astype(jnp.bfloat16)
        for share in range(cores):
            which = (lax.axis_index("tp") - share + cores) % cores
            rows = pl.ds(pl.multiple_of(which * pre_share, 16), pre_share)
            sent_ref[rows, columns] = done[share * both : share * both + pre_share]
            own_ref[pl.ds(pl.multiple_of(which * dec_share, 16), dec_share), columns] = done[
                share * both + pre_share : (share + 1) * both
            ]


def match_rows(owner_ref, len_ref, samples_ref, count):
    row = lax.axis_index("dp") * count + lax.broadcasted_iota(jnp.int32, (count, 1), 0)
    source = jnp.zeros((count, 1), jnp.int32)
    live = jnp.zeros((count, 1), jnp.int32)
    for prompt in range(samples_ref.shape[0]):
        hit = jnp.max(
            jnp.where(samples_ref[prompt : prompt + 1, :] == row, 1, 0), -1, keepdims=True
        )
        source = source + hit * owner_ref[prompt]
        live = live + hit * len_ref[prompt]
    return source, live


def absorb(owners, q_ref, source, live, head, blocks, top, mixed, own_ref):
    count, span = q_ref.shape[0], blocks[0].shape[0]
    factor = 1.0 / math.sqrt(HD)
    first = head * REP * HD
    low, mid, high = head * 2 * HD, head * 2 * HD + HD, head * 2 * HD + 2 * HD
    q = jnp.concatenate([q_ref[:, first + r * HD : first + (r + 1) * HD] for r in range(REP)], 0)
    picked = jnp.full((REP * count, span), NEG, jnp.float32)
    place = lax.broadcasted_iota(jnp.int32, (REP * count, span), 1)
    pairs = [slice(at, at + 2) for at in range(0, len(blocks), 2)]
    for pair in pairs:
        scores = lax.dot_general(
            q,
            jnp.concatenate([block[:, low:mid] for block in blocks[pair]], 0),
            (((1,), (1,)), ((), ())),
            preferred_element_type=jnp.float32,
        )
        for at, owner in enumerate(owners[pair]):
            mine = scores[:, at * span : (at + 1) * span]
            picked = jnp.where(source == owner, mine * factor, picked)
    picked = jnp.where(place < live, picked, NEG)
    new = jnp.maximum(jnp.max(picked, -1, keepdims=True), top)
    if own_ref is not None:
        own_k = jnp.concatenate([own_ref[:, low:mid].astype(jnp.float32)] * REP, 0)
        own_v = jnp.concatenate([own_ref[:, mid:high].astype(jnp.float32)] * REP, 0)
        score = jnp.sum(q.astype(jnp.float32) * own_k, -1, keepdims=True) * factor
        new = jnp.maximum(new, score)
    weights = jnp.exp(picked - new)
    kept = jnp.exp(top - new)
    total = kept + jnp.sum(weights, -1, keepdims=True)
    mixed = mixed * kept
    if own_ref is not None:
        weight = jnp.exp(score - new)
        total = total + weight
        mixed = mixed + weight * own_v
    for pair in pairs:
        shares = [jnp.where(source == owner, weights, 0.0) for owner in owners[pair]]
        mixed = mixed + jnp.dot(
            jnp.concatenate(shares, 1).astype(jnp.bfloat16),
            jnp.concatenate([block[:, mid:high] for block in blocks[pair]], 0),
            preferred_element_type=jnp.float32,
        )
    return new + jnp.log(total), mixed / total


def cache_kernel(heads, len_ref, q_ref, cache_ref, top_ref, mixed_ref):
    count, rows = q_ref.shape[0], heads * REP
    factor = 1.0 / math.sqrt(HD)
    query = [q_ref[:, r * HD : (r + 1) * HD].astype(jnp.float32) for r in range(rows)]
    query = jnp.swapaxes(jnp.stack(query), 0, 1).astype(jnp.bfloat16)
    head_of = lax.broadcasted_iota(jnp.int32, (rows, 1), 0) // REP
    spot = lax.broadcasted_iota(jnp.int32, (rows, cache_ref.shape[1]), 1)
    tops, mixes = [], []
    for sample in range(count):
        length = len_ref[pl.program_id(0) * count + sample]
        scores = mixed = None
        for head in range(heads):
            key = cache_ref[sample, :, head * 2 * HD : head * 2 * HD + HD]
            found = lax.dot_general(
                query[sample], key, (((1,), (1,)), ((), ())), preferred_element_type=jnp.float32
            )
            scores = found if head == 0 else jnp.where(head_of == head, found, scores)
        scores = jnp.where(spot < length, scores * factor, NEG)
        top = jnp.max(scores, -1, keepdims=True)
        weights = jnp.exp(scores - top)
        total = jnp.sum(weights, -1, keepdims=True)
        for head in range(heads):
            value = cache_ref[sample, :, head * 2 * HD + HD : (head + 1) * 2 * HD]
            found = jnp.dot(
                weights.astype(jnp.bfloat16), value, preferred_element_type=jnp.float32
            )
            mixed = found if head == 0 else jnp.where(head_of == head, found, mixed)
        tops.append(jnp.broadcast_to(top + jnp.log(total), (rows, HD)))
        mixes.append(mixed / total)
    top_ref[...] = jnp.swapaxes(jnp.stack(tops), 0, 1)
    mixed_ref[...] = jnp.swapaxes(jnp.stack(mixes), 0, 1)


def cached(query, cache, cache_len, heads):
    count, slots, width = cache.shape
    rows, each = heads * REP, 8
    state = jax.ShapeDtypeStruct((rows, count, HD), jnp.float32)
    return pl.pallas_call(
        functools.partial(cache_kernel, heads),
        grid=(count // each,),
        out_shape=[state, state],
        in_specs=[
            SMEM,
            pl.BlockSpec((each, rows * HD), lambda i: (i, 0)),
            pl.BlockSpec((each, slots, width), lambda i: (i, 0, 0)),
        ],
        out_specs=[pl.BlockSpec((rows, each, HD), lambda i: (0, i, 0))] * 2,
        compiler_params=grant(12),
        cost_estimate=pl.CostEstimate(
            flops=4 * count * rows * slots * HD * heads,
            bytes_accessed=2 * cache.size,
            transcendentals=count * rows * slots,
        ),
    )(cache_len, query, cache)


def first_kernel(
    heads, owners, owner_ref, len_ref, samples_ref, q_ref, top_ref, mixed_ref, own_ref, *refs
):
    blocks, (new_top, new_mixed, source_ref, live_ref, prompt_ref) = refs[:-5], refs[-5:]
    prompt_ref[...] = blocks[0][...]
    source, live = match_rows(owner_ref, len_ref, samples_ref, q_ref.shape[0])
    source = jnp.concatenate([source] * REP, 0)
    live = jnp.concatenate([live] * REP, 0)
    source_ref[...] = jnp.broadcast_to(source, source_ref.shape)
    live_ref[...] = jnp.broadcast_to(live, live_ref.shape)
    for head in range(heads):
        mine = slice(head * REP, (head + 1) * REP)
        top = top_ref[mine].reshape(new_top.shape[1:])
        mixed = mixed_ref[mine].reshape(new_top.shape[1:])
        new_top[head], new_mixed[head] = absorb(
            owners(), q_ref, source, live, head, blocks, top, mixed, own_ref
        )


def second_kernel(heads, owners, q_ref, source_ref, live_ref, top_ref, mixed_ref, *refs):
    blocks, out_ref = refs[:-1], refs[-1]
    count = q_ref.shape[0]
    for head in range(heads):
        _, mixed = absorb(
            owners(),
            q_ref,
            source_ref[...],
            live_ref[...],
            head,
            blocks,
            top_ref[head],
            mixed_ref[head],
            None,
        )
        first = head * REP * HD
        for r in range(REP):
            out_ref[:, first + r * HD : first + (r + 1) * HD] = mixed[
                r * count : (r + 1) * count
            ].astype(out_ref.dtype)


VMEM = pl.BlockSpec(memory_space=pltpu.VMEM)
SMEM = pl.BlockSpec(memory_space=pltpu.SMEM)
HBM = pl.BlockSpec(memory_space=pltpu.HBM)


def after(value, *others):
    return lax.optimization_barrier((value, *others))[0]


def grant(mib):
    return pltpu.CompilerParams(vmem_limit_bytes=mib * 1024 * 1024)


def stages(depth):
    unit = 128
    first = max(unit, depth // 2 // unit * unit)
    return (first, depth - first)


def local(
    pre_x,
    dec_x,
    w_kv,
    kv_scale,
    dec_q,
    cache,
    cache_len,
    prompt_owner,
    prompt_len,
    sample_rows,
    *,
    shape,
):
    teams, ranks, cores = shape["groups"], shape["dp"], shape["tp"]
    inner = INNER
    outer = ranks // inner
    span, features = pre_x.shape
    count = dec_x.shape[0]
    depth, width = w_kv.shape
    heads = width // (2 * HD)
    band = width // teams

    def to_inner(value, step):
        pairs = [(r, r // inner * inner + (r % inner ^ step)) for r in range(ranks)]
        return lax.ppermute(value, "dp", pairs)

    def to_outer(value, step=1):
        pairs = [(r, (r + step * inner) % ranks) for r in range(ranks)]
        return lax.ppermute(value, "dp", pairs)

    def to_team(value, step):
        return lax.ppermute(value, "groups", [(i, (i + step) % teams) for i in range(teams)])

    def to_core(value, step):
        return lax.ppermute(value, "tp", [(i, (i + step) % cores) for i in range(cores)])

    def pack(plan, places, shapes, mib, *arrays):
        sems = pltpu.SemaphoreType.DMA((len(plan),))
        return pl.pallas_call(
            functools.partial(pack_kernel, plan, places, len(arrays), len(shapes)),
            out_shape=shapes,
            in_specs=[HBM] * len(arrays),
            out_specs=[HBM] * len(shapes),
            scratch_shapes=[pltpu.VMEM(s.shape, s.dtype) for s in shapes] + [sems, sems],
            compiler_params=grant(mib),
        )(*arrays)

    sizes = stages(depth)
    pre_share, dec_share = span // cores, count // cores
    both = pre_share + dec_share
    def features(back, step):
        rank = lax.axis_index("dp")
        return ((rank // inner - back + outer) % outer * inner + (rank % inner ^ step)) * depth

    def band_place():
        return [0, lax.axis_index("groups") * band]

    shape = jax.ShapeDtypeStruct((sizes[0], band), jnp.bfloat16)
    (first_piece,) = pack([(0, (sizes[0], band), 0, 1, 0, 0, 0)], band_place, [shape], 56, w_kv)
    first_piece, pre_x, dec_x, w_kv = lax.optimization_barrier((first_piece, pre_x, dec_x, w_kv))

    plan = [(2, (sizes[1], band), 0, 1, 0, 0, 0)]
    shapes = [jax.ShapeDtypeStruct((sizes[1], band), jnp.bfloat16)]
    for number in range(inner - 1):
        for back in range(outer):
            column, to = 4 + number * outer + back, back * depth
            plan.append((0, (pre_share, depth), 2, column, len(shapes), 0, to))
            plan.append((1, (dec_share, depth), 3, column, len(shapes), pre_share, to))
        shapes.append(jax.ShapeDtypeStruct((both, outer * depth), jnp.bfloat16))

    def send_places():
        core = lax.axis_index("tp")
        at = [sizes[0], lax.axis_index("groups") * band, core * pre_share, core * dec_share]
        return at + [features(back, step) for step in STEPS for back in range(outer)]

    last_piece, *row_sends = pack(plan, send_places, shapes, 56, pre_x, dec_x, w_kv)
    moving = [first_piece, last_piece]
    row_sends, query, pre_x, dec_x = lax.optimization_barrier((row_sends, dec_q, pre_x, dec_x))

    plan = []
    for back in range(outer):
        for turn in range(cores):
            column, to, base = 2 * cores + back, back * depth, turn * both
            plan.append((0, (pre_share, depth), 2 * turn, column, 0, base, to))
            plan.append((1, (dec_share, depth), 2 * turn + 1, column, 0, base + pre_share, to))

    def own_places():
        core, at = lax.axis_index("tp"), []
        for turn in range(cores):
            which = (core - turn + cores) % cores
            at += [which * pre_share, which * dec_share]
        return at + [features(back, 0) for back in range(outer)]

    total_rows = span + count
    shapes = [jax.ShapeDtypeStruct((total_rows, outer * depth), jnp.bfloat16)]
    (own_rows,) = pack(plan, own_places, shapes, 4, pre_x, dec_x)

    top_c, mixed_c = cached(query, cache, cache_len, heads)
    far = []
    for back in range(1, outer):
        moving = [to_outer(m) for m in moving]
        if back == 1:
            row_sends[-1] = after(row_sends[-1], moving[0], top_c, own_rows)
        far.append([[m] for m in moving])

    got = [to_inner(rows, step) for rows, step in zip(row_sends, STEPS)]
    arrived = [[rows] + [to_core(rows, turn) for turn in range(1, cores)] for rows in got]

    for pieces in far:
        for number, piece in enumerate(pieces):
            if number:
                sent = after(piece[0], pieces[number - 1][-1])
            else:
                sent = piece[0]
            piece += [to_team(sent, turn) for turn in range(1, teams)]

    last = sizes[-1]
    own_rows = after(own_rows, got[-1])
    blocks = [own_rows] + [rows for step in arrived[:-1] for rows in step]
    early = [m for pieces in far for m in pieces[0]]
    first_rows = (inner - 1) * total_rows
    *summed, last_rows = pl.pallas_call(
        functools.partial(early_kernel, outer, teams, last),
        out_shape=[
            *[jax.ShapeDtypeStruct((first_rows, band), jnp.float32)] * teams,
            jax.ShapeDtypeStruct((first_rows, (outer - 1) * last), jnp.bfloat16),
        ],
        in_specs=[VMEM] * (1 + len(early) + len(blocks)),
        out_specs=[VMEM] * (1 + teams),
        scratch_shapes=[
            pltpu.VMEM((first_rows, outer * depth - (outer - 1) * last), jnp.bfloat16)
        ],
        compiler_params=grant(16),
    )(w_kv, *early, *blocks)
    parts = []
    for turn in range(teams):
        pieces = [piece[turn] for some in far for piece in some]
        mine, *others = pl.pallas_call(
            functools.partial(late_kernel, outer, cores, teams, turn),
            out_shape=[jax.ShapeDtypeStruct((total_rows, band), jnp.float32)]
            + [jax.ShapeDtypeStruct((total_rows, band), jnp.bfloat16)] * (inner - 1),
            in_specs=[VMEM] * (3 + len(pieces) + cores),
            out_specs=[VMEM] * inner,
            scratch_shapes=[pltpu.VMEM((total_rows, outer * depth), jnp.bfloat16)],
            compiler_params=grant(12),
        )(w_kv, summed[turn], last_rows, *pieces, *arrived[-1])
        sent = [to_inner(part, step) for part, step in zip(others[::-1], STEPS[::-1])]
        parts += [mine, *sent]
    shifted, own_kv = pl.pallas_call(
        functools.partial(finish_kernel, cores, teams),
        out_shape=[
            jax.ShapeDtypeStruct((span, width), jnp.bfloat16),
            jax.ShapeDtypeStruct((count, width), jnp.bfloat16),
        ],
        in_specs=[VMEM] * (1 + len(parts)),
        out_specs=[VMEM] * 2,
        compiler_params=grant(6),
    )(kv_scale[None, :], *parts)

    def owners(backs):
        rank = lax.axis_index("dp")
        return [
            (rank // inner - back + outer) % outer * inner + (rank % inner ^ step)
            for back in backs
            for step in ((0, 3, 2, 1) if back else range(inner))
        ]

    blocks = []
    for back in range(outer):
        if back:
            shifted = to_outer(shifted)
        if back:
            blocks += [to_inner(shifted, step) if step else shifted for step in (0, 3, 2, 1)]
        else:
            near = [shifted, to_inner(shifted, 1), to_inner(shifted, 2)]
            blocks += near + [to_inner(after(near[2], near[1]), 1)]

    state = jax.ShapeDtypeStruct((heads, REP * count, HD), jnp.float32)
    labels = jax.ShapeDtypeStruct((REP * count, HD), jnp.int32)
    *state, source, live, prompt_kv = pl.pallas_call(
        functools.partial(first_kernel, heads, lambda: owners([0])[:3]),
        out_shape=[state, state, labels, labels, jax.ShapeDtypeStruct((span, width), jnp.bfloat16)],
        in_specs=[SMEM] * 2 + [VMEM] * (3 + 3 + 2),
        out_specs=[VMEM] * 5,
        compiler_params=grant(12),
    )(
        prompt_owner,
        prompt_len,
        sample_rows,
        dec_q,
        top_c,
        mixed_c,
        own_kv,
        *blocks[:3],
    )
    attended = pl.pallas_call(
        functools.partial(second_kernel, heads, lambda: owners(range(outer))[3:]),
        out_shape=jax.ShapeDtypeStruct(dec_q.shape, jnp.bfloat16),
        in_specs=[VMEM] * (5 + len(blocks) - 3),
        out_specs=VMEM,
        compiler_params=grant(12),
    )(dec_q, source, live, *state, *blocks[3:])
    return (attended, prompt_kv)


def solution(mesh):
    in_specs = (
        P(("groups", "dp"), None),
        P(("groups", "dp"), None),
        P("dp", "tp"),
        P("tp"),
        P(("groups", "dp"), "tp"),
        P(("groups", "dp"), None, "tp"),
        P(("groups", "dp")),
        P("groups"),
        P("groups"),
        P("groups", None),
    )
    out_specs = (P(("groups", "dp"), "tp"), P(("groups", "dp"), "tp"))
    body = functools.partial(local, shape=dict(mesh.shape))
    return jax.shard_map(body, mesh=mesh, in_specs=in_specs, out_specs=out_specs, check_vma=False)
```

```python
import functools
import math

import jax
import jax.numpy as jnp
from jax import lax
from jax.experimental import pallas as pl
from jax.experimental.pallas import tpu as pltpu
from jax.sharding import PartitionSpec as P

HD = 128
REP = 12
NEG = -1e30
INNER = 4
STEPS = (1, 2, 3)


def pack_kernel(plan, places, n_in, n_out, *refs):
    ins, outs = refs[:n_in], refs[n_in : n_in + n_out]
    held, (in_sems, out_sems) = refs[n_in + n_out : -2], refs[-2:]
    at = places()
    arriving, leaving = [], []
    for number, (src, shape, row, column, dst, to_row, to_column) in enumerate(plan):
        rows, columns = pl.ds(to_row, shape[0]), pl.ds(to_column, shape[1])
        from_row = pl.multiple_of(at[row], 16)
        from_column = pl.multiple_of(at[column], 128)
        arriving.append(
            pltpu.make_async_copy(
                ins[src].at[pl.ds(from_row, shape[0]), pl.ds(from_column, shape[1])],
                held[dst].at[rows, columns],
                in_sems.at[number],
            )
        )
        leaving.append(
            pltpu.make_async_copy(
                held[dst].at[rows, columns], outs[dst].at[rows, columns], out_sems.at[number]
            )
        )
        arriving[-1].start()
    for came, left in zip(arriving, leaving):
        came.wait()
        left.start()
    for left in leaving:
        left.wait()


def band_columns(teams, turn, band):
    team = lax.axis_index("groups")
    return pl.ds(pl.multiple_of((team - turn + teams) % teams * band, 128), band)


def early_kernel(outer, teams, last, w_ref, *refs):
    n_late = teams + 2
    pieces, refs = refs[: teams * (outer - 1)], refs[teams * (outer - 1) :]
    blocks, sum_refs, (last_ref, row_ref) = refs[:-n_late], refs[-n_late:-2], refs[-2:]
    depth = w_ref.shape[0]
    early = depth - last
    base = 0
    for block in blocks:
        rows = slice(base, base + block.shape[0])
        row_ref[rows, :depth] = block[:, :depth]
        for back in range(1, outer):
            at = depth + (back - 1) * early
            row_ref[rows, at : at + early] = block[:, back * depth : back * depth + early]
            last_ref[rows, (back - 1) * last : back * last] = block[
                :, back * depth + early : (back + 1) * depth
            ]
        base += block.shape[0]
    for turn, sum_ref in enumerate(sum_refs):
        columns = band_columns(teams, turn, sum_ref.shape[1])
        summed = jnp.dot(row_ref[:, :depth], w_ref[:, columns], preferred_element_type=jnp.float32)
        for back in range(1, outer):
            at = depth + (back - 1) * early
            summed = summed + jnp.dot(
                row_ref[:, at : at + early],
                pieces[(back - 1) * teams + turn][...],
                preferred_element_type=jnp.float32,
            )
        sum_ref[...] = summed


def late_kernel(outer, cores, teams, turn, w_ref, sum_ref, last_ref, *refs):
    pieces, refs = refs[: 2 * (outer - 1)], refs[2 * (outer - 1) :]
    halves, outs, row_ref = refs[:cores], refs[cores:-1], refs[-1]
    depth = w_ref.shape[0]
    last = last_ref.shape[1] // (outer - 1)
    each, both = outs[0].shape[0], halves[0].shape[0]
    for number, half in enumerate(halves):
        row_ref[number * both : (number + 1) * both, :] = half[...]
    columns = band_columns(teams, turn, sum_ref.shape[1])
    first = sum_ref[...]
    final = jnp.dot(row_ref[:, :depth], w_ref[:, columns], preferred_element_type=jnp.float32)
    for back in range(1, outer):
        early_piece, last_piece = pieces[2 * back - 2 : 2 * back]
        at = back * depth
        cut = at + depth - last
        final = final + jnp.dot(
            row_ref[:, at:cut], early_piece[...], preferred_element_type=jnp.float32
        )
        final = final + jnp.dot(
            row_ref[:, cut : cut + last], last_piece[...], preferred_element_type=jnp.float32
        )
        first = first + jnp.dot(
            last_ref[:, (back - 1) * last : back * last],
            last_piece[...],
            preferred_element_type=jnp.float32,
        )
    for step, out in enumerate(outs[:-1]):
        out[...] = first[step * each : (step + 1) * each].astype(out.dtype)
    outs[-1][...] = final.astype(outs[-1].dtype)


def finish_kernel(cores, teams, scale_ref, *refs):
    parts, (sent_ref, own_ref) = refs[:-2], refs[-2:]
    span, count = sent_ref.shape[0], own_ref.shape[0]
    pre_share, dec_share = span // cores, count // cores
    both = pre_share + dec_share
    band = scale_ref.shape[1] // teams
    for turn in range(teams):
        columns = band_columns(teams, turn, band)
        own, *others = parts[turn * len(parts) // teams : (turn + 1) * len(parts) // teams]
        summed = own[...]
        for part in others:
            summed = summed + part[...].astype(jnp.float32)
        done = (summed * scale_ref[:, columns]).astype(jnp.bfloat16)
        for share in range(cores):
            which = (lax.axis_index("tp") - share + cores) % cores
            rows = pl.ds(pl.multiple_of(which * pre_share, 16), pre_share)
            sent_ref[rows, columns] = done[share * both : share * both + pre_share]
            own_ref[pl.ds(pl.multiple_of(which * dec_share, 16), dec_share), columns] = done[
                share * both + pre_share : (share + 1) * both
            ]


def match_rows(owner_ref, len_ref, samples_ref, count):
    row = lax.axis_index("dp") * count + lax.broadcasted_iota(jnp.int32, (count, 1), 0)
    source = jnp.zeros((count, 1), jnp.int32)
    live = jnp.zeros((count, 1), jnp.int32)
    for prompt in range(samples_ref.shape[0]):
        hit = jnp.max(
            jnp.where(samples_ref[prompt : prompt + 1, :] == row, 1, 0), -1, keepdims=True
        )
        source = source + hit * owner_ref[prompt]
        live = live + hit * len_ref[prompt]
    return source, live


def absorb(owners, q_ref, source, live, head, blocks, top, mixed, own_ref):
    count, span = q_ref.shape[0], blocks[0].shape[0]
    factor = 1.0 / math.sqrt(HD)
    first = head * REP * HD
    low, mid, high = head * 2 * HD, head * 2 * HD + HD, head * 2 * HD + 2 * HD
    q = jnp.concatenate([q_ref[:, first + r * HD : first + (r + 1) * HD] for r in range(REP)], 0)
    picked = jnp.full((REP * count, span), NEG, jnp.float32)
    place = lax.broadcasted_iota(jnp.int32, (REP * count, span), 1)
    pairs = [slice(at, at + 2) for at in range(0, len(blocks), 2)]
    for pair in pairs:
        scores = lax.dot_general(
            q,
            jnp.concatenate([block[:, low:mid] for block in blocks[pair]], 0),
            (((1,), (1,)), ((), ())),
            preferred_element_type=jnp.float32,
        )
        for at, owner in enumerate(owners[pair]):
            mine = scores[:, at * span : (at + 1) * span]
            picked = jnp.where(source == owner, mine * factor, picked)
    picked = jnp.where(place < live, picked, NEG)
    new = jnp.maximum(jnp.max(picked, -1, keepdims=True), top)
    if own_ref is not None:
        own_k = jnp.concatenate([own_ref[:, low:mid].astype(jnp.float32)] * REP, 0)
        own_v = jnp.concatenate([own_ref[:, mid:high].astype(jnp.float32)] * REP, 0)
        score = jnp.sum(q.astype(jnp.float32) * own_k, -1, keepdims=True) * factor
        new = jnp.maximum(new, score)
    weights = jnp.exp(picked - new)
    kept = jnp.exp(top - new)
    total = kept + jnp.sum(weights, -1, keepdims=True)
    mixed = mixed * kept
    if own_ref is not None:
        weight = jnp.exp(score - new)
        total = total + weight
        mixed = mixed + weight * own_v
    for pair in pairs:
        shares = [jnp.where(source == owner, weights, 0.0) for owner in owners[pair]]
        mixed = mixed + jnp.dot(
            jnp.concatenate(shares, 1).astype(jnp.bfloat16),
            jnp.concatenate([block[:, mid:high] for block in blocks[pair]], 0),
            preferred_element_type=jnp.float32,
        )
    return new + jnp.log(total), mixed / total


def cache_kernel(heads, len_ref, q_ref, cache_ref, top_ref, mixed_ref, query_ref):
    count, rows = cache_ref.shape[0], heads * REP
    factor = 1.0 / math.sqrt(HD)

    @pl.when(pl.program_id(0) == 0)
    def _():
        query = [q_ref[:, r * HD : (r + 1) * HD].astype(jnp.float32) for r in range(rows)]
        query_ref[...] = jnp.swapaxes(jnp.stack(query), 0, 1)

    query = query_ref[pl.ds(pl.program_id(0) * count, count)].astype(jnp.bfloat16)
    head_of = lax.broadcasted_iota(jnp.int32, (rows, 1), 0) // REP
    spot = lax.broadcasted_iota(jnp.int32, (rows, cache_ref.shape[1]), 1)
    tops, mixes = [], []
    for sample in range(count):
        length = len_ref[pl.program_id(0) * count + sample]
        scores = mixed = None
        for head in range(heads):
            key = cache_ref[sample, :, head * 2 * HD : head * 2 * HD + HD]
            found = lax.dot_general(
                query[sample], key, (((1,), (1,)), ((), ())), preferred_element_type=jnp.float32
            )
            scores = found if head == 0 else jnp.where(head_of == head, found, scores)
        scores = jnp.where(spot < length, scores * factor, NEG)
        top = jnp.max(scores, -1, keepdims=True)
        weights = jnp.exp(scores - top)
        total = jnp.sum(weights, -1, keepdims=True)
        for head in range(heads):
            value = cache_ref[sample, :, head * 2 * HD + HD : (head + 1) * 2 * HD]
            found = jnp.dot(
                weights.astype(jnp.bfloat16), value, preferred_element_type=jnp.float32
            )
            mixed = found if head == 0 else jnp.where(head_of == head, found, mixed)
        tops.append(jnp.broadcast_to(top + jnp.log(total), (rows, HD)))
        mixes.append(mixed / total)
    top_ref[...] = jnp.swapaxes(jnp.stack(tops), 0, 1)
    mixed_ref[...] = jnp.swapaxes(jnp.stack(mixes), 0, 1)


def cached(query, cache, cache_len, heads):
    count, slots, width = cache.shape
    rows, each = heads * REP, 8
    state = jax.ShapeDtypeStruct((rows, count, HD), jnp.float32)
    return pl.pallas_call(
        functools.partial(cache_kernel, heads),
        grid=(count // each,),
        out_shape=[state, state],
        in_specs=[
            SMEM,
            pl.BlockSpec((count, rows * HD), lambda i: (0, 0)),
            pl.BlockSpec((each, slots, width), lambda i: (i, 0, 0)),
        ],
        out_specs=[pl.BlockSpec((rows, each, HD), lambda i: (0, i, 0))] * 2,
        scratch_shapes=[pltpu.VMEM((count, rows, HD), jnp.float32)],
        compiler_params=grant(12),
        cost_estimate=pl.CostEstimate(
            flops=4 * count * rows * slots * HD * heads,
            bytes_accessed=2 * cache.size,
            transcendentals=count * rows * slots,
        ),
    )(cache_len, query, cache)


def first_kernel(
    heads, owners, owner_ref, len_ref, samples_ref, q_ref, top_ref, mixed_ref, own_ref, *refs
):
    blocks, (new_top, new_mixed, source_ref, live_ref, prompt_ref) = refs[:-5], refs[-5:]
    prompt_ref[...] = blocks[0][...]
    source, live = match_rows(owner_ref, len_ref, samples_ref, q_ref.shape[0])
    source = jnp.concatenate([source] * REP, 0)
    live = jnp.concatenate([live] * REP, 0)
    source_ref[...] = jnp.broadcast_to(source, source_ref.shape)
    live_ref[...] = jnp.broadcast_to(live, live_ref.shape)
    for head in range(heads):
        mine = slice(head * REP, (head + 1) * REP)
        top = top_ref[mine].reshape(new_top.shape[1:])
        mixed = mixed_ref[mine].reshape(new_top.shape[1:])
        new_top[head], new_mixed[head] = absorb(
            owners(), q_ref, source, live, head, blocks, top, mixed, own_ref
        )


def second_kernel(heads, owners, q_ref, source_ref, live_ref, top_ref, mixed_ref, *refs):
    blocks, out_ref = refs[:-1], refs[-1]
    count = q_ref.shape[0]
    for head in range(heads):
        _, mixed = absorb(
            owners(),
            q_ref,
            source_ref[...],
            live_ref[...],
            head,
            blocks,
            top_ref[head],
            mixed_ref[head],
            None,
        )
        first = head * REP * HD
        for r in range(REP):
            out_ref[:, first + r * HD : first + (r + 1) * HD] = mixed[
                r * count : (r + 1) * count
            ].astype(out_ref.dtype)


VMEM = pl.BlockSpec(memory_space=pltpu.VMEM)
SMEM = pl.BlockSpec(memory_space=pltpu.SMEM)
HBM = pl.BlockSpec(memory_space=pltpu.HBM)


def after(value, *others):
    return lax.optimization_barrier((value, *others))[0]


def grant(mib):
    return pltpu.CompilerParams(vmem_limit_bytes=mib * 1024 * 1024)


def stages(depth):
    unit = 128
    first = max(unit, depth * 7 // 12 // unit * unit)
    return (first, depth - first)


def local(
    pre_x,
    dec_x,
    w_kv,
    kv_scale,
    dec_q,
    cache,
    cache_len,
    prompt_owner,
    prompt_len,
    sample_rows,
    *,
    shape,
):
    teams, ranks, cores = shape["groups"], shape["dp"], shape["tp"]
    inner = INNER
    outer = ranks // inner
    span, features = pre_x.shape
    count = dec_x.shape[0]
    depth, width = w_kv.shape
    heads = width // (2 * HD)
    band = width // teams

    def to_inner(value, step):
        pairs = [(r, r // inner * inner + (r % inner ^ step)) for r in range(ranks)]
        return lax.ppermute(value, "dp", pairs)

    def to_outer(value, step=1):
        pairs = [(r, (r + step * inner) % ranks) for r in range(ranks)]
        return lax.ppermute(value, "dp", pairs)

    def to_team(value, step):
        return lax.ppermute(value, "groups", [(i, (i + step) % teams) for i in range(teams)])

    def to_core(value, step):
        return lax.ppermute(value, "tp", [(i, (i + step) % cores) for i in range(cores)])

    def pack(plan, places, shapes, mib, *arrays):
        sems = pltpu.SemaphoreType.DMA((len(plan),))
        return pl.pallas_call(
            functools.partial(pack_kernel, plan, places, len(arrays), len(shapes)),
            out_shape=shapes,
            in_specs=[HBM] * len(arrays),
            out_specs=[HBM] * len(shapes),
            scratch_shapes=[pltpu.VMEM(s.shape, s.dtype) for s in shapes] + [sems, sems],
            compiler_params=grant(mib),
        )(*arrays)

    sizes = stages(depth)
    pre_share, dec_share = span // cores, count // cores
    both = pre_share + dec_share
    def features(back, step):
        rank = lax.axis_index("dp")
        return ((rank // inner - back + outer) % outer * inner + (rank % inner ^ step)) * depth

    def band_place():
        return [0, lax.axis_index("groups") * band]

    shape = jax.ShapeDtypeStruct((sizes[0], band), jnp.bfloat16)
    (first_piece,) = pack([(0, (sizes[0], band), 0, 1, 0, 0, 0)], band_place, [shape], 56, w_kv)
    first_piece, pre_x, dec_x, w_kv = lax.optimization_barrier((first_piece, pre_x, dec_x, w_kv))

    plan = [(2, (sizes[1], band), 0, 1, 0, 0, 0)]
    shapes = [jax.ShapeDtypeStruct((sizes[1], band), jnp.bfloat16)]
    for number in range(inner - 1):
        for back in range(outer):
            column, to = 4 + number * outer + back, back * depth
            plan.append((0, (pre_share, depth), 2, column, len(shapes), 0, to))
            plan.append((1, (dec_share, depth), 3, column, len(shapes), pre_share, to))
        shapes.append(jax.ShapeDtypeStruct((both, outer * depth), jnp.bfloat16))

    def send_places():
        core = lax.axis_index("tp")
        at = [sizes[0], lax.axis_index("groups") * band, core * pre_share, core * dec_share]
        return at + [features(back, step) for step in STEPS for back in range(outer)]

    last_piece, *row_sends = pack(plan, send_places, shapes, 56, pre_x, dec_x, w_kv)
    moving = [first_piece, last_piece]
    row_sends, query, pre_x, dec_x = lax.optimization_barrier((row_sends, dec_q, pre_x, dec_x))

    plan = []
    for back in range(outer):
        for turn in range(cores):
            column, to, base = 2 * cores + back, back * depth, turn * both
            plan.append((0, (pre_share, depth), 2 * turn, column, 0, base, to))
            plan.append((1, (dec_share, depth), 2 * turn + 1, column, 0, base + pre_share, to))

    def own_places():
        core, at = lax.axis_index("tp"), []
        for turn in range(cores):
            which = (core - turn + cores) % cores
            at += [which * pre_share, which * dec_share]
        return at + [features(back, 0) for back in range(outer)]

    total_rows = span + count
    shapes = [jax.ShapeDtypeStruct((total_rows, outer * depth), jnp.bfloat16)]
    (own_rows,) = pack(plan, own_places, shapes, 4, pre_x, dec_x)

    top_c, mixed_c = cached(query, cache, cache_len, heads)
    far = []
    for back in range(1, outer):
        moving = [to_outer(m) for m in moving]
        if back == 1:
            row_sends[-1] = after(row_sends[-1], moving[0], top_c, own_rows)
        far.append([[m] for m in moving])

    got = [to_inner(rows, step) for rows, step in zip(row_sends, STEPS)]
    arrived = [[rows] + [to_core(rows, turn) for turn in range(1, cores)] for rows in got]

    for pieces in far:
        for number, piece in enumerate(pieces):
            if number:
                sent = after(piece[0], pieces[number - 1][-1])
            else:
                sent = piece[0]
            piece += [to_team(sent, turn) for turn in range(1, teams)]

    last = sizes[-1]
    own_rows = after(own_rows, got[-1])
    blocks = [own_rows] + [rows for step in arrived[:-1] for rows in step]
    early = [m for pieces in far for m in pieces[0]]
    first_rows = (inner - 1) * total_rows
    *summed, last_rows = pl.pallas_call(
        functools.partial(early_kernel, outer, teams, last),
        out_shape=[
            *[jax.ShapeDtypeStruct((first_rows, band), jnp.float32)] * teams,
            jax.ShapeDtypeStruct((first_rows, (outer - 1) * last), jnp.bfloat16),
        ],
        in_specs=[VMEM] * (1 + len(early) + len(blocks)),
        out_specs=[VMEM] * (1 + teams),
        scratch_shapes=[
            pltpu.VMEM((first_rows, outer * depth - (outer - 1) * last), jnp.bfloat16)
        ],
        compiler_params=grant(16),
    )(w_kv, *early, *blocks)
    parts = []
    for turn in range(teams):
        pieces = [piece[turn] for some in far for piece in some]
        mine, *others = pl.pallas_call(
            functools.partial(late_kernel, outer, cores, teams, turn),
            out_shape=[jax.ShapeDtypeStruct((total_rows, band), jnp.float32)]
            + [jax.ShapeDtypeStruct((total_rows, band), jnp.bfloat16)] * (inner - 1),
            in_specs=[VMEM] * (3 + len(pieces) + cores),
            out_specs=[VMEM] * inner,
            scratch_shapes=[pltpu.VMEM((total_rows, outer * depth), jnp.bfloat16)],
            compiler_params=grant(12),
        )(w_kv, summed[turn], last_rows, *pieces, *arrived[-1])
        sent = [to_inner(part, step) for part, step in zip(others[::-1], STEPS[::-1])]
        parts += [mine, *sent]
    shifted, own_kv = pl.pallas_call(
        functools.partial(finish_kernel, cores, teams),
        out_shape=[
            jax.ShapeDtypeStruct((span, width), jnp.bfloat16),
            jax.ShapeDtypeStruct((count, width), jnp.bfloat16),
        ],
        in_specs=[VMEM] * (1 + len(parts)),
        out_specs=[VMEM] * 2,
        compiler_params=grant(6),
    )(kv_scale[None, :], *parts)

    def owners(backs):
        rank = lax.axis_index("dp")
        return [
            (rank // inner - back + outer) % outer * inner + (rank % inner ^ step)
            for back in backs
            for step in ((0, 3, 2, 1) if back else range(inner))
        ]

    blocks = []
    for back in range(outer):
        if back:
            shifted = to_outer(shifted)
        if back:
            blocks += [to_inner(shifted, step) if step else shifted for step in (0, 3, 2, 1)]
        else:
            near = [shifted, to_inner(shifted, 1), to_inner(shifted, 2)]
            blocks += near + [to_inner(after(near[2], near[1]), 1)]

    state = jax.ShapeDtypeStruct((heads, REP * count, HD), jnp.float32)
    labels = jax.ShapeDtypeStruct((REP * count, HD), jnp.int32)
    *state, source, live, prompt_kv = pl.pallas_call(
        functools.partial(first_kernel, heads, lambda: owners([0])[:3]),
        out_shape=[state, state, labels, labels, jax.ShapeDtypeStruct((span, width), jnp.bfloat16)],
        in_specs=[SMEM] * 2 + [VMEM] * (3 + 3 + 2),
        out_specs=[VMEM] * 5,
        compiler_params=grant(12),
    )(
        prompt_owner,
        prompt_len,
        sample_rows,
        dec_q,
        top_c,
        mixed_c,
        own_kv,
        *blocks[:3],
    )
    attended = pl.pallas_call(
        functools.partial(second_kernel, heads, lambda: owners(range(outer))[3:]),
        out_shape=jax.ShapeDtypeStruct(dec_q.shape, jnp.bfloat16),
        in_specs=[VMEM] * (5 + len(blocks) - 3),
        out_specs=VMEM,
        compiler_params=grant(12),
    )(dec_q, source, live, *state, *blocks[3:])
    return (attended, prompt_kv)


def solution(mesh):
    in_specs = (
        P(("groups", "dp"), None),
        P(("groups", "dp"), None),
        P("dp", "tp"),
        P("tp"),
        P(("groups", "dp"), "tp"),
        P(("groups", "dp"), None, "tp"),
        P(("groups", "dp")),
        P("groups"),
        P("groups"),
        P("groups", None),
    )
    out_specs = (P(("groups", "dp"), "tp"), P(("groups", "dp"), "tp"))
    body = functools.partial(local, shape=dict(mesh.shape))
    return jax.shard_map(body, mesh=mesh, in_specs=in_specs, out_specs=out_specs, check_vma=False)
```

```python
import functools
import math

import jax
import jax.numpy as jnp
from jax import lax
from jax.experimental import pallas as pl
from jax.experimental.pallas import tpu as pltpu
from jax.sharding import PartitionSpec as P

HD = 128
REP = 12
NEG = -1e30
INNER = 4
STEPS = (1, 2, 3)


def pack_kernel(plan, places, n_in, n_out, *refs):
    ins, outs = refs[:n_in], refs[n_in : n_in + n_out]
    held, (in_sems, out_sems) = refs[n_in + n_out : -2], refs[-2:]
    at = places()
    arriving, leaving = [], []
    for number, (src, shape, row, column, dst, to_row, to_column) in enumerate(plan):
        rows, columns = pl.ds(to_row, shape[0]), pl.ds(to_column, shape[1])
        from_row = pl.multiple_of(at[row], 16)
        from_column = pl.multiple_of(at[column], 128)
        arriving.append(
            pltpu.make_async_copy(
                ins[src].at[pl.ds(from_row, shape[0]), pl.ds(from_column, shape[1])],
                held[dst].at[rows, columns],
                in_sems.at[number],
            )
        )
        leaving.append(
            pltpu.make_async_copy(
                held[dst].at[rows, columns], outs[dst].at[rows, columns], out_sems.at[number]
            )
        )
        arriving[-1].start()
    for came, left in zip(arriving, leaving):
        came.wait()
        left.start()
    for left in leaving:
        left.wait()


def band_columns(teams, turn, band):
    team = lax.axis_index("groups")
    return pl.ds(pl.multiple_of((team - turn + teams) % teams * band, 128), band)


def early_kernel(outer, teams, last, w_ref, *refs):
    n_late = teams + 2
    pieces, refs = refs[: teams * (outer - 1)], refs[teams * (outer - 1) :]
    blocks, sum_refs, (last_ref, row_ref) = refs[:-n_late], refs[-n_late:-2], refs[-2:]
    depth = w_ref.shape[0]
    early = depth - last
    base = 0
    for block in blocks:
        rows = slice(base, base + block.shape[0])
        row_ref[rows, :depth] = block[:, :depth]
        for back in range(1, outer):
            at = depth + (back - 1) * early
            row_ref[rows, at : at + early] = block[:, back * depth : back * depth + early]
            last_ref[rows, (back - 1) * last : back * last] = block[
                :, back * depth + early : (back + 1) * depth
            ]
        base += block.shape[0]
    for turn, sum_ref in enumerate(sum_refs):
        columns = band_columns(teams, turn, sum_ref.shape[1])
        summed = jnp.dot(row_ref[:, :depth], w_ref[:, columns], preferred_element_type=jnp.float32)
        for back in range(1, outer):
            at = depth + (back - 1) * early
            summed = summed + jnp.dot(
                row_ref[:, at : at + early],
                pieces[(back - 1) * teams + turn][...],
                preferred_element_type=jnp.float32,
            )
        sum_ref[...] = summed


def late_kernel(outer, cores, teams, turn, w_ref, sum_ref, last_ref, *refs):
    pieces, refs = refs[: 2 * (outer - 1)], refs[2 * (outer - 1) :]
    halves, outs, row_ref = refs[:cores], refs[cores:-1], refs[-1]
    depth = w_ref.shape[0]
    last = last_ref.shape[1] // (outer - 1)
    each, both = outs[0].shape[0], halves[0].shape[0]
    for number, half in enumerate(halves):
        row_ref[number * both : (number + 1) * both, :] = half[...]
    columns = band_columns(teams, turn, sum_ref.shape[1])
    first = sum_ref[...]
    final = jnp.dot(row_ref[:, :depth], w_ref[:, columns], preferred_element_type=jnp.float32)
    for back in range(1, outer):
        early_piece, last_piece = pieces[2 * back - 2 : 2 * back]
        at = back * depth
        cut = at + depth - last
        final = final + jnp.dot(
            row_ref[:, at:cut], early_piece[...], preferred_element_type=jnp.float32
        )
        final = final + jnp.dot(
            row_ref[:, cut : cut + last], last_piece[...], preferred_element_type=jnp.float32
        )
        first = first + jnp.dot(
            last_ref[:, (back - 1) * last : back * last],
            last_piece[...],
            preferred_element_type=jnp.float32,
        )
    for step, out in enumerate(outs[:-1]):
        out[...] = first[step * each : (step + 1) * each].astype(out.dtype)
    outs[-1][...] = final.astype(outs[-1].dtype)


def finish_kernel(cores, teams, scale_ref, *refs):
    parts, (sent_ref, own_ref) = refs[:-2], refs[-2:]
    span, count = sent_ref.shape[0], own_ref.shape[0]
    pre_share, dec_share = span // cores, count // cores
    both = pre_share + dec_share
    band = scale_ref.shape[1] // teams
    for turn in range(teams):
        columns = band_columns(teams, turn, band)
        own, *others = parts[turn * len(parts) // teams : (turn + 1) * len(parts) // teams]
        summed = own[...]
        for part in others:
            summed = summed + part[...].astype(jnp.float32)
        done = (summed * scale_ref[:, columns]).astype(jnp.bfloat16)
        for share in range(cores):
            which = (lax.axis_index("tp") - share + cores) % cores
            rows = pl.ds(pl.multiple_of(which * pre_share, 16), pre_share)
            sent_ref[rows, columns] = done[share * both : share * both + pre_share]
            own_ref[pl.ds(pl.multiple_of(which * dec_share, 16), dec_share), columns] = done[
                share * both + pre_share : (share + 1) * both
            ]


def match_rows(owner_ref, len_ref, samples_ref, count):
    row = lax.axis_index("dp") * count + lax.broadcasted_iota(jnp.int32, (count, 1), 0)
    source = jnp.zeros((count, 1), jnp.int32)
    live = jnp.zeros((count, 1), jnp.int32)
    for prompt in range(samples_ref.shape[0]):
        hit = jnp.max(
            jnp.where(samples_ref[prompt : prompt + 1, :] == row, 1, 0), -1, keepdims=True
        )
        source = source + hit * owner_ref[prompt]
        live = live + hit * len_ref[prompt]
    return source, live


def absorb(owners, q_ref, source, live, head, blocks, top, mixed, own_ref):
    count, span = q_ref.shape[0], blocks[0].shape[0]
    factor = 1.0 / math.sqrt(HD)
    first = head * REP * HD
    low, mid, high = head * 2 * HD, head * 2 * HD + HD, head * 2 * HD + 2 * HD
    q = jnp.concatenate([q_ref[:, first + r * HD : first + (r + 1) * HD] for r in range(REP)], 0)
    picked = jnp.full((REP * count, span), NEG, jnp.float32)
    place = lax.broadcasted_iota(jnp.int32, (REP * count, span), 1)
    pairs = [slice(at, at + 2) for at in range(0, len(blocks), 2)]
    for pair in pairs:
        scores = lax.dot_general(
            q,
            jnp.concatenate([block[:, low:mid] for block in blocks[pair]], 0),
            (((1,), (1,)), ((), ())),
            preferred_element_type=jnp.float32,
        )
        for at, owner in enumerate(owners[pair]):
            mine = scores[:, at * span : (at + 1) * span]
            picked = jnp.where(source == owner, mine * factor, picked)
    picked = jnp.where(place < live, picked, NEG)
    new = jnp.maximum(jnp.max(picked, -1, keepdims=True), top)
    if own_ref is not None:
        own_k = jnp.concatenate([own_ref[:, low:mid].astype(jnp.float32)] * REP, 0)
        own_v = jnp.concatenate([own_ref[:, mid:high].astype(jnp.float32)] * REP, 0)
        score = jnp.sum(q.astype(jnp.float32) * own_k, -1, keepdims=True) * factor
        new = jnp.maximum(new, score)
    weights = jnp.exp(picked - new)
    kept = jnp.exp(top - new)
    total = kept + jnp.sum(weights, -1, keepdims=True)
    mixed = mixed * kept
    if own_ref is not None:
        weight = jnp.exp(score - new)
        total = total + weight
        mixed = mixed + weight * own_v
    for pair in pairs:
        shares = [jnp.where(source == owner, weights, 0.0) for owner in owners[pair]]
        mixed = mixed + jnp.dot(
            jnp.concatenate(shares, 1).astype(jnp.bfloat16),
            jnp.concatenate([block[:, mid:high] for block in blocks[pair]], 0),
            preferred_element_type=jnp.float32,
        )
    return new + jnp.log(total), mixed / total


def cache_kernel(heads, len_ref, q_ref, cache_ref, top_ref, mixed_ref, query_ref):
    count, rows = cache_ref.shape[0], heads * REP
    factor = 1.0 / math.sqrt(HD)

    @pl.when(pl.program_id(0) == 0)
    def _():
        query = [q_ref[:, r * HD : (r + 1) * HD].astype(jnp.float32) for r in range(rows)]
        query_ref[...] = jnp.swapaxes(jnp.stack(query), 0, 1)

    query = query_ref[pl.ds(pl.program_id(0) * count, count)].astype(jnp.bfloat16)
    head_of = lax.broadcasted_iota(jnp.int32, (rows, 1), 0) // REP
    spot = lax.broadcasted_iota(jnp.int32, (rows, cache_ref.shape[1]), 1)
    tops, mixes = [], []
    for sample in range(count):
        length = len_ref[pl.program_id(0) * count + sample]
        scores = mixed = None
        for head in range(heads):
            key = cache_ref[sample, :, head * 2 * HD : head * 2 * HD + HD]
            found = lax.dot_general(
                query[sample], key, (((1,), (1,)), ((), ())), preferred_element_type=jnp.float32
            )
            scores = found if head == 0 else jnp.where(head_of == head, found, scores)
        scores = jnp.where(spot < length, scores * factor, NEG)
        top = jnp.max(scores, -1, keepdims=True)
        weights = jnp.exp(scores - top)
        total = jnp.sum(weights, -1, keepdims=True)
        for head in range(heads):
            value = cache_ref[sample, :, head * 2 * HD + HD : (head + 1) * 2 * HD]
            found = jnp.dot(
                weights.astype(jnp.bfloat16), value, preferred_element_type=jnp.float32
            )
            mixed = found if head == 0 else jnp.where(head_of == head, found, mixed)
        tops.append(jnp.broadcast_to(top + jnp.log(total), (rows, HD)))
        mixes.append(mixed / total)
    top_ref[...] = jnp.swapaxes(jnp.stack(tops), 0, 1)
    mixed_ref[...] = jnp.swapaxes(jnp.stack(mixes), 0, 1)


def cached(query, cache, cache_len, heads):
    count, slots, width = cache.shape
    rows, each = heads * REP, 8
    state = jax.ShapeDtypeStruct((rows, count, HD), jnp.float32)
    return pl.pallas_call(
        functools.partial(cache_kernel, heads),
        grid=(count // each,),
        out_shape=[state, state],
        in_specs=[
            SMEM,
            pl.BlockSpec((count, rows * HD), lambda i: (0, 0)),
            pl.BlockSpec((each, slots, width), lambda i: (i, 0, 0)),
        ],
        out_specs=[pl.BlockSpec((rows, each, HD), lambda i: (0, i, 0))] * 2,
        scratch_shapes=[pltpu.VMEM((count, rows, HD), jnp.float32)],
        compiler_params=grant(12),
        cost_estimate=pl.CostEstimate(
            flops=4 * count * rows * slots * HD * heads,
            bytes_accessed=2 * cache.size,
            transcendentals=count * rows * slots,
        ),
    )(cache_len, query, cache)


def first_kernel(
    heads, owners, owner_ref, len_ref, samples_ref, q_ref, top_ref, mixed_ref, own_ref, *refs
):
    blocks, (new_top, new_mixed, source_ref, live_ref, prompt_ref) = refs[:-5], refs[-5:]
    prompt_ref[...] = blocks[0][...]
    source, live = match_rows(owner_ref, len_ref, samples_ref, q_ref.shape[0])
    source = jnp.concatenate([source] * REP, 0)
    live = jnp.concatenate([live] * REP, 0)
    source_ref[...] = jnp.broadcast_to(source, source_ref.shape)
    live_ref[...] = jnp.broadcast_to(live, live_ref.shape)
    for head in range(heads):
        mine = slice(head * REP, (head + 1) * REP)
        top = top_ref[mine].reshape(new_top.shape[1:])
        mixed = mixed_ref[mine].reshape(new_top.shape[1:])
        new_top[head], new_mixed[head] = absorb(
            owners(), q_ref, source, live, head, blocks, top, mixed, own_ref
        )


def second_kernel(heads, owners, q_ref, source_ref, live_ref, top_ref, mixed_ref, *refs):
    blocks, out_ref = refs[:-1], refs[-1]
    count = q_ref.shape[0]
    for head in range(heads):
        _, mixed = absorb(
            owners(),
            q_ref,
            source_ref[...],
            live_ref[...],
            head,
            blocks,
            top_ref[head],
            mixed_ref[head],
            None,
        )
        first = head * REP * HD
        for r in range(REP):
            out_ref[:, first + r * HD : first + (r + 1) * HD] = mixed[
                r * count : (r + 1) * count
            ].astype(out_ref.dtype)


VMEM = pl.BlockSpec(memory_space=pltpu.VMEM)
SMEM = pl.BlockSpec(memory_space=pltpu.SMEM)
HBM = pl.BlockSpec(memory_space=pltpu.HBM)


def after(value, *others):
    return lax.optimization_barrier((value, *others))[0]


def grant(mib):
    return pltpu.CompilerParams(vmem_limit_bytes=mib * 1024 * 1024)


def stages(depth):
    unit = 128
    first = max(unit, depth * 7 // 12 // unit * unit)
    return (first, depth - first)


def local(
    pre_x,
    dec_x,
    w_kv,
    kv_scale,
    dec_q,
    cache,
    cache_len,
    prompt_owner,
    prompt_len,
    sample_rows,
    *,
    shape,
):
    teams, ranks, cores = shape["groups"], shape["dp"], shape["tp"]
    inner = INNER
    outer = ranks // inner
    span, features = pre_x.shape
    count = dec_x.shape[0]
    depth, width = w_kv.shape
    heads = width // (2 * HD)
    band = width // teams

    def to_inner(value, step):
        pairs = [(r, r // inner * inner + (r % inner ^ step)) for r in range(ranks)]
        return lax.ppermute(value, "dp", pairs)

    def to_outer(value, step=1):
        pairs = [(r, (r + step * inner) % ranks) for r in range(ranks)]
        return lax.ppermute(value, "dp", pairs)

    def to_team(value, step):
        return lax.ppermute(value, "groups", [(i, (i + step) % teams) for i in range(teams)])

    def to_core(value, step):
        return lax.ppermute(value, "tp", [(i, (i + step) % cores) for i in range(cores)])

    def pack(plan, places, shapes, mib, *arrays):
        sems = pltpu.SemaphoreType.DMA((len(plan),))
        return pl.pallas_call(
            functools.partial(pack_kernel, plan, places, len(arrays), len(shapes)),
            out_shape=shapes,
            in_specs=[HBM] * len(arrays),
            out_specs=[HBM] * len(shapes),
            scratch_shapes=[pltpu.VMEM(s.shape, s.dtype) for s in shapes] + [sems, sems],
            compiler_params=grant(mib),
        )(*arrays)

    sizes = stages(depth)
    pre_share, dec_share = span // cores, count // cores
    both = pre_share + dec_share
    def features(back, step):
        rank = lax.axis_index("dp")
        return ((rank // inner - back + outer) % outer * inner + (rank % inner ^ step)) * depth

    def band_place():
        return [0, lax.axis_index("groups") * band]

    shape = jax.ShapeDtypeStruct((sizes[0], band), jnp.bfloat16)
    (first_piece,) = pack([(0, (sizes[0], band), 0, 1, 0, 0, 0)], band_place, [shape], 56, w_kv)
    first_piece, pre_x, dec_x, w_kv = lax.optimization_barrier((first_piece, pre_x, dec_x, w_kv))

    plan = [(2, (sizes[1], band), 0, 1, 0, 0, 0)]
    shapes = [jax.ShapeDtypeStruct((sizes[1], band), jnp.bfloat16)]
    for number in range(inner - 1):
        for back in range(outer):
            column, to = 4 + number * outer + back, back * depth
            plan.append((0, (pre_share, depth), 2, column, len(shapes), 0, to))
            plan.append((1, (dec_share, depth), 3, column, len(shapes), pre_share, to))
        shapes.append(jax.ShapeDtypeStruct((both, outer * depth), jnp.bfloat16))

    def send_places():
        core = lax.axis_index("tp")
        at = [sizes[0], lax.axis_index("groups") * band, core * pre_share, core * dec_share]
        return at + [features(back, step) for step in STEPS for back in range(outer)]

    last_piece, *row_sends = pack(plan, send_places, shapes, 56, pre_x, dec_x, w_kv)
    moving = [first_piece, last_piece]
    row_sends, query, pre_x, dec_x = lax.optimization_barrier((row_sends, dec_q, pre_x, dec_x))

    plan = []
    for back in range(outer):
        for turn in range(cores):
            column, to, base = 2 * cores + back, back * depth, turn * both
            plan.append((0, (pre_share, depth), 2 * turn, column, 0, base, to))
            plan.append((1, (dec_share, depth), 2 * turn + 1, column, 0, base + pre_share, to))

    def own_places():
        core, at = lax.axis_index("tp"), []
        for turn in range(cores):
            which = (core - turn + cores) % cores
            at += [which * pre_share, which * dec_share]
        return at + [features(back, 0) for back in range(outer)]

    total_rows = span + count
    shapes = [jax.ShapeDtypeStruct((total_rows, outer * depth), jnp.bfloat16)]
    (own_rows,) = pack(plan, own_places, shapes, 4, pre_x, dec_x)

    top_c, mixed_c = cached(query, cache, cache_len, heads)
    far = []
    for back in range(1, outer):
        moving = [to_outer(m) for m in moving]
        if back == 1:
            row_sends[-1] = after(row_sends[-1], moving[0], top_c, own_rows)
        far.append([[m] for m in moving])

    got = [to_inner(rows, step) for rows, step in zip(row_sends, STEPS)]
    arrived = [[rows] + [to_core(rows, turn) for turn in range(1, cores)] for rows in got]

    for pieces in far:
        for number, piece in enumerate(pieces):
            if number:
                sent = after(piece[0], pieces[number - 1][-1])
            else:
                sent = piece[0]
            piece += [to_team(sent, turn) for turn in range(1, teams)]

    last = sizes[-1]
    own_rows = after(own_rows, got[-1])
    blocks = [own_rows] + [rows for step in arrived[:-1] for rows in step]
    early = [m for pieces in far for m in pieces[0]]
    first_rows = (inner - 1) * total_rows
    *summed, last_rows = pl.pallas_call(
        functools.partial(early_kernel, outer, teams, last),
        out_shape=[
            *[jax.ShapeDtypeStruct((first_rows, band), jnp.float32)] * teams,
            jax.ShapeDtypeStruct((first_rows, (outer - 1) * last), jnp.bfloat16),
        ],
        in_specs=[VMEM] * (1 + len(early) + len(blocks)),
        out_specs=[VMEM] * (1 + teams),
        scratch_shapes=[
            pltpu.VMEM((first_rows, outer * depth - (outer - 1) * last), jnp.bfloat16)
        ],
        compiler_params=grant(16),
    )(w_kv, *early, *blocks)
    parts = []
    for turn in range(teams):
        pieces = [piece[turn] for some in far for piece in some]
        mine, *others = pl.pallas_call(
            functools.partial(late_kernel, outer, cores, teams, turn),
            out_shape=[jax.ShapeDtypeStruct((total_rows, band), jnp.float32)]
            + [jax.ShapeDtypeStruct((total_rows, band), jnp.bfloat16)] * (inner - 1),
            in_specs=[VMEM] * (3 + len(pieces) + cores),
            out_specs=[VMEM] * inner,
            scratch_shapes=[pltpu.VMEM((total_rows, outer * depth), jnp.bfloat16)],
            compiler_params=grant(12),
        )(w_kv, summed[turn], last_rows, *pieces, *arrived[-1])
        sent = [to_inner(part, step) for part, step in zip(others[::-1], STEPS[::-1])]
        parts += [mine, *sent]
    shifted, own_kv = pl.pallas_call(
        functools.partial(finish_kernel, cores, teams),
        out_shape=[
            jax.ShapeDtypeStruct((span, width), jnp.bfloat16),
            jax.ShapeDtypeStruct((count, width), jnp.bfloat16),
        ],
        in_specs=[VMEM] * (1 + len(parts)),
        out_specs=[VMEM] * 2,
        compiler_params=grant(6),
    )(kv_scale[None, :], *parts)

    def owners(backs):
        rank = lax.axis_index("dp")
        return [
            (rank // inner - back + outer) % outer * inner + (rank % inner ^ step)
            for back in backs
            for step in ((0, 3, 2, 1) if back else range(inner))
        ]

    blocks = []
    for back in range(outer):
        if back:
            shifted = to_outer(shifted)
        if back:
            blocks += [to_inner(shifted, step) if step else shifted for step in (0, 3, 2, 1)]
        else:
            near = [shifted, to_inner(shifted, 1), to_inner(shifted, 2)]
            blocks += near + [to_inner(after(near[2], near[1]), 1)]

    state = jax.ShapeDtypeStruct((heads, REP * count, HD), jnp.float32)
    labels = jax.ShapeDtypeStruct((REP * count, HD), jnp.int32)
    *state, source, live, prompt_kv = pl.pallas_call(
        functools.partial(first_kernel, heads, lambda: owners([0])[:3] + owners([1])[:1]),
        out_shape=[state, state, labels, labels, jax.ShapeDtypeStruct((span, width), jnp.bfloat16)],
        in_specs=[SMEM] * 2 + [VMEM] * (3 + 4 + 2),
        out_specs=[VMEM] * 5,
        compiler_params=grant(12),
    )(
        prompt_owner,
        prompt_len,
        sample_rows,
        dec_q,
        top_c,
        mixed_c,
        own_kv,
        *blocks[:3],
        blocks[4],
    )
    attended = pl.pallas_call(
        functools.partial(second_kernel, heads, lambda: owners([0])[3:] + owners(range(1, outer))[1:]),
        out_shape=jax.ShapeDtypeStruct(dec_q.shape, jnp.bfloat16),
        in_specs=[VMEM] * (5 + len(blocks) - 4),
        out_specs=VMEM,
        compiler_params=grant(12),
    )(dec_q, source, live, *state, blocks[3], *blocks[5:])
    return (attended, prompt_kv)


def solution(mesh):
    in_specs = (
        P(("groups", "dp"), None),
        P(("groups", "dp"), None),
        P("dp", "tp"),
        P("tp"),
        P(("groups", "dp"), "tp"),
        P(("groups", "dp"), None, "tp"),
        P(("groups", "dp")),
        P("groups"),
        P("groups"),
        P("groups", None),
    )
    out_specs = (P(("groups", "dp"), "tp"), P(("groups", "dp"), "tp"))
    body = functools.partial(local, shape=dict(mesh.shape))
    return jax.shard_map(body, mesh=mesh, in_specs=in_specs, out_specs=out_specs, check_vma=False)
```
